32 devices in a mesh: dp: 8 (over y, x, core), tensor: 4 (over z).
Axes of the slice: x: 2, y: 2, z: 4, core: 2. Of those that a mesh axis runs over, the one named last changes fastest.
Arguments:
- tokens: bfloat16 [8192, 2048], P(('dp', 'tensor')), may hold values from -6 to 6
- qkv_weight: bfloat16 [3, 2048, 2048], P(None, 'dp', 'tensor'), may hold values from -0.125 to 0.125
- qkv_bias: bfloat16 [3, 2048], P(None, ('tensor', 'dp')), may hold values from -4 to 4
- out_weight: bfloat16 [2048, 2048], P('tensor', 'dp'), may hold values from -1 to 1
- norm1_gain: bfloat16 [2048], P('dp'), may hold values from 0.5 to 1.5
- norm1_shift: bfloat16 [2048], P('dp'), may hold values from -4 to 4
- gate_weight: bfloat16 [2048, 5632], P('dp', 'tensor'), may hold values from -0.125 to 0.125
- up_weight: bfloat16 [2048, 5632], P('dp', 'tensor'), may hold values from -0.125 to 0.125
- down_weight: bfloat16 [5632, 2048], P('tensor', 'dp'), may hold values from -0.078125 to 0.078125
- norm2_gain: bfloat16 [2048], P('dp'), may hold values from 0.5 to 1.5
- norm2_shift: bfloat16 [2048], P('dp'), may hold values from -4 to 4
- cotangent: bfloat16 [8192, 2048], P(('dp', 'tensor')), may hold values from -6 to 6
Outputs:
- layer_output: bfloat16 [8192, 2048], P(('dp', 'tensor'))
- token_gradient: bfloat16 [8192, 2048], P(('dp', 'tensor'))
- qkvw_grad: float32 [3, 2048, 2048], P(None, 'dp', 'tensor')
- qkvb_grad: float32 [3, 2048], P(None, ('tensor', 'dp'))
- outw_grad: float32 [2048, 2048], P('tensor', 'dp')
- gain1_grad: float32 [2048], P('dp')
- shift1_grad: float32 [2048], P('dp')
- gatew_grad: float32 [2048, 5632], P('dp', 'tensor')
- upw_grad: float32 [2048, 5632], P('dp', 'tensor')
- downw_grad: float32 [5632, 2048], P('tensor', 'dp')
- gain2_grad: float32 [2048], P('dp')
- shift2_grad: float32 [2048], P('dp')
The draws below stay inside these ranges and needn't reach their ends.
All inputs are finite; a program needn't handle non-finite values.
Results may differ from the reference program's by a relative error of at most 0.035.
Values may be sent and summed in bfloat16 or wider, within the bound.
A program may use at most 192 MiB of HBM per device.

```python
import jax
import jax.numpy as jnp
from jax import lax

D = 2048
HEADS = 32
HEAD_DIM = 64
ROT = 16
FF = 5632
SEQ = 1024
TOKENS = 8192
N_DP = 8


def steps_of(stream_key, dims, cuts, smallest, top_value):
    factor_of = 1.0
    for position, blocks in cuts:
        steps = jax.random.uniform(jax.random.fold_in(jax.random.fold_in(stream_key, 6), position), (blocks,), jnp.float32, smallest / len(cuts), top_value / len(cuts))
        factor_of = factor_of * jnp.repeat(jnp.exp(steps), dims[position] // blocks).reshape((-1,) + (1,) * (len(dims) - 1 - position))
    return factor_of


def centred(rng, extent, deviation, bound, shards=(), kind=jnp.bfloat16):
    array = jax.random.normal(rng, extent, jnp.float32) * deviation
    if len(shards) > 0:
        array = steps_of(rng, extent, shards, -0.22, 0.18) * array
    return jnp.clip(array, min=-bound, max=bound).astype(kind)


def setup_inputs(seed: int = 0) -> dict:
    seeds = jax.random.split(jax.random.key(seed), 13)
    return {
        "tokens": centred(seeds[0], (TOKENS, D), 1.0, 6.0, ((0, 32),)),
        "qkv_weight": centred(seeds[1], (3, D, HEADS * HEAD_DIM), D ** -0.5, 0.125, ((1, 8), (2, 4))),
        "qkv_bias": centred(seeds[2], (3, HEADS * HEAD_DIM), 0.3, 4.0, ((1, 32),)),
        "out_weight": centred(seeds[3], (HEADS * HEAD_DIM, D), (max(HEADS * HEAD_DIM // 64, 1)) ** -0.5, 1.0, ((0, 4), (1, 8))),
        "norm1_gain": jnp.clip(1.0 + 0.1 * jax.random.normal(seeds[4], (D,), jnp.float32), 0.5, 1.5).astype(jnp.bfloat16),
        "norm1_shift": centred(seeds[5], (D,), 0.3, 4.0, ((0, 8),)),
        "gate_weight": centred(seeds[6], (D, FF), D ** -0.5, 0.125, ((0, 8), (1, 4))),
        "up_weight": centred(seeds[7], (D, FF), D ** -0.5, 0.125, ((0, 8), (1, 4))),
        "down_weight": centred(seeds[8], (FF, D), FF ** -0.5, 0.078125, ((0, 4), (1, 8))),
        "norm2_gain": jnp.clip(1.0 + 0.1 * jax.random.normal(seeds[9], (D,), jnp.float32), 0.5, 1.5).astype(jnp.bfloat16),
        "norm2_shift": centred(seeds[10], (D,), 0.3, 4.0, ((0, 8),)),
        "cotangent": centred(seeds[11], (TOKENS, D), 1.0, 6.0, ((0, 32),)),
    }


@jax.custom_vjp
def low(v):
    return lax.optimization_barrier(v.astype(jnp.bfloat16)).astype(jnp.float32)

@jax.custom_vjp
def low_back(v):
    return v

def low_keep(v):
    return (low(v), None)

def low_pass(kept, output_gradient):
    return (output_gradient,)

def back_keep(v):
    return (v, None)

def back_low(kept, output_gradient):
    return (low(output_gradient),)
low.defvjp(low_keep, low_pass)
low_back.defvjp(back_keep, back_low)

def apply_layer_norm(value, norm_scale, norm_bias):
    centered_input = value - lax.optimization_barrier(jnp.mean(value, -1, keepdims=True))
    spread = lax.optimization_barrier(jnp.mean(centered_input * centered_input, -1, keepdims=True))
    return centered_input * lax.rsqrt(spread + 1e-05) * norm_scale + norm_bias

def tables(length):
    positions = jnp.arange(length, dtype=jnp.float32)
    freqs = 10000.0 ** (-jnp.arange(0, ROT, 2, dtype=jnp.float32) / ROT)
    angles = positions[:, None] * freqs[None, :]
    angles = jnp.concatenate([angles, angles], -1)
    return (jnp.cos(angles), jnp.sin(angles))

def rotate(heads, cosine, sine):
    half = ROT // 2
    part = heads[..., :ROT]
    turned = jnp.concatenate([-part[..., half:], part[..., :half]], -1)
    moved = part * cosine[:, None, :] + turned * sine[:, None, :]
    return jnp.concatenate([moved, heads[..., ROT:]], -1)

def layer(input_rows, qkv_w, qkv_b, out_w, first_norm_scale, first_norm_bias, gate_w, up_w, down_w, second_norm_scale, second_norm_bias):
    high = lax.Precision.HIGHEST
    length = input_rows.shape[0]
    scale = HEAD_DIM ** (-0.5)
    normed = low(apply_layer_norm(input_rows, first_norm_scale, first_norm_bias))
    pre = jnp.einsum('sd,jdc->jsc', normed, qkv_w, precision=high) + qkv_b[:, None, :]
    pre = low_back(pre)
    cosine, sine = tables(length)
    query = low(rotate(pre[0].reshape(length, HEADS, HEAD_DIM), cosine, sine))
    keys = low(rotate(pre[1].reshape(length, HEADS, HEAD_DIM), cosine, sine))
    values = low(pre[2].reshape(length, HEADS, HEAD_DIM))
    block = min(length, 512)
    count = length // block

    def attend(item):
        qblock, start = item
        scores = jnp.einsum('qhd,khd->hqk', qblock, keys, precision=high) * scale
        scores = low_back(scores)
        rows = start + jnp.arange(block, dtype=jnp.int32)
        cols = jnp.arange(length, dtype=jnp.int32)
        keep = rows[:, None] >= cols[None, :]
        scores = jnp.where(keep[None], scores, -1e+30)
        most = lax.optimization_barrier(jnp.max(scores, -1, keepdims=True))
        expo = jnp.exp(scores - most)
        probs = low(expo / lax.optimization_barrier(jnp.sum(expo, -1, keepdims=True)))
        return jnp.einsum('hqk,khd->qhd', probs, values, precision=high)
    starts = jnp.arange(count, dtype=jnp.int32) * block
    attended = lax.map(jax.checkpoint(attend), (query.reshape(count, block, HEADS, HEAD_DIM), starts))
    attended = low_back(low(attended.reshape(length, HEADS * HEAD_DIM)))
    branch = jnp.dot(attended, out_w, precision=high, preferred_element_type=jnp.float32)
    hidden_state = input_rows + low_back(branch)
    second_normed_rows = low(apply_layer_norm(hidden_state, second_norm_scale, second_norm_bias))
    gate = low_back(jnp.dot(second_normed_rows, gate_w, precision=high, preferred_element_type=jnp.float32))
    up = low_back(jnp.dot(second_normed_rows, up_w, precision=high, preferred_element_type=jnp.float32))
    act = low(jax.nn.silu(gate) * up)
    mixed = jnp.dot(act, down_w, precision=high, preferred_element_type=jnp.float32)
    return hidden_state + low_back(mixed)

def reference(tokens, qkv_weight, qkv_bias, out_weight, norm1_gain, norm1_shift, gate_weight, up_weight, down_weight, norm2_gain, norm2_shift, cotangent):
    params = (qkv_weight.astype(jnp.float32), qkv_bias.astype(jnp.float32), out_weight.astype(jnp.float32), norm1_gain.astype(jnp.float32), norm1_shift.astype(jnp.float32), gate_weight.astype(jnp.float32), up_weight.astype(jnp.float32), down_weight.astype(jnp.float32), norm2_gain.astype(jnp.float32), norm2_shift.astype(jnp.float32))
    input_rows = tokens.astype(jnp.float32).reshape(N_DP, SEQ, D)
    cots = cotangent.astype(jnp.float32).reshape(N_DP, SEQ, D)

    def step(carry, item):
        single, single_cot = item
        result, pull = jax.vjp(layer, single, *params)
        grads = pull(single_cot)
        carry = tuple((total + output_gradient for total, output_gradient in zip(carry, grads[1:])))
        return (carry, (result, grads[0]))
    zeros = tuple((jnp.zeros_like(param) for param in params))
    totals, (results, input_grads) = lax.scan(step, zeros, (input_rows, cots))
    return (results.reshape(TOKENS, D).astype(jnp.bfloat16), input_grads.reshape(TOKENS, D).astype(jnp.bfloat16), totals[0], totals[1], totals[2], totals[3], totals[4], totals[5], totals[6], totals[7], totals[8], totals[9])
```

```python
import functools

import jax
import jax.numpy as jnp
from jax import lax
from jax.experimental import pallas as pl
from jax.experimental.pallas import tpu as pltpu
from jax.sharding import PartitionSpec as P

MESH = pl.DeviceIdType.MESH
HEAD_DIM = 64
ROT = 16
BF = jnp.bfloat16
F32 = jnp.float32
VMEM_LIMIT = 56 * 1024 * 1024
ANY = pl.BlockSpec(memory_space=pl.ANY)
INV = pl.BlockSpec(memory_space=pltpu.VMEM)


def nt(a, b):
    return lax.dot_general(a, b, (((1,), (1,)), ((), ())), preferred_element_type=F32)


def tn(a, b):
    return lax.dot_general(a, b, (((0,), (0,)), ((), ())), preferred_element_type=F32)


def nn(a, b):
    return jnp.dot(a, b, preferred_element_type=F32)


def place():
    d = lax.axis_index("dp")
    z = lax.axis_index("tensor")
    dy = 4 * (1 - 2 * lax.div(d, 4))
    dx = 2 * (1 - 2 * lax.rem(lax.div(d, 2), 2))
    dc = 1 - 2 * lax.rem(d, 2)
    return d, z, (0, dc, dx, dx + dc, dy, dy + dc, dy + dx, dy + dx + dc)


def send(src, dst, ssem, rsem, d, z):
    return pltpu.make_async_remote_copy(
        src_ref=src, dst_ref=dst, send_sem=ssem, recv_sem=rsem, device_id=(d, z), device_id_type=MESH
    )


def greet(d, z, flips, line, plane):
    barrier = pltpu.get_barrier_semaphore()
    for k in range(1, line):
        pl.semaphore_signal(
            barrier, inc=1, device_id=(d, lax.rem(z + k, line)), device_id_type=MESH
        )
    for r in plane:
        pl.semaphore_signal(barrier, inc=1, device_id=(d + flips[r], z), device_id_type=MESH)
    pl.semaphore_wait(barrier, line - 1 + len(plane))


class LineGather:
    def __init__(self, view, chunks, d, z, line, send_sems, recv_sems):
        self.view, self.chunks, self.d, self.z, self.line = view, chunks, d, z, line
        self.ss, self.rs = send_sems, recv_sems

    def copy(self, s, h, way, src=None):
        ref = self.view(s, h)
        return send(
            ref if src is None else src, ref, self.ss.at[way, s, h], self.rs.at[s, h],
            self.d, self.z + (1 if way == 0 else -1),
        )

    def start(self, h, src=None):
        pl.when(self.z < self.line - 1)(lambda: self.copy(self.z, h, 0, src).start())
        pl.when(self.z > 0)(lambda: self.copy(self.z, h, 1, src).start())

    def step(self, k, h):
        z, line = self.z, self.line

        @pl.when(z - k >= 0)
        def _():
            self.copy(z - k, h, 0).wait_recv()
            pl.when(z < line - 1)(lambda: self.copy(z - k, h, 0).start())

        @pl.when(z + k < line)
        def _():
            self.copy(z + k, h, 1).wait_recv()
            pl.when(z > 0)(lambda: self.copy(z + k, h, 1).start())

    def finish(self):
        z, line = self.z, self.line
        for k in range(line):
            for h in range(self.chunks):
                pl.when((z - k >= 0) & (z < line - 1))(lambda: self.copy(z - k, h, 0).wait_send())
                pl.when((z + k < line) & (z > 0))(lambda: self.copy(z + k, h, 1).wait_send())


def arrival(z, i):
    orders = ((0, 1, 2, 3), (1, 0, 2, 3), (2, 3, 1, 0), (3, 2, 1, 0))
    codes = [sum(s * 4**j for j, s in enumerate(o)) for o in orders]
    code = jnp.where(
        z == 0, codes[0], jnp.where(z == 1, codes[1], jnp.where(z == 2, codes[2], codes[3]))
    )
    power = jnp.where(i == 0, 1, jnp.where(i == 1, 4, jnp.where(i == 2, 16, 64)))
    return lax.rem(lax.div(code, power), 4)


def turn(u, cos, sin_up, sin_down, sign=1.0):
    moved = pltpu.roll(u, 8, 1) * sin_up + pltpu.roll(u, 120, 1) * sin_down
    return u * cos + moved if sign > 0 else u * cos - moved


def attention_kernel(
    tok, cot, wq, smalls, cos, sin_up, sin_down,
    xall, cotall, n1, qkv, lse, attall, wqkv, small_sum,
    xbuf, n1buf, wbuf, qbuf, abuf, smbuf,
    tss, trs, css, crs, ass, ars, wss, wrs, mss, mrs, local,
):
    rows = tok.shape[0]
    width = wq.shape[2]
    pairs = width // 128
    line = 4
    d, z, flips = place()
    greet(d, z, flips, line, range(1, 8))

    tok_in = pltpu.make_async_copy(tok, xbuf.at[z], local.at[0])
    tok_in.start()
    cot_in = pltpu.make_async_copy(cot, cotall.at[pl.ds(z * rows, rows)], local.at[1])
    cot_in.start()
    depth = wq.shape[1]

    def wblock(i):
        return wbuf.at[:, pl.ds(pl.multiple_of(i * depth, 256), depth), :]

    w_in = pltpu.make_async_copy(wq, wblock(d), local.at[2])
    w_in.start()
    small_copies = [
        send(smalls, smbuf.at[r], mss.at[r], mrs.at[r], d + flips[r], z) for r in range(1, 8)
    ]
    for copy in small_copies:
        copy.start()
    w_sends = {
        r: send(wq, wblock(d), wss.at[r], wrs.at[r], d + flips[r], z) for r in (4, 2, 1, 6)
    }
    half = rows // 2

    def tview(s, h):
        return xbuf.at[s, pl.ds(h * half, half)]

    def cview(s, h):
        return cotall.at[pl.ds(pl.multiple_of(s * rows + h * half, 128), half)]

    def aview(s, h):
        return attall.at[:, pl.ds(pl.multiple_of(s * width + h * 128, 128), 128)]

    toks = LineGather(tview, 2, d, z, line, tss, trs)
    cots = LineGather(cview, 2, d, z, line, css, crs)
    atts = LineGather(aview, pairs, d, z, line, ass, ars)
    tok_in.wait()
    for h in range(2):
        toks.start(h)
    for copy in w_sends.values():
        copy.start()
    for copy in small_copies:
        copy.wait()
    total = smalls[...].astype(F32)
    for r in range(1, 8):
        total = total + smbuf[r].astype(F32)
    small_sum[...] = total

    def normalise(s):
        piece = 32

        @pl.loop(0, rows // piece)
        def _(i):
            at = pl.ds(pl.multiple_of(i * piece, piece), piece)
            x = xbuf[s, at, :].astype(F32)
            centred = x - jnp.mean(x, -1, keepdims=True)
            spread = jnp.mean(centred * centred, -1, keepdims=True)
            n = centred * lax.rsqrt(spread + 1e-05) * small_sum[0:1, :] + small_sum[1:2, :]
            n1buf[pl.ds(pl.multiple_of(s * rows + i * piece, piece), piece), :] = n.astype(BF)

    def project(s):
        at = pl.ds(pl.multiple_of(s * rows, rows), rows)
        for j in range(3):
            pre = nn(n1buf[at, :], wbuf[j]) + small_sum[4 + j : 5 + j, :width]
            for p in range(pairs):
                part = pre[:, p * 128 : (p + 1) * 128]
                if j < 2:
                    part = turn(part, cos[at, :], sin_up[at, :], sin_down[at, :])
                qbuf[j, p, at, :] = part.astype(BF)

    for h in range(2):
        toks.step(1, h)
    for r in (2, 4, 6):
        w_sends[r].wait_recv()
        send(wblock(d + flips[r]), wblock(d + flips[r]), wss.at[r + 1], wrs.at[r + 1], d + flips[1], z).start()
    w_in.wait()
    w_sends[1].wait_recv()
    for r in (3, 5, 7):
        send(wblock(d), wblock(d), wss.at[r], wrs.at[r], d + flips[1], z).wait_recv()

    @pl.loop(0, line)
    def _(i):
        @pl.when(i == line - 1)
        def _():
            cot_in.wait()
            for h in range(2):
                cots.start(h)

        s = arrival(z, i)
        normalise(s)
        project(s)

        @pl.when((i >= 1) & (i < line - 1))
        def _():
            for h in range(2):
                toks.step(i + 1, h)

    outs = [
        pltpu.make_async_copy(n1buf, n1, local.at[3]),
        pltpu.make_async_copy(wbuf, wqkv, local.at[4]),
        pltpu.make_async_copy(qbuf, qkv, local.at[5]),
    ] + [
        pltpu.make_async_copy(xbuf.at[s], xall.at[pl.ds(s * rows, rows)], local.at[6 + s])
        for s in range(line)
    ]
    for copy in outs:
        copy.start()

    lanes = lax.broadcasted_iota(jnp.int32, (1, 128), 1)
    first = lanes < 64
    lse[...] = jnp.zeros_like(lse)
    length = rows * line

    def attend(p, start):
        for qi in range(line):
            count = (qi + 1) * rows
            at = pl.ds(qi * rows, rows)
            q = qbuf[0, p, at, :] * BF(HEAD_DIM**-0.5)
            k = qbuf[1, p, pl.ds(0, count), :]
            v = qbuf[2, p, pl.ds(0, count), :]
            row = lax.broadcasted_iota(jnp.int32, (rows, count), 0) + qi * rows
            col = lax.broadcasted_iota(jnp.int32, (rows, count), 1)
            keep = row >= col
            results = []
            stats = lse[at, :]
            for a in range(2):
                mine = first if a == 0 else ~first
                s = nt(jnp.where(mine, q, BF(0)), k)
                s = jnp.where(keep, s, -1e30)
                most = jnp.max(s, -1, keepdims=True)
                e = jnp.exp(s - most)
                total = jnp.sum(e, -1, keepdims=True)
                results.append(nn(e.astype(BF), v) / total)
                stats = jnp.where(lanes == 2 * p + a, most + jnp.log(total), stats)
            lse[at, :] = stats
            abuf[p, at, :] = jnp.where(first, results[0], results[1]).astype(BF)

    def own_columns(p):
        return pltpu.make_async_copy(abuf.at[p], aview(z, p), local.at[10 + p])

    @pl.loop(0, pairs)
    def _(p):
        attend(p, None)
        own_columns(p).start()
        atts.start(p, abuf.at[p])

    for k in range(1, line):
        for h in range(2):
            cots.step(k, h)
        for p in range(pairs):
            atts.step(k, p)
    for gather in (toks, cots, atts):
        gather.finish()
    for r in range(1, 8):
        send(wblock(d), wblock(d), wss.at[r], wrs.at[r], d + flips[1], z).wait_send()
    for copy in outs:
        copy.wait()
    for p in range(pairs):
        own_columns(p).wait()


def attention_forward(tok, cot, wq, smalls, tabs):
    rows, model = tok.shape
    line = 4
    length = rows * line
    _, depth, width = wq.shape
    pairs = width // 128
    dp = model // depth
    sds = jax.ShapeDtypeStruct
    return pl.pallas_call(
        attention_kernel,
        out_shape=(
            sds((length, model), BF), sds((length, model), BF), sds((length, model), BF),
            sds((3, pairs, length, 128), BF), sds((length, 128), F32), sds((length, model), BF),
            sds((3, model, width), BF), sds((16, model), F32),
        ),
        in_specs=[ANY, ANY, ANY, INV, INV, INV, INV],
        out_specs=(ANY, ANY, ANY, ANY, INV, ANY, ANY, INV),
        scratch_shapes=[
            pltpu.VMEM((line, rows, model), BF),
            pltpu.VMEM((length, model), BF),
            pltpu.VMEM((3, model, width), BF),
            pltpu.VMEM((3, pairs, length, 128), BF),
            pltpu.VMEM((pairs, length, 128), BF),
            pltpu.VMEM((dp, 16, model), BF),
            pltpu.SemaphoreType.DMA((2, line, 2)),
            pltpu.SemaphoreType.DMA((line, 2)),
            pltpu.SemaphoreType.DMA((2, line, 2)),
            pltpu.SemaphoreType.DMA((line, 2)),
            pltpu.SemaphoreType.DMA((2, line, pairs)),
            pltpu.SemaphoreType.DMA((line, pairs)),
            pltpu.SemaphoreType.DMA((8,)),
            pltpu.SemaphoreType.DMA((8,)),
            pltpu.SemaphoreType.DMA((8,)),
            pltpu.SemaphoreType.DMA((8,)),
            pltpu.SemaphoreType.DMA((16,)),
        ],
        compiler_params=pltpu.CompilerParams(
            collective_id=1, has_side_effects=True, vmem_limit_bytes=VMEM_LIMIT
        ),
        cost_estimate=pl.CostEstimate(flops=2 * 10**11, bytes_accessed=10**8, transcendentals=0),
        name="attention_forward",
    )(tok, cot, wq, smalls, *tabs)


def apply_layer_norm(value, norm_scale, norm_bias):
    centered_input = value - jnp.mean(value, -1, keepdims=True)
    spread = jnp.mean(centered_input * centered_input, -1, keepdims=True)
    inverse_deviation = lax.rsqrt(spread + 1e-05)
    standardized_input = centered_input * inverse_deviation
    return (
        standardized_input * norm_scale.astype(jnp.float32) + norm_bias.astype(jnp.float32),
        standardized_input,
        inverse_deviation,
    )


def layer_norm_backward(output_gradient, standardized_input, inverse_deviation, norm_scale):
    scaled_gradient = output_gradient * norm_scale.astype(jnp.float32)
    return inverse_deviation * (
        scaled_gradient
        - jnp.mean(scaled_gradient, -1, keepdims=True)
        - standardized_input * jnp.mean(scaled_gradient * standardized_input, -1, keepdims=True)
    )


def tables(length):
    positions = jnp.arange(length, dtype=jnp.float32)
    freqs = 10000.0 ** (-jnp.arange(0, ROT, 2, dtype=jnp.float32) / ROT)
    angles = positions[:, None] * freqs[None, :]
    angles = jnp.concatenate([angles, angles], -1)
    return (jnp.cos(angles), jnp.sin(angles))


def rotate(heads, cosine, sine):
    half = ROT // 2
    part = heads[..., :ROT]
    turned = jnp.concatenate([-part[..., half:], part[..., :half]], -1)
    moved = part * cosine[:, None, :] + turned * sine[:, None, :]
    return jnp.concatenate([moved, heads[..., ROT:]], -1)


def unrotate(output_gradient, cosine, sine):
    half = ROT // 2
    part = output_gradient[..., :ROT]
    scaled_gradient = part * sine[:, None, :]
    back = jnp.concatenate([scaled_gradient[..., half:], -scaled_gradient[..., :half]], -1)
    moved = part * cosine[:, None, :] + back
    return jnp.concatenate([moved, output_gradient[..., ROT:]], -1)


def attn_params(qkv_weight, qkv_bias, out_weight, norm1_gain, norm1_shift):
    return (
        lax.all_gather(qkv_weight, "dp", axis=1, tiled=True),
        lax.all_gather(qkv_bias, "dp", axis=1, tiled=True),
        lax.all_gather(out_weight, "dp", axis=1, tiled=True),
        lax.all_gather(norm1_gain, "dp", axis=0, tiled=True),
        lax.all_gather(norm1_shift, "dp", axis=0, tiled=True),
    )


def mlp_params(gate_weight, up_weight, down_weight, norm2_gain, norm2_shift):
    return (
        lax.all_gather(gate_weight, "dp", axis=0, tiled=True),
        lax.all_gather(up_weight, "dp", axis=0, tiled=True),
        lax.all_gather(down_weight, "dp", axis=1, tiled=True),
        lax.all_gather(norm2_gain, "dp", axis=0, tiled=True),
        lax.all_gather(norm2_shift, "dp", axis=0, tiled=True),
    )


def gather_rows(rows):
    return lax.all_gather(rows, "tensor", axis=0, tiled=True)


def sum_rows(partial_value):
    return lax.psum_scatter(
        partial_value.astype(jnp.bfloat16), "tensor", scatter_dimension=0, tiled=True
    ).astype(jnp.float32)


def gather_grads(rows):
    return lax.all_gather(rows, "tensor", axis=0, tiled=True)


def sum_grads(partial_value):
    return lax.psum_scatter(
        partial_value.astype(jnp.bfloat16), "tensor", scatter_dimension=0, tiled=True
    ).astype(jnp.float32)


def local(
    tokens,
    qkv_weight,
    qkv_bias,
    out_weight,
    norm1_gain,
    norm1_shift,
    gate_weight,
    up_weight,
    down_weight,
    norm2_gain,
    norm2_shift,
    cotangent,
):
    scale = HEAD_DIM ** (-0.5)
    input_rows = tokens.astype(jnp.float32)
    wqkv, bqkv, wout, first_norm_scale, first_norm_bias = attn_params(
        qkv_weight, qkv_bias, out_weight, norm1_gain, norm1_shift
    )
    first_normed_rows, first_standardized, first_inverse_deviation = apply_layer_norm(
        input_rows, first_norm_scale, first_norm_bias
    )
    rows1 = gather_rows(first_normed_rows.astype(jnp.bfloat16))
    length = rows1.shape[0]
    width = wqkv.shape[2]
    local_heads = width // HEAD_DIM
    pre = (
        jnp.einsum("sd,jdc->jsc", rows1, wqkv, preferred_element_type=jnp.float32)
        + bqkv.astype(jnp.float32)[:, None, :]
    )
    cosine, sine = tables(length)
    query = rotate(pre[0].reshape(length, local_heads, HEAD_DIM), cosine, sine).astype(jnp.bfloat16)
    keys = rotate(pre[1].reshape(length, local_heads, HEAD_DIM), cosine, sine).astype(jnp.bfloat16)
    values = pre[2].reshape(length, local_heads, HEAD_DIM).astype(jnp.bfloat16)
    block = min(length, 512)
    count = length // block
    cols = jnp.arange(length, dtype=jnp.int32)

    def block_probs(qblock, start):
        scores = (
            jnp.einsum("qhd,khd->hqk", qblock, keys, preferred_element_type=jnp.float32) * scale
        )
        rows = start + jnp.arange(block, dtype=jnp.int32)
        keep = rows[:, None] >= cols[None, :]
        return jnp.where(keep[None], scores, -1e30)

    def forward_block(index):
        qblock = lax.dynamic_slice_in_dim(query, index * block, block, 0)
        scores = block_probs(qblock, index * block)
        most = jnp.max(scores, -1, keepdims=True)
        expo = jnp.exp(scores - most)
        total = jnp.sum(expo, -1, keepdims=True)
        probs = (expo / total).astype(jnp.bfloat16)
        out_block = jnp.einsum("hqk,khd->qhd", probs, values, preferred_element_type=jnp.float32)
        return (out_block.astype(jnp.bfloat16), most[..., 0] + jnp.log(total[..., 0]))

    indices = jnp.arange(count, dtype=jnp.int32)
    out_blocks, lse = lax.map(forward_block, indices)
    attended = out_blocks.reshape(length, width)
    branch = jnp.dot(attended, wout, preferred_element_type=jnp.float32)
    hidden_state = input_rows + sum_rows(branch)
    wgate, wup, wdown, second_norm_scale, second_norm_bias = mlp_params(
        gate_weight, up_weight, down_weight, norm2_gain, norm2_shift
    )
    second_normed_rows, second_standardized, second_inverse_deviation = apply_layer_norm(
        hidden_state, second_norm_scale, second_norm_bias
    )
    rows2 = gather_rows(second_normed_rows.astype(jnp.bfloat16))
    gate = jnp.dot(rows2, wgate, preferred_element_type=jnp.float32)
    up = jnp.dot(rows2, wup, preferred_element_type=jnp.float32)
    sigma = jax.nn.sigmoid(gate)
    silu = gate * sigma
    act = (silu * up).astype(jnp.bfloat16)
    mixed = sum_rows(jnp.dot(act, wdown, preferred_element_type=jnp.float32))
    layer_output = (hidden_state + mixed).astype(jnp.bfloat16)
    wgate, wup, wdown, second_norm_scale, second_norm_bias = mlp_params(
        gate_weight, up_weight, down_weight, norm2_gain, norm2_shift
    )
    incoming_gradient = cotangent.astype(jnp.float32)
    down_rows = gather_grads(cotangent)
    down_grad = jnp.einsum("sf,sd->fd", act, down_rows, preferred_element_type=jnp.float32)
    dact = jnp.einsum("sd,fd->sf", down_rows, wdown, preferred_element_type=jnp.float32)
    dgate = (dact * up * (sigma * (1.0 + gate * (1.0 - sigma)))).astype(jnp.bfloat16)
    dup = (dact * silu).astype(jnp.bfloat16)
    gate_grad = jnp.einsum("sd,sf->df", rows2, dgate, preferred_element_type=jnp.float32)
    up_grad = jnp.einsum("sd,sf->df", rows2, dup, preferred_element_type=jnp.float32)
    second_norm_gradient = jnp.einsum(
        "sf,df->sd", dgate, wgate, preferred_element_type=jnp.float32
    ) + jnp.einsum("sf,df->sd", dup, wup, preferred_element_type=jnp.float32)
    second_norm_gradient = sum_grads(second_norm_gradient)
    second_scale_partial = jnp.sum(second_norm_gradient * second_standardized, 0)
    shift2_part = jnp.sum(second_norm_gradient, 0)
    hidden_gradient = incoming_gradient + layer_norm_backward(
        second_norm_gradient, second_standardized, second_inverse_deviation, second_norm_scale
    )
    gatew_grad, upw_grad, downw_grad, gain2_total, shift2_total = (
        lax.psum_scatter(
            gate_grad.astype(jnp.bfloat16), "dp", scatter_dimension=0, tiled=True
        ).astype(jnp.float32),
        lax.psum_scatter(
            up_grad.astype(jnp.bfloat16), "dp", scatter_dimension=0, tiled=True
        ).astype(jnp.float32),
        lax.psum_scatter(
            down_grad.astype(jnp.bfloat16), "dp", scatter_dimension=1, tiled=True
        ).astype(jnp.float32),
        lax.psum_scatter(
            second_scale_partial.astype(jnp.bfloat16), "dp", scatter_dimension=0, tiled=True
        ).astype(jnp.float32),
        lax.psum_scatter(
            shift2_part.astype(jnp.bfloat16), "dp", scatter_dimension=0, tiled=True
        ).astype(jnp.float32),
    )
    wqkv, bqkv, wout, first_norm_scale, first_norm_bias = attn_params(
        qkv_weight, qkv_bias, out_weight, norm1_gain, norm1_shift
    )
    branch_rows = gather_grads(hidden_gradient.astype(jnp.bfloat16))
    out_grad = jnp.einsum("sc,sd->cd", attended, branch_rows, preferred_element_type=jnp.float32)
    dattended = jnp.einsum(
        "sd,cd->sc", branch_rows, wout, preferred_element_type=jnp.float32
    ).astype(jnp.bfloat16)
    dattended = dattended.reshape(length, local_heads, HEAD_DIM)

    def backward_block(carry, item):
        dkeys, dvalues = carry
        index, block_lse = item
        qblock = lax.dynamic_slice_in_dim(query, index * block, block, 0)
        dblock = lax.dynamic_slice_in_dim(dattended, index * block, block, 0)
        scores = block_probs(qblock, index * block)
        probs = jnp.exp(scores - block_lse[..., None])
        probs16 = probs.astype(jnp.bfloat16)
        dvalues = dvalues + jnp.einsum(
            "hqk,qhd->khd", probs16, dblock, preferred_element_type=jnp.float32
        )
        dprobs = jnp.einsum("qhd,khd->hqk", dblock, values, preferred_element_type=jnp.float32)
        inner = jnp.sum(dprobs * probs, -1, keepdims=True)
        dscores = (probs * (dprobs - inner)).astype(jnp.bfloat16)
        dquery = (
            jnp.einsum("hqk,khd->qhd", dscores, keys, preferred_element_type=jnp.float32) * scale
        )
        dkeys = (
            dkeys
            + jnp.einsum("hqk,qhd->khd", dscores, qblock, preferred_element_type=jnp.float32)
            * scale
        )
        return ((dkeys, dvalues), dquery)

    empty = jnp.zeros((length, local_heads, HEAD_DIM), jnp.float32)
    (dkeys, dvalues), dquery = lax.scan(backward_block, (empty, empty), (indices, lse))
    dquery = dquery.reshape(length, local_heads, HEAD_DIM)
    dpre = jnp.stack(
        [
            unrotate(dquery, cosine, sine).reshape(length, width),
            unrotate(dkeys, cosine, sine).reshape(length, width),
            dvalues.reshape(length, width),
        ],
        0,
    ).astype(jnp.bfloat16)
    qkv_grad = jnp.einsum("sd,jsc->jdc", rows1, dpre, preferred_element_type=jnp.float32)
    bias_grad = jnp.sum(dpre, axis=1, dtype=jnp.float32)
    first_norm_gradient = sum_grads(
        jnp.einsum("jsc,jdc->sd", dpre, wqkv, preferred_element_type=jnp.float32)
    )
    first_scale_partial = jnp.sum(first_norm_gradient * first_standardized, 0)
    shift1_part = jnp.sum(first_norm_gradient, 0)
    token_gradient = (
        hidden_gradient
        + layer_norm_backward(
            first_norm_gradient, first_standardized, first_inverse_deviation, first_norm_scale
        )
    ).astype(jnp.bfloat16)
    qkvw_grad, qkvb_grad, outw_grad, gain1_total, shift1_total = (
        lax.psum_scatter(
            qkv_grad.astype(jnp.bfloat16), "dp", scatter_dimension=1, tiled=True
        ).astype(jnp.float32),
        lax.psum_scatter(
            bias_grad.astype(jnp.bfloat16), "dp", scatter_dimension=1, tiled=True
        ).astype(jnp.float32),
        lax.psum_scatter(
            out_grad.astype(jnp.bfloat16), "dp", scatter_dimension=1, tiled=True
        ).astype(jnp.float32),
        lax.psum_scatter(
            first_scale_partial.astype(jnp.bfloat16), "dp", scatter_dimension=0, tiled=True
        ).astype(jnp.float32),
        lax.psum_scatter(
            shift1_part.astype(jnp.bfloat16), "dp", scatter_dimension=0, tiled=True
        ).astype(jnp.float32),
    )
    gain1_grad, shift1_grad, gain2_grad, shift2_grad = lax.psum(
        (gain1_total, shift1_total, gain2_total, shift2_total), "tensor"
    )
    return (
        layer_output,
        token_gradient,
        qkvw_grad,
        qkvb_grad,
        outw_grad,
        gain1_grad,
        shift1_grad,
        gatew_grad,
        upw_grad,
        downw_grad,
        gain2_grad,
        shift2_grad,
    )


def turn_tables(length):
    cosine, sine = tables(length)
    rest = HEAD_DIM - ROT
    half = ROT // 2
    cos = jnp.concatenate([cosine, jnp.ones((length, rest), F32)], -1)
    none = jnp.zeros((length, half), F32)
    tail = jnp.zeros((length, rest), F32)
    up = jnp.concatenate([none, sine[:, half:], tail], -1)
    down = jnp.concatenate([-sine[:, :half], none, tail], -1)
    return tuple(jnp.concatenate([t, t], -1) for t in (cos, up, down))


def pack_smalls(d, model, qkv_bias, *vectors):
    col = lax.broadcasted_iota(jnp.int32, (1, model), 1)
    each = vectors[0].shape[0]
    gains = jnp.stack([jnp.tile(v, model // each) for v in vectors], 0)
    gains = jnp.where(col // each == d, gains, 0)
    part = qkv_bias.shape[1]
    bias = jnp.where(col // part == d, jnp.tile(qkv_bias, (1, model // part)), 0)
    return jnp.concatenate([gains, bias, jnp.zeros((9, model), BF)], 0).astype(BF)


def fast(
    tokens, qkv_weight, qkv_bias, out_weight, norm1_gain, norm1_shift, gate_weight, up_weight,
    down_weight, norm2_gain, norm2_shift, cotangent,
):
    scale = HEAD_DIM ** (-0.5)
    d = lax.axis_index("dp")
    z = lax.axis_index("tensor")
    rows, model = tokens.shape
    length = 4 * rows
    tabs = turn_tables(length)
    smalls = pack_smalls(d, model, qkv_bias, norm1_gain, norm1_shift, norm2_gain, norm2_shift)
    xall, cotall, n1, qkv, lse, attall, wqkv, small_sum = attention_forward(
        tokens, cotangent, qkv_weight, smalls, tabs
    )
    wout = lax.all_gather(out_weight, "tensor", axis=0, tiled=True)
    wout = lax.all_gather(wout, "dp", axis=1, tiled=True)
    wgate = lax.all_gather(gate_weight, "dp", axis=0, tiled=True)
    wup = lax.all_gather(up_weight, "dp", axis=0, tiled=True)
    wdown = lax.all_gather(down_weight, "dp", axis=1, tiled=True)
    g1, b1, g2, b2 = small_sum[0], small_sum[1], small_sum[2], small_sum[3]

    def own(a):
        return lax.dynamic_slice_in_dim(a, z * rows, rows, 0)

    hidden_all = xall.astype(F32) + nn(attall, wout)
    n2_all, xhat_all, inv_all = apply_layer_norm(hidden_all, g2, b2)
    rows2 = n2_all.astype(BF)
    hidden_state, second_standardized, second_inverse_deviation = own(hidden_all), own(xhat_all), own(inv_all)
    gate = nn(rows2, wgate)
    up = nn(rows2, wup)
    sigma = jax.nn.sigmoid(gate)
    silu = gate * sigma
    act = (silu * up).astype(BF)
    mixed = sum_rows(nn(act, wdown))
    layer_output = (hidden_state + mixed).astype(BF)
    down_grad = tn(act, cotall)
    dact = nt(cotall, wdown)
    dgate = (dact * up * (sigma * (1.0 + gate * (1.0 - sigma)))).astype(BF)
    dup = (dact * silu).astype(BF)
    gate_grad = tn(rows2, dgate)
    up_grad = tn(rows2, dup)
    dn2 = sum_grads(nt(dgate, wgate) + nt(dup, wup))
    second_scale_partial = jnp.sum(dn2 * second_standardized, 0)
    shift2_part = jnp.sum(dn2, 0)
    hidden_gradient = cotangent.astype(F32) + layer_norm_backward(
        dn2, second_standardized, second_inverse_deviation, g2
    )

    def scatter(a, axis):
        return lax.psum_scatter(a.astype(BF), "dp", scatter_dimension=axis, tiled=True)

    gatew_grad = scatter(gate_grad, 0).astype(F32)
    upw_grad = scatter(up_grad, 0).astype(F32)
    downw_grad = scatter(down_grad, 1).astype(F32)
    da = hidden_gradient.astype(BF)
    out_grad = scatter(tn(own(attall), da), 1)
    outw_grad = lax.psum_scatter(out_grad, "tensor", scatter_dimension=0, tiled=True).astype(F32)
    dattended = nt(da, wout).astype(BF)
    dattended = lax.all_to_all(dattended, "tensor", split_axis=1, concat_axis=0, tiled=True)
    cosine, sine = tables(length)
    width = wqkv.shape[2]
    local_heads = width // HEAD_DIM
    dattended = dattended.reshape(length, local_heads, HEAD_DIM)
    query, keys, values = [
        qkv[j].transpose(1, 0, 2).reshape(length, local_heads, HEAD_DIM) for j in range(3)
    ]
    stats = lse[:, :local_heads].T
    cols = jnp.arange(length, dtype=jnp.int32)
    block = 512

    def backward_block(carry, index):
        dkeys, dvalues = carry
        qblock = lax.dynamic_slice_in_dim(query, index * block, block, 0)
        dblock = lax.dynamic_slice_in_dim(dattended, index * block, block, 0)
        block_lse = lax.dynamic_slice_in_dim(stats, index * block, block, 1)
        scores = jnp.einsum("qhd,khd->hqk", qblock, keys, preferred_element_type=F32) * scale
        keep = (index * block + jnp.arange(block, dtype=jnp.int32))[:, None] >= cols[None, :]
        scores = jnp.where(keep[None], scores, -1e30)
        probs = jnp.exp(scores - block_lse[..., None])
        probs16 = probs.astype(BF)
        dvalues = dvalues + jnp.einsum("hqk,qhd->khd", probs16, dblock, preferred_element_type=F32)
        dprobs = jnp.einsum("qhd,khd->hqk", dblock, values, preferred_element_type=F32)
        inner = jnp.sum(dprobs * probs, -1, keepdims=True)
        dscores = (probs * (dprobs - inner)).astype(BF)
        dquery = jnp.einsum("hqk,khd->qhd", dscores, keys, preferred_element_type=F32) * scale
        dkeys = dkeys + jnp.einsum("hqk,qhd->khd", dscores, qblock, preferred_element_type=F32) * scale
        return ((dkeys, dvalues), dquery)

    empty = jnp.zeros((length, local_heads, HEAD_DIM), F32)
    (dkeys, dvalues), dquery = lax.scan(backward_block, (empty, empty), jnp.arange(2, dtype=jnp.int32))
    dquery = dquery.reshape(length, local_heads, HEAD_DIM)
    dpre = jnp.stack(
        [
            unrotate(dquery, cosine, sine).reshape(length, width),
            unrotate(dkeys, cosine, sine).reshape(length, width),
            dvalues.reshape(length, width),
        ],
        0,
    ).astype(BF)
    qkv_grad = jnp.einsum("sd,jsc->jdc", n1, dpre, preferred_element_type=F32)
    bias_grad = jnp.sum(dpre, axis=1, dtype=F32)
    dn1 = sum_grads(jnp.einsum("jsc,jdc->sd", dpre, wqkv, preferred_element_type=F32))
    _, first_standardized, first_inverse_deviation = apply_layer_norm(tokens.astype(F32), g1, b1)
    token_gradient = (
        hidden_gradient
        + layer_norm_backward(dn1, first_standardized, first_inverse_deviation, g1)
    ).astype(BF)
    qkvw_grad = scatter(qkv_grad, 1).astype(F32)
    small = jnp.concatenate(
        [
            jnp.stack(
                [jnp.sum(dn1 * first_standardized, 0), jnp.sum(dn1, 0), second_scale_partial, shift2_part], 0
            ),
        ],
        0,
    )
    small = lax.psum_scatter(lax.psum(small, "tensor"), "dp", scatter_dimension=1, tiled=True)
    qkvb_grad = lax.psum_scatter(bias_grad, "dp", scatter_dimension=1, tiled=True)
    return (
        layer_output, token_gradient, qkvw_grad, qkvb_grad, outw_grad, small[0], small[1],
        gatew_grad, upw_grad, downw_grad, small[2], small[3],
    )


def solution(mesh):
    placed = (
        P(("dp", "tensor"), None),
        P(None, "dp", "tensor"),
        P(None, ("tensor", "dp")),
        P("tensor", "dp"),
        P("dp"),
        P("dp"),
        P("dp", "tensor"),
        P("dp", "tensor"),
        P("tensor", "dp"),
        P("dp"),
        P("dp"),
        P(("dp", "tensor"), None),
    )
    return jax.shard_map(
        fast if dict(mesh.shape) == {"dp": 8, "tensor": 4} else local,
        mesh=mesh,
        in_specs=placed,
        out_specs=(
            P(("dp", "tensor"), None),
            P(("dp", "tensor"), None),
            P(None, "dp", "tensor"),
            P(None, ("tensor", "dp")),
            P("tensor", "dp"),
            P("dp"),
            P("dp"),
            P("dp", "tensor"),
            P("dp", "tensor"),
            P("tensor", "dp"),
            P("dp"),
            P("dp"),
        ),
        check_vma=False,
    )
```

```python
import functools

import jax
import jax.numpy as jnp
from jax import lax
from jax.experimental import pallas as pl
from jax.experimental.pallas import tpu as pltpu
from jax.sharding import PartitionSpec as P

MESH = pl.DeviceIdType.MESH
HEAD_DIM = 64
ROT = 16
BF = jnp.bfloat16
F32 = jnp.float32
VMEM_LIMIT = 56 * 1024 * 1024
ANY = pl.BlockSpec(memory_space=pl.ANY)
INV = pl.BlockSpec(memory_space=pltpu.VMEM)


def nt(a, b):
    return lax.dot_general(a, b, (((1,), (1,)), ((), ())), preferred_element_type=F32)


def tn(a, b):
    return lax.dot_general(a, b, (((0,), (0,)), ((), ())), preferred_element_type=F32)


def nn(a, b):
    return jnp.dot(a, b, preferred_element_type=F32)


def place():
    d = lax.axis_index("dp")
    z = lax.axis_index("tensor")
    dy = 4 * (1 - 2 * lax.div(d, 4))
    dx = 2 * (1 - 2 * lax.rem(lax.div(d, 2), 2))
    dc = 1 - 2 * lax.rem(d, 2)
    return d, z, (0, dc, dx, dx + dc, dy, dy + dc, dy + dx, dy + dx + dc)


def send(src, dst, ssem, rsem, d, z):
    return pltpu.make_async_remote_copy(
        src_ref=src, dst_ref=dst, send_sem=ssem, recv_sem=rsem, device_id=(d, z), device_id_type=MESH
    )


def greet(d, z, flips, line, plane):
    barrier = pltpu.get_barrier_semaphore()
    for k in range(1, line):
        pl.semaphore_signal(
            barrier, inc=1, device_id=(d, lax.rem(z + k, line)), device_id_type=MESH
        )
    for r in plane:
        pl.semaphore_signal(barrier, inc=1, device_id=(d + flips[r], z), device_id_type=MESH)
    pl.semaphore_wait(barrier, line - 1 + len(plane))


class LineGather:
    def __init__(self, view, chunks, d, z, line, send_sems, recv_sems):
        self.view, self.chunks, self.d, self.z, self.line = view, chunks, d, z, line
        self.ss, self.rs = send_sems, recv_sems

    def copy(self, s, h, way, src=None):
        ref = self.view(s, h)
        return send(
            ref if src is None else src, ref, self.ss.at[way, s, h], self.rs.at[s, h],
            self.d, self.z + (1 if way == 0 else -1),
        )

    def start(self, h, src=None):
        pl.when(self.z < self.line - 1)(lambda: self.copy(self.z, h, 0, src).start())
        pl.when(self.z > 0)(lambda: self.copy(self.z, h, 1, src).start())

    def step(self, k, h):
        z, line = self.z, self.line

        @pl.when(z - k >= 0)
        def _():
            self.copy(z - k, h, 0).wait_recv()
            pl.when(z < line - 1)(lambda: self.copy(z - k, h, 0).start())

        @pl.when(z + k < line)
        def _():
            self.copy(z + k, h, 1).wait_recv()
            pl.when(z > 0)(lambda: self.copy(z + k, h, 1).start())

    def finish(self):
        z, line = self.z, self.line
        for k in range(line):
            for h in range(self.chunks):
                pl.when((z - k >= 0) & (z < line - 1))(lambda: self.copy(z - k, h, 0).wait_send())
                pl.when((z + k < line) & (z > 0))(lambda: self.copy(z + k, h, 1).wait_send())


def arrival(z, i):
    orders = ((0, 1, 2, 3), (1, 0, 2, 3), (2, 3, 1, 0), (3, 2, 1, 0))
    codes = [sum(s * 4**j for j, s in enumerate(o)) for o in orders]
    code = jnp.where(
        z == 0, codes[0], jnp.where(z == 1, codes[1], jnp.where(z == 2, codes[2], codes[3]))
    )
    power = jnp.where(i == 0, 1, jnp.where(i == 1, 4, jnp.where(i == 2, 16, 64)))
    return lax.rem(lax.div(code, power), 4)


def turn(u, cos, sin_up, sin_down, sign=1.0):
    moved = pltpu.roll(u, 8, 1) * sin_up + pltpu.roll(u, 120, 1) * sin_down
    return u * cos + moved if sign > 0 else u * cos - moved


def attention_kernel(
    tok, cot, wq, smalls, cos, sin_up, sin_down,
    xall, cotall, n1, qkv, lse, attall, wqkv, small_sum,
    xbuf, n1buf, wbuf, qbuf, abuf, smbuf,
    tss, trs, css, crs, ass, ars, wss, wrs, mss, mrs, local,
):
    rows = tok.shape[0]
    width = wq.shape[1] // 3
    pairs = width // 128
    line = 4
    d, z, flips = place()
    greet(d, z, flips, line, range(1, 8))

    tok_in = pltpu.make_async_copy(tok, xbuf.at[z], local.at[0])
    tok_in.start()
    cot_in = pltpu.make_async_copy(cot, cotall.at[pl.ds(z * rows, rows)], local.at[1])
    cot_in.start()
    depth = wq.shape[0]

    def wblock(i):
        return wbuf.at[pl.ds(pl.multiple_of(i * depth, 256), depth), :]

    w_in = pltpu.make_async_copy(wq, wblock(d), local.at[2])
    w_in.start()
    small_copies = [
        send(smalls, smbuf.at[r], mss.at[r], mrs.at[r], d + flips[r], z) for r in range(1, 8)
    ]
    for copy in small_copies:
        copy.start()
    w_sends = {
        r: send(wq, wblock(d), wss.at[r], wrs.at[r], d + flips[r], z) for r in (4, 2, 1, 6)
    }
    half = rows // 2

    def tview(s, h):
        return xbuf.at[s, pl.ds(h * half, half)]

    def cview(s, h):
        return cotall.at[pl.ds(pl.multiple_of(s * rows + h * half, 128), half)]

    def aview(s, h):
        return attall.at[:, pl.ds(pl.multiple_of(s * width + h * 128, 128), 128)]

    toks = LineGather(tview, 2, d, z, line, tss, trs)
    cots = LineGather(cview, 2, d, z, line, css, crs)
    atts = LineGather(aview, pairs, d, z, line, ass, ars)
    tok_in.wait()
    for h in range(2):
        toks.start(h)
    for copy in w_sends.values():
        copy.start()
    for copy in small_copies:
        copy.wait()
    total = smalls[...].astype(F32)
    for r in range(1, 8):
        total = total + smbuf[r].astype(F32)
    small_sum[...] = total

    def normalise(s):
        piece = 32

        @pl.loop(0, rows // piece)
        def _(i):
            at = pl.ds(pl.multiple_of(i * piece, piece), piece)
            x = xbuf[s, at, :].astype(F32)
            centred = x - jnp.mean(x, -1, keepdims=True)
            spread = jnp.mean(centred * centred, -1, keepdims=True)
            n = centred * lax.rsqrt(spread + 1e-05) * small_sum[0:1, :] + small_sum[1:2, :]
            n1buf[pl.ds(pl.multiple_of(s * rows + i * piece, piece), piece), :] = n.astype(BF)

    def project(s):
        at = pl.ds(pl.multiple_of(s * rows, rows), rows)
        for j in range(3):
            cols = pl.ds(j * width, width)
            pre = nn(n1buf[at, :], wbuf[:, cols]) + small_sum[4:5, cols]
            for p in range(pairs):
                part = pre[:, p * 128 : (p + 1) * 128]
                if j < 2:
                    part = turn(part, cos[at, :], sin_up[at, :], sin_down[at, :])
                qbuf[j, p, at, :] = part.astype(BF)

    for h in range(2):
        toks.step(1, h)
    for r in (2, 4, 6):
        w_sends[r].wait_recv()
        send(wblock(d + flips[r]), wblock(d + flips[r]), wss.at[r + 1], wrs.at[r + 1], d + flips[1], z).start()
    w_in.wait()
    w_sends[1].wait_recv()
    for r in (3, 5, 7):
        send(wblock(d), wblock(d), wss.at[r], wrs.at[r], d + flips[1], z).wait_recv()

    @pl.loop(0, line)
    def _(i):
        @pl.when(i == line - 1)
        def _():
            cot_in.wait()
            for h in range(2):
                cots.start(h)

        s = arrival(z, i)
        normalise(s)
        project(s)

        @pl.when((i >= 1) & (i < line - 1))
        def _():
            for h in range(2):
                toks.step(i + 1, h)

    outs = [
        pltpu.make_async_copy(n1buf, n1, local.at[3]),
        pltpu.make_async_copy(wbuf, wqkv, local.at[4]),
        pltpu.make_async_copy(qbuf, qkv, local.at[5]),
    ] + [
        pltpu.make_async_copy(xbuf.at[s], xall.at[pl.ds(s * rows, rows)], local.at[6 + s])
        for s in range(line)
    ]
    for copy in outs:
        copy.start()

    lanes = lax.broadcasted_iota(jnp.int32, (1, 128), 1)
    first = lanes < 64
    lse[...] = jnp.zeros_like(lse)
    length = rows * line

    def attend(p, start):
        for qi in range(line):
            count = (qi + 1) * rows
            at = pl.ds(qi * rows, rows)
            q = qbuf[0, p, at, :] * BF(HEAD_DIM**-0.5)
            k = qbuf[1, p, pl.ds(0, count), :]
            v = qbuf[2, p, pl.ds(0, count), :]
            row = lax.broadcasted_iota(jnp.int32, (rows, count), 0) + qi * rows
            col = lax.broadcasted_iota(jnp.int32, (rows, count), 1)
            keep = row >= col
            results = []
            stats = lse[at, :]
            for a in range(2):
                mine = first if a == 0 else ~first
                s = nt(jnp.where(mine, q, BF(0)), k)
                s = jnp.where(keep, s, -1e30)
                most = jnp.max(s, -1, keepdims=True)
                e = jnp.exp(s - most)
                total = jnp.sum(e, -1, keepdims=True)
                results.append(nn(e.astype(BF), v) / total)
                stats = jnp.where(lanes == 2 * p + a, most + jnp.log(total), stats)
            lse[at, :] = stats
            abuf[p, at, :] = jnp.where(first, results[0], results[1]).astype(BF)

    def own_columns(p):
        return pltpu.make_async_copy(abuf.at[p], aview(z, p), local.at[10 + p])

    @pl.loop(0, pairs)
    def _(p):
        attend(p, None)
        own_columns(p).start()
        atts.start(p, abuf.at[p])

    for k in range(1, line):
        for h in range(2):
            cots.step(k, h)
        for p in range(pairs):
            atts.step(k, p)
    for gather in (toks, cots, atts):
        gather.finish()
    for r in range(1, 8):
        send(wblock(d), wblock(d), wss.at[r], wrs.at[r], d + flips[1], z).wait_send()
    for copy in outs:
        copy.wait()
    for p in range(pairs):
        own_columns(p).wait()


def attention_forward(tok, cot, wq, smalls, tabs):
    rows, model = tok.shape
    line = 4
    length = rows * line
    depth, width = wq.shape
    width //= 3
    pairs = width // 128
    dp = model // depth
    sds = jax.ShapeDtypeStruct
    return pl.pallas_call(
        attention_kernel,
        out_shape=(
            sds((length, model), BF), sds((length, model), BF), sds((length, model), BF),
            sds((3, pairs, length, 128), BF), sds((length, 128), F32), sds((length, model), BF),
            sds((model, 3 * width), BF), sds((16, model), F32),
        ),
        in_specs=[ANY, ANY, ANY, INV, INV, INV, INV],
        out_specs=(ANY, ANY, ANY, ANY, INV, ANY, ANY, INV),
        scratch_shapes=[
            pltpu.VMEM((line, rows, model), BF),
            pltpu.VMEM((length, model), BF),
            pltpu.VMEM((model, 3 * width), BF),
            pltpu.VMEM((3, pairs, length, 128), BF),
            pltpu.VMEM((pairs, length, 128), BF),
            pltpu.VMEM((dp, 16, model), BF),
            pltpu.SemaphoreType.DMA((2, line, 2)),
            pltpu.SemaphoreType.DMA((line, 2)),
            pltpu.SemaphoreType.DMA((2, line, 2)),
            pltpu.SemaphoreType.DMA((line, 2)),
            pltpu.SemaphoreType.DMA((2, line, pairs)),
            pltpu.SemaphoreType.DMA((line, pairs)),
            pltpu.SemaphoreType.DMA((8,)),
            pltpu.SemaphoreType.DMA((8,)),
            pltpu.SemaphoreType.DMA((8,)),
            pltpu.SemaphoreType.DMA((8,)),
            pltpu.SemaphoreType.DMA((16,)),
        ],
        compiler_params=pltpu.CompilerParams(
            collective_id=1, has_side_effects=True, vmem_limit_bytes=VMEM_LIMIT
        ),
        cost_estimate=pl.CostEstimate(flops=2 * 10**11, bytes_accessed=10**8, transcendentals=0),
        name="attention_forward",
    )(tok, cot, wq, smalls, *tabs)


def apply_layer_norm(value, norm_scale, norm_bias):
    centered_input = value - jnp.mean(value, -1, keepdims=True)
    spread = jnp.mean(centered_input * centered_input, -1, keepdims=True)
    inverse_deviation = lax.rsqrt(spread + 1e-05)
    standardized_input = centered_input * inverse_deviation
    return (
        standardized_input * norm_scale.astype(jnp.float32) + norm_bias.astype(jnp.float32),
        standardized_input,
        inverse_deviation,
    )


def layer_norm_backward(output_gradient, standardized_input, inverse_deviation, norm_scale):
    scaled_gradient = output_gradient * norm_scale.astype(jnp.float32)
    return inverse_deviation * (
        scaled_gradient
        - jnp.mean(scaled_gradient, -1, keepdims=True)
        - standardized_input * jnp.mean(scaled_gradient * standardized_input, -1, keepdims=True)
    )


def tables(length):
    positions = jnp.arange(length, dtype=jnp.float32)
    freqs = 10000.0 ** (-jnp.arange(0, ROT, 2, dtype=jnp.float32) / ROT)
    angles = positions[:, None] * freqs[None, :]
    angles = jnp.concatenate([angles, angles], -1)
    return (jnp.cos(angles), jnp.sin(angles))


def rotate(heads, cosine, sine):
    half = ROT // 2
    part = heads[..., :ROT]
    turned = jnp.concatenate([-part[..., half:], part[..., :half]], -1)
    moved = part * cosine[:, None, :] + turned * sine[:, None, :]
    return jnp.concatenate([moved, heads[..., ROT:]], -1)


def unrotate(output_gradient, cosine, sine):
    half = ROT // 2
    part = output_gradient[..., :ROT]
    scaled_gradient = part * sine[:, None, :]
    back = jnp.concatenate([scaled_gradient[..., half:], -scaled_gradient[..., :half]], -1)
    moved = part * cosine[:, None, :] + back
    return jnp.concatenate([moved, output_gradient[..., ROT:]], -1)


def attn_params(qkv_weight, qkv_bias, out_weight, norm1_gain, norm1_shift):
    return (
        lax.all_gather(qkv_weight, "dp", axis=1, tiled=True),
        lax.all_gather(qkv_bias, "dp", axis=1, tiled=True),
        lax.all_gather(out_weight, "dp", axis=1, tiled=True),
        lax.all_gather(norm1_gain, "dp", axis=0, tiled=True),
        lax.all_gather(norm1_shift, "dp", axis=0, tiled=True),
    )


def mlp_params(gate_weight, up_weight, down_weight, norm2_gain, norm2_shift):
    return (
        lax.all_gather(gate_weight, "dp", axis=0, tiled=True),
        lax.all_gather(up_weight, "dp", axis=0, tiled=True),
        lax.all_gather(down_weight, "dp", axis=1, tiled=True),
        lax.all_gather(norm2_gain, "dp", axis=0, tiled=True),
        lax.all_gather(norm2_shift, "dp", axis=0, tiled=True),
    )


def gather_rows(rows):
    return lax.all_gather(rows, "tensor", axis=0, tiled=True)


def sum_rows(partial_value):
    return lax.psum_scatter(
        partial_value.astype(jnp.bfloat16), "tensor", scatter_dimension=0, tiled=True
    ).astype(jnp.float32)


def gather_grads(rows):
    return lax.all_gather(rows, "tensor", axis=0, tiled=True)


def sum_grads(partial_value):
    return lax.psum_scatter(
        partial_value.astype(jnp.bfloat16), "tensor", scatter_dimension=0, tiled=True
    ).astype(jnp.float32)


def local(
    tokens,
    qkv_weight,
    qkv_bias,
    out_weight,
    norm1_gain,
    norm1_shift,
    gate_weight,
    up_weight,
    down_weight,
    norm2_gain,
    norm2_shift,
    cotangent,
):
    scale = HEAD_DIM ** (-0.5)
    input_rows = tokens.astype(jnp.float32)
    wqkv, bqkv, wout, first_norm_scale, first_norm_bias = attn_params(
        qkv_weight, qkv_bias, out_weight, norm1_gain, norm1_shift
    )
    first_normed_rows, first_standardized, first_inverse_deviation = apply_layer_norm(
        input_rows, first_norm_scale, first_norm_bias
    )
    rows1 = gather_rows(first_normed_rows.astype(jnp.bfloat16))
    length = rows1.shape[0]
    width = wqkv.shape[2]
    local_heads = width // HEAD_DIM
    pre = (
        jnp.einsum("sd,jdc->jsc", rows1, wqkv, preferred_element_type=jnp.float32)
        + bqkv.astype(jnp.float32)[:, None, :]
    )
    cosine, sine = tables(length)
    query = rotate(pre[0].reshape(length, local_heads, HEAD_DIM), cosine, sine).astype(jnp.bfloat16)
    keys = rotate(pre[1].reshape(length, local_heads, HEAD_DIM), cosine, sine).astype(jnp.bfloat16)
    values = pre[2].reshape(length, local_heads, HEAD_DIM).astype(jnp.bfloat16)
    block = min(length, 512)
    count = length // block
    cols = jnp.arange(length, dtype=jnp.int32)

    def block_probs(qblock, start):
        scores = (
            jnp.einsum("qhd,khd->hqk", qblock, keys, preferred_element_type=jnp.float32) * scale
        )
        rows = start + jnp.arange(block, dtype=jnp.int32)
        keep = rows[:, None] >= cols[None, :]
        return jnp.where(keep[None], scores, -1e30)

    def forward_block(index):
        qblock = lax.dynamic_slice_in_dim(query, index * block, block, 0)
        scores = block_probs(qblock, index * block)
        most = jnp.max(scores, -1, keepdims=True)
        expo = jnp.exp(scores - most)
        total = jnp.sum(expo, -1, keepdims=True)
        probs = (expo / total).astype(jnp.bfloat16)
        out_block = jnp.einsum("hqk,khd->qhd", probs, values, preferred_element_type=jnp.float32)
        return (out_block.astype(jnp.bfloat16), most[..., 0] + jnp.log(total[..., 0]))

    indices = jnp.arange(count, dtype=jnp.int32)
    out_blocks, lse = lax.map(forward_block, indices)
    attended = out_blocks.reshape(length, width)
    branch = jnp.dot(attended, wout, preferred_element_type=jnp.float32)
    hidden_state = input_rows + sum_rows(branch)
    wgate, wup, wdown, second_norm_scale, second_norm_bias = mlp_params(
        gate_weight, up_weight, down_weight, norm2_gain, norm2_shift
    )
    second_normed_rows, second_standardized, second_inverse_deviation = apply_layer_norm(
        hidden_state, second_norm_scale, second_norm_bias
    )
    rows2 = gather_rows(second_normed_rows.astype(jnp.bfloat16))
    gate = jnp.dot(rows2, wgate, preferred_element_type=jnp.float32)
    up = jnp.dot(rows2, wup, preferred_element_type=jnp.float32)
    sigma = jax.nn.sigmoid(gate)
    silu = gate * sigma
    act = (silu * up).astype(jnp.bfloat16)
    mixed = sum_rows(jnp.dot(act, wdown, preferred_element_type=jnp.float32))
    layer_output = (hidden_state + mixed).astype(jnp.bfloat16)
    wgate, wup, wdown, second_norm_scale, second_norm_bias = mlp_params(
        gate_weight, up_weight, down_weight, norm2_gain, norm2_shift
    )
    incoming_gradient = cotangent.astype(jnp.float32)
    down_rows = gather_grads(cotangent)
    down_grad = jnp.einsum("sf,sd->fd", act, down_rows, preferred_element_type=jnp.float32)
    dact = jnp.einsum("sd,fd->sf", down_rows, wdown, preferred_element_type=jnp.float32)
    dgate = (dact * up * (sigma * (1.0 + gate * (1.0 - sigma)))).astype(jnp.bfloat16)
    dup = (dact * silu).astype(jnp.bfloat16)
    gate_grad = jnp.einsum("sd,sf->df", rows2, dgate, preferred_element_type=jnp.float32)
    up_grad = jnp.einsum("sd,sf->df", rows2, dup, preferred_element_type=jnp.float32)
    second_norm_gradient = jnp.einsum(
        "sf,df->sd", dgate, wgate, preferred_element_type=jnp.float32
    ) + jnp.einsum("sf,df->sd", dup, wup, preferred_element_type=jnp.float32)
    second_norm_gradient = sum_grads(second_norm_gradient)
    second_scale_partial = jnp.sum(second_norm_gradient * second_standardized, 0)
    shift2_part = jnp.sum(second_norm_gradient, 0)
    hidden_gradient = incoming_gradient + layer_norm_backward(
        second_norm_gradient, second_standardized, second_inverse_deviation, second_norm_scale
    )
    gatew_grad, upw_grad, downw_grad, gain2_total, shift2_total = (
        lax.psum_scatter(
            gate_grad.astype(jnp.bfloat16), "dp", scatter_dimension=0, tiled=True
        ).astype(jnp.float32),
        lax.psum_scatter(
            up_grad.astype(jnp.bfloat16), "dp", scatter_dimension=0, tiled=True
        ).astype(jnp.float32),
        lax.psum_scatter(
            down_grad.astype(jnp.bfloat16), "dp", scatter_dimension=1, tiled=True
        ).astype(jnp.float32),
        lax.psum_scatter(
            second_scale_partial.astype(jnp.bfloat16), "dp", scatter_dimension=0, tiled=True
        ).astype(jnp.float32),
        lax.psum_scatter(
            shift2_part.astype(jnp.bfloat16), "dp", scatter_dimension=0, tiled=True
        ).astype(jnp.float32),
    )
    wqkv, bqkv, wout, first_norm_scale, first_norm_bias = attn_params(
        qkv_weight, qkv_bias, out_weight, norm1_gain, norm1_shift
    )
    branch_rows = gather_grads(hidden_gradient.astype(jnp.bfloat16))
    out_grad = jnp.einsum("sc,sd->cd", attended, branch_rows, preferred_element_type=jnp.float32)
    dattended = jnp.einsum(
        "sd,cd->sc", branch_rows, wout, preferred_element_type=jnp.float32
    ).astype(jnp.bfloat16)
    dattended = dattended.reshape(length, local_heads, HEAD_DIM)

    def backward_block(carry, item):
        dkeys, dvalues = carry
        index, block_lse = item
        qblock = lax.dynamic_slice_in_dim(query, index * block, block, 0)
        dblock = lax.dynamic_slice_in_dim(dattended, index * block, block, 0)
        scores = block_probs(qblock, index * block)
        probs = jnp.exp(scores - block_lse[..., None])
        probs16 = probs.astype(jnp.bfloat16)
        dvalues = dvalues + jnp.einsum(
            "hqk,qhd->khd", probs16, dblock, preferred_element_type=jnp.float32
        )
        dprobs = jnp.einsum("qhd,khd->hqk", dblock, values, preferred_element_type=jnp.float32)
        inner = jnp.sum(dprobs * probs, -1, keepdims=True)
        dscores = (probs * (dprobs - inner)).astype(jnp.bfloat16)
        dquery = (
            jnp.einsum("hqk,khd->qhd", dscores, keys, preferred_element_type=jnp.float32) * scale
        )
        dkeys = (
            dkeys
            + jnp.einsum("hqk,qhd->khd", dscores, qblock, preferred_element_type=jnp.float32)
            * scale
        )
        return ((dkeys, dvalues), dquery)

    empty = jnp.zeros((length, local_heads, HEAD_DIM), jnp.float32)
    (dkeys, dvalues), dquery = lax.scan(backward_block, (empty, empty), (indices, lse))
    dquery = dquery.reshape(length, local_heads, HEAD_DIM)
    dpre = jnp.stack(
        [
            unrotate(dquery, cosine, sine).reshape(length, width),
            unrotate(dkeys, cosine, sine).reshape(length, width),
            dvalues.reshape(length, width),
        ],
        0,
    ).astype(jnp.bfloat16)
    qkv_grad = jnp.einsum("sd,jsc->jdc", rows1, dpre, preferred_element_type=jnp.float32)
    bias_grad = jnp.sum(dpre, axis=1, dtype=jnp.float32)
    first_norm_gradient = sum_grads(
        jnp.einsum("jsc,jdc->sd", dpre, wqkv, preferred_element_type=jnp.float32)
    )
    first_scale_partial = jnp.sum(first_norm_gradient * first_standardized, 0)
    shift1_part = jnp.sum(first_norm_gradient, 0)
    token_gradient = (
        hidden_gradient
        + layer_norm_backward(
            first_norm_gradient, first_standardized, first_inverse_deviation, first_norm_scale
        )
    ).astype(jnp.bfloat16)
    qkvw_grad, qkvb_grad, outw_grad, gain1_total, shift1_total = (
        lax.psum_scatter(
            qkv_grad.astype(jnp.bfloat16), "dp", scatter_dimension=1, tiled=True
        ).astype(jnp.float32),
        lax.psum_scatter(
            bias_grad.astype(jnp.bfloat16), "dp", scatter_dimension=1, tiled=True
        ).astype(jnp.float32),
        lax.psum_scatter(
            out_grad.astype(jnp.bfloat16), "dp", scatter_dimension=1, tiled=True
        ).astype(jnp.float32),
        lax.psum_scatter(
            first_scale_partial.astype(jnp.bfloat16), "dp", scatter_dimension=0, tiled=True
        ).astype(jnp.float32),
        lax.psum_scatter(
            shift1_part.astype(jnp.bfloat16), "dp", scatter_dimension=0, tiled=True
        ).astype(jnp.float32),
    )
    gain1_grad, shift1_grad, gain2_grad, shift2_grad = lax.psum(
        (gain1_total, shift1_total, gain2_total, shift2_total), "tensor"
    )
    return (
        layer_output,
        token_gradient,
        qkvw_grad,
        qkvb_grad,
        outw_grad,
        gain1_grad,
        shift1_grad,
        gatew_grad,
        upw_grad,
        downw_grad,
        gain2_grad,
        shift2_grad,
    )


class LineScatter:
    def __init__(self, part, slot, chunks, d, z, line, send_sems, recv_sems):
        self.part, self.slot, self.chunks, self.d, self.z, self.line = part, slot, chunks, d, z, line
        self.ss, self.rs = send_sems, recv_sems

    def copy(self, s, h, way, target, place):
        return send(
            self.part(s, h), self.slot(place, h), self.ss.at[s, h], self.rs.at[place, h], self.d, target
        )

    def right(self, s, h):
        return self.copy(s, h, 0, self.z + 1, s)

    def left(self, s, h):
        return self.copy(s, h, 1, self.z - 1, jnp.where(self.z - 1 == s, self.line, s))

    def head(self, s):
        z, line = self.z, self.line
        for h in range(self.chunks):
            pl.when((z == 0) & (s > 0))(lambda: self.right(s, h).start())
            pl.when((z == line - 1) & (s < z))(lambda: self.left(s, h).start())

    def add(self, s, h):
        part = self.part(s, h)
        part[...] = (part[...].astype(F32) + self.slot(s, h)[...].astype(F32)).astype(BF)

    def relay(self, t):
        z, line = self.z, self.line
        up = line - 1 - t + z
        down = t - (line - 1 - z)
        for h in range(self.chunks):
            @pl.when((z > 0) & (up > z) & (up < line))
            def _():
                self.copy(z, h, 0, z, up).wait_recv()
                self.add(up, h)
                self.right(up, h).start()

            @pl.when((z < line - 1) & (down >= 0) & (down < z))
            def _():
                self.copy(z, h, 0, z, down).wait_recv()
                self.add(down, h)
                self.left(down, h).start()

    def arrive(self, h):
        z, line = self.z, self.line
        pl.when(z > 0)(lambda: self.copy(z, h, 0, z, z).wait_recv())
        pl.when(z < line - 1)(lambda: self.copy(z, h, 0, z, line).wait_recv())

    def total(self, h, rows):
        z = self.z
        return (
            self.part(z, h)[rows].astype(F32)
            + self.slot(z, h)[rows].astype(F32)
            + self.slot(self.line, h)[rows].astype(F32)
        )

    def finish(self):
        z = self.z
        for s in range(self.line):
            for h in range(self.chunks):
                pl.when(z != s)(lambda: self.copy(s, h, 0, z, s).wait_send())


def far_first(z, i):
    orders = ((3, 2, 1, 0), (3, 0, 2, 1), (0, 3, 1, 2), (0, 1, 2, 3))
    codes = [sum(s * 4**j for j, s in enumerate(o)) for o in orders]
    code = jnp.where(
        z == 0, codes[0], jnp.where(z == 1, codes[1], jnp.where(z == 2, codes[2], codes[3]))
    )
    power = jnp.where(i == 0, 1, jnp.where(i == 1, 4, jnp.where(i == 2, 16, 64)))
    return lax.rem(lax.div(code, power), 4)


def spans(total, step):
    return [(i, min(step, total - i)) for i in range(0, total, step)]


def mlp_kernel(
    n2, cot, wgate, wup, wdown,
    dn2, mixed, gex, uex, dex, ghalf, uhalf, dhalf, grecv,
    nbuf, cbuf, gw, uw, dw, act, act_t, dga, dup, part, slots, mixbuf, wide, tall, wide_in, tall_in,
    ss, rs, local, mixsem, outsem, exs, exr, gss, grs,
):
    line = 4
    rows = n2.shape[0] // line
    model = n2.shape[1]
    hidden = wgate.shape[1]
    d, z, flips = place()
    greet(d, z, flips, line, (1, 2, 4, 6))
    core = lax.rem(d, 2)
    chip = lax.div(d, 2)
    loads = [
        pltpu.make_async_copy(a, b, local.at[i])
        for i, (a, b) in enumerate(((n2, nbuf), (wgate, gw), (wup, uw), (cot, cbuf), (wdown, dw)))
    ]
    for copy in loads:
        copy.start()
    half = rows // 2
    scatter = LineScatter(
        lambda s, h: part.at[s, pl.ds(h * half, half)],
        lambda i, h: slots.at[i, pl.ds(h * half, half)],
        2, d, z, line, ss, rs,
    )
    pl.when(z == 0)(lambda: slots.__setitem__((0,), jnp.zeros((rows, model), BF)))
    pl.when(z == line - 1)(lambda: slots.__setitem__((line,), jnp.zeros((rows, model), BF)))
    for copy in loads:
        copy.wait()

    @pl.loop(0, line)
    def _(i):
        s = far_first(z, i)
        at = pl.ds(pl.multiple_of(s * rows, rows), rows)
        for lo, size in spans(hidden, 512):
            cols = pl.ds(lo, size)
            gate = nn(nbuf[at, :], gw[:, cols])
            up = nn(nbuf[at, :], uw[:, cols])
            dact = nt(cbuf[at, :], dw[cols, :])
            sigma = lax.logistic(gate)
            silu = gate * sigma
            act[at, cols] = (silu * up).astype(BF)
            dga[at, cols] = (dact * up * (sigma * (1.0 + gate * (1.0 - sigma)))).astype(BF)
            dup[at, cols] = (dact * silu).astype(BF)
        for lo, size in spans(model, 512):
            cols = pl.ds(lo, size)
            part[s, :, cols] = (nt(dga[at, :], gw[cols, :]) + nt(dup[at, :], uw[cols, :])).astype(BF)
        scatter.head(s)

    scatter.relay(1)
    blocks = model // rows // 2

    def exchanged(m):
        outs = (ghalf, uhalf, dhalf)
        exes = (gex, uex, dex)
        stage = tall if m == 2 else wide
        stage_in = tall_in if m == 2 else wide_in

        def block(t):
            cols = pl.ds(pl.multiple_of(t * rows, rows), rows)
            if m == 2:
                return lambda lo, size: nn(act_t[pl.ds(lo, size), :], cbuf[:, cols])
            right = dga if m == 0 else dup
            return lambda lo, size: tn(nbuf[:, cols], right[:, pl.ds(lo, size)])

        def piece(ref, lo, size):
            return ref.at[pl.ds(lo, size), :] if m == 2 else ref.at[:, pl.ds(lo, size)]

        def away(k):
            slot = lax.rem(k, 2)
            return send(stage.at[slot], exes[m].at[k], exs.at[m, k], exr.at[m, k], d + flips[1], z)

        @pl.loop(0, blocks)
        def _(k):
            slot = lax.rem(k, 2)
            pl.when(k >= 2)(lambda: away(k - 2).wait_send())
            make = block(2 * k + 1 - core)
            for lo, size in spans(hidden, 512):
                piece(stage.at[slot], lo, size)[...] = make(lo, size).astype(BF)
            away(k).start()

        away(blocks - 2).wait_send()
        away(blocks - 1).wait_send()

        def chip_at(j):
            return lax.rem(chip + 1 + j, blocks)

        def store(j):
            slot = lax.rem(j, 2)
            return pltpu.make_async_copy(stage.at[slot], outs[m].at[chip_at(j)], outsem.at[slot])

        def onward(j):
            k = chip_at(j)
            return send(ghalf.at[k], grecv.at[blocks - 2 - j], gss.at[j], grs.at[blocks - 2 - j], 2 * k + core, z)

        @pl.loop(0, blocks)
        def _(j):
            slot = lax.rem(j, 2)
            k = chip_at(j)

            @pl.when(j >= 2)
            def _():
                store(j - 2).wait()
                if m == 0:
                    onward(j - 2).start()

            away(k).wait_recv()
            fetch = pltpu.make_async_copy(exes[m].at[k], stage_in, local.at[5])
            fetch.start()
            fetch.wait()
            make = block(2 * k + core)
            for lo, size in spans(hidden, 512):
                piece(stage.at[slot], lo, size)[...] = (
                    make(lo, size) + piece(stage_in, lo, size)[...].astype(F32)
                ).astype(BF)
            store(j).start()

        for j in (blocks - 2, blocks - 1):
            store(j).wait()
            if m == 0 and j < blocks - 1:
                onward(j).start()
        return onward

    onward = exchanged(0)

    def mixed_out(i):
        cols = pl.ds(pl.multiple_of(i * 512, 512), 512)
        return pltpu.make_async_copy(mixbuf.at[lax.rem(i, 2)], mixed.at[:, cols], mixsem.at[lax.rem(i, 2)])

    @pl.loop(0, line)
    def _(s):
        at = pl.ds(pl.multiple_of(s * rows, rows), rows)
        for lo, size in spans(hidden, 512):
            act_t[pl.ds(lo, size), at] = act[at, pl.ds(lo, size)].T

    @pl.loop(0, model // 512)
    def _(i):
        pl.when(i >= 2)(lambda: mixed_out(i - 2).wait())
        cols = pl.ds(pl.multiple_of(i * 512, 512), 512)
        for s in range(line):
            at = pl.ds(s * rows, rows)
            mixbuf[lax.rem(i, 2), at, :] = nn(act[at, :], dw[:, cols]).astype(BF)
        mixed_out(i).start()

    scatter.relay(2)
    exchanged(1)
    exchanged(2)
    for h in range(2):
        scatter.arrive(h)

        @pl.loop(0, half // 32)
        def _(i):
            rows_at = pl.ds(pl.multiple_of(i * 32, 32), 32)
            dn2[pl.ds(pl.multiple_of(h * half + i * 32, 32), 32), :] = scatter.total(h, rows_at)

    scatter.finish()
    for i in (model // 512 - 2, model // 512 - 1):
        mixed_out(i).wait()
    for j in range(blocks - 1):
        onward(j).wait()


def mlp(n2, cot, wgate, wup, wdown):
    length, model = n2.shape
    hidden = wgate.shape[1]
    line = 4
    rows = length // line
    blocks = model // rows // 2
    sds = jax.ShapeDtypeStruct
    wide = sds((blocks, rows, hidden), BF)
    tall = sds((blocks, hidden, rows), BF)
    return pl.pallas_call(
        mlp_kernel,
        out_shape=(
            sds((rows, model), F32), sds((length, model), BF),
            wide, wide, tall, wide, wide, tall, sds((blocks - 1, rows, hidden), BF),
        ),
        in_specs=[ANY] * 5,
        out_specs=(INV,) + (ANY,) * 8,
        scratch_shapes=[
            pltpu.VMEM((length, model), BF),
            pltpu.VMEM((length, model), BF),
            pltpu.VMEM((model, hidden), BF),
            pltpu.VMEM((model, hidden), BF),
            pltpu.VMEM((hidden, model), BF),
            pltpu.VMEM((length, hidden), BF),
            pltpu.VMEM((hidden, length), BF),
            pltpu.VMEM((length, hidden), BF),
            pltpu.VMEM((length, hidden), BF),
            pltpu.VMEM((line, rows, model), BF),
            pltpu.VMEM((line + 1, rows, model), BF),
            pltpu.VMEM((2, length, 512), BF),
            pltpu.VMEM((2, rows, hidden), BF),
            pltpu.VMEM((2, hidden, rows), BF),
            pltpu.VMEM((rows, hidden), BF),
            pltpu.VMEM((hidden, rows), BF),
            pltpu.SemaphoreType.DMA((line, 2)),
            pltpu.SemaphoreType.DMA((line + 1, 2)),
            pltpu.SemaphoreType.DMA((6,)),
            pltpu.SemaphoreType.DMA((2,)),
            pltpu.SemaphoreType.DMA((2,)),
            pltpu.SemaphoreType.DMA((3, blocks)),
            pltpu.SemaphoreType.DMA((3, blocks)),
            pltpu.SemaphoreType.DMA((blocks,)),
            pltpu.SemaphoreType.DMA((blocks,)),
        ],
        compiler_params=pltpu.CompilerParams(
            collective_id=2, has_side_effects=True, vmem_limit_bytes=62 * 1024 * 1024
        ),
        cost_estimate=pl.CostEstimate(flops=10**11, bytes_accessed=10**8, transcendentals=0),
        name="mlp",
    )(n2, cot, wgate, wup, wdown)


def norm_parts(x):
    centred = x - jnp.mean(x, -1, keepdims=True)
    inverse = lax.rsqrt(jnp.mean(centred * centred, -1, keepdims=True) + 1e-05)
    return centred * inverse, inverse


def norm_back(grad, standard, inverse, gain):
    scaled = grad * gain
    return inverse * (
        scaled
        - jnp.mean(scaled, -1, keepdims=True)
        - standard * jnp.mean(scaled * standard, -1, keepdims=True)
    )


def each_piece(rows, piece, body):
    @pl.loop(0, rows // piece)
    def _(i):
        body(pl.ds(pl.multiple_of(i * piece, piece), piece))


class PlaneSum:
    def __init__(self, half, recv, d, z, blocks, send_sems, recv_sems):
        self.half, self.recv, self.d, self.z, self.blocks = half, recv, d, z, blocks
        self.ss, self.rs = send_sems, recv_sems
        self.chip, self.core = lax.div(d, 2), lax.rem(d, 2)

    def chip_at(self, j):
        return lax.rem(self.chip + 1 + j, self.blocks)

    def copy(self, j):
        k, to = self.chip_at(j), self.blocks - 2 - j
        return send(self.half.at[k], self.recv.at[to], self.ss.at[j], self.rs.at[to], 2 * k + self.core, self.z)

    def wait(self):
        for j in range(self.blocks - 1):
            self.copy(j).wait()


def sum_blocks(own, recv, out, buf, obuf, sems, pieces):
    count = recv.shape[0]
    rows = buf.shape[1]

    @pl.loop(0, pieces)
    def _(i):
        at = pl.ds(pl.multiple_of(i * rows, rows), rows)
        ins = [pltpu.make_async_copy(own.at[at], buf.at[0], sems.at[0])] + [
            pltpu.make_async_copy(recv.at[j, at], buf.at[j + 1], sems.at[j + 1]) for j in range(count)
        ]
        for copy in ins:
            copy.start()
        for copy in ins:
            copy.wait()
        total = buf[0].astype(F32)
        for j in range(count):
            total = total + buf[j + 1].astype(F32)
        obuf[...] = total
        back = pltpu.make_async_copy(obuf, out.at[at], sems.at[count + 1])
        back.start()
        back.wait()


def attention_back_kernel(
    dn2, hid, cot, small, wout, attall, qkv, lse, mixed, ghalf, grecv, uhalf, cos, sin_up, sin_down,
    lay, dhid, dpre, ograd, ggrad, ugrad, sums, urecv, oex,
    wo, da, attr, att_t, attc, qbuf, dsend, datt, lse_t, part, slots, ostage, ofetch, osum, orecv, ofull, ozr,
    sbuf, sobuf, dq,
    mss, mrs, ass, ars, oss, ors, pss, prs, uss, urs, zss, zrs, local, ssem,
):
    line = 4
    rows, model = hid.shape
    length = rows * line
    width = attc.shape[1]
    pairs = width // 128
    blocks = model // rows // 2
    d, z, flips = place()
    greet(d, z, flips, line, (1, 2, 4, 6))
    core, chip = lax.rem(d, 2), lax.div(d, 2)
    ups = PlaneSum(uhalf, urecv, d, z, blocks, uss, urs)
    loads = [pltpu.make_async_copy(mixed.at[pl.ds(s * rows, rows)], part.at[s], local.at[s]) for s in range(line)]
    loads += [
        pltpu.make_async_copy(wout, wo, local.at[4]),
        pltpu.make_async_copy(attall.at[pl.ds(pl.multiple_of(z * rows, rows), rows)], attr, local.at[5]),
        pltpu.make_async_copy(attall.at[:, pl.ds(pl.multiple_of(z * width, width), width)], attc, local.at[6]),
        pltpu.make_async_copy(qkv, qbuf, local.at[7]),
    ]
    for copy in loads:
        copy.start()
    for j in range(blocks - 1):
        ups.copy(j).start()
    half = rows // 2
    scatter = LineScatter(
        lambda s, h: part.at[s, pl.ds(h * half, half)],
        lambda i, h: slots.at[i, pl.ds(h * half, half)],
        2, d, z, line, mss, mrs,
    )
    pl.when(z == 0)(lambda: slots.__setitem__((0,), jnp.zeros((rows, model), BF)))
    pl.when(z == line - 1)(lambda: slots.__setitem__((line,), jnp.zeros((rows, model), BF)))
    for copy in loads[:4]:
        copy.wait()
    for i in range(line - 1):
        pl.when(z == 0)(lambda: scatter.head(jnp.int32(line - 1 - i)))
        pl.when(z == line - 1)(lambda: scatter.head(jnp.int32(i)))

    sums[...] = jnp.zeros_like(sums)

    def back(at):
        grad = dn2[at, :]
        standard, inverse = norm_parts(hid[at, :])
        sums[2:3, :] += jnp.sum(grad * standard, 0, keepdims=True)
        sums[3:4, :] += jnp.sum(grad, 0, keepdims=True)
        total = cot[at, :].astype(F32) + norm_back(grad, standard, inverse, small[2:3, :])
        dhid[at, :] = total
        da[at, :] = total.astype(BF)

    each_piece(rows, 32, back)
    for copy in loads[4:]:
        copy.wait()

    def away(k):
        to = lax.rem(z + k, line)
        return send(
            dsend.at[to], datt.at[pl.ds(pl.multiple_of(z * rows, rows), rows)], ass.at[k], ars.at[z], d, to
        )

    @pl.loop(1, line + 1)
    def _(k):
        to = lax.rem(z + k, line)
        dsend[to] = nt(da[...], wo[pl.ds(pl.multiple_of(to * width, width), width), :]).astype(BF)
        pl.when(k < line)(lambda: away(k).start())

    datt[pl.ds(pl.multiple_of(z * rows, rows), rows), :] = dsend[z]
    for lo, size in spans(model, 512):
        att_t[pl.ds(lo, size), :] = attr[:, pl.ds(lo, size)].T
    lse_t[...] = lse[...].T

    def oblock(t):
        return nn(att_t[...], da[:, pl.ds(pl.multiple_of(t * rows, rows), rows)])

    def across(k):
        return send(ostage.at[lax.rem(k, 2)], oex.at[k], oss.at[k], ors.at[k], d + flips[1], z)

    @pl.loop(0, blocks)
    def _(k):
        pl.when(k >= 2)(lambda: across(k - 2).wait_send())
        ostage[lax.rem(k, 2)] = oblock(2 * k + 1 - core).astype(BF)
        across(k).start()

    planes = PlaneSum(osum, orecv, d, z, blocks, pss, prs)

    @pl.loop(0, blocks)
    def _(j):
        k = planes.chip_at(j)
        across(k).wait_recv()
        fetch = pltpu.make_async_copy(oex.at[k], ofetch, local.at[8])
        fetch.start()
        fetch.wait()
        osum[k] = (oblock(2 * k + core) + ofetch[...].astype(F32)).astype(BF)
        pl.when(j < blocks - 1)(lambda: planes.copy(j).start())

    across(blocks - 2).wait_send()
    across(blocks - 1).wait_send()
    sum_blocks(ghalf.at[chip], grecv, ggrad, sbuf, sobuf, ssem, rows // sbuf.shape[1])
    for k in range(1, line):
        frm = lax.rem(z + k, line)
        send(dsend.at[frm], datt.at[pl.ds(pl.multiple_of(frm * rows, rows), rows)], ass.at[k], ars.at[frm], d, frm).wait_recv()

    scatter.relay(1)
    lanes = lax.broadcasted_iota(jnp.int32, (1, 128), 1)
    mine = (lanes < 64, lanes >= 64)
    which = lax.broadcasted_iota(jnp.int32, (16, 128), 0)
    lane16 = lax.broadcasted_iota(jnp.int32, (16, 128), 1)
    pick = jnp.where(which == lax.div(lane16, 64), 1.0, 0.0).astype(BF)
    scale = HEAD_DIM**-0.5

    def zaway(k):
        to = lax.rem(z + k, line)
        return send(
            ofull.at[pl.ds(pl.multiple_of(to * width, width), width)], ozr.at[k - 1], zss.at[k], zrs.at[k - 1], d, to
        )

    def plane_total():
        planes.wait()

        def add(at):
            total = osum[chip, at, :].astype(F32)
            for j in range(blocks - 1):
                total = total + orecv[j, at, :].astype(F32)
            ofull[at, :] = total.astype(BF)

        each_piece(model, 256, add)
        for k in range(1, line):
            zaway(k).start()

    def back_pair(p):
        cols = pl.ds(pl.multiple_of(p * 128, 128), 128)
        do = datt[:, cols]
        prod = do.astype(F32) * attc[:, cols].astype(F32)
        high = prod.astype(BF)
        inner = nt(pick, high) + nt(pick, (prod - high.astype(F32)).astype(BF))
        q = qbuf[0, p] * BF(scale)
        dq[...] = jnp.zeros_like(dq)
        for kj in range(line):
            at = pl.ds(kj * rows, rows)
            lo, count = kj * rows, length - kj * rows
            k, v = qbuf[1, p, at, :], qbuf[2, p, at, :]
            row = lax.broadcasted_iota(jnp.int32, (rows, count), 0)
            col = lax.broadcasted_iota(jnp.int32, (rows, count), 1)
            keep = col >= row
            dk = jnp.zeros((rows, 128), F32)
            dv = jnp.zeros((rows, 128), F32)
            for a in range(2):
                km, vm = jnp.where(mine[a], k, BF(0)), jnp.where(mine[a], v, BF(0))
                qm, dm = jnp.where(mine[a], q[lo:], BF(0)), jnp.where(mine[a], do[lo:], BF(0))
                s = jnp.where(keep, nt(km, q[lo:]), -1e30)
                probs = jnp.exp(s - lse_t[pl.ds(2 * p + a, 1), pl.ds(lo, count)])
                dv += nn(probs.astype(BF), dm)
                dprobs = nt(vm, do[lo:])
                ds = (probs * (dprobs - inner[a : a + 1, lo:])).astype(BF)
                dk += nn(ds, qm)
                dq[pl.ds(lo, count), :] += tn(ds, km)
            dk = turn(dk, cos[at, :], sin_up[at, :], sin_down[at, :], -1.0)
            dpre[at, pl.ds(pl.multiple_of(width + p * 128, 128), 128)] = dk.astype(BF)
            dpre[at, pl.ds(pl.multiple_of(2 * width + p * 128, 128), 128)] = dv.astype(BF)
        dpre[:, cols] = turn(dq[...] * scale, cos[...], sin_up[...], sin_down[...], -1.0).astype(BF)

    @pl.loop(0, pairs)
    def _(p):
        back_pair(p)
        pl.when(p == 1)(lambda: scatter.relay(2))

    plane_total()
    ups.wait()
    sum_blocks(uhalf.at[chip], urecv, ugrad, sbuf, sobuf, ssem, rows // sbuf.shape[1])
    for h in range(2):
        scatter.arrive(h)

        @pl.loop(0, half // 32)
        def _(i):
            at = pl.ds(pl.multiple_of(h * half + i * 32, 32), 32)
            total = scatter.total(h, pl.ds(pl.multiple_of(i * 32, 32), 32))
            lay[at, :] = (hid[at, :] + total).astype(BF)

    total = ofull[pl.ds(pl.multiple_of(z * width, width), width), :].astype(F32)
    for k in range(1, line):
        zaway(k).wait()
        total = total + ozr[k - 1].astype(F32)
    ograd[...] = total
    for k in range(1, line):
        away(k).wait_send()
    scatter.finish()


def attention_backward(dn2, hid, cot, small, wout, attall, qkv, lse, mixed, ghalf, grecv, uhalf, tabs):
    rows, model = hid.shape
    line = 4
    length = rows * line
    width = model // line
    pairs = width // 128
    blocks = model // rows // 2
    hidden = ghalf.shape[2]
    sds = jax.ShapeDtypeStruct
    dma = pltpu.SemaphoreType.DMA
    return pl.pallas_call(
        attention_back_kernel,
        out_shape=(
            sds((rows, model), BF), sds((rows, model), F32), sds((length, 3 * width), BF),
            sds((width, rows), F32), sds((rows, hidden), F32), sds((rows, hidden), F32), sds((8, model), F32),
            sds((blocks - 1, rows, hidden), BF), sds((blocks, model, rows), BF),
        ),
        in_specs=[INV, INV, INV, INV, ANY, ANY, ANY, INV, ANY, ANY, ANY, ANY, INV, INV, INV],
        out_specs=(INV, INV, INV, INV, ANY, ANY, INV, ANY, ANY),
        scratch_shapes=[
            pltpu.VMEM((model, model), BF),
            pltpu.VMEM((rows, model), BF),
            pltpu.VMEM((rows, model), BF),
            pltpu.VMEM((model, rows), BF),
            pltpu.VMEM((length, width), BF),
            pltpu.VMEM((3, pairs, length, 128), BF),
            pltpu.VMEM((line, rows, width), BF),
            pltpu.VMEM((length, width), BF),
            pltpu.VMEM((128, length), F32),
            pltpu.VMEM((line, rows, model), BF),
            pltpu.VMEM((line + 1, rows, model), BF),
            pltpu.VMEM((2, model, rows), BF),
            pltpu.VMEM((model, rows), BF),
            pltpu.VMEM((blocks, model, rows), BF),
            pltpu.VMEM((blocks - 1, model, rows), BF),
            pltpu.VMEM((model, rows), BF),
            pltpu.VMEM((line - 1, width, rows), BF),
            pltpu.VMEM((blocks, 64, hidden), BF),
            pltpu.VMEM((64, hidden), F32),
            pltpu.VMEM((length, 128), F32),
            dma((line, 2)), dma((line + 1, 2)), dma((line,)), dma((line,)), dma((blocks,)), dma((blocks,)),
            dma((blocks,)), dma((blocks,)), dma((blocks,)), dma((blocks,)), dma((line,)), dma((line,)),
            dma((10,)), dma((blocks + 1,)),
        ],
        compiler_params=pltpu.CompilerParams(
            collective_id=3, has_side_effects=True, vmem_limit_bytes=62 * 1024 * 1024
        ),
        cost_estimate=pl.CostEstimate(flops=10**11, bytes_accessed=10**8, transcendentals=0),
        name="attention_backward",
    )(dn2, hid, cot, small, wout, attall, qkv, lse, mixed, ghalf, grecv, uhalf, *tabs)


def input_back_kernel(
    dpre, wqkv, n1, dhalf, tok, dhid, small, sums_in,
    tgrad, qgrad, dgrad, sums, drecv, qex,
    pbuf, wbuf, nbuf, part, slots, qstage, qfetch, qsum, qrecv, zsums, dsums, sbuf, sobuf,
    ss, rs, xss, xrs, pss, prs, dss, drs, zss, zrs, gss, grs, local, ssem,
):
    line = 4
    rows, model = tok.shape
    width = dpre.shape[1] // 3
    blocks = model // rows // 2
    d, z, flips = place()
    greet(d, z, flips, line, range(1, 8))
    core, chip = lax.rem(d, 2), lax.div(d, 2)
    loads = [
        pltpu.make_async_copy(a, b, local.at[i]) for i, (a, b) in enumerate(((dpre, pbuf), (wqkv, wbuf), (n1, nbuf)))
    ]
    for copy in loads:
        copy.start()
    downs = PlaneSum(dhalf, drecv, d, z, blocks, dss, drs)
    half = rows // 2
    scatter = LineScatter(
        lambda s, h: part.at[s, pl.ds(h * half, half)],
        lambda i, h: slots.at[i, pl.ds(h * half, half)],
        2, d, z, line, ss, rs,
    )
    pl.when(z == 0)(lambda: slots.__setitem__((0,), jnp.zeros((rows, model), BF)))
    pl.when(z == line - 1)(lambda: slots.__setitem__((line,), jnp.zeros((rows, model), BF)))
    for copy in loads[:2]:
        copy.wait()

    @pl.loop(0, line)
    def _(i):
        s = far_first(z, i)
        at = pl.ds(pl.multiple_of(s * rows, rows), rows)
        for lo, size in spans(model, 512):
            part[s, :, pl.ds(lo, size)] = nt(pbuf[at, :], wbuf[pl.ds(lo, size), :]).astype(BF)
        scatter.head(s)

    loads[2].wait()
    sums[...] = sums_in[...]

    def bias(at):
        sums[4:5, : 3 * width] += jnp.sum(pbuf[at, :].astype(F32), 0, keepdims=True)

    each_piece(rows * line, 64, bias)

    def qblock(t):
        return lambda lo, size: tn(nbuf[:, pl.ds(pl.multiple_of(t * rows, rows), rows)], pbuf[:, pl.ds(lo, size)])

    def across(k):
        return send(qstage.at[k], qex.at[k], xss.at[k], xrs.at[k], d + flips[1], z)

    @pl.loop(0, blocks)
    def _(k):
        make = qblock(2 * k + 1 - core)
        for lo, size in spans(3 * width, 512):
            qstage[k, :, pl.ds(lo, size)] = make(lo, size).astype(BF)
        across(k).start()

    scatter.relay(1)
    planes = PlaneSum(qsum, qrecv, d, z, blocks, pss, prs)

    @pl.loop(0, blocks)
    def _(j):
        k = planes.chip_at(j)
        across(k).wait_recv()
        fetch = pltpu.make_async_copy(qex.at[k], qfetch, local.at[3])
        fetch.start()
        fetch.wait()
        make = qblock(2 * k + core)
        for lo, size in spans(3 * width, 512):
            qsum[k, :, pl.ds(lo, size)] = (make(lo, size) + qfetch[:, pl.ds(lo, size)].astype(F32)).astype(BF)
        pl.when(j < blocks - 1)(lambda: planes.copy(j).start())

    for j in range(blocks - 1):
        downs.copy(j).start()
    scatter.relay(2)
    planes.wait()
    for j in range(3):
        cols = pl.ds(j * width, width)
        total = qsum[chip, :, cols].astype(F32)
        for i in range(blocks - 1):
            total = total + qrecv[i, :, cols].astype(F32)
        qgrad[j] = total
    downs.wait()
    sum_blocks(dhalf.at[chip], drecv, dgrad, sbuf, sobuf, ssem, dhalf.shape[1] // sbuf.shape[1])
    for h in range(2):
        scatter.arrive(h)

        @pl.loop(0, half // 32)
        def _(i):
            at = pl.ds(pl.multiple_of(h * half + i * 32, 32), 32)
            grad = scatter.total(h, pl.ds(pl.multiple_of(i * 32, 32), 32))
            standard, inverse = norm_parts(tok[at, :].astype(F32))
            sums[0:1, :] += jnp.sum(grad * standard, 0, keepdims=True)
            sums[1:2, :] += jnp.sum(grad, 0, keepdims=True)
            tgrad[at, :] = (dhid[at, :] + norm_back(grad, standard, inverse, small[0:1, :])).astype(BF)

    def zcopy(k):
        to = lax.rem(z + k, line)
        return send(sums, zsums.at[k - 1], zss.at[k], zrs.at[k - 1], d, to)

    def dcopy(r):
        return send(dsums.at[0], dsums.at[r], gss.at[r], grs.at[r], d + flips[r], z)

    for k in range(1, line):
        zcopy(k).start()
    for k in range(1, line):
        zcopy(k).wait()
    dsums[0] = sums[...]
    dsums[0, 0:4, :] = sums[0:4, :] + zsums[0, 0:4, :] + zsums[1, 0:4, :] + zsums[2, 0:4, :]
    for r in range(1, 8):
        dcopy(r).start()
    for r in range(1, 8):
        dcopy(r).wait()
    total = dsums[0]
    for r in range(1, 8):
        total = total + dsums[r]
    sums[...] = total
    for k in range(blocks):
        across(k).wait_send()
    scatter.finish()


def input_backward(dpre, wqkv, n1, dhalf, tok, dhid, small, sums):
    rows, model = tok.shape
    line = 4
    length = rows * line
    triple = dpre.shape[1]
    blocks = model // rows // 2
    hidden = dhalf.shape[1]
    sds = jax.ShapeDtypeStruct
    dma = pltpu.SemaphoreType.DMA
    return pl.pallas_call(
        input_back_kernel,
        out_shape=(
            sds((rows, model), BF), sds((3, rows, triple // 3), F32), sds((hidden, rows), F32), sds((8, model), F32),
            sds((blocks - 1, hidden, rows), BF), sds((blocks, rows, triple), BF),
        ),
        in_specs=[ANY, ANY, ANY, ANY, INV, INV, INV, INV],
        out_specs=(INV, INV, ANY, INV, ANY, ANY),
        scratch_shapes=[
            pltpu.VMEM((length, triple), BF),
            pltpu.VMEM((model, triple), BF),
            pltpu.VMEM((length, model), BF),
            pltpu.VMEM((line, rows, model), BF),
            pltpu.VMEM((line + 1, rows, model), BF),
            pltpu.VMEM((blocks, rows, triple), BF),
            pltpu.VMEM((rows, triple), BF),
            pltpu.VMEM((blocks, rows, triple), BF),
            pltpu.VMEM((blocks - 1, rows, triple), BF),
            pltpu.VMEM((line - 1, 8, model), F32),
            pltpu.VMEM((8, 8, model), F32),
            pltpu.VMEM((blocks, 352, rows), BF),
            pltpu.VMEM((352, rows), F32),
            dma((line, 2)), dma((line + 1, 2)), dma((blocks,)), dma((blocks,)), dma((blocks,)), dma((blocks,)),
            dma((blocks,)), dma((blocks,)), dma((line,)), dma((line,)), dma((8,)), dma((8,)),
            dma((4,)), dma((blocks + 1,)),
        ],
        compiler_params=pltpu.CompilerParams(
            collective_id=4, has_side_effects=True, vmem_limit_bytes=62 * 1024 * 1024
        ),
        cost_estimate=pl.CostEstimate(flops=10**11, bytes_accessed=10**8, transcendentals=0),
        name="input_backward",
    )(dpre, wqkv, n1, dhalf, tok, dhid, small, sums)


def turn_tables(length):
    cosine, sine = tables(length)
    rest = HEAD_DIM - ROT
    half = ROT // 2
    cos = jnp.concatenate([cosine, jnp.ones((length, rest), F32)], -1)
    none = jnp.zeros((length, half), F32)
    tail = jnp.zeros((length, rest), F32)
    up = jnp.concatenate([none, sine[:, half:], tail], -1)
    down = jnp.concatenate([-sine[:, :half], none, tail], -1)
    return tuple(jnp.concatenate([t, t], -1) for t in (cos, up, down))


def pack_smalls(d, model, width, qkv_bias, *vectors):
    col = lax.broadcasted_iota(jnp.int32, (1, model), 1)
    each = vectors[0].shape[0]
    gains = jnp.stack([jnp.tile(v, model // each) for v in vectors], 0)
    gains = jnp.where(col // each == d, gains, 0)
    part = qkv_bias.shape[1]
    bias = jnp.tile(qkv_bias, (1, width // part)).reshape(1, 3 * width)
    bias = jnp.pad(bias, ((0, 0), (0, model - 3 * width)))
    bias = jnp.where(col % width // part == d, bias, 0)
    return jnp.concatenate([gains, bias, jnp.zeros((11, model), BF)], 0).astype(BF)


def fast(
    tokens, qkv_weight, qkv_bias, out_weight, norm1_gain, norm1_shift, gate_weight, up_weight,
    down_weight, norm2_gain, norm2_shift, cotangent,
):
    d = lax.axis_index("dp")
    z = lax.axis_index("tensor")
    rows, model = tokens.shape
    length = 4 * rows
    tabs = turn_tables(length)
    depth, width = qkv_weight.shape[1:]
    smalls = pack_smalls(d, model, width, qkv_bias, norm1_gain, norm1_shift, norm2_gain, norm2_shift)
    wq = qkv_weight.transpose(1, 0, 2).reshape(depth, 3 * width)
    xall, cotall, n1, qkv, lse, attall, wqkv, small = attention_forward(tokens, cotangent, wq, smalls, tabs)
    wout = lax.all_gather(out_weight, "tensor", axis=0, tiled=True)
    wout = lax.all_gather(wout, "dp", axis=1, tiled=True)
    wgate = lax.all_gather(gate_weight, "dp", axis=0, tiled=True)
    wup = lax.all_gather(up_weight, "dp", axis=0, tiled=True)
    wdown = lax.all_gather(down_weight, "dp", axis=1, tiled=True)
    hidden_all = xall.astype(F32) + nn(attall, wout)
    n2, _, _ = apply_layer_norm(hidden_all, small[2], small[3])
    hidden = lax.dynamic_slice_in_dim(hidden_all, z * rows, rows, 0)
    dn2, mixed, _, _, _, ghalf, uhalf, dhalf, grecv = mlp(n2.astype(BF), cotall, wgate, wup, wdown)
    layer_output, dhid, dpre, outw_grad, gatew_grad, upw_grad, sums, _, _ = attention_backward(
        dn2, hidden, cotangent, small, wout, attall, qkv, lse, mixed, ghalf, grecv, uhalf, tabs
    )
    token_gradient, qkvw_grad, downw_grad, sums, _, _ = input_backward(
        dpre, wqkv, n1, dhalf, tokens, dhid, small, sums
    )
    gains = lax.dynamic_slice_in_dim(sums[:4], d * depth, depth, 1)
    part = qkv_bias.shape[1]
    bias = sums[4, : 3 * width].reshape(3, width)
    qkvb_grad = lax.dynamic_slice_in_dim(bias, d * part, part, 1)
    return (
        layer_output, token_gradient, qkvw_grad, qkvb_grad, outw_grad, gains[0], gains[1],
        gatew_grad, upw_grad, downw_grad, gains[2], gains[3],
    )


def solution(mesh):
    placed = (
        P(("dp", "tensor"), None),
        P(None, "dp", "tensor"),
        P(None, ("tensor", "dp")),
        P("tensor", "dp"),
        P("dp"),
        P("dp"),
        P("dp", "tensor"),
        P("dp", "tensor"),
        P("tensor", "dp"),
        P("dp"),
        P("dp"),
        P(("dp", "tensor"), None),
    )
    return jax.shard_map(
        fast if dict(mesh.shape) == {"dp": 8, "tensor": 4} else local,
        mesh=mesh,
        in_specs=placed,
        out_specs=(
            P(("dp", "tensor"), None),
            P(("dp", "tensor"), None),
            P(None, "dp", "tensor"),
            P(None, ("tensor", "dp")),
            P("tensor", "dp"),
            P("dp"),
            P("dp"),
            P("dp", "tensor"),
            P("dp", "tensor"),
            P("tensor", "dp"),
            P("dp"),
            P("dp"),
        ),
        check_vma=False,
    )
```

```python
import functools

import jax
import jax.numpy as jnp
import numpy as np
from jax import lax
from jax.experimental import pallas as pl
from jax.experimental.pallas import tpu as pltpu
from jax.sharding import PartitionSpec as P

MESH = pl.DeviceIdType.MESH
HEAD_DIM = 64
ROT = 16
BF = jnp.bfloat16
F32 = jnp.float32
VMEM_LIMIT = 56 * 1024 * 1024
ANY = pl.BlockSpec(memory_space=pl.ANY)
INV = pl.BlockSpec(memory_space=pltpu.VMEM)


def nt(a, b):
    return lax.dot_general(a, b, (((1,), (1,)), ((), ())), preferred_element_type=F32)


def tn(a, b):
    return lax.dot_general(a, b, (((0,), (0,)), ((), ())), preferred_element_type=F32)


def nn(a, b):
    return jnp.dot(a, b, preferred_element_type=F32)


def spans(total, step):
    return [(i, min(step, total - i)) for i in range(0, total, step)]


def place():
    d = lax.axis_index("dp")
    z = lax.axis_index("tensor")
    dy = 4 * (1 - 2 * lax.div(d, 4))
    dx = 2 * (1 - 2 * lax.rem(lax.div(d, 2), 2))
    dc = 1 - 2 * lax.rem(d, 2)
    return d, z, (0, dc, dx, dx + dc, dy, dy + dc, dy + dx, dy + dx + dc)


def send(src, dst, ssem, rsem, d, z):
    return pltpu.make_async_remote_copy(
        src_ref=src, dst_ref=dst, send_sem=ssem, recv_sem=rsem, device_id=(d, z), device_id_type=MESH
    )


def greet(d, z, flips, line, plane):
    barrier = pltpu.get_barrier_semaphore()
    for k in range(1, line):
        pl.semaphore_signal(
            barrier, inc=1, device_id=(d, lax.rem(z + k, line)), device_id_type=MESH
        )
    for r in plane:
        pl.semaphore_signal(barrier, inc=1, device_id=(d + flips[r], z), device_id_type=MESH)
    pl.semaphore_wait(barrier, line - 1 + len(plane))


class LineGather:
    def __init__(self, view, chunks, d, z, line, send_sems, recv_sems):
        self.view, self.chunks, self.d, self.z, self.line = view, chunks, d, z, line
        self.ss, self.rs = send_sems, recv_sems

    def copy(self, s, h, way, src=None):
        ref = self.view(s, h)
        return send(
            ref if src is None else src, ref, self.ss.at[way, s, h], self.rs.at[s, h],
            self.d, self.z + (1 if way == 0 else -1),
        )

    def start(self, h, src=None):
        pl.when(self.z < self.line - 1)(lambda: self.copy(self.z, h, 0, src).start())
        pl.when(self.z > 0)(lambda: self.copy(self.z, h, 1, src).start())

    def step(self, k, h, forward=True):
        z, line = self.z, self.line

        @pl.when(z - k >= 0)
        def _():
            self.copy(z - k, h, 0).wait_recv()
            if forward:
                pl.when(z < line - 1)(lambda: self.copy(z - k, h, 0).start())

        @pl.when(z + k < line)
        def _():
            self.copy(z + k, h, 1).wait_recv()
            if forward:
                pl.when(z > 0)(lambda: self.copy(z + k, h, 1).start())

    def finish(self, first=0, last=None):
        z, line = self.z, self.line
        for k in range(first, line if last is None else last):
            for h in range(self.chunks):
                pl.when((z - k >= 0) & (z < line - 1))(lambda: self.copy(z - k, h, 0).wait_send())
                pl.when((z + k < line) & (z > 0))(lambda: self.copy(z + k, h, 1).wait_send())


class PlaneGather:
    def __init__(self, src, view, d, z, flips, send_sems, recv_sems):
        self.src, self.view, self.d, self.z, self.flips = src, view, d, z, flips
        self.ss, self.rs = send_sems, recv_sems
        self.half = src.shape[0] // 2

    def copy(self, key):
        d, f = self.d, self.flips
        block, to, part = {
            1: (0, 1, None), 2: (0, 2, None), 4: (0, 4, None), 3: (2, 1, None), 5: (4, 1, None),
            6: (2, 4, 0), 7: (4, 2, 1), 8: (6, 1, 0), 9: (6, 1, 1),
        }[key]
        dst = self.view(d + f[block])
        src = self.src if block == 0 else dst
        if part is not None:
            at = pl.ds(part * self.half, self.half)
            src, dst = src.at[at], dst.at[at]
        return send(src, dst, self.ss.at[key], self.rs.at[key], d + f[to], self.z)

    def start(self):
        for key in (4, 2, 1):
            self.copy(key).start()

    def relay(self):
        for key, onward in ((2, (6, 3)), (4, (7, 5))):
            self.copy(key).wait_recv()
            for to in onward:
                self.copy(to).start()

    def pass_on(self):
        for key, onward in ((6, 8), (7, 9)):
            self.copy(key).wait_recv()
            self.copy(onward).start()

    def arrive(self):
        for key in (1, 3, 5, 8, 9):
            self.copy(key).wait_recv()

    def finish(self):
        for key in range(1, 10):
            self.copy(key).wait_send()


def arrival(z, i):
    orders = ((0, 1, 2, 3), (1, 0, 2, 3), (2, 3, 1, 0), (3, 2, 1, 0))
    codes = [sum(s * 4**j for j, s in enumerate(o)) for o in orders]
    code = jnp.where(
        z == 0, codes[0], jnp.where(z == 1, codes[1], jnp.where(z == 2, codes[2], codes[3]))
    )
    power = jnp.where(i == 0, 1, jnp.where(i == 1, 4, jnp.where(i == 2, 16, 64)))
    return lax.rem(lax.div(code, power), 4)


def turn(u, cos, sin_up, sin_down, sign=1.0):
    moved = pltpu.roll(u, 8, 1) * sin_up + pltpu.roll(u, 120, 1) * sin_down
    return u * cos + moved if sign > 0 else u * cos - moved


def attention_kernel(
    tok, cot, wq, ow, gw, uw, dw, smalls, cos, sin_up, sin_down,
    cotnear, n1, qkv, lse, attall, wqkv, small_sum, wout, n2, hidden, wgate, wup, wdown,
    xbuf, n1buf, wbuf, qbuf, attv, wz, wo, acc, smbuf,
    tss, trs, css, crs, ass, ars, mss, mrs, yss, yrs, pss, prs, local,
):
    rows, model = tok.shape
    width = wq.shape[1] // 3
    pairs = width // 128
    line = 4
    d, z, flips = place()
    greet(d, z, flips, line, range(1, 8))

    tok_in = pltpu.make_async_copy(tok, xbuf.at[z], local.at[0])
    tok_in.start()
    depth = wq.shape[0]

    def wblock(i):
        return wbuf.at[pl.ds(pl.multiple_of(i * depth, 256), depth), :]

    w_in = pltpu.make_async_copy(wq, wblock(d), local.at[2])
    w_in.start()
    tall = ow.shape[0]

    def oview(s, h):
        return wz.at[pl.ds(pl.multiple_of(s * tall, tall), tall)]

    def oblock(i):
        return wo.at[:, pl.ds(pl.multiple_of(i * depth, 256), depth)]

    o_in = pltpu.make_async_copy(ow, oview(z, 0), local.at[14])
    o_in.start()
    outs_z = LineGather(oview, 1, d, z, line, yss, yrs)
    small_copies = [
        send(smalls, smbuf.at[r], mss.at[r], mrs.at[r], d + flips[r], z) for r in range(1, 8)
    ]
    for copy in small_copies:
        copy.start()
    tall_block = dw.shape[1]

    def rows_of(ref, i):
        return ref.at[pl.ds(pl.multiple_of(i * depth, 256), depth)]

    def columns_of(ref, i):
        return ref.at[:, pl.ds(pl.multiple_of(i * tall_block, 256), tall_block)]

    planes = [
        PlaneGather(src, view, d, z, flips, pss.at[i], prs.at[i])
        for i, (src, view) in enumerate((
            (wq, wblock),
            (wz, oblock),
            (gw, lambda i: rows_of(wgate, i)),
            (uw, lambda i: rows_of(wup, i)),
            (dw, lambda i: columns_of(wdown, i)),
        ))
    ]
    qkv_plane, out_plane, gate_plane, up_plane, down_plane = planes
    keep_own = [
        pltpu.make_async_copy(gw, rows_of(wgate, d), local.at[10]),
        pltpu.make_async_copy(uw, rows_of(wup, d), local.at[11]),
        pltpu.make_async_copy(dw, columns_of(wdown, d), local.at[12]),
    ]
    for copy in keep_own:
        copy.start()
    half = rows // 2

    def tview(s, h):
        return xbuf.at[s, pl.ds(h * half, half)]

    def cview(s, h):
        return cotnear.at[s, pl.ds(h * half, half)]

    def aview(s, h):
        return attv.at[:, pl.ds(pl.multiple_of(s * width + h * 128, 128), 128)]

    toks = LineGather(tview, 2, d, z, line, tss, trs)
    cots = LineGather(cview, 2, d, z, line, css, crs)
    atts = LineGather(aview, pairs, d, z, line, ass, ars)
    tok_in.wait()
    for h in range(2):
        toks.start(h)
    qkv_plane.start()
    o_in.wait()
    outs_z.start(0)
    for copy in small_copies:
        copy.wait()
    total = smalls[...].astype(F32)
    for r in range(1, 8):
        total = total + smbuf[r].astype(F32)
    small_sum[...] = total

    def normalise(s):
        piece = 32

        @pl.loop(0, rows // piece)
        def _(i):
            at = pl.ds(pl.multiple_of(i * piece, piece), piece)
            x = xbuf[s, at, :].astype(F32)
            centred = x - jnp.mean(x, -1, keepdims=True)
            spread = jnp.mean(centred * centred, -1, keepdims=True)
            n = centred * lax.rsqrt(spread + 1e-05) * small_sum[0:1, :] + small_sum[1:2, :]
            n1buf[pl.ds(pl.multiple_of(s * rows + i * piece, piece), piece), :] = n.astype(BF)

    def project(s):
        at = pl.ds(pl.multiple_of(s * rows, rows), rows)
        for j in range(3):
            cols = pl.ds(j * width, width)
            pre = nn(n1buf[at, :], wbuf[:, cols]) + small_sum[4:5, cols]
            for p in range(pairs):
                part = pre[:, p * 128 : (p + 1) * 128]
                if j < 2:
                    part = turn(part, cos[at, :], sin_up[at, :], sin_down[at, :])
                qbuf[j, p, at, :] = part.astype(BF)

    normalise(z)
    for h in range(2):
        toks.step(1, h)
    outs_z.step(1, 0)
    qkv_plane.relay()
    gate_plane.start()
    normalise(arrival(z, 1))
    qkv_plane.pass_on()
    for h in range(2):
        toks.step(2, h)
    outs_z.step(2, 0)
    normalise(arrival(z, 2))
    gate_plane.relay()
    w_in.wait()
    qkv_plane.arrive()

    @pl.loop(0, line)
    def _(i):
        s = arrival(z, i)

        @pl.when(i == line - 1)
        def _():
            gate_plane.pass_on()
            for h in range(2):
                toks.step(3, h)
            for h in range(2):
                cots.start(h, cot.at[pl.ds(h * half, half)])
            outs_z.step(3, 0)
            out_plane.start()
            normalise(s)

        project(s)

    o_own = pltpu.make_async_copy(wz, oblock(d), local.at[15])
    o_own.start()

    outs = [
        pltpu.make_async_copy(n1buf, n1, local.at[3]),
        pltpu.make_async_copy(wbuf, wqkv, local.at[4]),
        pltpu.make_async_copy(qbuf, qkv, local.at[5]),
    ]
    for copy in outs:
        copy.start()

    lanes = lax.broadcasted_iota(jnp.int32, (1, 128), 1)
    first = lanes < 64
    lse[...] = jnp.zeros_like(lse)
    length = rows * line

    def attend(p):
        for qi in range(line):
            count = (qi + 1) * rows
            at = pl.ds(qi * rows, rows)
            q = qbuf[0, p, at, :] * BF(HEAD_DIM**-0.5)
            k = qbuf[1, p, pl.ds(0, count), :]
            v = qbuf[2, p, pl.ds(0, count), :]
            row = lax.broadcasted_iota(jnp.int32, (rows, count), 0) + qi * rows
            col = lax.broadcasted_iota(jnp.int32, (rows, count), 1)
            keep = row >= col
            results = []
            stats = lse[at, :]
            for a in range(2):
                mine = first if a == 0 else ~first
                s = nt(jnp.where(mine, q, BF(0)), k)
                s = jnp.where(keep, s, -1e30)
                most = jnp.max(s, -1, keepdims=True)
                e = jnp.exp(s - most)
                total = jnp.sum(e, -1, keepdims=True)
                results.append(nn(e.astype(BF), v) / total)
                stats = jnp.where(lanes == 2 * p + a, most + jnp.log(total), stats)
            lse[at, :] = stats
            attv[at, pl.ds(pl.multiple_of(z * width + p * 128, 128), 128)] = jnp.where(
                first, results[0], results[1]
            ).astype(BF)

    @pl.loop(0, pairs)
    def _(p):
        attend(p)
        atts.start(p)

    up_plane.start()
    for p in range(pairs):
        atts.step(1, p)
    for h in range(2):
        cots.step(1, h, forward=False)
    out_plane.relay()
    down_plane.start()
    out_plane.pass_on()
    for p in range(pairs):
        atts.step(2, p)
    o_own.wait()
    out_plane.arrive()
    keep_wo = pltpu.make_async_copy(wo, wout, local.at[6])
    keep_wo.start()

    def project_out(s, at, lo, size):
        heads = pl.ds(pl.multiple_of(s * width, width), width)
        return nn(attv[at, heads], wo[heads, pl.ds(lo, size)])

    for i in range(line - 1):
        s = arrival(z, i)

        @pl.loop(0, line)
        def _(r):
            at = pl.ds(pl.multiple_of(r * rows, rows), rows)
            for lo, size in spans(model, 512):
                base = xbuf[r, :, pl.ds(lo, size)].astype(F32) if i == 0 else acc[at, pl.ds(lo, size)]
                acc[at, pl.ds(lo, size)] = base + project_out(s, at, lo, size)

        if i == 1:
            up_plane.relay()
    for copy in outs:
        copy.wait()
    down_plane.relay()
    up_plane.pass_on()
    for p in range(pairs):
        atts.step(3, p)
    keep_att = pltpu.make_async_copy(attv, attall, local.at[7])
    keep_att.start()
    last = arrival(z, line - 1)

    @pl.loop(0, line)
    def _(r):
        at = pl.ds(pl.multiple_of(r * rows, rows), rows)
        for lo, size in spans(model, 512):
            acc[at, pl.ds(lo, size)] += project_out(last, at, lo, size)

        @pl.loop(0, rows // 32)
        def _(i):
            piece = pl.ds(pl.multiple_of(r * rows + i * 32, 32), 32)
            x = acc[piece, :]
            centred = x - jnp.mean(x, -1, keepdims=True)
            spread = jnp.mean(centred * centred, -1, keepdims=True)
            n = centred * lax.rsqrt(spread + 1e-05) * small_sum[2:3, :] + small_sum[3:4, :]
            n1buf[piece, :] = n.astype(BF)

    keep = [
        pltpu.make_async_copy(n1buf, n2, local.at[8]),
        pltpu.make_async_copy(acc.at[pl.ds(pl.multiple_of(z * rows, rows), rows)], hidden, local.at[9]),
        keep_wo, keep_att,
    ]
    for copy in keep[:2]:
        copy.start()
    down_plane.pass_on()
    for gather in (toks, atts, outs_z):
        gather.finish()
    cots.finish(0, 1)
    for plane in (gate_plane, up_plane, down_plane):
        plane.arrive()
    for plane in planes:
        plane.finish()
    for copy in keep_own:
        copy.wait()
    for copy in keep:
        copy.wait()


def attention_forward(tok, cot, wq, ow, gw, uw, dw, smalls, tabs):
    rows, model = tok.shape
    line = 4
    length = rows * line
    depth, width = wq.shape
    width //= 3
    pairs = width // 128
    dp = model // depth
    hidden = gw.shape[1]
    sds = jax.ShapeDtypeStruct
    return pl.pallas_call(
        attention_kernel,
        out_shape=(
            sds((line, rows, model), BF), sds((length, model), BF),
            sds((3, pairs, length, 128), BF), sds((length, 128), F32), sds((length, model), BF),
            sds((model, 3 * width), BF), sds((16, model), F32),
            sds((model, model), BF), sds((length, model), BF), sds((rows, model), F32),
            sds((model, hidden), BF), sds((model, hidden), BF), sds((hidden, model), BF),
        ),
        in_specs=[ANY] * 7 + [INV] * 4,
        out_specs=(ANY, ANY, ANY, INV, ANY, ANY, INV) + (ANY,) * 6,
        scratch_shapes=[
            pltpu.VMEM((line, rows, model), BF),
            pltpu.VMEM((length, model), BF),
            pltpu.VMEM((model, 3 * width), BF),
            pltpu.VMEM((3, pairs, length, 128), BF),
            pltpu.VMEM((length, model), BF),
            pltpu.VMEM((model, depth), BF),
            pltpu.VMEM((model, model), BF),
            pltpu.VMEM((length, model), F32),
            pltpu.VMEM((dp, 16, model), BF),
            pltpu.SemaphoreType.DMA((2, line, 2)),
            pltpu.SemaphoreType.DMA((line, 2)),
            pltpu.SemaphoreType.DMA((2, line, 2)),
            pltpu.SemaphoreType.DMA((line, 2)),
            pltpu.SemaphoreType.DMA((2, line, pairs)),
            pltpu.SemaphoreType.DMA((line, pairs)),
            pltpu.SemaphoreType.DMA((8,)),
            pltpu.SemaphoreType.DMA((8,)),
            pltpu.SemaphoreType.DMA((2, line, 1)),
            pltpu.SemaphoreType.DMA((line, 1)),
            pltpu.SemaphoreType.DMA((5, 10)),
            pltpu.SemaphoreType.DMA((5, 10)),
            pltpu.SemaphoreType.DMA((16,)),
        ],
        compiler_params=pltpu.CompilerParams(
            collective_id=1, has_side_effects=True, vmem_limit_bytes=VMEM_LIMIT
        ),
        cost_estimate=pl.CostEstimate(flops=2 * 10**11, bytes_accessed=10**8, transcendentals=0),
        name="attention_forward",
    )(tok, cot, wq, ow, gw, uw, dw, smalls, *tabs)


def apply_layer_norm(value, norm_scale, norm_bias):
    centered_input = value - jnp.mean(value, -1, keepdims=True)
    spread = jnp.mean(centered_input * centered_input, -1, keepdims=True)
    inverse_deviation = lax.rsqrt(spread + 1e-05)
    standardized_input = centered_input * inverse_deviation
    return (
        standardized_input * norm_scale.astype(jnp.float32) + norm_bias.astype(jnp.float32),
        standardized_input,
        inverse_deviation,
    )


def layer_norm_backward(output_gradient, standardized_input, inverse_deviation, norm_scale):
    scaled_gradient = output_gradient * norm_scale.astype(jnp.float32)
    return inverse_deviation * (
        scaled_gradient
        - jnp.mean(scaled_gradient, -1, keepdims=True)
        - standardized_input * jnp.mean(scaled_gradient * standardized_input, -1, keepdims=True)
    )


def tables(length):
    positions = jnp.arange(length, dtype=jnp.float32)
    freqs = 10000.0 ** (-jnp.arange(0, ROT, 2, dtype=jnp.float32) / ROT)
    angles = positions[:, None] * freqs[None, :]
    angles = jnp.concatenate([angles, angles], -1)
    return (jnp.cos(angles), jnp.sin(angles))


def rotate(heads, cosine, sine):
    half = ROT // 2
    part = heads[..., :ROT]
    turned = jnp.concatenate([-part[..., half:], part[..., :half]], -1)
    moved = part * cosine[:, None, :] + turned * sine[:, None, :]
    return jnp.concatenate([moved, heads[..., ROT:]], -1)


def unrotate(output_gradient, cosine, sine):
    half = ROT // 2
    part = output_gradient[..., :ROT]
    scaled_gradient = part * sine[:, None, :]
    back = jnp.concatenate([scaled_gradient[..., half:], -scaled_gradient[..., :half]], -1)
    moved = part * cosine[:, None, :] + back
    return jnp.concatenate([moved, output_gradient[..., ROT:]], -1)


def attn_params(qkv_weight, qkv_bias, out_weight, norm1_gain, norm1_shift):
    return (
        lax.all_gather(qkv_weight, "dp", axis=1, tiled=True),
        lax.all_gather(qkv_bias, "dp", axis=1, tiled=True),
        lax.all_gather(out_weight, "dp", axis=1, tiled=True),
        lax.all_gather(norm1_gain, "dp", axis=0, tiled=True),
        lax.all_gather(norm1_shift, "dp", axis=0, tiled=True),
    )


def mlp_params(gate_weight, up_weight, down_weight, norm2_gain, norm2_shift):
    return (
        lax.all_gather(gate_weight, "dp", axis=0, tiled=True),
        lax.all_gather(up_weight, "dp", axis=0, tiled=True),
        lax.all_gather(down_weight, "dp", axis=1, tiled=True),
        lax.all_gather(norm2_gain, "dp", axis=0, tiled=True),
        lax.all_gather(norm2_shift, "dp", axis=0, tiled=True),
    )


def gather_rows(rows):
    return lax.all_gather(rows, "tensor", axis=0, tiled=True)


def sum_rows(partial_value):
    return lax.psum_scatter(
        partial_value.astype(jnp.bfloat16), "tensor", scatter_dimension=0, tiled=True
    ).astype(jnp.float32)


def gather_grads(rows):
    return lax.all_gather(rows, "tensor", axis=0, tiled=True)


def sum_grads(partial_value):
    return lax.psum_scatter(
        partial_value.astype(jnp.bfloat16), "tensor", scatter_dimension=0, tiled=True
    ).astype(jnp.float32)


def local(
    tokens,
    qkv_weight,
    qkv_bias,
    out_weight,
    norm1_gain,
    norm1_shift,
    gate_weight,
    up_weight,
    down_weight,
    norm2_gain,
    norm2_shift,
    cotangent,
):
    scale = HEAD_DIM ** (-0.5)
    input_rows = tokens.astype(jnp.float32)
    wqkv, bqkv, wout, first_norm_scale, first_norm_bias = attn_params(
        qkv_weight, qkv_bias, out_weight, norm1_gain, norm1_shift
    )
    first_normed_rows, first_standardized, first_inverse_deviation = apply_layer_norm(
        input_rows, first_norm_scale, first_norm_bias
    )
    rows1 = gather_rows(first_normed_rows.astype(jnp.bfloat16))
    length = rows1.shape[0]
    width = wqkv.shape[2]
    local_heads = width // HEAD_DIM
    pre = (
        jnp.einsum("sd,jdc->jsc", rows1, wqkv, preferred_element_type=jnp.float32)
        + bqkv.astype(jnp.float32)[:, None, :]
    )
    cosine, sine = tables(length)
    query = rotate(pre[0].reshape(length, local_heads, HEAD_DIM), cosine, sine).astype(jnp.bfloat16)
    keys = rotate(pre[1].reshape(length, local_heads, HEAD_DIM), cosine, sine).astype(jnp.bfloat16)
    values = pre[2].reshape(length, local_heads, HEAD_DIM).astype(jnp.bfloat16)
    block = min(length, 512)
    count = length // block
    cols = jnp.arange(length, dtype=jnp.int32)

    def block_probs(qblock, start):
        scores = (
            jnp.einsum("qhd,khd->hqk", qblock, keys, preferred_element_type=jnp.float32) * scale
        )
        rows = start + jnp.arange(block, dtype=jnp.int32)
        keep = rows[:, None] >= cols[None, :]
        return jnp.where(keep[None], scores, -1e30)

    def forward_block(index):
        qblock = lax.dynamic_slice_in_dim(query, index * block, block, 0)
        scores = block_probs(qblock, index * block)
        most = jnp.max(scores, -1, keepdims=True)
        expo = jnp.exp(scores - most)
        total = jnp.sum(expo, -1, keepdims=True)
        probs = (expo / total).astype(jnp.bfloat16)
        out_block = jnp.einsum("hqk,khd->qhd", probs, values, preferred_element_type=jnp.float32)
        return (out_block.astype(jnp.bfloat16), most[..., 0] + jnp.log(total[..., 0]))

    indices = jnp.arange(count, dtype=jnp.int32)
    out_blocks, lse = lax.map(forward_block, indices)
    attended = out_blocks.reshape(length, width)
    branch = jnp.dot(attended, wout, preferred_element_type=jnp.float32)
    hidden_state = input_rows + sum_rows(branch)
    wgate, wup, wdown, second_norm_scale, second_norm_bias = mlp_params(
        gate_weight, up_weight, down_weight, norm2_gain, norm2_shift
    )
    second_normed_rows, second_standardized, second_inverse_deviation = apply_layer_norm(
        hidden_state, second_norm_scale, second_norm_bias
    )
    rows2 = gather_rows(second_normed_rows.astype(jnp.bfloat16))
    gate = jnp.dot(rows2, wgate, preferred_element_type=jnp.float32)
    up = jnp.dot(rows2, wup, preferred_element_type=jnp.float32)
    sigma = jax.nn.sigmoid(gate)
    silu = gate * sigma
    act = (silu * up).astype(jnp.bfloat16)
    mixed = sum_rows(jnp.dot(act, wdown, preferred_element_type=jnp.float32))
    layer_output = (hidden_state + mixed).astype(jnp.bfloat16)
    wgate, wup, wdown, second_norm_scale, second_norm_bias = mlp_params(
        gate_weight, up_weight, down_weight, norm2_gain, norm2_shift
    )
    incoming_gradient = cotangent.astype(jnp.float32)
    down_rows = gather_grads(cotangent)
    down_grad = jnp.einsum("sf,sd->fd", act, down_rows, preferred_element_type=jnp.float32)
    dact = jnp.einsum("sd,fd->sf", down_rows, wdown, preferred_element_type=jnp.float32)
    dgate = (dact * up * (sigma * (1.0 + gate * (1.0 - sigma)))).astype(jnp.bfloat16)
    dup = (dact * silu).astype(jnp.bfloat16)
    gate_grad = jnp.einsum("sd,sf->df", rows2, dgate, preferred_element_type=jnp.float32)
    up_grad = jnp.einsum("sd,sf->df", rows2, dup, preferred_element_type=jnp.float32)
    second_norm_gradient = jnp.einsum(
        "sf,df->sd", dgate, wgate, preferred_element_type=jnp.float32
    ) + jnp.einsum("sf,df->sd", dup, wup, preferred_element_type=jnp.float32)
    second_norm_gradient = sum_grads(second_norm_gradient)
    second_scale_partial = jnp.sum(second_norm_gradient * second_standardized, 0)
    shift2_part = jnp.sum(second_norm_gradient, 0)
    hidden_gradient = incoming_gradient + layer_norm_backward(
        second_norm_gradient, second_standardized, second_inverse_deviation, second_norm_scale
    )
    gatew_grad, upw_grad, downw_grad, gain2_total, shift2_total = (
        lax.psum_scatter(
            gate_grad.astype(jnp.bfloat16), "dp", scatter_dimension=0, tiled=True
        ).astype(jnp.float32),
        lax.psum_scatter(
            up_grad.astype(jnp.bfloat16), "dp", scatter_dimension=0, tiled=True
        ).astype(jnp.float32),
        lax.psum_scatter(
            down_grad.astype(jnp.bfloat16), "dp", scatter_dimension=1, tiled=True
        ).astype(jnp.float32),
        lax.psum_scatter(
            second_scale_partial.astype(jnp.bfloat16), "dp", scatter_dimension=0, tiled=True
        ).astype(jnp.float32),
        lax.psum_scatter(
            shift2_part.astype(jnp.bfloat16), "dp", scatter_dimension=0, tiled=True
        ).astype(jnp.float32),
    )
    wqkv, bqkv, wout, first_norm_scale, first_norm_bias = attn_params(
        qkv_weight, qkv_bias, out_weight, norm1_gain, norm1_shift
    )
    branch_rows = gather_grads(hidden_gradient.astype(jnp.bfloat16))
    out_grad = jnp.einsum("sc,sd->cd", attended, branch_rows, preferred_element_type=jnp.float32)
    dattended = jnp.einsum(
        "sd,cd->sc", branch_rows, wout, preferred_element_type=jnp.float32
    ).astype(jnp.bfloat16)
    dattended = dattended.reshape(length, local_heads, HEAD_DIM)

    def backward_block(carry, item):
        dkeys, dvalues = carry
        index, block_lse = item
        qblock = lax.dynamic_slice_in_dim(query, index * block, block, 0)
        dblock = lax.dynamic_slice_in_dim(dattended, index * block, block, 0)
        scores = block_probs(qblock, index * block)
        probs = jnp.exp(scores - block_lse[..., None])
        probs16 = probs.astype(jnp.bfloat16)
        dvalues = dvalues + jnp.einsum(
            "hqk,qhd->khd", probs16, dblock, preferred_element_type=jnp.float32
        )
        dprobs = jnp.einsum("qhd,khd->hqk", dblock, values, preferred_element_type=jnp.float32)
        inner = jnp.sum(dprobs * probs, -1, keepdims=True)
        dscores = (probs * (dprobs - inner)).astype(jnp.bfloat16)
        dquery = (
            jnp.einsum("hqk,khd->qhd", dscores, keys, preferred_element_type=jnp.float32) * scale
        )
        dkeys = (
            dkeys
            + jnp.einsum("hqk,qhd->khd", dscores, qblock, preferred_element_type=jnp.float32)
            * scale
        )
        return ((dkeys, dvalues), dquery)

    empty = jnp.zeros((length, local_heads, HEAD_DIM), jnp.float32)
    (dkeys, dvalues), dquery = lax.scan(backward_block, (empty, empty), (indices, lse))
    dquery = dquery.reshape(length, local_heads, HEAD_DIM)
    dpre = jnp.stack(
        [
            unrotate(dquery, cosine, sine).reshape(length, width),
            unrotate(dkeys, cosine, sine).reshape(length, width),
            dvalues.reshape(length, width),
        ],
        0,
    ).astype(jnp.bfloat16)
    qkv_grad = jnp.einsum("sd,jsc->jdc", rows1, dpre, preferred_element_type=jnp.float32)
    bias_grad = jnp.sum(dpre, axis=1, dtype=jnp.float32)
    first_norm_gradient = sum_grads(
        jnp.einsum("jsc,jdc->sd", dpre, wqkv, preferred_element_type=jnp.float32)
    )
    first_scale_partial = jnp.sum(first_norm_gradient * first_standardized, 0)
    shift1_part = jnp.sum(first_norm_gradient, 0)
    token_gradient = (
        hidden_gradient
        + layer_norm_backward(
            first_norm_gradient, first_standardized, first_inverse_deviation, first_norm_scale
        )
    ).astype(jnp.bfloat16)
    qkvw_grad, qkvb_grad, outw_grad, gain1_total, shift1_total = (
        lax.psum_scatter(
            qkv_grad.astype(jnp.bfloat16), "dp", scatter_dimension=1, tiled=True
        ).astype(jnp.float32),
        lax.psum_scatter(
            bias_grad.astype(jnp.bfloat16), "dp", scatter_dimension=1, tiled=True
        ).astype(jnp.float32),
        lax.psum_scatter(
            out_grad.astype(jnp.bfloat16), "dp", scatter_dimension=1, tiled=True
        ).astype(jnp.float32),
        lax.psum_scatter(
            first_scale_partial.astype(jnp.bfloat16), "dp", scatter_dimension=0, tiled=True
        ).astype(jnp.float32),
        lax.psum_scatter(
            shift1_part.astype(jnp.bfloat16), "dp", scatter_dimension=0, tiled=True
        ).astype(jnp.float32),
    )
    gain1_grad, shift1_grad, gain2_grad, shift2_grad = lax.psum(
        (gain1_total, shift1_total, gain2_total, shift2_total), "tensor"
    )
    return (
        layer_output,
        token_gradient,
        qkvw_grad,
        qkvb_grad,
        outw_grad,
        gain1_grad,
        shift1_grad,
        gatew_grad,
        upw_grad,
        downw_grad,
        gain2_grad,
        shift2_grad,
    )


class LineScatter:
    def __init__(self, part, slot, chunks, d, z, line, send_sems, recv_sems):
        self.part, self.slot, self.chunks, self.d, self.z, self.line = part, slot, chunks, d, z, line
        self.ss, self.rs = send_sems, recv_sems

    def copy(self, s, h, way, target, place):
        return send(
            self.part(s, h), self.slot(place, h), self.ss.at[s, h], self.rs.at[place, h], self.d, target
        )

    def right(self, s, h):
        return self.copy(s, h, 0, self.z + 1, s)

    def left(self, s, h):
        return self.copy(s, h, 1, self.z - 1, jnp.where(self.z - 1 == s, self.line, s))

    def head(self, s):
        z, line = self.z, self.line
        for h in range(self.chunks):
            pl.when((z == 0) & (s > 0))(lambda: self.right(s, h).start())
            pl.when((z == line - 1) & (s < z))(lambda: self.left(s, h).start())

    def add(self, s, h):
        part = self.part(s, h)
        part[...] = (part[...].astype(F32) + self.slot(s, h)[...].astype(F32)).astype(BF)

    def relay(self, t):
        z, line = self.z, self.line
        up = line - 1 - t + z
        down = t - (line - 1 - z)
        for h in range(self.chunks):
            @pl.when((z > 0) & (up > z) & (up < line))
            def _():
                self.copy(z, h, 0, z, up).wait_recv()
                self.add(up, h)
                self.right(up, h).start()

            @pl.when((z < line - 1) & (down >= 0) & (down < z))
            def _():
                self.copy(z, h, 0, z, down).wait_recv()
                self.add(down, h)
                self.left(down, h).start()

    def arrive(self, h):
        z, line = self.z, self.line
        pl.when(z > 0)(lambda: self.copy(z, h, 0, z, z).wait_recv())
        pl.when(z < line - 1)(lambda: self.copy(z, h, 0, z, line).wait_recv())

    def total(self, h, rows):
        z = self.z
        return (
            self.part(z, h)[rows].astype(F32)
            + self.slot(z, h)[rows].astype(F32)
            + self.slot(self.line, h)[rows].astype(F32)
        )

    def finish(self):
        z = self.z
        for s in range(self.line):
            for h in range(self.chunks):
                pl.when(z != s)(lambda: self.copy(s, h, 0, z, s).wait_send())


def far_first(z, i):
    orders = ((3, 2, 1, 0), (3, 0, 2, 1), (0, 3, 1, 2), (0, 1, 2, 3))
    codes = [sum(s * 4**j for j, s in enumerate(o)) for o in orders]
    code = jnp.where(
        z == 0, codes[0], jnp.where(z == 1, codes[1], jnp.where(z == 2, codes[2], codes[3]))
    )
    power = jnp.where(i == 0, 1, jnp.where(i == 1, 4, jnp.where(i == 2, 16, 64)))
    return lax.rem(lax.div(code, power), 4)


def mlp_kernel(
    n2, cot, cotnear, wgate, wup, wdown,
    dn2, mixed, mland, gex, uex, dex, ghalf, uhalf, dhalf, grecv,
    nbuf, cbuf, gw, uw, dw, act, act_t, dga, dup, part, slots, mixbuf, wide, tall, wide_in, tall_in,
    ss, rs, css, crs, lss, lrs, local, mixsem, outsem, exs, exr, gss, grs,
):
    line = 4
    rows = n2.shape[0] // line
    model = n2.shape[1]
    hidden = wgate.shape[1]
    d, z, flips = place()
    greet(d, z, flips, line, (1, 2, 4, 6))
    core = lax.rem(d, 2)
    chip = lax.div(d, 2)
    loads = [
        pltpu.make_async_copy(a, b, local.at[i])
        for i, (a, b) in enumerate(((n2, nbuf), (wgate, gw), (wup, uw), (wdown, dw)))
    ]
    for copy in loads:
        copy.start()
    half = rows // 2
    scatter = LineScatter(
        lambda s, h: part.at[s, pl.ds(h * half, half)],
        lambda i, h: slots.at[i, pl.ds(h * half, half)],
        2, d, z, line, ss, rs,
    )
    pl.when(z == 0)(lambda: slots.__setitem__((0,), jnp.zeros((rows, model), BF)))
    pl.when(z == line - 1)(lambda: slots.__setitem__((line,), jnp.zeros((rows, model), BF)))
    cots = LineGather(
        lambda s, h: cbuf.at[pl.ds(pl.multiple_of(s * rows + h * half, half), half)], 2, d, z, line, css, crs
    )

    def near(s, k):
        return pltpu.make_async_copy(
            cot if k == 0 else cotnear.at[s], cbuf.at[pl.ds(pl.multiple_of(s * rows, rows), rows)], local.at[5 + k]
        )

    for h in range(2):
        @pl.when((z > 0) & (z < line - 1))
        def _():
            cots.copy(z - 1, h, 0, cotnear.at[z - 1, pl.ds(h * half, half)]).start()
            cots.copy(z + 1, h, 1, cotnear.at[z + 1, pl.ds(h * half, half)]).start()
    near(z, 0).start()
    pl.when(z > 0)(lambda: near(z - 1, 1).start())
    pl.when(z < line - 1)(lambda: near(z + 1, 2).start())
    for copy in loads:
        copy.wait()

    def mixed_out(i):
        s = far_first(z, i)
        at = pl.ds(pl.multiple_of(s * rows, rows), rows)
        return pltpu.make_async_copy(mixbuf.at[lax.rem(i, 2)], mixed.at[at], mixsem.at[lax.rem(i, 2)])

    def mixed_ahead(i):
        at = pl.ds(pl.multiple_of(far_first(z, i) * rows, rows), rows)
        to = jnp.where(z == 0, 1, line - 2)
        return send(mixed.at[at], mland.at[i], lss.at[i], lrs.at[i], d, to)

    at_end = (z == 0) | (z == line - 1)

    @pl.loop(0, line)
    def _(i):
        s = far_first(z, i)
        at = pl.ds(pl.multiple_of(s * rows, rows), rows)
        for lo, size in spans(hidden, 512):
            cols = pl.ds(lo, size)
            gate = nn(nbuf[at, :], gw[:, cols])
            up = nn(nbuf[at, :], uw[:, cols])
            sigma = lax.logistic(gate)
            silu = gate * sigma
            value = (silu * up).astype(BF)
            act[:, cols] = value
            act_t[cols, at] = value.T
            dga[at, cols] = (up * (sigma * (1.0 + gate * (1.0 - sigma)))).astype(BF)
            dup[at, cols] = silu.astype(BF)
        for lo, size in spans(model, 512):
            mixbuf[lax.rem(i, 2), :, pl.ds(lo, size)] = nn(act[...], dw[:, pl.ds(lo, size)]).astype(BF)
        mixed_out(i).start()

        @pl.when(i >= 1)
        def _():
            mixed_out(i - 1).wait()
            pl.when(at_end & (i <= 2))(lambda: mixed_ahead(i - 1).start())

        @pl.when(i == line - 2)
        def _():
            for h in range(2):
                cots.step(2, h)

    mixed_out(line - 1).wait()
    near(z, 0).wait()
    pl.when(z > 0)(lambda: near(z - 1, 1).wait())
    pl.when(z < line - 1)(lambda: near(z + 1, 2).wait())
    for h in range(2):
        cots.step(3, h)

    @pl.loop(0, line)
    def _(i):
        s = far_first(z, i)
        at = pl.ds(pl.multiple_of(s * rows, rows), rows)
        for lo, size in spans(hidden, 512):
            cols = pl.ds(lo, size)
            dact = nt(cbuf[at, :], dw[cols, :])
            dga[at, cols] = (dact * dga[at, cols].astype(F32)).astype(BF)
            dup[at, cols] = (dact * dup[at, cols].astype(F32)).astype(BF)
        for lo, size in spans(model, 512):
            cols = pl.ds(lo, size)
            part[s, :, cols] = (nt(dga[at, :], gw[cols, :]) + nt(dup[at, :], uw[cols, :])).astype(BF)
        scatter.head(s)

    scatter.relay(1)
    blocks = model // rows // 2

    def exchanged(m):
        outs = (ghalf, uhalf, dhalf)
        exes = (gex, uex, dex)
        stage = tall if m == 2 else wide
        stage_in = tall_in if m == 2 else wide_in

        def block(t):
            cols = pl.ds(pl.multiple_of(t * rows, rows), rows)
            if m == 2:
                return lambda lo, size: nn(act_t[pl.ds(lo, size), :], cbuf[:, cols])
            right = dga if m == 0 else dup
            return lambda lo, size: tn(nbuf[:, cols], right[:, pl.ds(lo, size)])

        def piece(ref, lo, size):
            return ref.at[pl.ds(lo, size), :] if m == 2 else ref.at[:, pl.ds(lo, size)]

        def away(k):
            slot = lax.rem(k, 2)
            return send(stage.at[slot], exes[m].at[k], exs.at[m, k], exr.at[m, k], d + flips[1], z)

        @pl.loop(0, blocks)
        def _(k):
            slot = lax.rem(k, 2)
            pl.when(k >= 2)(lambda: away(k - 2).wait_send())
            make = block(2 * k + 1 - core)
            for lo, size in spans(hidden, 512):
                piece(stage.at[slot], lo, size)[...] = make(lo, size).astype(BF)
            away(k).start()

        away(blocks - 2).wait_send()
        away(blocks - 1).wait_send()

        def chip_at(j):
            return lax.rem(chip + 1 + j, blocks)

        def store(j):
            slot = lax.rem(j, 2)
            return pltpu.make_async_copy(stage.at[slot], outs[m].at[chip_at(j)], outsem.at[slot])

        def onward(j):
            k = chip_at(j)
            return send(ghalf.at[k], grecv.at[blocks - 2 - j], gss.at[j], grs.at[blocks - 2 - j], 2 * k + core, z)

        @pl.loop(0, blocks)
        def _(j):
            slot = lax.rem(j, 2)
            k = chip_at(j)

            @pl.when(j >= 2)
            def _():
                store(j - 2).wait()
                if m == 0:
                    onward(j - 2).start()

            away(k).wait_recv()
            fetch = pltpu.make_async_copy(exes[m].at[k], stage_in, local.at[4])
            fetch.start()
            fetch.wait()
            make = block(2 * k + core)
            for lo, size in spans(hidden, 512):
                piece(stage.at[slot], lo, size)[...] = (
                    make(lo, size) + piece(stage_in, lo, size)[...].astype(F32)
                ).astype(BF)
            store(j).start()

        for j in (blocks - 2, blocks - 1):
            store(j).wait()
            if m == 0 and j < blocks - 1:
                onward(j).start()
        return onward

    onward = exchanged(0)

    scatter.relay(2)
    exchanged(1)
    exchanged(2)
    for h in range(2):
        scatter.arrive(h)

        @pl.loop(0, half // 32)
        def _(i):
            rows_at = pl.ds(pl.multiple_of(i * 32, 32), 32)
            dn2[pl.ds(pl.multiple_of(h * half + i * 32, 32), 32), :] = scatter.total(h, rows_at)

    scatter.finish()
    for i in range(2):
        pl.when(at_end)(lambda: mixed_ahead(i).wait_send())
        pl.when(~at_end)(lambda: mixed_ahead(i).wait_recv())
    cots.finish(1, line - 1)
    for j in range(blocks - 1):
        onward(j).wait()


def mlp(n2, cot, cotnear, wgate, wup, wdown):
    length, model = n2.shape
    hidden = wgate.shape[1]
    line = 4
    rows = length // line
    blocks = model // rows // 2
    sds = jax.ShapeDtypeStruct
    wide = sds((blocks, rows, hidden), BF)
    tall = sds((blocks, hidden, rows), BF)
    return pl.pallas_call(
        mlp_kernel,
        out_shape=(
            sds((rows, model), F32), sds((length, model), BF), sds((2, rows, model), BF),
            wide, wide, tall, wide, wide, tall, sds((blocks - 1, rows, hidden), BF),
        ),
        in_specs=[ANY] * 6,
        out_specs=(INV,) + (ANY,) * 9,
        scratch_shapes=[
            pltpu.VMEM((length, model), BF),
            pltpu.VMEM((length, model), BF),
            pltpu.VMEM((model, hidden), BF),
            pltpu.VMEM((model, hidden), BF),
            pltpu.VMEM((hidden, model), BF),
            pltpu.VMEM((rows, hidden), BF),
            pltpu.VMEM((hidden, length), BF),
            pltpu.VMEM((length, hidden), BF),
            pltpu.VMEM((length, hidden), BF),
            pltpu.VMEM((line, rows, model), BF),
            pltpu.VMEM((line + 1, rows, model), BF),
            pltpu.VMEM((2, rows, model), BF),
            pltpu.VMEM((2, rows, hidden), BF),
            pltpu.VMEM((2, hidden, rows), BF),
            pltpu.VMEM((rows, hidden), BF),
            pltpu.VMEM((hidden, rows), BF),
            pltpu.SemaphoreType.DMA((line, 2)),
            pltpu.SemaphoreType.DMA((line + 1, 2)),
            pltpu.SemaphoreType.DMA((2, line, 2)),
            pltpu.SemaphoreType.DMA((line, 2)),
            pltpu.SemaphoreType.DMA((2,)),
            pltpu.SemaphoreType.DMA((2,)),
            pltpu.SemaphoreType.DMA((8,)),
            pltpu.SemaphoreType.DMA((2,)),
            pltpu.SemaphoreType.DMA((2,)),
            pltpu.SemaphoreType.DMA((3, blocks)),
            pltpu.SemaphoreType.DMA((3, blocks)),
            pltpu.SemaphoreType.DMA((blocks,)),
            pltpu.SemaphoreType.DMA((blocks,)),
        ],
        compiler_params=pltpu.CompilerParams(
            collective_id=2, has_side_effects=True, vmem_limit_bytes=62 * 1024 * 1024
        ),
        cost_estimate=pl.CostEstimate(flops=10**11, bytes_accessed=10**8, transcendentals=0),
        name="mlp",
    )(n2, cot, cotnear, wgate, wup, wdown)


def norm_parts(x):
    centred = x - jnp.mean(x, -1, keepdims=True)
    inverse = lax.rsqrt(jnp.mean(centred * centred, -1, keepdims=True) + 1e-05)
    return centred * inverse, inverse


def norm_back(grad, standard, inverse, gain):
    scaled = grad * gain
    return inverse * (
        scaled
        - jnp.mean(scaled, -1, keepdims=True)
        - standard * jnp.mean(scaled * standard, -1, keepdims=True)
    )


def each_piece(rows, piece, body):
    @pl.loop(0, rows // piece)
    def _(i):
        body(pl.ds(pl.multiple_of(i * piece, piece), piece))


class PlaneSum:
    def __init__(self, half, recv, d, z, blocks, send_sems, recv_sems):
        self.half, self.recv, self.d, self.z, self.blocks = half, recv, d, z, blocks
        self.ss, self.rs = send_sems, recv_sems
        self.chip, self.core = lax.div(d, 2), lax.rem(d, 2)

    def chip_at(self, j):
        return lax.rem(self.chip + 1 + j, self.blocks)

    def copy(self, j):
        k, to = self.chip_at(j), self.blocks - 2 - j
        return send(self.half.at[k], self.recv.at[to], self.ss.at[j], self.rs.at[to], 2 * k + self.core, self.z)

    def wait(self):
        for j in range(self.blocks - 1):
            self.copy(j).wait()


class PlaneChain:
    def __init__(self, half, recv, mid, d, z, flips, send_sems, recv_sems):
        self.half, self.recv, self.mid, self.d, self.z, self.flips = half, recv, mid, d, z, flips
        self.ss, self.rs = send_sems, recv_sems
        self.rows = half.shape[1] // 2

    def block(self, r):
        return lax.div(self.d + self.flips[r], 2)

    def copy(self, key):
        block, over, part = ((6, 2, 0), (6, 4, 1), (4, 4, 1), (2, 2, 0), (4, 4, 0), (2, 2, 1))[key]
        at = pl.ds(part * self.rows, self.rows)
        dst = self.mid.at[key] if key < 2 else self.recv.at[0 if over == 2 else 1, at]
        return send(
            self.half.at[self.block(block), at], dst, self.ss.at[key], self.rs.at[key], self.d + self.flips[over], self.z
        )

    def start(self):
        for key in range(4):
            self.copy(key).start()

    def relay(self):
        for key, block, part in ((0, 4, 0), (1, 2, 1)):
            self.copy(key).wait_recv()
            k = self.block(block)
            piece = min(self.rows, 128)

            @pl.loop(0, self.rows // piece)
            def _(i):
                at = pl.ds(pl.multiple_of(part * self.rows + i * piece, piece), piece)
                mid = self.mid[key, pl.ds(pl.multiple_of(i * piece, piece), piece), :]
                self.half[k, at, :] = (self.half[k, at, :].astype(F32) + mid.astype(F32)).astype(BF)

            self.copy(key + 4).start()

    def arrive(self):
        for key in range(2, 6):
            self.copy(key).wait_recv()

    def total(self, at):
        return (
            self.half[(self.block(0),) + at].astype(F32)
            + self.recv[(0,) + at].astype(F32)
            + self.recv[(1,) + at].astype(F32)
        )

    def finish(self):
        for key in range(6):
            self.copy(key).wait_send()


def sum_blocks(own, recv, out, buf, obuf, sems, pieces):
    count = recv.shape[0]
    rows = buf.shape[1]

    @pl.loop(0, pieces)
    def _(i):
        at = pl.ds(pl.multiple_of(i * rows, rows), rows)
        ins = [pltpu.make_async_copy(own.at[at], buf.at[0], sems.at[0])] + [
            pltpu.make_async_copy(recv.at[j, at], buf.at[j + 1], sems.at[j + 1]) for j in range(count)
        ]
        for copy in ins:
            copy.start()
        for copy in ins:
            copy.wait()
        total = buf[0].astype(F32)
        for j in range(count):
            total = total + buf[j + 1].astype(F32)
        obuf[...] = total
        back = pltpu.make_async_copy(obuf, out.at[at], sems.at[count + 1])
        back.start()
        back.wait()


def attention_back_kernel(
    dn2, hid, cot, small, wout, attall, qkv, lse, mixed, mland, ghalf, grecv, uhalf, cos, sin_up, sin_down,
    lay, dhid, dpre, ograd, ggrad, ugrad, sums, urecv, oex,
    wo, da, attr, att_t, attc, qbuf, dsend, datt, lse_t, part, slots, ostage, ofetch, osum, orecv, omid, ofull, ozr,
    sbuf, sobuf, dq,
    mss, mrs, ass, ars, oss, ors, pss, prs, uss, urs, zss, zrs, local, ssem,
):
    line = 4
    rows, model = hid.shape
    length = rows * line
    width = attc.shape[1]
    pairs = width // 128
    blocks = model // rows // 2
    d, z, flips = place()
    greet(d, z, flips, line, (1, 2, 4, 6))
    core, chip = lax.rem(d, 2), lax.div(d, 2)
    ups = PlaneSum(uhalf, urecv, d, z, blocks, uss, urs)
    loads = [pltpu.make_async_copy(mixed.at[pl.ds(s * rows, rows)], part.at[s], local.at[s]) for s in range(line)]
    loads += [
        pltpu.make_async_copy(wout, wo, local.at[4]),
        pltpu.make_async_copy(attall.at[pl.ds(pl.multiple_of(z * rows, rows), rows)], attr, local.at[5]),
        pltpu.make_async_copy(attall.at[:, pl.ds(pl.multiple_of(z * width, width), width)], attc, local.at[6]),
        pltpu.make_async_copy(qkv, qbuf, local.at[7]),
    ]

    def landed(i):
        return pltpu.make_async_copy(mland.at[i], slots.at[jnp.where(z == 1, line - 1 - i, i)], local.at[9 + i])

    between = (z > 0) & (z < line - 1)
    for i in range(2):
        pl.when(between)(lambda: landed(i).start())
    for copy in loads:
        copy.start()
    for j in range(blocks - 1):
        ups.copy(j).start()
    half = rows // 2
    scatter = LineScatter(
        lambda s, h: part.at[s, pl.ds(h * half, half)],
        lambda i, h: slots.at[i, pl.ds(h * half, half)],
        2, d, z, line, mss, mrs,
    )
    pl.when(z == 0)(lambda: slots.__setitem__((0,), jnp.zeros((rows, model), BF)))
    pl.when(z == line - 1)(lambda: slots.__setitem__((line,), jnp.zeros((rows, model), BF)))
    def onward(i, h):
        @pl.when(z == 1)
        def _():
            scatter.add(line - 1 - i, h)
            scatter.right(line - 1 - i, h).start()

        @pl.when(z == line - 2)
        def _():
            scatter.add(i, h)
            scatter.left(i, h).start()

    for copy in loads[:4]:
        copy.wait()
    for i in range(2):
        pl.when(between)(lambda: landed(i).wait())
    onward(0, 0)
    sums[...] = jnp.zeros_like(sums)

    def back(at):
        grad = dn2[at, :]
        standard, inverse = norm_parts(hid[at, :])
        sums[2:3, :] += jnp.sum(grad * standard, 0, keepdims=True)
        sums[3:4, :] += jnp.sum(grad, 0, keepdims=True)
        total = cot[at, :].astype(F32) + norm_back(grad, standard, inverse, small[2:3, :])
        dhid[at, :] = total
        da[at, :] = total.astype(BF)

    each_piece(rows, 32, back)
    for copy in loads[4:]:
        copy.wait()

    def away(k):
        to = lax.rem(z + k, line)
        return send(
            dsend.at[to], datt.at[pl.ds(pl.multiple_of(z * rows, rows), rows)], ass.at[k], ars.at[z], d, to
        )

    @pl.loop(1, line + 1)
    def _(k):
        to = lax.rem(z + k, line)
        dsend[to] = nt(da[...], wo[pl.ds(pl.multiple_of(to * width, width), width), :]).astype(BF)
        pl.when(k < line)(lambda: away(k).start())

    onward(0, 1)
    for h in range(2):
        onward(1, h)
        pl.when(z == 0)(lambda: scatter.right(jnp.int32(1), h).start())
        pl.when(z == line - 1)(lambda: scatter.left(jnp.int32(line - 2), h).start())

    def relay(h):
        @pl.when(z == 1)
        def _():
            scatter.copy(z, h, 0, z, 0).wait_recv()
            scatter.add(0, h)
            scatter.left(0, h).start()

        @pl.when(z == line - 2)
        def _():
            scatter.copy(z, h, 0, z, line - 1).wait_recv()
            scatter.add(line - 1, h)
            scatter.right(line - 1, h).start()

    datt[pl.ds(pl.multiple_of(z * rows, rows), rows), :] = dsend[z]
    for lo, size in spans(model, 512):
        att_t[pl.ds(lo, size), :] = attr[:, pl.ds(lo, size)].T
    lse_t[...] = lse[...].T

    def oblock(t):
        return nn(att_t[...], da[:, pl.ds(pl.multiple_of(t * rows, rows), rows)])

    def across(k):
        return send(ostage.at[lax.rem(k, 2)], oex.at[k], oss.at[k], ors.at[k], d + flips[1], z)

    @pl.loop(0, blocks)
    def _(k):
        pl.when(k >= 2)(lambda: across(k - 2).wait_send())
        ostage[lax.rem(k, 2)] = oblock(2 * k + 1 - core).astype(BF)
        across(k).start()

    planes = PlaneChain(osum, orecv, omid, d, z, flips, pss, prs)

    @pl.loop(0, blocks)
    def _(k):
        across(k).wait_recv()
        fetch = pltpu.make_async_copy(oex.at[k], ofetch, local.at[8])
        fetch.start()
        fetch.wait()
        osum[k] = (oblock(2 * k + core) + ofetch[...].astype(F32)).astype(BF)

    planes.start()
    across(blocks - 2).wait_send()
    across(blocks - 1).wait_send()
    sum_blocks(ghalf.at[chip], grecv, ggrad, sbuf, sobuf, ssem, rows // sbuf.shape[1])
    for k in range(1, line):
        frm = lax.rem(z + k, line)
        send(dsend.at[frm], datt.at[pl.ds(pl.multiple_of(frm * rows, rows), rows)], ass.at[k], ars.at[frm], d, frm).wait_recv()

    relay(0)
    lanes = lax.broadcasted_iota(jnp.int32, (1, 128), 1)
    mine = (lanes < 64, lanes >= 64)
    which = lax.broadcasted_iota(jnp.int32, (16, 128), 0)
    lane16 = lax.broadcasted_iota(jnp.int32, (16, 128), 1)
    pick = jnp.where(which == lax.div(lane16, 64), 1.0, 0.0).astype(BF)
    scale = HEAD_DIM**-0.5

    def zaway(k):
        to = lax.rem(z + k, line)
        return send(
            ofull.at[pl.ds(pl.multiple_of(to * width, width), width)], ozr.at[k - 1], zss.at[k], zrs.at[k - 1], d, to
        )

    def plane_total():
        planes.arrive()

        def add(at):
            ofull[at, :] = planes.total((at, slice(None))).astype(BF)

        each_piece(model, 256, add)
        for k in range(1, line):
            zaway(k).start()

    def back_pair(p):
        cols = pl.ds(pl.multiple_of(p * 128, 128), 128)
        do = datt[:, cols]
        prod = do.astype(F32) * attc[:, cols].astype(F32)
        high = prod.astype(BF)
        inner = nt(pick, high) + nt(pick, (prod - high.astype(F32)).astype(BF))
        q = qbuf[0, p] * BF(scale)
        dq[...] = jnp.zeros_like(dq)
        for kj in range(line):
            at = pl.ds(kj * rows, rows)
            lo, count = kj * rows, length - kj * rows
            k, v = qbuf[1, p, at, :], qbuf[2, p, at, :]
            row = lax.broadcasted_iota(jnp.int32, (rows, count), 0)
            col = lax.broadcasted_iota(jnp.int32, (rows, count), 1)
            keep = col >= row
            dk = jnp.zeros((rows, 128), F32)
            dv = jnp.zeros((rows, 128), F32)
            for a in range(2):
                km, vm = jnp.where(mine[a], k, BF(0)), jnp.where(mine[a], v, BF(0))
                qm, dm = jnp.where(mine[a], q[lo:], BF(0)), jnp.where(mine[a], do[lo:], BF(0))
                s = jnp.where(keep, nt(km, q[lo:]), -1e30)
                probs = jnp.exp(s - lse_t[pl.ds(2 * p + a, 1), pl.ds(lo, count)])
                dv += nn(probs.astype(BF), dm)
                dprobs = nt(vm, do[lo:])
                ds = (probs * (dprobs - inner[a : a + 1, lo:])).astype(BF)
                dk += nn(ds, qm)
                dq[pl.ds(lo, count), :] += tn(ds, km)
            dk = turn(dk, cos[at, :], sin_up[at, :], sin_down[at, :], -1.0)
            dpre[at, pl.ds(pl.multiple_of(width + p * 128, 128), 128)] = dk.astype(BF)
            dpre[at, pl.ds(pl.multiple_of(2 * width + p * 128, 128), 128)] = dv.astype(BF)
        dpre[:, cols] = turn(dq[...] * scale, cos[...], sin_up[...], sin_down[...], -1.0).astype(BF)

    @pl.loop(0, pairs)
    def _(p):
        back_pair(p)
        pl.when(p == 0)(lambda: planes.relay())
        pl.when(p == 1)(lambda: relay(1))
        pl.when(p == 2)(lambda: plane_total())

    ups.wait()
    sum_blocks(uhalf.at[chip], urecv, ugrad, sbuf, sobuf, ssem, rows // sbuf.shape[1])
    for h in range(2):
        scatter.arrive(h)

        @pl.loop(0, half // 32)
        def _(i):
            at = pl.ds(pl.multiple_of(h * half + i * 32, 32), 32)
            total = scatter.total(h, pl.ds(pl.multiple_of(i * 32, 32), 32))
            lay[at, :] = (hid[at, :] + total).astype(BF)

    total = ofull[pl.ds(pl.multiple_of(z * width, width), width), :].astype(F32)
    for k in range(1, line):
        zaway(k).wait()
        total = total + ozr[k - 1].astype(F32)
    ograd[...] = total
    for k in range(1, line):
        away(k).wait_send()
    planes.finish()
    for s in range(line):
        for h in range(2):
            sent = (z != s) & ((z > 0) | (s == 1)) & ((z < line - 1) | (s == line - 2))
            pl.when(sent)(lambda: scatter.copy(s, h, 0, z, s).wait_send())


def attention_backward(dn2, hid, cot, small, wout, attall, qkv, lse, mixed, mland, ghalf, grecv, uhalf, tabs):
    rows, model = hid.shape
    line = 4
    length = rows * line
    width = model // line
    pairs = width // 128
    blocks = model // rows // 2
    hidden = ghalf.shape[2]
    sds = jax.ShapeDtypeStruct
    dma = pltpu.SemaphoreType.DMA
    return pl.pallas_call(
        attention_back_kernel,
        out_shape=(
            sds((rows, model), BF), sds((rows, model), F32), sds((length, 3 * width), BF),
            sds((width, rows), F32), sds((rows, hidden), F32), sds((rows, hidden), F32), sds((8, model), F32),
            sds((blocks - 1, rows, hidden), BF), sds((blocks, model, rows), BF),
        ),
        in_specs=[INV] * 4 + [ANY] * 3 + [INV] + [ANY] * 5 + [INV] * 3,
        out_specs=(INV, INV, INV, INV, ANY, ANY, INV, ANY, ANY),
        scratch_shapes=[
            pltpu.VMEM((model, model), BF),
            pltpu.VMEM((rows, model), BF),
            pltpu.VMEM((rows, model), BF),
            pltpu.VMEM((model, rows), BF),
            pltpu.VMEM((length, width), BF),
            pltpu.VMEM((3, pairs, length, 128), BF),
            pltpu.VMEM((line, rows, width), BF),
            pltpu.VMEM((length, width), BF),
            pltpu.VMEM((128, length), F32),
            pltpu.VMEM((line, rows, model), BF),
            pltpu.VMEM((line + 1, rows, model), BF),
            pltpu.VMEM((2, model, rows), BF),
            pltpu.VMEM((model, rows), BF),
            pltpu.VMEM((blocks, model, rows), BF),
            pltpu.VMEM((2, model, rows), BF),
            pltpu.VMEM((2, model // 2, rows), BF),
            pltpu.VMEM((model, rows), BF),
            pltpu.VMEM((line - 1, width, rows), BF),
            pltpu.VMEM((blocks, 64, hidden), BF),
            pltpu.VMEM((64, hidden), F32),
            pltpu.VMEM((length, 128), F32),
            dma((line, 2)), dma((line + 1, 2)), dma((line,)), dma((line,)), dma((blocks,)), dma((blocks,)),
            dma((6,)), dma((6,)), dma((blocks,)), dma((blocks,)), dma((line,)), dma((line,)),
            dma((12,)), dma((blocks + 1,)),
        ],
        compiler_params=pltpu.CompilerParams(
            collective_id=3, has_side_effects=True, vmem_limit_bytes=62 * 1024 * 1024
        ),
        cost_estimate=pl.CostEstimate(flops=10**11, bytes_accessed=10**8, transcendentals=0),
        name="attention_backward",
    )(dn2, hid, cot, small, wout, attall, qkv, lse, mixed, mland, ghalf, grecv, uhalf, *tabs)


def input_back_kernel(
    dpre, wqkv, n1, dhalf, tok, dhid, small, sums_in,
    tgrad, qgrad, dgrad, gains, bout, drecv, qex,
    pbuf, wbuf, nbuf, part, slots, qstage, qfetch, qsum, qrecv, qmid, sums, zsums, dsums, bsums, sbuf, sobuf,
    ss, rs, xss, xrs, pss, prs, dss, drs, zss, zrs, gss, grs, bss, brs, local, ssem,
):
    line = 4
    rows, model = tok.shape
    width = dpre.shape[1] // 3
    blocks = model // rows // 2
    d, z, flips = place()
    greet(d, z, flips, line, range(1, 8))
    core, chip = lax.rem(d, 2), lax.div(d, 2)
    loads = [
        pltpu.make_async_copy(a, b, local.at[i]) for i, (a, b) in enumerate(((dpre, pbuf), (wqkv, wbuf), (n1, nbuf)))
    ]
    for copy in loads:
        copy.start()
    downs = PlaneSum(dhalf, drecv, d, z, blocks, dss, drs)
    for j in range(blocks - 1):
        downs.copy(j).start()
    half = rows // 2
    scatter = LineScatter(
        lambda s, h: part.at[s, pl.ds(h * half, half)],
        lambda i, h: slots.at[i, pl.ds(h * half, half)],
        2, d, z, line, ss, rs,
    )
    pl.when(z == 0)(lambda: slots.__setitem__((0,), jnp.zeros((rows, model), BF)))
    pl.when(z == line - 1)(lambda: slots.__setitem__((line,), jnp.zeros((rows, model), BF)))
    for copy in loads[:2]:
        copy.wait()

    @pl.loop(0, line)
    def _(i):
        s = far_first(z, i)
        at = pl.ds(pl.multiple_of(s * rows, rows), rows)
        for lo, size in spans(model, 512):
            part[s, :, pl.ds(lo, size)] = nt(pbuf[at, :], wbuf[pl.ds(lo, size), :]).astype(BF)
        scatter.head(s)

    loads[2].wait()

    def qblock(t):
        return lambda lo, size: tn(nbuf[:, pl.ds(pl.multiple_of(t * rows, rows), rows)], pbuf[:, pl.ds(lo, size)])

    def across(k):
        return send(qstage.at[k], qex.at[k], xss.at[k], xrs.at[k], d + flips[1], z)

    @pl.loop(0, blocks)
    def _(k):
        make = qblock(2 * k + 1 - core)
        for lo, size in spans(3 * width, 512):
            qstage[k, :, pl.ds(lo, size)] = make(lo, size).astype(BF)
        across(k).start()

    planes = PlaneChain(qsum, qrecv, qmid, d, z, flips, pss, prs)

    @pl.loop(0, blocks)
    def _(k):
        across(k).wait_recv()
        fetch = pltpu.make_async_copy(qex.at[k], qfetch, local.at[3])
        fetch.start()
        fetch.wait()
        make = qblock(2 * k + core)
        for lo, size in spans(3 * width, 512):
            qsum[k, :, pl.ds(lo, size)] = (make(lo, size) + qfetch[:, pl.ds(lo, size)].astype(F32)).astype(BF)

    planes.start()
    scatter.relay(1)
    bsums[0] = jnp.zeros(bsums.shape[1:], F32)

    def bias(at):
        bsums[0, 0:1, :] += jnp.sum(pbuf[at, :].astype(F32), 0, keepdims=True)

    each_piece(rows * line, 64, bias)

    def bcopy(r):
        return send(bsums.at[0], bsums.at[r], bss.at[r], brs.at[r], d + flips[r], z)

    for r in range(1, 8):
        bcopy(r).start()
    planes.relay()
    scatter.relay(2)
    planes.arrive()
    for j in range(3):
        cols = pl.ds(j * width, width)
        qgrad[j] = planes.total((slice(None), cols))
    downs.wait()
    sum_blocks(dhalf.at[chip], drecv, dgrad, sbuf, sobuf, ssem, dhalf.shape[1] // sbuf.shape[1])
    total = jnp.zeros(bout.shape, F32)
    for r in range(8):
        if r:
            bcopy(r).wait()
        total = total + bsums[r]
    bout[...] = total
    sums[...] = sums_in[...]
    for h in range(2):
        scatter.arrive(h)

        @pl.loop(0, half // 32)
        def _(i):
            at = pl.ds(pl.multiple_of(h * half + i * 32, 32), 32)
            grad = scatter.total(h, pl.ds(pl.multiple_of(i * 32, 32), 32))
            standard, inverse = norm_parts(tok[at, :].astype(F32))
            sums[0:1, :] += jnp.sum(grad * standard, 0, keepdims=True)
            sums[1:2, :] += jnp.sum(grad, 0, keepdims=True)
            tgrad[at, :] = (dhid[at, :] + norm_back(grad, standard, inverse, small[0:1, :])).astype(BF)

    depth = gains.shape[1]

    def columns(i):
        return sums.at[:, pl.ds(pl.multiple_of(i * depth, 256), depth)]

    def dcopy(r):
        return send(columns(d + flips[r]), dsums.at[r], gss.at[r], grs.at[r], d + flips[r], z)

    def zcopy(k):
        return send(zsums.at[0], zsums.at[k], zss.at[k], zrs.at[k], d, lax.rem(z + k, line))

    for r in range(1, 8):
        dcopy(r).start()
    total = columns(d)[...]
    for r in range(1, 8):
        dcopy(r).wait()
        total = total + dsums[r]
    zsums[0] = total
    for k in range(1, line):
        zcopy(k).start()
    for k in range(1, line):
        zcopy(k).wait()
        total = total + zsums[k]
    gains[...] = total
    planes.finish()
    for k in range(blocks):
        across(k).wait_send()
    scatter.finish()


def input_backward(dpre, wqkv, n1, dhalf, tok, dhid, small, sums):
    rows, model = tok.shape
    line = 4
    length = rows * line
    triple = dpre.shape[1]
    blocks = model // rows // 2
    hidden = dhalf.shape[1]
    sds = jax.ShapeDtypeStruct
    dma = pltpu.SemaphoreType.DMA
    return pl.pallas_call(
        input_back_kernel,
        out_shape=(
            sds((rows, model), BF), sds((3, rows, triple // 3), F32), sds((hidden, rows), F32), sds((8, rows), F32),
            sds((8, triple), F32), sds((blocks - 1, hidden, rows), BF), sds((blocks, rows, triple), BF),
        ),
        in_specs=[ANY, ANY, ANY, ANY, INV, INV, INV, INV],
        out_specs=(INV, INV, ANY, INV, INV, ANY, ANY),
        scratch_shapes=[
            pltpu.VMEM((length, triple), BF),
            pltpu.VMEM((model, triple), BF),
            pltpu.VMEM((length, model), BF),
            pltpu.VMEM((line, rows, model), BF),
            pltpu.VMEM((line + 1, rows, model), BF),
            pltpu.VMEM((blocks, rows, triple), BF),
            pltpu.VMEM((rows, triple), BF),
            pltpu.VMEM((blocks, rows, triple), BF),
            pltpu.VMEM((2, rows, triple), BF),
            pltpu.VMEM((2, rows // 2, triple), BF),
            pltpu.VMEM((8, model), F32),
            pltpu.VMEM((line, 8, rows), F32),
            pltpu.VMEM((8, 8, rows), F32),
            pltpu.VMEM((8, 8, triple), F32),
            pltpu.VMEM((blocks, 352, rows), BF),
            pltpu.VMEM((352, rows), F32),
            dma((line, 2)), dma((line + 1, 2)), dma((blocks,)), dma((blocks,)), dma((6,)), dma((6,)),
            dma((blocks,)), dma((blocks,)), dma((line,)), dma((line,)), dma((8,)), dma((8,)),
            dma((8,)), dma((8,)), dma((4,)), dma((blocks + 1,)),
        ],
        compiler_params=pltpu.CompilerParams(
            collective_id=4, has_side_effects=True, vmem_limit_bytes=62 * 1024 * 1024
        ),
        cost_estimate=pl.CostEstimate(flops=10**11, bytes_accessed=10**8, transcendentals=0),
        name="input_backward",
    )(dpre, wqkv, n1, dhalf, tok, dhid, small, sums)


def turn_tables(length):
    half = ROT // 2
    freqs = np.float32(10000.0) ** (-np.arange(0, ROT, 2, dtype=np.float32) / np.float32(ROT))
    angles = np.arange(length, dtype=np.float32)[:, None] * freqs[None, :]
    cos = np.ones((length, HEAD_DIM), np.float32)
    up = np.zeros((length, HEAD_DIM), np.float32)
    down = np.zeros((length, HEAD_DIM), np.float32)
    cos[:, :half] = cos[:, half:ROT] = np.cos(angles)
    up[:, half:ROT] = np.sin(angles)
    down[:, :half] = -np.sin(angles)
    return tuple(jnp.asarray(np.tile(t, (1, 2))) for t in (cos, up, down))


def pack_smalls(d, model, width, qkv_bias, *vectors):
    col = lax.broadcasted_iota(jnp.int32, (1, model), 1)
    each = vectors[0].shape[0]
    gains = jnp.stack([jnp.tile(v, model // each) for v in vectors], 0)
    gains = jnp.where(col // each == d, gains, 0)
    part = qkv_bias.shape[1]
    bias = jnp.tile(qkv_bias, (1, width // part)).reshape(1, 3 * width)
    bias = jnp.pad(bias, ((0, 0), (0, model - 3 * width)))
    bias = jnp.where(col % width // part == d, bias, 0)
    return jnp.concatenate([gains, bias, jnp.zeros((11, model), BF)], 0).astype(BF)


def fast(
    tokens, qkv_weight, qkv_bias, out_weight, norm1_gain, norm1_shift, gate_weight, up_weight,
    down_weight, norm2_gain, norm2_shift, cotangent,
):
    d = lax.axis_index("dp")
    rows, model = tokens.shape
    length = 4 * rows
    tabs = turn_tables(length)
    depth, width = qkv_weight.shape[1:]
    smalls = pack_smalls(d, model, width, qkv_bias, norm1_gain, norm1_shift, norm2_gain, norm2_shift)
    wq = qkv_weight.transpose(1, 0, 2).reshape(depth, 3 * width)
    cotnear, n1, qkv, lse, attall, wqkv, small, wout, n2, hidden, wgate, wup, wdown = attention_forward(
        tokens, cotangent, wq, out_weight, gate_weight, up_weight, down_weight, smalls, tabs
    )
    dn2, mixed, mland, _, _, _, ghalf, uhalf, dhalf, grecv = mlp(n2, cotangent, cotnear, wgate, wup, wdown)
    layer_output, dhid, dpre, outw_grad, gatew_grad, upw_grad, sums, _, _ = attention_backward(
        dn2, hidden, cotangent, small, wout, attall, qkv, lse, mixed, mland, ghalf, grecv, uhalf, tabs
    )
    token_gradient, qkvw_grad, downw_grad, gains, bias, _, _ = input_backward(
        dpre, wqkv, n1, dhalf, tokens, dhid, small, sums
    )
    part = qkv_bias.shape[1]
    bias = bias[0].reshape(3, width)
    qkvb_grad = lax.dynamic_slice_in_dim(bias, d * part, part, 1)
    return (
        layer_output, token_gradient, qkvw_grad, qkvb_grad, outw_grad, gains[0], gains[1],
        gatew_grad, upw_grad, downw_grad, gains[2], gains[3],
    )


def solution(mesh):
    placed = (
        P(("dp", "tensor"), None),
        P(None, "dp", "tensor"),
        P(None, ("tensor", "dp")),
        P("tensor", "dp"),
        P("dp"),
        P("dp"),
        P("dp", "tensor"),
        P("dp", "tensor"),
        P("tensor", "dp"),
        P("dp"),
        P("dp"),
        P(("dp", "tensor"), None),
    )
    return jax.shard_map(
        fast if dict(mesh.shape) == {"dp": 8, "tensor": 4} else local,
        mesh=mesh,
        in_specs=placed,
        out_specs=(
            P(("dp", "tensor"), None),
            P(("dp", "tensor"), None),
            P(None, "dp", "tensor"),
            P(None, ("tensor", "dp")),
            P("tensor", "dp"),
            P("dp"),
            P("dp"),
            P("dp", "tensor"),
            P("dp", "tensor"),
            P("tensor", "dp"),
            P("dp"),
            P("dp"),
        ),
        check_vma=False,
    )
```

```python
import functools

import jax
import jax.numpy as jnp
import numpy as np
from jax import lax
from jax.experimental import pallas as pl
from jax.experimental.pallas import tpu as pltpu
from jax.sharding import PartitionSpec as P

MESH = pl.DeviceIdType.MESH
HEAD_DIM = 64
ROT = 16
BF = jnp.bfloat16
F32 = jnp.float32
VMEM_LIMIT = 56 * 1024 * 1024
ANY = pl.BlockSpec(memory_space=pl.ANY)
INV = pl.BlockSpec(memory_space=pltpu.VMEM)


def nt(a, b):
    return lax.dot_general(a, b, (((1,), (1,)), ((), ())), preferred_element_type=F32)


def tn(a, b):
    return lax.dot_general(a, b, (((0,), (0,)), ((), ())), preferred_element_type=F32)


def nn(a, b):
    return jnp.dot(a, b, preferred_element_type=F32)


def spans(total, step):
    return [(i, min(step, total - i)) for i in range(0, total, step)]


def place():
    d = lax.axis_index("dp")
    z = lax.axis_index("tensor")
    dy = 4 * (1 - 2 * lax.div(d, 4))
    dx = 2 * (1 - 2 * lax.rem(lax.div(d, 2), 2))
    dc = 1 - 2 * lax.rem(d, 2)
    return d, z, (0, dc, dx, dx + dc, dy, dy + dc, dy + dx, dy + dx + dc)


def send(src, dst, ssem, rsem, d, z):
    return pltpu.make_async_remote_copy(
        src_ref=src, dst_ref=dst, send_sem=ssem, recv_sem=rsem, device_id=(d, z), device_id_type=MESH
    )


def greet(d, z, flips, line, plane):
    barrier = pltpu.get_barrier_semaphore()
    for k in range(1, line):
        pl.semaphore_signal(
            barrier, inc=1, device_id=(d, lax.rem(z + k, line)), device_id_type=MESH
        )
    for r in plane:
        pl.semaphore_signal(barrier, inc=1, device_id=(d + flips[r], z), device_id_type=MESH)
    pl.semaphore_wait(barrier, line - 1 + len(plane))


class LineGather:
    def __init__(self, view, chunks, d, z, line, send_sems, recv_sems):
        self.view, self.chunks, self.d, self.z, self.line = view, chunks, d, z, line
        self.ss, self.rs = send_sems, recv_sems

    def copy(self, s, h, way, src=None):
        ref = self.view(s, h)
        return send(
            ref if src is None else src, ref, self.ss.at[way, s, h], self.rs.at[s, h],
            self.d, self.z + (1 if way == 0 else -1),
        )

    def start(self, h, src=None):
        pl.when(self.z < self.line - 1)(lambda: self.copy(self.z, h, 0, src).start())
        pl.when(self.z > 0)(lambda: self.copy(self.z, h, 1, src).start())

    def step(self, k, h, forward=True):
        z, line = self.z, self.line

        @pl.when(z - k >= 0)
        def _():
            self.copy(z - k, h, 0).wait_recv()
            if forward:
                pl.when(z < line - 1)(lambda: self.copy(z - k, h, 0).start())

        @pl.when(z + k < line)
        def _():
            self.copy(z + k, h, 1).wait_recv()
            if forward:
                pl.when(z > 0)(lambda: self.copy(z + k, h, 1).start())

    def finish(self, first=0, last=None):
        z, line = self.z, self.line
        for k in range(first, line if last is None else last):
            for h in range(self.chunks):
                pl.when((z - k >= 0) & (z < line - 1))(lambda: self.copy(z - k, h, 0).wait_send())
                pl.when((z + k < line) & (z > 0))(lambda: self.copy(z + k, h, 1).wait_send())


class PlaneGather:
    def __init__(self, src, view, d, z, flips, send_sems, recv_sems):
        self.src, self.view, self.d, self.z, self.flips = src, view, d, z, flips
        self.ss, self.rs = send_sems, recv_sems
        self.half = src.shape[0] // 2

    def copy(self, key):
        d, f = self.d, self.flips
        block, to, part = {
            1: (0, 1, None), 2: (0, 2, None), 4: (0, 4, None), 3: (2, 1, None), 5: (4, 1, None),
            6: (2, 4, 0), 7: (4, 2, 1), 8: (6, 1, 0), 9: (6, 1, 1),
        }[key]
        dst = self.view(d + f[block])
        src = self.src if block == 0 else dst
        if part is not None:
            at = pl.ds(part * self.half, self.half)
            src, dst = src.at[at], dst.at[at]
        return send(src, dst, self.ss.at[key], self.rs.at[key], d + f[to], self.z)

    def start(self):
        for key in (4, 2, 1):
            self.copy(key).start()

    def relay(self):
        for key, onward in ((2, (6, 3)), (4, (7, 5))):
            self.copy(key).wait_recv()
            for to in onward:
                self.copy(to).start()

    def pass_on(self):
        for key, onward in ((6, 8), (7, 9)):
            self.copy(key).wait_recv()
            self.copy(onward).start()

    def arrive(self):
        for key in (1, 3, 5, 8, 9):
            self.copy(key).wait_recv()

    def finish(self):
        for key in range(1, 10):
            self.copy(key).wait_send()


def arrival(z, i):
    orders = ((0, 1, 2, 3), (1, 0, 2, 3), (2, 3, 1, 0), (3, 2, 1, 0))
    codes = [sum(s * 4**j for j, s in enumerate(o)) for o in orders]
    code = jnp.where(
        z == 0, codes[0], jnp.where(z == 1, codes[1], jnp.where(z == 2, codes[2], codes[3]))
    )
    power = jnp.where(i == 0, 1, jnp.where(i == 1, 4, jnp.where(i == 2, 16, 64)))
    return lax.rem(lax.div(code, power), 4)


def turn(u, cos, sin, sign=1.0):
    low = lax.rem(lax.broadcasted_iota(jnp.int32, (1, 128), 1), HEAD_DIM) < ROT // 2
    moved = jnp.where(low, pltpu.roll(u, 128 - ROT // 2, 1), pltpu.roll(u, ROT // 2, 1)) * sin
    return u * cos + moved if sign > 0 else u * cos - moved


def attention_kernel(
    tok, cot, wq, ow, gw, uw, dw, smalls, cos, sin,
    cotnear, n1, qkv, lse_t, attall, wqkv, small_sum, wout, n2, hidden, wgate, wup, wdown,
    xbuf, n1buf, wbuf, qbuf, attv, wz, wo, acc, smbuf, lse,
    tss, trs, css, crs, ass, ars, mss, mrs, yss, yrs, pss, prs, local,
):
    rows, model = tok.shape
    width = wq.shape[2]
    pairs = width // 128
    line = 4
    d, z, flips = place()
    greet(d, z, flips, line, range(1, 8))

    tok_in = pltpu.make_async_copy(tok, xbuf.at[z], local.at[0])
    tok_in.start()
    depth = wq.shape[1]

    def wblock(i):
        return wbuf.at[pl.ds(pl.multiple_of(i * depth, 256), depth), :]

    w_in = [
        pltpu.make_async_copy(wq.at[j], wblock(d).at[:, pl.ds(j * width, width)], local.at[(2, 1, 13)[j]])
        for j in range(3)
    ]
    for copy in w_in:
        copy.start()
    tall = ow.shape[0]

    def oview(s, h):
        return wz.at[pl.ds(pl.multiple_of(s * tall, tall), tall)]

    def oblock(i):
        return wo.at[:, pl.ds(pl.multiple_of(i * depth, 256), depth)]

    o_in = pltpu.make_async_copy(ow, oview(z, 0), local.at[14])
    o_in.start()
    outs_z = LineGather(oview, 1, d, z, line, yss, yrs)
    small_copies = [
        send(smalls, smbuf.at[r], mss.at[r], mrs.at[r], d + flips[r], z) for r in range(1, 8)
    ]
    for copy in small_copies:
        copy.start()
    tall_block = dw.shape[1]

    def rows_of(ref, i):
        return ref.at[pl.ds(pl.multiple_of(i * depth, 256), depth)]

    def columns_of(ref, i):
        return ref.at[:, pl.ds(pl.multiple_of(i * tall_block, 256), tall_block)]

    planes = [
        PlaneGather(src, view, d, z, flips, pss.at[i], prs.at[i])
        for i, (src, view) in enumerate((
            (wblock(d), wblock),
            (wz, oblock),
            (gw, lambda i: rows_of(wgate, i)),
            (uw, lambda i: rows_of(wup, i)),
            (dw, lambda i: columns_of(wdown, i)),
        ))
    ]
    qkv_plane, out_plane, gate_plane, up_plane, down_plane = planes
    keep_own = [
        pltpu.make_async_copy(gw, rows_of(wgate, d), local.at[10]),
        pltpu.make_async_copy(uw, rows_of(wup, d), local.at[11]),
        pltpu.make_async_copy(dw, columns_of(wdown, d), local.at[12]),
    ]
    for copy in keep_own:
        copy.start()
    half = rows // 2

    def tview(s, h):
        return xbuf.at[s, pl.ds(h * half, half)]

    def cview(s, h):
        return cotnear.at[s, pl.ds(h * half, half)]

    def aview(s, h):
        return attv.at[:, pl.ds(pl.multiple_of(s * width + h * 128, 128), 128)]

    toks = LineGather(tview, 2, d, z, line, tss, trs)
    cots = LineGather(cview, 2, d, z, line, css, crs)
    atts = LineGather(aview, pairs, d, z, line, ass, ars)
    tok_in.wait()
    for h in range(2):
        toks.start(h)
    for copy in w_in:
        copy.wait()
    qkv_plane.start()
    o_in.wait()
    outs_z.start(0)
    for copy in small_copies:
        copy.wait()
    total = smalls[...].astype(F32)
    for r in range(1, 8):
        total = total + smbuf[r].astype(F32)
    small_sum[...] = total

    def normalise(s):
        piece = 32

        @pl.loop(0, rows // piece)
        def _(i):
            at = pl.ds(pl.multiple_of(i * piece, piece), piece)
            x = xbuf[s, at, :].astype(F32)
            centred = x - jnp.mean(x, -1, keepdims=True)
            spread = jnp.mean(centred * centred, -1, keepdims=True)
            n = centred * lax.rsqrt(spread + 1e-05) * small_sum[0:1, :] + small_sum[1:2, :]
            n1buf[pl.ds(pl.multiple_of(s * rows + i * piece, piece), piece), :] = n.astype(BF)

    def project(s):
        at = pl.ds(pl.multiple_of(s * rows, rows), rows)
        for j in range(3):
            cols = pl.ds(j * width, width)
            pre = nn(n1buf[at, :], wbuf[:, cols]) + small_sum[4:5, cols]
            for p in range(pairs):
                part = pre[:, p * 128 : (p + 1) * 128]
                if j < 2:
                    part = turn(part, cos[at, :], sin[at, :])
                qbuf[j, p, at, :] = part.astype(BF)

    normalise(z)
    for h in range(2):
        toks.step(1, h)
    outs_z.step(1, 0)
    qkv_plane.relay()
    gate_plane.start()
    normalise(arrival(z, 1))
    qkv_plane.pass_on()
    for h in range(2):
        toks.step(2, h)
    outs_z.step(2, 0)
    normalise(arrival(z, 2))
    gate_plane.relay()
    qkv_plane.arrive()

    @pl.loop(0, line)
    def _(i):
        s = arrival(z, i)

        @pl.when(i == line - 1)
        def _():
            gate_plane.pass_on()
            for h in range(2):
                toks.step(3, h)
            for h in range(2):
                cots.start(h, cot.at[pl.ds(h * half, half)])
            outs_z.step(3, 0)
            out_plane.start()
            normalise(s)

        project(s)

    o_own = pltpu.make_async_copy(wz, oblock(d), local.at[15])
    o_own.start()

    outs = [
        pltpu.make_async_copy(n1buf, n1, local.at[3]),
        pltpu.make_async_copy(wbuf, wqkv, local.at[4]),
        pltpu.make_async_copy(qbuf, qkv, local.at[5]),
    ]
    for copy in outs:
        copy.start()

    lanes = lax.broadcasted_iota(jnp.int32, (1, 128), 1)
    first = lanes < 64
    lse[...] = jnp.zeros_like(lse)
    length = rows * line

    def attend(p):
        for qi in range(line):
            count = (qi + 1) * rows
            at = pl.ds(qi * rows, rows)
            q = qbuf[0, p, at, :] * BF(HEAD_DIM**-0.5)
            k = qbuf[1, p, pl.ds(0, count), :]
            v = qbuf[2, p, pl.ds(0, count), :]
            row = lax.broadcasted_iota(jnp.int32, (rows, count), 0) + qi * rows
            col = lax.broadcasted_iota(jnp.int32, (rows, count), 1)
            keep = row >= col
            results = []
            stats = lse[at, :]
            for a in range(2):
                mine = first if a == 0 else ~first
                s = nt(jnp.where(mine, q, BF(0)), k)
                s = jnp.where(keep, s, -1e30)
                most = jnp.max(s, -1, keepdims=True)
                e = jnp.exp(s - most)
                total = jnp.sum(e, -1, keepdims=True)
                results.append(nn(e.astype(BF), v) / total)
                stats = jnp.where(lanes == 2 * p + a, most + jnp.log(total), stats)
            lse[at, :] = stats
            attv[at, pl.ds(pl.multiple_of(z * width + p * 128, 128), 128)] = jnp.where(
                first, results[0], results[1]
            ).astype(BF)

    @pl.loop(0, pairs)
    def _(p):
        attend(p)
        atts.start(p)

    lse_t[...] = lse[...].T
    up_plane.start()
    for p in range(pairs):
        atts.step(1, p)
    for h in range(2):
        cots.step(1, h, forward=False)
    out_plane.relay()
    down_plane.start()
    out_plane.pass_on()
    for p in range(pairs):
        atts.step(2, p)
    o_own.wait()
    out_plane.arrive()
    keep_wo = pltpu.make_async_copy(wo, wout, local.at[6])
    keep_wo.start()

    def project_out(s, at, lo, size):
        heads = pl.ds(pl.multiple_of(s * width, width), width)
        return nn(attv[at, heads], wo[heads, pl.ds(lo, size)])

    for i in range(line - 1):
        s = arrival(z, i)

        @pl.loop(0, line)
        def _(r):
            at = pl.ds(pl.multiple_of(r * rows, rows), rows)
            for lo, size in spans(model, 512):
                base = xbuf[r, :, pl.ds(lo, size)].astype(F32) if i == 0 else acc[at, pl.ds(lo, size)]
                acc[at, pl.ds(lo, size)] = base + project_out(s, at, lo, size)

        if i == 1:
            up_plane.relay()
    for copy in outs:
        copy.wait()
    down_plane.relay()
    up_plane.pass_on()
    for p in range(pairs):
        atts.step(3, p)
    inner = (z > 0) & (z < line - 1)

    @pl.when(inner)
    def _():
        cots.copy(z - 1, 0, 0).start()
        cots.copy(z + 1, 0, 1).start()

    keep_att = pltpu.make_async_copy(attv, attall, local.at[7])
    keep_att.start()
    last = arrival(z, line - 1)

    @pl.loop(0, line)
    def _(r):
        at = pl.ds(pl.multiple_of(r * rows, rows), rows)
        for lo, size in spans(model, 512):
            acc[at, pl.ds(lo, size)] += project_out(last, at, lo, size)

        @pl.loop(0, rows // 32)
        def _(i):
            piece = pl.ds(pl.multiple_of(r * rows + i * 32, 32), 32)
            x = acc[piece, :]
            centred = x - jnp.mean(x, -1, keepdims=True)
            spread = jnp.mean(centred * centred, -1, keepdims=True)
            n = centred * lax.rsqrt(spread + 1e-05) * small_sum[2:3, :] + small_sum[3:4, :]
            n1buf[piece, :] = n.astype(BF)

    keep = [
        pltpu.make_async_copy(n1buf, n2, local.at[8]),
        pltpu.make_async_copy(acc.at[pl.ds(pl.multiple_of(z * rows, rows), rows)], hidden, local.at[9]),
        keep_wo, keep_att,
    ]
    for copy in keep[:2]:
        copy.start()
    down_plane.pass_on()
    for gather in (toks, atts, outs_z):
        gather.finish()
    cots.finish(0, 1)

    @pl.when(inner)
    def _():
        cots.copy(z - 1, 0, 0).wait_send()
        cots.copy(z + 1, 0, 1).wait_send()

    pl.when(z >= 2)(lambda: cots.copy(z - 2, 0, 0).wait_recv())
    pl.when(z + 2 < line)(lambda: cots.copy(z + 2, 0, 1).wait_recv())
    for plane in (gate_plane, up_plane, down_plane):
        plane.arrive()
    for plane in planes:
        plane.finish()
    for copy in keep_own:
        copy.wait()
    for copy in keep:
        copy.wait()


def attention_forward(tok, cot, wq, ow, gw, uw, dw, smalls, tabs):
    rows, model = tok.shape
    line = 4
    length = rows * line
    _, depth, width = wq.shape
    pairs = width // 128
    dp = model // depth
    hidden = gw.shape[1]
    sds = jax.ShapeDtypeStruct
    return pl.pallas_call(
        attention_kernel,
        out_shape=(
            sds((line, rows, model), BF), sds((length, model), BF),
            sds((3, pairs, length, 128), BF), sds((128, length), F32), sds((length, model), BF),
            sds((model, 3 * width), BF), sds((16, model), F32),
            sds((model, model), BF), sds((length, model), BF), sds((rows, model), F32),
            sds((model, hidden), BF), sds((model, hidden), BF), sds((hidden, model), BF),
        ),
        in_specs=[ANY] * 7 + [INV] * 3,
        out_specs=(ANY, ANY, ANY, INV, ANY, ANY, INV) + (ANY,) * 6,
        scratch_shapes=[
            pltpu.VMEM((line, rows, model), BF),
            pltpu.VMEM((length, model), BF),
            pltpu.VMEM((model, 3 * width), BF),
            pltpu.VMEM((3, pairs, length, 128), BF),
            pltpu.VMEM((length, model), BF),
            pltpu.VMEM((model, depth), BF),
            pltpu.VMEM((model, model), BF),
            pltpu.VMEM((length, model), F32),
            pltpu.VMEM((dp, 16, model), BF),
            pltpu.VMEM((length, 128), F32),
            pltpu.SemaphoreType.DMA((2, line, 2)),
            pltpu.SemaphoreType.DMA((line, 2)),
            pltpu.SemaphoreType.DMA((2, line, 2)),
            pltpu.SemaphoreType.DMA((line, 2)),
            pltpu.SemaphoreType.DMA((2, line, pairs)),
            pltpu.SemaphoreType.DMA((line, pairs)),
            pltpu.SemaphoreType.DMA((8,)),
            pltpu.SemaphoreType.DMA((8,)),
            pltpu.SemaphoreType.DMA((2, line, 1)),
            pltpu.SemaphoreType.DMA((line, 1)),
            pltpu.SemaphoreType.DMA((5, 10)),
            pltpu.SemaphoreType.DMA((5, 10)),
            pltpu.SemaphoreType.DMA((16,)),
        ],
        compiler_params=pltpu.CompilerParams(
            collective_id=1, has_side_effects=True, vmem_limit_bytes=VMEM_LIMIT
        ),
        cost_estimate=pl.CostEstimate(flops=2 * 10**11, bytes_accessed=10**8, transcendentals=0),
        name="attention_forward",
    )(tok, cot, wq, ow, gw, uw, dw, smalls, *tabs)


def apply_layer_norm(value, norm_scale, norm_bias):
    centered_input = value - jnp.mean(value, -1, keepdims=True)
    spread = jnp.mean(centered_input * centered_input, -1, keepdims=True)
    inverse_deviation = lax.rsqrt(spread + 1e-05)
    standardized_input = centered_input * inverse_deviation
    return (
        standardized_input * norm_scale.astype(jnp.float32) + norm_bias.astype(jnp.float32),
        standardized_input,
        inverse_deviation,
    )


def layer_norm_backward(output_gradient, standardized_input, inverse_deviation, norm_scale):
    scaled_gradient = output_gradient * norm_scale.astype(jnp.float32)
    return inverse_deviation * (
        scaled_gradient
        - jnp.mean(scaled_gradient, -1, keepdims=True)
        - standardized_input * jnp.mean(scaled_gradient * standardized_input, -1, keepdims=True)
    )


def tables(length):
    positions = jnp.arange(length, dtype=jnp.float32)
    freqs = 10000.0 ** (-jnp.arange(0, ROT, 2, dtype=jnp.float32) / ROT)
    angles = positions[:, None] * freqs[None, :]
    angles = jnp.concatenate([angles, angles], -1)
    return (jnp.cos(angles), jnp.sin(angles))


def rotate(heads, cosine, sine):
    half = ROT // 2
    part = heads[..., :ROT]
    turned = jnp.concatenate([-part[..., half:], part[..., :half]], -1)
    moved = part * cosine[:, None, :] + turned * sine[:, None, :]
    return jnp.concatenate([moved, heads[..., ROT:]], -1)


def unrotate(output_gradient, cosine, sine):
    half = ROT // 2
    part = output_gradient[..., :ROT]
    scaled_gradient = part * sine[:, None, :]
    back = jnp.concatenate([scaled_gradient[..., half:], -scaled_gradient[..., :half]], -1)
    moved = part * cosine[:, None, :] + back
    return jnp.concatenate([moved, output_gradient[..., ROT:]], -1)


def attn_params(qkv_weight, qkv_bias, out_weight, norm1_gain, norm1_shift):
    return (
        lax.all_gather(qkv_weight, "dp", axis=1, tiled=True),
        lax.all_gather(qkv_bias, "dp", axis=1, tiled=True),
        lax.all_gather(out_weight, "dp", axis=1, tiled=True),
        lax.all_gather(norm1_gain, "dp", axis=0, tiled=True),
        lax.all_gather(norm1_shift, "dp", axis=0, tiled=True),
    )


def mlp_params(gate_weight, up_weight, down_weight, norm2_gain, norm2_shift):
    return (
        lax.all_gather(gate_weight, "dp", axis=0, tiled=True),
        lax.all_gather(up_weight, "dp", axis=0, tiled=True),
        lax.all_gather(down_weight, "dp", axis=1, tiled=True),
        lax.all_gather(norm2_gain, "dp", axis=0, tiled=True),
        lax.all_gather(norm2_shift, "dp", axis=0, tiled=True),
    )


def gather_rows(rows):
    return lax.all_gather(rows, "tensor", axis=0, tiled=True)


def sum_rows(partial_value):
    return lax.psum_scatter(
        partial_value.astype(jnp.bfloat16), "tensor", scatter_dimension=0, tiled=True
    ).astype(jnp.float32)


def gather_grads(rows):
    return lax.all_gather(rows, "tensor", axis=0, tiled=True)


def sum_grads(partial_value):
    return lax.psum_scatter(
        partial_value.astype(jnp.bfloat16), "tensor", scatter_dimension=0, tiled=True
    ).astype(jnp.float32)


def local(
    tokens,
    qkv_weight,
    qkv_bias,
    out_weight,
    norm1_gain,
    norm1_shift,
    gate_weight,
    up_weight,
    down_weight,
    norm2_gain,
    norm2_shift,
    cotangent,
):
    scale = HEAD_DIM ** (-0.5)
    input_rows = tokens.astype(jnp.float32)
    wqkv, bqkv, wout, first_norm_scale, first_norm_bias = attn_params(
        qkv_weight, qkv_bias, out_weight, norm1_gain, norm1_shift
    )
    first_normed_rows, first_standardized, first_inverse_deviation = apply_layer_norm(
        input_rows, first_norm_scale, first_norm_bias
    )
    rows1 = gather_rows(first_normed_rows.astype(jnp.bfloat16))
    length = rows1.shape[0]
    width = wqkv.shape[2]
    local_heads = width // HEAD_DIM
    pre = (
        jnp.einsum("sd,jdc->jsc", rows1, wqkv, preferred_element_type=jnp.float32)
        + bqkv.astype(jnp.float32)[:, None, :]
    )
    cosine, sine = tables(length)
    query = rotate(pre[0].reshape(length, local_heads, HEAD_DIM), cosine, sine).astype(jnp.bfloat16)
    keys = rotate(pre[1].reshape(length, local_heads, HEAD_DIM), cosine, sine).astype(jnp.bfloat16)
    values = pre[2].reshape(length, local_heads, HEAD_DIM).astype(jnp.bfloat16)
    block = min(length, 512)
    count = length // block
    cols = jnp.arange(length, dtype=jnp.int32)

    def block_probs(qblock, start):
        scores = (
            jnp.einsum("qhd,khd->hqk", qblock, keys, preferred_element_type=jnp.float32) * scale
        )
        rows = start + jnp.arange(block, dtype=jnp.int32)
        keep = rows[:, None] >= cols[None, :]
        return jnp.where(keep[None], scores, -1e30)

    def forward_block(index):
        qblock = lax.dynamic_slice_in_dim(query, index * block, block, 0)
        scores = block_probs(qblock, index * block)
        most = jnp.max(scores, -1, keepdims=True)
        expo = jnp.exp(scores - most)
        total = jnp.sum(expo, -1, keepdims=True)
        probs = (expo / total).astype(jnp.bfloat16)
        out_block = jnp.einsum("hqk,khd->qhd", probs, values, preferred_element_type=jnp.float32)
        return (out_block.astype(jnp.bfloat16), most[..., 0] + jnp.log(total[..., 0]))

    indices = jnp.arange(count, dtype=jnp.int32)
    out_blocks, lse = lax.map(forward_block, indices)
    attended = out_blocks.reshape(length, width)
    branch = jnp.dot(attended, wout, preferred_element_type=jnp.float32)
    hidden_state = input_rows + sum_rows(branch)
    wgate, wup, wdown, second_norm_scale, second_norm_bias = mlp_params(
        gate_weight, up_weight, down_weight, norm2_gain, norm2_shift
    )
    second_normed_rows, second_standardized, second_inverse_deviation = apply_layer_norm(
        hidden_state, second_norm_scale, second_norm_bias
    )
    rows2 = gather_rows(second_normed_rows.astype(jnp.bfloat16))
    gate = jnp.dot(rows2, wgate, preferred_element_type=jnp.float32)
    up = jnp.dot(rows2, wup, preferred_element_type=jnp.float32)
    sigma = jax.nn.sigmoid(gate)
    silu = gate * sigma
    act = (silu * up).astype(jnp.bfloat16)
    mixed = sum_rows(jnp.dot(act, wdown, preferred_element_type=jnp.float32))
    layer_output = (hidden_state + mixed).astype(jnp.bfloat16)
    wgate, wup, wdown, second_norm_scale, second_norm_bias = mlp_params(
        gate_weight, up_weight, down_weight, norm2_gain, norm2_shift
    )
    incoming_gradient = cotangent.astype(jnp.float32)
    down_rows = gather_grads(cotangent)
    down_grad = jnp.einsum("sf,sd->fd", act, down_rows, preferred_element_type=jnp.float32)
    dact = jnp.einsum("sd,fd->sf", down_rows, wdown, preferred_element_type=jnp.float32)
    dgate = (dact * up * (sigma * (1.0 + gate * (1.0 - sigma)))).astype(jnp.bfloat16)
    dup = (dact * silu).astype(jnp.bfloat16)
    gate_grad = jnp.einsum("sd,sf->df", rows2, dgate, preferred_element_type=jnp.float32)
    up_grad = jnp.einsum("sd,sf->df", rows2, dup, preferred_element_type=jnp.float32)
    second_norm_gradient = jnp.einsum(
        "sf,df->sd", dgate, wgate, preferred_element_type=jnp.float32
    ) + jnp.einsum("sf,df->sd", dup, wup, preferred_element_type=jnp.float32)
    second_norm_gradient = sum_grads(second_norm_gradient)
    second_scale_partial = jnp.sum(second_norm_gradient * second_standardized, 0)
    shift2_part = jnp.sum(second_norm_gradient, 0)
    hidden_gradient = incoming_gradient + layer_norm_backward(
        second_norm_gradient, second_standardized, second_inverse_deviation, second_norm_scale
    )
    gatew_grad, upw_grad, downw_grad, gain2_total, shift2_total = (
        lax.psum_scatter(
            gate_grad.astype(jnp.bfloat16), "dp", scatter_dimension=0, tiled=True
        ).astype(jnp.float32),
        lax.psum_scatter(
            up_grad.astype(jnp.bfloat16), "dp", scatter_dimension=0, tiled=True
        ).astype(jnp.float32),
        lax.psum_scatter(
            down_grad.astype(jnp.bfloat16), "dp", scatter_dimension=1, tiled=True
        ).astype(jnp.float32),
        lax.psum_scatter(
            second_scale_partial.astype(jnp.bfloat16), "dp", scatter_dimension=0, tiled=True
        ).astype(jnp.float32),
        lax.psum_scatter(
            shift2_part.astype(jnp.bfloat16), "dp", scatter_dimension=0, tiled=True
        ).astype(jnp.float32),
    )
    wqkv, bqkv, wout, first_norm_scale, first_norm_bias = attn_params(
        qkv_weight, qkv_bias, out_weight, norm1_gain, norm1_shift
    )
    branch_rows = gather_grads(hidden_gradient.astype(jnp.bfloat16))
    out_grad = jnp.einsum("sc,sd->cd", attended, branch_rows, preferred_element_type=jnp.float32)
    dattended = jnp.einsum(
        "sd,cd->sc", branch_rows, wout, preferred_element_type=jnp.float32
    ).astype(jnp.bfloat16)
    dattended = dattended.reshape(length, local_heads, HEAD_DIM)

    def backward_block(carry, item):
        dkeys, dvalues = carry
        index, block_lse = item
        qblock = lax.dynamic_slice_in_dim(query, index * block, block, 0)
        dblock = lax.dynamic_slice_in_dim(dattended, index * block, block, 0)
        scores = block_probs(qblock, index * block)
        probs = jnp.exp(scores - block_lse[..., None])
        probs16 = probs.astype(jnp.bfloat16)
        dvalues = dvalues + jnp.einsum(
            "hqk,qhd->khd", probs16, dblock, preferred_element_type=jnp.float32
        )
        dprobs = jnp.einsum("qhd,khd->hqk", dblock, values, preferred_element_type=jnp.float32)
        inner = jnp.sum(dprobs * probs, -1, keepdims=True)
        dscores = (probs * (dprobs - inner)).astype(jnp.bfloat16)
        dquery = (
            jnp.einsum("hqk,khd->qhd", dscores, keys, preferred_element_type=jnp.float32) * scale
        )
        dkeys = (
            dkeys
            + jnp.einsum("hqk,qhd->khd", dscores, qblock, preferred_element_type=jnp.float32)
            * scale
        )
        return ((dkeys, dvalues), dquery)

    empty = jnp.zeros((length, local_heads, HEAD_DIM), jnp.float32)
    (dkeys, dvalues), dquery = lax.scan(backward_block, (empty, empty), (indices, lse))
    dquery = dquery.reshape(length, local_heads, HEAD_DIM)
    dpre = jnp.stack(
        [
            unrotate(dquery, cosine, sine).reshape(length, width),
            unrotate(dkeys, cosine, sine).reshape(length, width),
            dvalues.reshape(length, width),
        ],
        0,
    ).astype(jnp.bfloat16)
    qkv_grad = jnp.einsum("sd,jsc->jdc", rows1, dpre, preferred_element_type=jnp.float32)
    bias_grad = jnp.sum(dpre, axis=1, dtype=jnp.float32)
    first_norm_gradient = sum_grads(
        jnp.einsum("jsc,jdc->sd", dpre, wqkv, preferred_element_type=jnp.float32)
    )
    first_scale_partial = jnp.sum(first_norm_gradient * first_standardized, 0)
    shift1_part = jnp.sum(first_norm_gradient, 0)
    token_gradient = (
        hidden_gradient
        + layer_norm_backward(
            first_norm_gradient, first_standardized, first_inverse_deviation, first_norm_scale
        )
    ).astype(jnp.bfloat16)
    qkvw_grad, qkvb_grad, outw_grad, gain1_total, shift1_total = (
        lax.psum_scatter(
            qkv_grad.astype(jnp.bfloat16), "dp", scatter_dimension=1, tiled=True
        ).astype(jnp.float32),
        lax.psum_scatter(
            bias_grad.astype(jnp.bfloat16), "dp", scatter_dimension=1, tiled=True
        ).astype(jnp.float32),
        lax.psum_scatter(
            out_grad.astype(jnp.bfloat16), "dp", scatter_dimension=1, tiled=True
        ).astype(jnp.float32),
        lax.psum_scatter(
            first_scale_partial.astype(jnp.bfloat16), "dp", scatter_dimension=0, tiled=True
        ).astype(jnp.float32),
        lax.psum_scatter(
            shift1_part.astype(jnp.bfloat16), "dp", scatter_dimension=0, tiled=True
        ).astype(jnp.float32),
    )
    gain1_grad, shift1_grad, gain2_grad, shift2_grad = lax.psum(
        (gain1_total, shift1_total, gain2_total, shift2_total), "tensor"
    )
    return (
        layer_output,
        token_gradient,
        qkvw_grad,
        qkvb_grad,
        outw_grad,
        gain1_grad,
        shift1_grad,
        gatew_grad,
        upw_grad,
        downw_grad,
        gain2_grad,
        shift2_grad,
    )


class LineScatter:
    def __init__(self, part, slot, chunks, d, z, line, send_sems, recv_sems):
        self.part, self.slot, self.chunks, self.d, self.z, self.line = part, slot, chunks, d, z, line
        self.ss, self.rs = send_sems, recv_sems

    def copy(self, s, h, way, target, place):
        return send(
            self.part(s, h), self.slot(place, h), self.ss.at[s, h], self.rs.at[place, h], self.d, target
        )

    def right(self, s, h):
        return self.copy(s, h, 0, self.z + 1, s)

    def left(self, s, h):
        return self.copy(s, h, 1, self.z - 1, jnp.where(self.z - 1 == s, self.line, s))

    def head(self, s):
        z, line = self.z, self.line
        for h in range(self.chunks):
            pl.when((z == 0) & (s > 0))(lambda: self.right(s, h).start())
            pl.when((z == line - 1) & (s < z))(lambda: self.left(s, h).start())

    def add(self, s, h):
        part = self.part(s, h)
        part[...] = (part[...].astype(F32) + self.slot(s, h)[...].astype(F32)).astype(BF)

    def relay(self, t):
        z, line = self.z, self.line
        up = line - 1 - t + z
        down = t - (line - 1 - z)
        for h in range(self.chunks):
            @pl.when((z > 0) & (up > z) & (up < line))
            def _():
                self.copy(z, h, 0, z, up).wait_recv()
                self.add(up, h)
                self.right(up, h).start()

            @pl.when((z < line - 1) & (down >= 0) & (down < z))
            def _():
                self.copy(z, h, 0, z, down).wait_recv()
                self.add(down, h)
                self.left(down, h).start()

    def arrive(self, h):
        z, line = self.z, self.line
        pl.when(z > 0)(lambda: self.copy(z, h, 0, z, z).wait_recv())
        pl.when(z < line - 1)(lambda: self.copy(z, h, 0, z, line).wait_recv())

    def total(self, h, rows):
        z = self.z
        return (
            self.part(z, h)[rows].astype(F32)
            + self.slot(z, h)[rows].astype(F32)
            + self.slot(self.line, h)[rows].astype(F32)
        )

    def finish(self):
        z = self.z
        for s in range(self.line):
            for h in range(self.chunks):
                pl.when(z != s)(lambda: self.copy(s, h, 0, z, s).wait_send())


def far_first(z, i):
    orders = ((3, 2, 1, 0), (3, 0, 2, 1), (0, 3, 1, 2), (0, 1, 2, 3))
    codes = [sum(s * 4**j for j, s in enumerate(o)) for o in orders]
    code = jnp.where(
        z == 0, codes[0], jnp.where(z == 1, codes[1], jnp.where(z == 2, codes[2], codes[3]))
    )
    power = jnp.where(i == 0, 1, jnp.where(i == 1, 4, jnp.where(i == 2, 16, 64)))
    return lax.rem(lax.div(code, power), 4)


def mlp_kernel(
    n2, cot, cotnear, wgate, wup, wdown,
    dn2, mixed, mland, gex, uex, dex, ghalf, uhalf, dhalf, grecv,
    nbuf, cbuf, gw, uw, dw, act, act_t, dga, dup, part, slots, mixbuf, wide, tall, wide_in, tall_in,
    ss, rs, css, crs, lss, lrs, local, mixsem, outsem, exs, exr, gss, grs,
):
    line = 4
    rows = n2.shape[0] // line
    model = n2.shape[1]
    hidden = wgate.shape[1]
    d, z, flips = place()
    greet(d, z, flips, line, (1, 2, 4, 6))
    core = lax.rem(d, 2)
    chip = lax.div(d, 2)
    loads = [
        pltpu.make_async_copy(a, b, local.at[i])
        for i, (a, b) in enumerate(((n2, nbuf), (wgate, gw), (wup, uw), (wdown, dw)))
    ]
    for copy in loads:
        copy.start()
    half = rows // 2
    scatter = LineScatter(
        lambda s, h: part.at[s, pl.ds(h * half, half)],
        lambda i, h: slots.at[i, pl.ds(h * half, half)],
        2, d, z, line, ss, rs,
    )
    pl.when(z == 0)(lambda: slots.__setitem__((0,), jnp.zeros((rows, model), BF)))
    pl.when(z == line - 1)(lambda: slots.__setitem__((line,), jnp.zeros((rows, model), BF)))
    cots = LineGather(
        lambda s, h: cbuf.at[pl.ds(pl.multiple_of(s * rows + h * half, half), half)], 2, d, z, line, css, crs
    )

    def near(s, k):
        return pltpu.make_async_copy(
            cot if k == 0 else cotnear.at[s], cbuf.at[pl.ds(pl.multiple_of(s * rows, rows), rows)], local.at[5 + k]
        )

    for h in (1, 0):
        @pl.when((z > 0) & (z < line - 1))
        def _():
            if h == 1:
                cots.copy(z - 1, h, 0, cotnear.at[z - 1, pl.ds(h * half, half)]).start()
                cots.copy(z + 1, h, 1, cotnear.at[z + 1, pl.ds(h * half, half)]).start()
            else:
                pl.when(z == 2)(lambda: cots.copy(z - 2, h, 0, cotnear.at[z - 2, pl.ds(0, half)]).start())
                pl.when(z == 1)(lambda: cots.copy(z + 2, h, 1, cotnear.at[z + 2, pl.ds(0, half)]).start())
    def first_half(s, k):
        return pltpu.make_async_copy(
            cotnear.at[s, pl.ds(0, half)], cbuf.at[pl.ds(pl.multiple_of(s * rows, rows), half)], local.at[8 + k]
        )

    pl.when(z >= 2)(lambda: first_half(z - 2, 0).start())
    pl.when(z + 2 < line)(lambda: first_half(z + 2, 1).start())
    near(z, 0).start()
    pl.when(z > 0)(lambda: near(z - 1, 1).start())
    pl.when(z < line - 1)(lambda: near(z + 1, 2).start())
    for copy in loads:
        copy.wait()

    def mixed_out(i):
        s = far_first(z, i)
        at = pl.ds(pl.multiple_of(s * rows, rows), rows)
        return pltpu.make_async_copy(mixbuf.at[lax.rem(i, 2)], mixed.at[at], mixsem.at[lax.rem(i, 2)])

    def mixed_ahead(i):
        at = pl.ds(pl.multiple_of(far_first(z, i) * rows, rows), rows)
        to = jnp.where(z == 0, 1, line - 2)
        return send(mixed.at[at], mland.at[i], lss.at[i], lrs.at[i], d, to)

    at_end = (z == 0) | (z == line - 1)

    @pl.loop(0, line)
    def _(i):
        s = far_first(z, i)
        at = pl.ds(pl.multiple_of(s * rows, rows), rows)
        for lo, size in spans(hidden, 512):
            cols = pl.ds(lo, size)
            gate = nn(nbuf[at, :], gw[:, cols])
            up = nn(nbuf[at, :], uw[:, cols])
            sigma = lax.logistic(gate)
            silu = gate * sigma
            value = (silu * up).astype(BF)
            act[:, cols] = value
            act_t[cols, at] = value.T
            dga[at, cols] = (up * (sigma * (1.0 + gate * (1.0 - sigma)))).astype(BF)
            dup[at, cols] = silu.astype(BF)
        for lo, size in spans(model, 512):
            mixbuf[lax.rem(i, 2), :, pl.ds(lo, size)] = nn(act[...], dw[:, pl.ds(lo, size)]).astype(BF)
        mixed_out(i).start()
        mixed_out(i).wait()
        pl.when(at_end & (i < 2))(lambda: mixed_ahead(i).start())
        pl.when(i == 1)(lambda: cots.step(2, 1))

    def add_mixed(s, slot, send_slot, to, lands):
        at = pl.ds(pl.multiple_of(s * rows, rows), rows)
        ins = [
            pltpu.make_async_copy(mixed.at[at], mixbuf.at[0], mixsem.at[0]),
            pltpu.make_async_copy(mland.at[slot], mixbuf.at[1], mixsem.at[1]),
        ]
        for copy in ins:
            copy.start()
        for copy in ins:
            copy.wait()

        @pl.loop(0, rows // 32)
        def _(i):
            piece = pl.ds(pl.multiple_of(i * 32, 32), 32)
            mixbuf[0, piece, :] = (mixbuf[0, piece, :].astype(F32) + mixbuf[1, piece, :].astype(F32)).astype(BF)

        back = pltpu.make_async_copy(mixbuf.at[0], mixed.at[at], mixsem.at[0])
        back.start()
        back.wait()
        send(mixed.at[at], mland.at[lands], lss.at[send_slot], lrs.at[lands], d, to).start()

    def landing(slot, send_slot):
        return send(mland.at[slot], mland.at[slot], lss.at[send_slot], lrs.at[slot], d, z)

    other = line - 1 - z
    edge = jnp.where(z == 1, 0, line - 1)

    def mixed_on(i):
        @pl.when(~at_end)
        def _():
            landing(i, i).wait_recv()
            add_mixed(line - 1 - edge if i == 0 else other, i, 2 + i, other, 2 + i)

    def mixed_relay():
        @pl.when(~at_end)
        def _():
            landing(2, 2).wait_recv()
            add_mixed(edge, 2, 0, edge, 3)

    mixed_on(0)
    near(z, 0).wait()
    pl.when(z >= 2)(lambda: first_half(z - 2, 0).wait())
    pl.when(z + 2 < line)(lambda: first_half(z + 2, 1).wait())
    pl.when(z > 0)(lambda: near(z - 1, 1).wait())
    pl.when(z < line - 1)(lambda: near(z + 1, 2).wait())
    for h in range(2):
        cots.step(3, h)

    @pl.loop(0, line)
    def _(i):
        s = far_first(z, i)
        at = pl.ds(pl.multiple_of(s * rows, rows), rows)
        for lo, size in spans(hidden, 512):
            cols = pl.ds(lo, size)
            dact = nt(cbuf[at, :], dw[cols, :])
            dga[at, cols] = (dact * dga[at, cols].astype(F32)).astype(BF)
            dup[at, cols] = (dact * dup[at, cols].astype(F32)).astype(BF)
        for lo, size in spans(model, 512):
            cols = pl.ds(lo, size)
            part[s, :, cols] = (nt(dga[at, :], gw[cols, :]) + nt(dup[at, :], uw[cols, :])).astype(BF)
        scatter.head(s)

    blocks = model // rows // 2

    def exchanged(m):
        outs = (ghalf, uhalf, dhalf)
        exes = (gex, uex, dex)
        stage = tall if m == 2 else wide
        stage_in = tall_in if m == 2 else wide_in

        def block(t):
            cols = pl.ds(pl.multiple_of(t * rows, rows), rows)
            if m == 2:
                return lambda lo, size: nn(act_t[pl.ds(lo, size), :], cbuf[:, cols])
            right = dga if m == 0 else dup
            return lambda lo, size: tn(nbuf[:, cols], right[:, pl.ds(lo, size)])

        def piece(ref, lo, size):
            return ref.at[pl.ds(lo, size), :] if m == 2 else ref.at[:, pl.ds(lo, size)]

        def away(k):
            slot = lax.rem(k, 2)
            return send(stage.at[slot], exes[m].at[k], exs.at[m, k], exr.at[m, k], d + flips[1], z)

        @pl.loop(0, blocks)
        def _(k):
            slot = lax.rem(k, 2)
            pl.when(k >= 2)(lambda: away(k - 2).wait_send())
            make = block(2 * k + 1 - core)
            for lo, size in spans(hidden, 512):
                piece(stage.at[slot], lo, size)[...] = make(lo, size).astype(BF)
            away(k).start()

        away(blocks - 2).wait_send()
        away(blocks - 1).wait_send()

        def chip_at(j):
            return lax.rem(chip + 1 + j, blocks)

        def store(j):
            slot = lax.rem(j, 2)
            return pltpu.make_async_copy(stage.at[slot], outs[m].at[chip_at(j)], outsem.at[slot])

        def onward(j):
            k = chip_at(j)
            return send(ghalf.at[k], grecv.at[blocks - 2 - j], gss.at[j], grs.at[blocks - 2 - j], 2 * k + core, z)

        @pl.loop(0, blocks)
        def _(j):
            slot = lax.rem(j, 2)
            k = chip_at(j)

            @pl.when(j >= 2)
            def _():
                store(j - 2).wait()
                if m == 0:
                    onward(j - 2).start()

            away(k).wait_recv()
            fetch = pltpu.make_async_copy(exes[m].at[k], stage_in, local.at[4])
            fetch.start()
            fetch.wait()
            make = block(2 * k + core)
            for lo, size in spans(hidden, 512):
                piece(stage.at[slot], lo, size)[...] = (
                    make(lo, size) + piece(stage_in, lo, size)[...].astype(F32)
                ).astype(BF)
            store(j).start()

        for j in (blocks - 2, blocks - 1):
            store(j).wait()
            if m == 0 and j < blocks - 1:
                onward(j).start()
        return onward

    mixed_on(1)
    onward = exchanged(0)
    scatter.relay(1)
    mixed_relay()

    exchanged(1)
    scatter.relay(2)
    exchanged(2)
    for h in range(2):
        scatter.arrive(h)

        @pl.loop(0, half // 32)
        def _(i):
            rows_at = pl.ds(pl.multiple_of(i * 32, 32), 32)
            dn2[pl.ds(pl.multiple_of(h * half + i * 32, 32), 32), :] = scatter.total(h, rows_at)

    scatter.finish()
    for i in range(2):
        pl.when(at_end)(lambda: mixed_ahead(i).wait_send())
    for i in (0, 2, 3):
        pl.when(~at_end)(lambda: landing(3, i).wait_send())
    landing(3, 3).wait_recv()
    for k, h in ((1, 1), (2, 0), (2, 1)):
        pl.when((z - k >= 0) & (z < line - 1))(lambda: cots.copy(z - k, h, 0).wait_send())
        pl.when((z + k < line) & (z > 0))(lambda: cots.copy(z + k, h, 1).wait_send())
    for j in range(blocks - 1):
        onward(j).wait()


def mlp(n2, cot, cotnear, wgate, wup, wdown):
    length, model = n2.shape
    hidden = wgate.shape[1]
    line = 4
    rows = length // line
    blocks = model // rows // 2
    sds = jax.ShapeDtypeStruct
    wide = sds((blocks, rows, hidden), BF)
    tall = sds((blocks, hidden, rows), BF)
    return pl.pallas_call(
        mlp_kernel,
        out_shape=(
            sds((rows, model), F32), sds((length, model), BF), sds((4, rows, model), BF),
            wide, wide, tall, wide, wide, tall, sds((blocks - 1, rows, hidden), BF),
        ),
        in_specs=[ANY] * 6,
        out_specs=(INV,) + (ANY,) * 9,
        scratch_shapes=[
            pltpu.VMEM((length, model), BF),
            pltpu.VMEM((length, model), BF),
            pltpu.VMEM((model, hidden), BF),
            pltpu.VMEM((model, hidden), BF),
            pltpu.VMEM((hidden, model), BF),
            pltpu.VMEM((rows, hidden), BF),
            pltpu.VMEM((hidden, length), BF),
            pltpu.VMEM((length, hidden), BF),
            pltpu.VMEM((length, hidden), BF),
            pltpu.VMEM((line, rows, model), BF),
            pltpu.VMEM((line + 1, rows, model), BF),
            pltpu.VMEM((2, rows, model), BF),
            pltpu.VMEM((2, rows, hidden), BF),
            pltpu.VMEM((2, hidden, rows), BF),
            pltpu.VMEM((rows, hidden), BF),
            pltpu.VMEM((hidden, rows), BF),
            pltpu.SemaphoreType.DMA((line, 2)),
            pltpu.SemaphoreType.DMA((line + 1, 2)),
            pltpu.SemaphoreType.DMA((2, line, 2)),
            pltpu.SemaphoreType.DMA((line, 2)),
            pltpu.SemaphoreType.DMA((4,)),
            pltpu.SemaphoreType.DMA((4,)),
            pltpu.SemaphoreType.DMA((10,)),
            pltpu.SemaphoreType.DMA((2,)),
            pltpu.SemaphoreType.DMA((2,)),
            pltpu.SemaphoreType.DMA((3, blocks)),
            pltpu.SemaphoreType.DMA((3, blocks)),
            pltpu.SemaphoreType.DMA((blocks,)),
            pltpu.SemaphoreType.DMA((blocks,)),
        ],
        compiler_params=pltpu.CompilerParams(
            collective_id=2, has_side_effects=True, vmem_limit_bytes=62 * 1024 * 1024
        ),
        cost_estimate=pl.CostEstimate(flops=10**11, bytes_accessed=10**8, transcendentals=0),
        name="mlp",
    )(n2, cot, cotnear, wgate, wup, wdown)


def norm_parts(x):
    centred = x - jnp.mean(x, -1, keepdims=True)
    inverse = lax.rsqrt(jnp.mean(centred * centred, -1, keepdims=True) + 1e-05)
    return centred * inverse, inverse


def norm_back(grad, standard, inverse, gain):
    scaled = grad * gain
    return inverse * (
        scaled
        - jnp.mean(scaled, -1, keepdims=True)
        - standard * jnp.mean(scaled * standard, -1, keepdims=True)
    )


def each_piece(rows, piece, body):
    @pl.loop(0, rows // piece)
    def _(i):
        body(pl.ds(pl.multiple_of(i * piece, piece), piece))


class PlaneSum:
    def __init__(self, half, recv, d, z, flips, send_sems, recv_sems):
        self.half, self.recv, self.d, self.z, self.flips = half, recv, d, z, flips
        self.ss, self.rs = send_sems, recv_sems

    def copy(self, r):
        to, slot = self.d + self.flips[r], r // 2 - 1
        return send(self.half.at[lax.div(to, 2)], self.recv.at[slot], self.ss.at[slot], self.rs.at[slot], to, self.z)

    def start(self, *which):
        for r in which:
            self.copy(r).start()

    def wait(self):
        for r in (2, 4, 6):
            self.copy(r).wait()


class PlaneChain:
    def __init__(self, half, recv, mid, d, z, flips, send_sems, recv_sems):
        self.half, self.recv, self.mid, self.d, self.z, self.flips = half, recv, mid, d, z, flips
        self.ss, self.rs = send_sems, recv_sems
        self.rows = half.shape[1] // 2

    def block(self, r):
        return lax.div(self.d + self.flips[r], 2)

    def copy(self, key):
        block, over, part = ((6, 2, 0), (6, 4, 1), (4, 4, 1), (2, 2, 0), (4, 4, 0), (2, 2, 1))[key]
        at = pl.ds(part * self.rows, self.rows)
        dst = self.mid.at[key] if key < 2 else self.recv.at[0 if over == 2 else 1, at]
        return send(
            self.half.at[self.block(block), at], dst, self.ss.at[key], self.rs.at[key], self.d + self.flips[over], self.z
        )

    def start(self):
        for key in range(4):
            self.copy(key).start()

    def relay(self):
        for key, block, part in ((0, 4, 0), (1, 2, 1)):
            self.copy(key).wait_recv()
            k = self.block(block)
            piece = min(self.rows, 128)

            @pl.loop(0, self.rows // piece)
            def _(i):
                at = pl.ds(pl.multiple_of(part * self.rows + i * piece, piece), piece)
                mid = self.mid[key, pl.ds(pl.multiple_of(i * piece, piece), piece), :]
                self.half[k, at, :] = (self.half[k, at, :].astype(F32) + mid.astype(F32)).astype(BF)

            self.copy(key + 4).start()

    def arrive(self):
        for key in range(2, 6):
            self.copy(key).wait_recv()

    def total(self, at):
        return (
            self.half[(self.block(0),) + at].astype(F32)
            + self.recv[(0,) + at].astype(F32)
            + self.recv[(1,) + at].astype(F32)
        )

    def finish(self):
        for key in range(6):
            self.copy(key).wait_send()


class BlockSum:
    def __init__(self, own, recv, bufs, stage, out, in_sems, out_sems):
        self.ins = [own] + [recv.at[j] for j in range(recv.shape[0])]
        self.bufs, self.stage, self.out, self.in_sems, self.out_sems = bufs, stage, out, in_sems, out_sems

    def copies(self):
        return [pltpu.make_async_copy(a, b, self.in_sems.at[i]) for i, (a, b) in enumerate(zip(self.ins, self.bufs))]

    def fetch(self):
        for copy in self.copies():
            copy.start()

    def store(self, i):
        rows = self.stage.shape[1]
        at = pl.ds(pl.multiple_of(i * rows, rows), rows)
        return pltpu.make_async_copy(self.stage.at[lax.rem(i, 2)], self.out.at[at], self.out_sems.at[lax.rem(i, 2)])

    def add(self):
        for copy in self.copies():
            copy.wait()
        rows = self.stage.shape[1]
        pieces = self.out.shape[0] // rows
        small = 32

        @pl.loop(0, pieces)
        def _(i):
            pl.when(i >= 2)(lambda: self.store(i - 2).wait())

            @pl.loop(0, rows // small)
            def _(j):
                at = pl.ds(pl.multiple_of(i * rows + j * small, small), small)
                total = self.bufs[0][at, :].astype(F32)
                for buf in self.bufs[1:]:
                    total = total + buf[at, :].astype(F32)
                self.stage[lax.rem(i, 2), pl.ds(pl.multiple_of(j * small, small), small), :] = total

            self.store(i).start()

        self.store(jnp.int32(pieces - 2)).wait()
        self.store(jnp.int32(pieces - 1)).wait()


def attention_back_kernel(
    hid, small, lse_t, cos, sin, dn2, cot, tok, wout, attall, qkv, mixed, mland, ghalf, grecv, uhalf, dhalf, wqkv, n1,
    tgrad, ograd, gains, bout, lay, ggrad, ugrad, dgrad, qgrad, urecv, drecv, oex, qex,
    wo, da, dhid, attr, att_t, attc, qbuf, dsend, datt, part, slots, marr, ofull, osum, orecv, omid, ozr,
    dq, dpre, nbuf, qstage, qfetch, qsum, qrecv, qmid, wide_sum, tall_sum, qtotal, sums, zsums, dsums, bsums,
    mss, mrs, ass, ars, oss, ors, pss, prs, uss, urs, zss, zrs,
    ss, rs, xss, xrs, qss, qrs, dss, drs, yss, yrs, gss, grs, bss, brs, local, tsem, fsem, gsem,
):
    line = 4
    rows, model = hid.shape
    length = rows * line
    width = attc.shape[1]
    pairs = width // 128
    blocks = model // rows // 2
    half = rows // 2
    d, z, flips = place()
    greet(d, z, flips, line, range(1, 8))
    core = lax.rem(d, 2)
    ups = PlaneSum(uhalf, urecv, d, z, flips, uss, urs)
    downs = PlaneSum(dhalf, drecv, d, z, flips, dss, drs)
    loads = [
        pltpu.make_async_copy(wout, wo, local.at[4]),
        pltpu.make_async_copy(attall.at[pl.ds(pl.multiple_of(z * rows, rows), rows)], attr, local.at[5]),
        pltpu.make_async_copy(attall.at[:, pl.ds(pl.multiple_of(z * width, width), width)], attc, local.at[6]),
        pltpu.make_async_copy(qkv, qbuf, local.at[7]),
    ]
    rows_in = [pltpu.make_async_copy(dn2, dhid, local.at[11]), pltpu.make_async_copy(cot, da, local.at[12])]
    for copy in rows_in:
        copy.start()

    at_end = (z == 0) | (z == line - 1)
    inner = jnp.where(z == 0, 1, line - 2)

    def mixed_last(h):
        at = pl.ds(pl.multiple_of(inner * rows + h * half, half), half)
        return send(mixed.at[at], marr.at[pl.ds(h * half, half)], mss.at[h], mrs.at[h], d, inner)

    pl.when(at_end)(lambda: mixed_last(0).start())
    pl.when(at_end)(lambda: marr.__setitem__(Ellipsis, jnp.zeros((rows, model), BF)))
    for copy in loads:
        copy.start()
    ups.start(2, 4)

    def chain(part, slots, send_sems, recv_sems):
        pl.when(z == 0)(lambda: slots.__setitem__((0,), jnp.zeros((rows, model), BF)))
        pl.when(z == line - 1)(lambda: slots.__setitem__((line,), jnp.zeros((rows, model), BF)))
        return LineScatter(
            lambda s, h: part.at[s, pl.ds(h * half, half)],
            lambda i, h: slots.at[i, pl.ds(h * half, half)],
            2, d, z, line, send_sems, recv_sems,
        )

    for copy in rows_in:
        copy.wait()
    sums[...] = jnp.zeros_like(sums)

    def back(at):
        grad = dhid[at, :]
        standard, inverse = norm_parts(hid[at, :])
        sums[2:3, :] += jnp.sum(grad * standard, 0, keepdims=True)
        sums[3:4, :] += jnp.sum(grad, 0, keepdims=True)
        total = da[at, :].astype(F32) + norm_back(grad, standard, inverse, small[2:3, :])
        dhid[at, :] = total
        da[at, :] = total.astype(BF)

    each_piece(rows, 32, back)
    for copy in loads:
        copy.wait()

    def away(k, p):
        to = lax.rem(z + k, line)
        cols = pl.ds(p * 128, 128)
        return send(
            dsend.at[to, :, cols], datt.at[pl.ds(pl.multiple_of(z * rows, rows), rows), cols],
            ass.at[k, p], ars.at[z, p], d, to,
        )

    def taken(k, p):
        frm = lax.rem(z + k, line)
        cols = pl.ds(pl.multiple_of(p * 128, 128), 128)
        return send(
            dsend.at[frm, :, cols], datt.at[pl.ds(pl.multiple_of(frm * rows, rows), rows), cols],
            ass.at[k, p], ars.at[frm, p], d, frm,
        )

    @pl.loop(1, line + 1)
    def _(k):
        to = lax.rem(z + k, line)
        dsend[to] = nt(da[...], wo[pl.ds(pl.multiple_of(to * width, width), width), :]).astype(BF)

    for p in range(pairs):
        for k in range(1, line):
            away(k, p).start()
    pl.when(at_end)(lambda: mixed_last(1).start())
    weights_in = pltpu.make_async_copy(wqkv, wo.at[:, pl.ds(0, 3 * width)], local.at[4])
    weights_in.start()
    datt[pl.ds(pl.multiple_of(z * rows, rows), rows), :] = dsend[z]
    for lo, size in spans(model, 512):
        att_t[pl.ds(lo, size), :] = attr[:, pl.ds(lo, size)].T
    tok_in = pltpu.make_async_copy(tok, attr, local.at[6])
    tok_in.start()

    def oblock(t):
        return nn(att_t[...], da[:, pl.ds(pl.multiple_of(t * rows, rows), rows)])

    def ostage(k):
        return wo.at[:, pl.ds(pl.multiple_of(3 * width + lax.rem(k, 2) * rows, rows), rows)]

    def oacross(k):
        return send(ostage(k), oex.at[k], oss.at[k], ors.at[k], d + flips[1], z)

    @pl.loop(0, blocks)
    def _(k):
        pl.when(k >= 2)(lambda: oacross(k - 2).wait_send())
        ostage(k)[...] = oblock(2 * k + 1 - core).astype(BF)
        oacross(k).start()

    oplanes = PlaneChain(osum, orecv, omid, d, z, flips, pss, prs)

    @pl.loop(0, blocks)
    def _(k):
        oacross(k).wait_recv()
        fetch = pltpu.make_async_copy(oex.at[k], ofull, local.at[8])
        fetch.start()
        fetch.wait()
        osum[k] = (oblock(2 * k + core) + ofull[...].astype(F32)).astype(BF)

    oplanes.start()
    oacross(blocks - 2).wait_send()
    oacross(blocks - 1).wait_send()
    lanes = lax.broadcasted_iota(jnp.int32, (1, 128), 1)
    mine = (lanes < 64, lanes >= 64)
    which = lax.broadcasted_iota(jnp.int32, (16, 128), 0)
    lane16 = lax.broadcasted_iota(jnp.int32, (16, 128), 1)
    pick = jnp.where(which == lax.div(lane16, 64), 1.0, 0.0).astype(BF)
    scale = HEAD_DIM**-0.5

    def zaway(k):
        to = lax.rem(z + k, line)
        return send(
            ofull.at[pl.ds(pl.multiple_of(to * width, width), width)], ozr.at[k - 1], zss.at[k], zrs.at[k - 1], d, to
        )

    def plane_total():
        oplanes.arrive()

        def add(at):
            ofull[at, :] = oplanes.total((at, slice(None))).astype(BF)

        each_piece(model, 256, add)
        for k in range(1, line):
            zaway(k).start()

    def back_pair(p):
        cols = pl.ds(pl.multiple_of(p * 128, 128), 128)
        do = datt[:, cols]
        prod = do.astype(F32) * attc[:, cols].astype(F32)
        high = prod.astype(BF)
        inner = nt(pick, high) + nt(pick, (prod - high.astype(F32)).astype(BF))
        q = qbuf[0, p] * BF(scale)
        dq[...] = jnp.zeros_like(dq)
        for kj in range(line):
            at = pl.ds(kj * rows, rows)
            lo, count = kj * rows, length - kj * rows
            k, v = qbuf[1, p, at, :], qbuf[2, p, at, :]
            row = lax.broadcasted_iota(jnp.int32, (rows, count), 0)
            col = lax.broadcasted_iota(jnp.int32, (rows, count), 1)
            keep = col >= row
            dk = jnp.zeros((rows, 128), F32)
            dv = jnp.zeros((rows, 128), F32)
            for a in range(2):
                km, vm = jnp.where(mine[a], k, BF(0)), jnp.where(mine[a], v, BF(0))
                qm, dm = jnp.where(mine[a], q[lo:], BF(0)), jnp.where(mine[a], do[lo:], BF(0))
                s = jnp.where(keep, nt(km, q[lo:]), -1e30)
                probs = jnp.exp(s - lse_t[pl.ds(2 * p + a, 1), pl.ds(lo, count)])
                dv += nn(probs.astype(BF), dm)
                dprobs = nt(vm, do[lo:])
                ds = (probs * (dprobs - inner[a : a + 1, lo:])).astype(BF)
                dk += nn(ds, qm)
                dq[pl.ds(lo, count), :] += tn(ds, km)
            dk = turn(dk, cos[at, :], sin[at, :], -1.0)
            dpre[at, pl.ds(pl.multiple_of(width + p * 128, 128), 128)] = dk.astype(BF)
            dpre[at, pl.ds(pl.multiple_of(2 * width + p * 128, 128), 128)] = dv.astype(BF)
        dpre[:, cols] = turn(dq[...] * scale, cos[...], sin[...], -1.0).astype(BF)

    @pl.loop(0, pairs)
    def _(p):
        for k in range(1, line):
            taken(k, p).wait_recv()
        back_pair(p)

        @pl.when(p == 1)
        def _():
            oplanes.relay()
            ups.start(6)
            downs.start(2, 4, 6)

        pl.when(p == pairs - 1)(lambda: plane_total())

    weights_in.wait()
    chains = chain(part, slots, ss, rs)

    @pl.loop(0, line)
    def _(i):
        s = far_first(z, i)
        at = pl.ds(pl.multiple_of(s * rows, rows), rows)
        for lo, size in spans(model, 512):
            part[s, :, pl.ds(lo, size)] = nt(dpre[at, :], wo[pl.ds(lo, size), pl.ds(0, 3 * width)]).astype(BF)
        chains.head(s)

    hidden = uhalf.shape[2]
    chip = lax.div(d, 2)

    def wide(i):
        return [wo.at[pl.ds((i + k) * rows, rows), pl.ds(0, hidden)] for k in range(blocks)]

    gate_sum = BlockSum(ghalf.at[chip], grecv, wide(0), wide_sum, ggrad, fsem.at[0], gsem)
    up_sum = BlockSum(uhalf.at[chip], urecv, wide(blocks), wide_sum, ugrad, fsem.at[1], gsem)
    tall = [osum.at[k, pl.ds(0, hidden)] for k in range(blocks)]
    down_sum = BlockSum(dhalf.at[chip], drecv, tall, tall_sum, dgrad, fsem.at[2], gsem)
    gate_sum.fetch()
    mixed_in = [
        pltpu.make_async_copy(mixed.at[pl.ds(pl.multiple_of(z * rows, rows), rows)], wo.at[pl.ds(4 * rows, rows)], local.at[0]),
        pltpu.make_async_copy(mland.at[3], wo.at[pl.ds(5 * rows, rows)], local.at[1]),
    ]
    for copy in mixed_in:
        copy.start()

    def tile_in(i):
        t = 2 * lax.rem(i, blocks) + jnp.where(i < blocks, 1 - core, core)
        cols = pl.ds(pl.multiple_of(t * rows, rows), rows)
        return pltpu.make_async_copy(n1.at[:, cols], nbuf.at[lax.rem(i, 2)], tsem.at[lax.rem(i, 2)])

    def qblock(i):
        tile_in(i).wait()
        pl.when(i < 2 * blocks - 1)(lambda: tile_in(i + 1).start())
        return lambda lo, size: tn(nbuf[lax.rem(i, 2)], dpre[:, pl.ds(lo, size)])

    tile_in(jnp.int32(0)).start()

    def qacross(k):
        return send(qstage.at[lax.rem(k, 2)], qex.at[k], xss.at[k], xrs.at[k], d + flips[1], z)

    @pl.loop(0, blocks)
    def _(k):
        pl.when(k >= 2)(lambda: qacross(k - 2).wait_send())
        make = qblock(k)
        for lo, size in spans(3 * width, 512):
            qstage[lax.rem(k, 2), :, pl.ds(lo, size)] = make(lo, size).astype(BF)
        qacross(k).start()

    qplanes = PlaneChain(qsum, qrecv, qmid, d, z, flips, qss, qrs)

    @pl.loop(0, blocks)
    def _(k):
        qacross(k).wait_recv()
        fetch = pltpu.make_async_copy(qex.at[k], qfetch, local.at[8])
        fetch.start()
        fetch.wait()
        make = qblock(k + blocks)
        for lo, size in spans(3 * width, 512):
            qsum[k, :, pl.ds(lo, size)] = (make(lo, size) + qfetch[:, pl.ds(lo, size)].astype(F32)).astype(BF)

    qplanes.start()
    chains.relay(1)
    for h in range(2):
        pl.when(~at_end)(lambda: mixed_last(h).wait_recv())

    for copy in mixed_in:
        copy.wait()

    @pl.loop(0, rows // 32)
    def _(i):
        at = pl.ds(pl.multiple_of(i * 32, 32), 32)
        total = marr[at, :].astype(F32)
        for k in (4, 5):
            total = total + wo[pl.ds(pl.multiple_of(k * rows + i * 32, 32), 32), :].astype(F32)
        da[at, :] = (hid[at, :] + total).astype(BF)

    lay_out = pltpu.make_async_copy(da, lay, local.at[0])
    lay_out.start()
    bsums[0] = jnp.zeros(bsums.shape[1:], F32)

    def bias(at):
        bsums[0, 0:1, :] += jnp.sum(dpre[at, :].astype(F32), 0, keepdims=True)

    each_piece(length, 64, bias)

    def bcopy(r):
        return send(bsums.at[0], bsums.at[r], bss.at[r], brs.at[r], d + flips[r], z)

    for r in range(1, 8):
        bcopy(r).start()
    qplanes.relay()
    ups.wait()
    up_sum.fetch()
    gate_sum.add()
    chains.relay(2)
    oplanes.finish()
    total = ofull[pl.ds(pl.multiple_of(z * width, width), width), :].astype(F32)
    for k in range(1, line):
        zaway(k).wait()
        total = total + ozr[k - 1].astype(F32)
    ograd[...] = total
    downs.wait()
    down_sum.fetch()
    up_sum.add()
    down_sum.add()
    qplanes.arrive()
    piece = qtotal.shape[1]

    @pl.loop(0, rows // piece)
    def _(i):
        at = pl.ds(pl.multiple_of(i * piece, piece), piece)
        for j in range(3):
            qtotal[j] = qplanes.total((at, pl.ds(j * width, width)))
        back = pltpu.make_async_copy(qtotal, qgrad.at[:, at], local.at[1])
        back.start()
        back.wait()

    total = jnp.zeros(bout.shape, F32)
    for r in range(8):
        if r:
            bcopy(r).wait()
        total = total + bsums[r]
    bout[...] = total
    tok_in.wait()
    for h in range(2):
        chains.arrive(h)

        @pl.loop(0, half // 32)
        def _(i):
            at = pl.ds(pl.multiple_of(h * half + i * 32, 32), 32)
            grad = chains.total(h, pl.ds(pl.multiple_of(i * 32, 32), 32))
            standard, inverse = norm_parts(attr[at, :].astype(F32))
            sums[0:1, :] += jnp.sum(grad * standard, 0, keepdims=True)
            sums[1:2, :] += jnp.sum(grad, 0, keepdims=True)
            tgrad[at, :] = (dhid[at, :] + norm_back(grad, standard, inverse, small[0:1, :])).astype(BF)

    depth = gains.shape[1]

    def columns(i):
        return sums.at[:, pl.ds(pl.multiple_of(i * depth, 256), depth)]

    def dcopy(r):
        return send(columns(d + flips[r]), dsums.at[r], gss.at[r], grs.at[r], d + flips[r], z)

    def zcopy(k):
        return send(zsums.at[0], zsums.at[k], yss.at[k], yrs.at[k], d, lax.rem(z + k, line))

    for r in range(1, 8):
        dcopy(r).start()
    total = columns(d)[...]
    for r in range(1, 8):
        dcopy(r).wait()
        total = total + dsums[r]
    zsums[0] = total
    for k in range(1, line):
        zcopy(k).start()
    for k in range(1, line):
        zcopy(k).wait()
        total = total + zsums[k]
    gains[...] = total
    for k in range(1, line):
        for p in range(pairs):
            away(k, p).wait_send()
    qplanes.finish()
    qacross(blocks - 2).wait_send()
    qacross(blocks - 1).wait_send()
    lay_out.wait()
    for h in range(2):
        pl.when(at_end)(lambda: mixed_last(h).wait_send())
    chains.finish()


def attention_backward(dn2, hid, cot, small, lse, tok, tabs, wout, attall, qkv, mixed, mland, ghalf, grecv, uhalf, dhalf, wqkv, n1):
    rows, model = hid.shape
    line = 4
    length = rows * line
    width = model // line
    pairs = width // 128
    blocks = model // rows // 2
    hidden = uhalf.shape[2]
    sds = jax.ShapeDtypeStruct
    dma = pltpu.SemaphoreType.DMA
    vmem = pltpu.VMEM
    return pl.pallas_call(
        attention_back_kernel,
        out_shape=(
            sds((rows, model), BF), sds((width, rows), F32),
            sds((8, rows), F32), sds((8, 3 * width), F32), sds((rows, model), BF),
            sds((rows, hidden), F32), sds((rows, hidden), F32), sds((hidden, rows), F32), sds((3, rows, width), F32),
            sds((blocks - 1, rows, hidden), BF), sds((blocks - 1, hidden, rows), BF),
            sds((blocks, model, rows), BF), sds((blocks, rows, 3 * width), BF),
        ),
        in_specs=[INV] * 5 + [ANY] * 14,
        out_specs=(INV,) * 4 + (ANY,) * 9,
        scratch_shapes=[
            vmem((model, model), BF), vmem((rows, model), BF), vmem((rows, model), F32), vmem((rows, model), BF),
            vmem((model, rows), BF), vmem((length, width), BF), vmem((3, pairs, length, 128), BF),
            vmem((line, rows, width), BF), vmem((length, width), BF),
            vmem((line, rows, model), BF), vmem((line + 1, rows, model), BF),
            vmem((rows, model), BF),
            vmem((model, rows), BF), vmem((blocks, model, rows), BF),
            vmem((2, model, rows), BF), vmem((2, model // 2, rows), BF),
            vmem((line - 1, width, rows), BF),
            vmem((length, 128), F32), vmem((length, 3 * width), BF), vmem((2, length, rows), BF),
            vmem((2, rows, 3 * width), BF), vmem((rows, 3 * width), BF), vmem((blocks, rows, 3 * width), BF),
            vmem((2, rows, 3 * width), BF), vmem((2, rows // 2, 3 * width), BF),
            vmem((2, 64, hidden), F32), vmem((2, hidden // 4, rows), F32), vmem((3, 64, width), F32),
            vmem((8, model), F32), vmem((line, 8, rows), F32), vmem((8, 8, rows), F32), vmem((8, 8, 3 * width), F32),
            dma((2,)), dma((2,)), dma((line, pairs)), dma((line, pairs)), dma((blocks,)), dma((blocks,)),
            dma((6,)), dma((6,)), dma((3,)), dma((3,)), dma((line,)), dma((line,)),
            dma((line, 2)), dma((line + 1, 2)), dma((blocks,)), dma((blocks,)), dma((6,)), dma((6,)),
            dma((3,)), dma((3,)), dma((line,)), dma((line,)), dma((8,)), dma((8,)), dma((8,)), dma((8,)), dma((13,)), dma((2,)),
            dma((3, blocks)), dma((2,)),
        ],
        compiler_params=pltpu.CompilerParams(
            collective_id=3, has_side_effects=True, vmem_limit_bytes=63 * 1024 * 1024
        ),
        cost_estimate=pl.CostEstimate(flops=10**11, bytes_accessed=10**8, transcendentals=0),
        name="attention_backward",
    )(hid, small, lse, *tabs, dn2, cot, tok, wout, attall, qkv, mixed, mland, ghalf, grecv, uhalf, dhalf, wqkv, n1)


def turn_tables(length):
    half = ROT // 2
    freqs = np.float32(10000.0) ** (-np.arange(0, ROT, 2, dtype=np.float32) / np.float32(ROT))
    angles = np.arange(length, dtype=np.float32)[:, None] * freqs[None, :]
    cos = np.ones((length, HEAD_DIM), np.float32)
    sin = np.zeros((length, HEAD_DIM), np.float32)
    cos[:, :half] = cos[:, half:ROT] = np.cos(angles)
    sin[:, half:ROT] = np.sin(angles)
    sin[:, :half] = -np.sin(angles)
    return tuple(jnp.asarray(np.tile(t, (1, 2))) for t in (cos, sin))


def pack_smalls(d, model, width, qkv_bias, *vectors):
    col = lax.broadcasted_iota(jnp.int32, (1, model), 1)
    each = vectors[0].shape[0]
    gains = jnp.stack([jnp.tile(v, model // each) for v in vectors], 0)
    gains = jnp.where(col // each == d, gains, 0)
    part = qkv_bias.shape[1]
    bias = jnp.tile(qkv_bias, (1, width // part)).reshape(1, 3 * width)
    bias = jnp.pad(bias, ((0, 0), (0, model - 3 * width)))
    bias = jnp.where(col % width // part == d, bias, 0)
    return jnp.concatenate([gains, bias, jnp.zeros((11, model), BF)], 0).astype(BF)


def fast(
    tokens, qkv_weight, qkv_bias, out_weight, norm1_gain, norm1_shift, gate_weight, up_weight,
    down_weight, norm2_gain, norm2_shift, cotangent,
):
    d = lax.axis_index("dp")
    rows, model = tokens.shape
    length = 4 * rows
    tabs = turn_tables(length)
    depth, width = qkv_weight.shape[1:]
    smalls = pack_smalls(d, model, width, qkv_bias, norm1_gain, norm1_shift, norm2_gain, norm2_shift)
    cotnear, n1, qkv, lse, attall, wqkv, small, wout, n2, hidden, wgate, wup, wdown = attention_forward(
        tokens, cotangent, qkv_weight, out_weight, gate_weight, up_weight, down_weight, smalls, tabs
    )
    dn2, mixed, mland, _, _, _, ghalf, uhalf, dhalf, grecv = mlp(n2, cotangent, cotnear, wgate, wup, wdown)
    (
        token_gradient, outw_grad, gains, bias, layer_output, gatew_grad, upw_grad, downw_grad, qkvw_grad, _, _, _, _
    ) = attention_backward(
        dn2, hidden, cotangent, small, lse, tokens, tabs, wout, attall, qkv, mixed, mland, ghalf, grecv, uhalf, dhalf,
        wqkv, n1,
    )
    part = qkv_bias.shape[1]
    bias = bias[0].reshape(3, width)
    qkvb_grad = lax.dynamic_slice_in_dim(bias, d * part, part, 1)
    return (
        layer_output, token_gradient, qkvw_grad, qkvb_grad, outw_grad, gains[0], gains[1],
        gatew_grad, upw_grad, downw_grad, gains[2], gains[3],
    )


def solution(mesh):
    placed = (
        P(("dp", "tensor"), None),
        P(None, "dp", "tensor"),
        P(None, ("tensor", "dp")),
        P("tensor", "dp"),
        P("dp"),
        P("dp"),
        P("dp", "tensor"),
        P("dp", "tensor"),
        P("tensor", "dp"),
        P("dp"),
        P("dp"),
        P(("dp", "tensor"), None),
    )
    return jax.shard_map(
        fast if dict(mesh.shape) == {"dp": 8, "tensor": 4} else local,
        mesh=mesh,
        in_specs=placed,
        out_specs=(
            P(("dp", "tensor"), None),
            P(("dp", "tensor"), None),
            P(None, "dp", "tensor"),
            P(None, ("tensor", "dp")),
            P("tensor", "dp"),
            P("dp"),
            P("dp"),
            P("dp", "tensor"),
            P("dp", "tensor"),
            P("tensor", "dp"),
            P("dp"),
            P("dp"),
        ),
        check_vma=False,
    )
```

```python
import functools

import jax
import jax.numpy as jnp
import numpy as np
from jax import lax
from jax.experimental import pallas as pl
from jax.experimental.pallas import tpu as pltpu
from jax.sharding import PartitionSpec as P

MESH = pl.DeviceIdType.MESH
HEAD_DIM = 64
ROT = 16
BF = jnp.bfloat16
F32 = jnp.float32
VMEM_LIMIT = 56 * 1024 * 1024
ANY = pl.BlockSpec(memory_space=pl.ANY)
INV = pl.BlockSpec(memory_space=pltpu.VMEM)


def nt(a, b):
    return lax.dot_general(a, b, (((1,), (1,)), ((), ())), preferred_element_type=F32)


def tn(a, b):
    return lax.dot_general(a, b, (((0,), (0,)), ((), ())), preferred_element_type=F32)


def nn(a, b):
    return jnp.dot(a, b, preferred_element_type=F32)


def spans(total, step):
    return [(i, min(step, total - i)) for i in range(0, total, step)]


def place():
    d = lax.axis_index("dp")
    z = lax.axis_index("tensor")
    dy = 4 * (1 - 2 * lax.div(d, 4))
    dx = 2 * (1 - 2 * lax.rem(lax.div(d, 2), 2))
    dc = 1 - 2 * lax.rem(d, 2)
    return d, z, (0, dc, dx, dx + dc, dy, dy + dc, dy + dx, dy + dx + dc)


def send(src, dst, ssem, rsem, d, z):
    return pltpu.make_async_remote_copy(
        src_ref=src, dst_ref=dst, send_sem=ssem, recv_sem=rsem, device_id=(d, z), device_id_type=MESH
    )


def greet(d, z, flips, line, plane):
    barrier = pltpu.get_barrier_semaphore()
    for k in range(1, line):
        pl.semaphore_signal(
            barrier, inc=1, device_id=(d, lax.rem(z + k, line)), device_id_type=MESH
        )
    for r in plane:
        pl.semaphore_signal(barrier, inc=1, device_id=(d + flips[r], z), device_id_type=MESH)
    pl.semaphore_wait(barrier, line - 1 + len(plane))


class LineGather:
    def __init__(self, view, chunks, d, z, line, send_sems, recv_sems):
        self.view, self.chunks, self.d, self.z, self.line = view, chunks, d, z, line
        self.ss, self.rs = send_sems, recv_sems

    def copy(self, s, h, way, src=None):
        ref = self.view(s, h)
        return send(
            ref if src is None else src, ref, self.ss.at[way, s, h], self.rs.at[s, h],
            self.d, self.z + (1 if way == 0 else -1),
        )

    def start(self, h, src=None):
        pl.when(self.z < self.line - 1)(lambda: self.copy(self.z, h, 0, src).start())
        pl.when(self.z > 0)(lambda: self.copy(self.z, h, 1, src).start())

    def step(self, k, h, forward=True):
        z, line = self.z, self.line

        @pl.when(z - k >= 0)
        def _():
            self.copy(z - k, h, 0).wait_recv()
            if forward:
                pl.when(z < line - 1)(lambda: self.copy(z - k, h, 0).start())

        @pl.when(z + k < line)
        def _():
            self.copy(z + k, h, 1).wait_recv()
            if forward:
                pl.when(z > 0)(lambda: self.copy(z + k, h, 1).start())

    def finish(self, first=0, last=None):
        z, line = self.z, self.line
        for k in range(first, line if last is None else last):
            for h in range(self.chunks):
                pl.when((z - k >= 0) & (z < line - 1))(lambda: self.copy(z - k, h, 0).wait_send())
                pl.when((z + k < line) & (z > 0))(lambda: self.copy(z + k, h, 1).wait_send())


class PlaneGather:
    def __init__(self, src, view, d, z, flips, send_sems, recv_sems):
        self.src, self.view, self.d, self.z, self.flips = src, view, d, z, flips
        self.ss, self.rs = send_sems, recv_sems
        self.half = src.shape[0] // 2

    def copy(self, key):
        d, f = self.d, self.flips
        block, to, part = {
            1: (0, 1, None), 2: (0, 2, None), 4: (0, 4, None), 3: (2, 1, None), 5: (4, 1, None),
            6: (2, 4, 0), 7: (4, 2, 1), 8: (6, 1, 0), 9: (6, 1, 1),
        }[key]
        dst = self.view(d + f[block])
        src = self.src if block == 0 else dst
        if part is not None:
            at = pl.ds(part * self.half, self.half)
            src, dst = src.at[at], dst.at[at]
        return send(src, dst, self.ss.at[key], self.rs.at[key], d + f[to], self.z)

    def start(self):
        for key in (4, 2, 1):
            self.copy(key).start()

    def relay(self):
        for key, onward in ((2, (6, 3)), (4, (7, 5))):
            self.copy(key).wait_recv()
            for to in onward:
                self.copy(to).start()

    def pass_on(self):
        for key, onward in ((6, 8), (7, 9)):
            self.copy(key).wait_recv()
            self.copy(onward).start()

    def arrive(self):
        for key in (1, 3, 5, 8, 9):
            self.copy(key).wait_recv()

    def finish(self):
        for key in range(1, 10):
            self.copy(key).wait_send()


def arrival(z, i):
    orders = ((0, 1, 2, 3), (1, 0, 2, 3), (2, 3, 1, 0), (3, 2, 1, 0))
    codes = [sum(s * 4**j for j, s in enumerate(o)) for o in orders]
    code = jnp.where(
        z == 0, codes[0], jnp.where(z == 1, codes[1], jnp.where(z == 2, codes[2], codes[3]))
    )
    power = jnp.where(i == 0, 1, jnp.where(i == 1, 4, jnp.where(i == 2, 16, 64)))
    return lax.rem(lax.div(code, power), 4)


def turn(u, cos, sin, sign=1.0):
    low = lax.rem(lax.broadcasted_iota(jnp.int32, (1, 128), 1), HEAD_DIM) < ROT // 2
    moved = jnp.where(low, pltpu.roll(u, 128 - ROT // 2, 1), pltpu.roll(u, ROT // 2, 1)) * sin
    return u * cos + moved if sign > 0 else u * cos - moved


def attention_kernel(
    tok, cot, wq, ow, gw, uw, dw, smalls, cos, sin,
    cotnear, n1, qkv, lse_t, attall, wqkv, small_sum, wout, n2, hidden, wgate, wup, wdown,
    xbuf, n1buf, wbuf, qbuf, attv, wz, wo, acc, smbuf, lse,
    tss, trs, css, crs, ass, ars, mss, mrs, yss, yrs, pss, prs, local,
):
    rows, model = tok.shape
    width = wq.shape[2]
    pairs = width // 128
    line = 4
    d, z, flips = place()
    greet(d, z, flips, line, range(1, 8))

    tok_in = pltpu.make_async_copy(tok, xbuf.at[z], local.at[0])
    tok_in.start()
    depth = wq.shape[1]

    def wblock(i):
        return wbuf.at[pl.ds(pl.multiple_of(i * depth, 256), depth), :]

    w_in = [
        pltpu.make_async_copy(wq.at[j], wblock(d).at[:, pl.ds(j * width, width)], local.at[(2, 1, 13)[j]])
        for j in range(3)
    ]
    for copy in w_in:
        copy.start()
    tall = ow.shape[0]

    def oview(s, h):
        return wz.at[pl.ds(pl.multiple_of(s * tall, tall), tall)]

    def oblock(i):
        return wo.at[:, pl.ds(pl.multiple_of(i * depth, 256), depth)]

    o_in = pltpu.make_async_copy(ow, oview(z, 0), local.at[14])
    o_in.start()
    outs_z = LineGather(oview, 1, d, z, line, yss, yrs)
    small_copies = [
        send(smalls, smbuf.at[r], mss.at[r], mrs.at[r], d + flips[r], z) for r in range(1, 8)
    ]
    for copy in small_copies:
        copy.start()
    tall_block = dw.shape[1]

    def rows_of(ref, i):
        return ref.at[pl.ds(pl.multiple_of(i * depth, 256), depth)]

    def columns_of(ref, i):
        return ref.at[:, pl.ds(pl.multiple_of(i * tall_block, 256), tall_block)]

    planes = [
        PlaneGather(src, view, d, z, flips, pss.at[i], prs.at[i])
        for i, (src, view) in enumerate((
            (wblock(d), wblock),
            (wz, oblock),
            (gw, lambda i: rows_of(wgate, i)),
            (uw, lambda i: rows_of(wup, i)),
            (dw, lambda i: columns_of(wdown, i)),
        ))
    ]
    qkv_plane, out_plane, gate_plane, up_plane, down_plane = planes
    keep_own = [
        pltpu.make_async_copy(gw, rows_of(wgate, d), local.at[10]),
        pltpu.make_async_copy(uw, rows_of(wup, d), local.at[11]),
        pltpu.make_async_copy(dw, columns_of(wdown, d), local.at[12]),
    ]
    for copy in keep_own:
        copy.start()
    half = rows // 2

    def tview(s, h):
        return xbuf.at[s, pl.ds(h * half, half)]

    def cview(s, h):
        return cotnear.at[s, pl.ds(h * half, half)]

    def aview(s, h):
        return attv.at[:, pl.ds(pl.multiple_of(s * width + h * 128, 128), 128)]

    toks = LineGather(tview, 2, d, z, line, tss, trs)
    cots = LineGather(cview, 2, d, z, line, css, crs)
    atts = LineGather(aview, pairs, d, z, line, ass, ars)
    tok_in.wait()
    for h in range(2):
        toks.start(h)
    for copy in w_in:
        copy.wait()
    qkv_plane.start()
    o_in.wait()
    outs_z.start(0)
    for copy in small_copies:
        copy.wait()
    total = smalls[...].astype(F32)
    for r in range(1, 8):
        total = total + smbuf[r].astype(F32)
    small_sum[...] = total

    def normalise(s):
        piece = 32

        @pl.loop(0, rows // piece)
        def _(i):
            at = pl.ds(pl.multiple_of(i * piece, piece), piece)
            x = xbuf[s, at, :].astype(F32)
            centred = x - jnp.mean(x, -1, keepdims=True)
            spread = jnp.mean(centred * centred, -1, keepdims=True)
            n = centred * lax.rsqrt(spread + 1e-05) * small_sum[0:1, :] + small_sum[1:2, :]
            n1buf[pl.ds(pl.multiple_of(s * rows + i * piece, piece), piece), :] = n.astype(BF)

    def project(s):
        at = pl.ds(pl.multiple_of(s * rows, rows), rows)
        for j in range(3):
            cols = pl.ds(j * width, width)
            pre = nn(n1buf[at, :], wbuf[:, cols]) + small_sum[4:5, cols]
            for p in range(pairs):
                part = pre[:, p * 128 : (p + 1) * 128]
                if j < 2:
                    part = turn(part, cos[at, :], sin[at, :])
                qbuf[j, p, at, :] = part.astype(BF)

    normalise(z)
    for h in range(2):
        toks.step(1, h)
    outs_z.step(1, 0)
    qkv_plane.relay()
    gate_plane.start()
    normalise(arrival(z, 1))
    qkv_plane.pass_on()
    for h in range(2):
        toks.step(2, h)
    outs_z.step(2, 0)
    normalise(arrival(z, 2))
    gate_plane.relay()
    qkv_plane.arrive()

    @pl.loop(0, line)
    def _(i):
        s = arrival(z, i)

        @pl.when(i == line - 1)
        def _():
            gate_plane.pass_on()
            for h in range(2):
                toks.step(3, h)
            for h in range(2):
                cots.start(h, cot.at[pl.ds(h * half, half)])
            outs_z.step(3, 0)
            out_plane.start()
            normalise(s)

        project(s)

    o_own = pltpu.make_async_copy(wz, oblock(d), local.at[15])
    o_own.start()

    outs = [
        pltpu.make_async_copy(n1buf, n1, local.at[3]),
        pltpu.make_async_copy(wbuf, wqkv, local.at[4]),
        pltpu.make_async_copy(qbuf, qkv, local.at[5]),
    ]
    for copy in outs:
        copy.start()

    lanes = lax.broadcasted_iota(jnp.int32, (1, 128), 1)
    first = lanes < 64
    lse[...] = jnp.zeros_like(lse)
    length = rows * line

    def attend(p):
        for qi in range(line):
            count = (qi + 1) * rows
            at = pl.ds(qi * rows, rows)
            q = qbuf[0, p, at, :] * BF(HEAD_DIM**-0.5)
            k = qbuf[1, p, pl.ds(0, count), :]
            v = qbuf[2, p, pl.ds(0, count), :]
            row = lax.broadcasted_iota(jnp.int32, (rows, count), 0) + qi * rows
            col = lax.broadcasted_iota(jnp.int32, (rows, count), 1)
            keep = row >= col
            results = []
            stats = lse[at, :]
            for a in range(2):
                mine = first if a == 0 else ~first
                s = nt(jnp.where(mine, q, BF(0)), k)
                s = jnp.where(keep, s, -1e30)
                most = jnp.max(s, -1, keepdims=True)
                e = jnp.exp(s - most)
                total = jnp.sum(e, -1, keepdims=True)
                results.append(nn(e.astype(BF), v) / total)
                stats = jnp.where(lanes == 2 * p + a, most + jnp.log(total), stats)
            lse[at, :] = stats
            attv[at, pl.ds(pl.multiple_of(z * width + p * 128, 128), 128)] = jnp.where(
                first, results[0], results[1]
            ).astype(BF)

    @pl.loop(0, pairs)
    def _(p):
        attend(p)
        atts.start(p)

    lse_t[...] = lse[...].T
    up_plane.start()
    for p in range(pairs):
        atts.step(1, p)
    for h in range(2):
        cots.step(1, h, forward=False)
    out_plane.relay()
    down_plane.start()
    out_plane.pass_on()
    for p in range(pairs):
        atts.step(2, p)
    o_own.wait()
    out_plane.arrive()
    keep_wo = pltpu.make_async_copy(wo, wout, local.at[6])
    keep_wo.start()

    def project_out(s, at, lo, size):
        heads = pl.ds(pl.multiple_of(s * width, width), width)
        return nn(attv[at, heads], wo[heads, pl.ds(lo, size)])

    for i in range(line - 1):
        s = arrival(z, i)

        @pl.loop(0, line)
        def _(r):
            at = pl.ds(pl.multiple_of(r * rows, rows), rows)
            for lo, size in spans(model, 512):
                base = xbuf[r, :, pl.ds(lo, size)].astype(F32) if i == 0 else acc[at, pl.ds(lo, size)]
                acc[at, pl.ds(lo, size)] = base + project_out(s, at, lo, size)

        if i == 1:
            up_plane.relay()
    for copy in outs:
        copy.wait()
    down_plane.relay()
    up_plane.pass_on()
    for p in range(pairs):
        atts.step(3, p)
    inner = (z > 0) & (z < line - 1)

    @pl.when(inner)
    def _():
        cots.copy(z - 1, 0, 0).start()
        cots.copy(z + 1, 0, 1).start()

    keep_att = pltpu.make_async_copy(attv, attall, local.at[7])
    keep_att.start()
    last = arrival(z, line - 1)

    @pl.loop(0, line)
    def _(r):
        at = pl.ds(pl.multiple_of(r * rows, rows), rows)
        for lo, size in spans(model, 512):
            acc[at, pl.ds(lo, size)] += project_out(last, at, lo, size)

        @pl.loop(0, rows // 32)
        def _(i):
            piece = pl.ds(pl.multiple_of(r * rows + i * 32, 32), 32)
            x = acc[piece, :]
            centred = x - jnp.mean(x, -1, keepdims=True)
            spread = jnp.mean(centred * centred, -1, keepdims=True)
            n = centred * lax.rsqrt(spread + 1e-05) * small_sum[2:3, :] + small_sum[3:4, :]
            n1buf[piece, :] = n.astype(BF)

    keep = [
        pltpu.make_async_copy(n1buf, n2, local.at[8]),
        pltpu.make_async_copy(acc.at[pl.ds(pl.multiple_of(z * rows, rows), rows)], hidden, local.at[9]),
        keep_wo, keep_att,
    ]
    for copy in keep[:2]:
        copy.start()
    down_plane.pass_on()
    for gather in (toks, atts, outs_z):
        gather.finish()
    cots.finish(0, 1)

    @pl.when(inner)
    def _():
        cots.copy(z - 1, 0, 0).wait_send()
        cots.copy(z + 1, 0, 1).wait_send()

    pl.when(z >= 2)(lambda: cots.copy(z - 2, 0, 0).wait_recv())
    pl.when(z + 2 < line)(lambda: cots.copy(z + 2, 0, 1).wait_recv())
    for plane in (gate_plane, up_plane, down_plane):
        plane.arrive()
    for plane in planes:
        plane.finish()
    for copy in keep_own:
        copy.wait()
    for copy in keep:
        copy.wait()


def attention_forward(tok, cot, wq, ow, gw, uw, dw, smalls, tabs):
    rows, model = tok.shape
    line = 4
    length = rows * line
    _, depth, width = wq.shape
    pairs = width // 128
    dp = model // depth
    hidden = gw.shape[1]
    sds = jax.ShapeDtypeStruct
    return pl.pallas_call(
        attention_kernel,
        out_shape=(
            sds((line, rows, model), BF), sds((length, model), BF),
            sds((3, pairs, length, 128), BF), sds((128, length), F32), sds((length, model), BF),
            sds((model, 3 * width), BF), sds((16, model), F32),
            sds((model, model), BF), sds((length, model), BF), sds((rows, model), F32),
            sds((model, hidden), BF), sds((model, hidden), BF), sds((hidden, model), BF),
        ),
        in_specs=[ANY] * 7 + [INV] * 3,
        out_specs=(ANY, ANY, ANY, INV, ANY, ANY, INV) + (ANY,) * 6,
        scratch_shapes=[
            pltpu.VMEM((line, rows, model), BF),
            pltpu.VMEM((length, model), BF),
            pltpu.VMEM((model, 3 * width), BF),
            pltpu.VMEM((3, pairs, length, 128), BF),
            pltpu.VMEM((length, model), BF),
            pltpu.VMEM((model, depth), BF),
            pltpu.VMEM((model, model), BF),
            pltpu.VMEM((length, model), F32),
            pltpu.VMEM((dp, 16, model), BF),
            pltpu.VMEM((length, 128), F32),
            pltpu.SemaphoreType.DMA((2, line, 2)),
            pltpu.SemaphoreType.DMA((line, 2)),
            pltpu.SemaphoreType.DMA((2, line, 2)),
            pltpu.SemaphoreType.DMA((line, 2)),
            pltpu.SemaphoreType.DMA((2, line, pairs)),
            pltpu.SemaphoreType.DMA((line, pairs)),
            pltpu.SemaphoreType.DMA((8,)),
            pltpu.SemaphoreType.DMA((8,)),
            pltpu.SemaphoreType.DMA((2, line, 1)),
            pltpu.SemaphoreType.DMA((line, 1)),
            pltpu.SemaphoreType.DMA((5, 10)),
            pltpu.SemaphoreType.DMA((5, 10)),
            pltpu.SemaphoreType.DMA((16,)),
        ],
        compiler_params=pltpu.CompilerParams(
            collective_id=1, has_side_effects=True, vmem_limit_bytes=VMEM_LIMIT
        ),
        cost_estimate=pl.CostEstimate(flops=2 * 10**11, bytes_accessed=10**8, transcendentals=0),
        name="attention_forward",
    )(tok, cot, wq, ow, gw, uw, dw, smalls, *tabs)


def apply_layer_norm(value, norm_scale, norm_bias):
    centered_input = value - jnp.mean(value, -1, keepdims=True)
    spread = jnp.mean(centered_input * centered_input, -1, keepdims=True)
    inverse_deviation = lax.rsqrt(spread + 1e-05)
    standardized_input = centered_input * inverse_deviation
    return (
        standardized_input * norm_scale.astype(jnp.float32) + norm_bias.astype(jnp.float32),
        standardized_input,
        inverse_deviation,
    )


def layer_norm_backward(output_gradient, standardized_input, inverse_deviation, norm_scale):
    scaled_gradient = output_gradient * norm_scale.astype(jnp.float32)
    return inverse_deviation * (
        scaled_gradient
        - jnp.mean(scaled_gradient, -1, keepdims=True)
        - standardized_input * jnp.mean(scaled_gradient * standardized_input, -1, keepdims=True)
    )


def tables(length):
    positions = jnp.arange(length, dtype=jnp.float32)
    freqs = 10000.0 ** (-jnp.arange(0, ROT, 2, dtype=jnp.float32) / ROT)
    angles = positions[:, None] * freqs[None, :]
    angles = jnp.concatenate([angles, angles], -1)
    return (jnp.cos(angles), jnp.sin(angles))


def rotate(heads, cosine, sine):
    half = ROT // 2
    part = heads[..., :ROT]
    turned = jnp.concatenate([-part[..., half:], part[..., :half]], -1)
    moved = part * cosine[:, None, :] + turned * sine[:, None, :]
    return jnp.concatenate([moved, heads[..., ROT:]], -1)


def unrotate(output_gradient, cosine, sine):
    half = ROT // 2
    part = output_gradient[..., :ROT]
    scaled_gradient = part * sine[:, None, :]
    back = jnp.concatenate([scaled_gradient[..., half:], -scaled_gradient[..., :half]], -1)
    moved = part * cosine[:, None, :] + back
    return jnp.concatenate([moved, output_gradient[..., ROT:]], -1)


def attn_params(qkv_weight, qkv_bias, out_weight, norm1_gain, norm1_shift):
    return (
        lax.all_gather(qkv_weight, "dp", axis=1, tiled=True),
        lax.all_gather(qkv_bias, "dp", axis=1, tiled=True),
        lax.all_gather(out_weight, "dp", axis=1, tiled=True),
        lax.all_gather(norm1_gain, "dp", axis=0, tiled=True),
        lax.all_gather(norm1_shift, "dp", axis=0, tiled=True),
    )


def mlp_params(gate_weight, up_weight, down_weight, norm2_gain, norm2_shift):
    return (
        lax.all_gather(gate_weight, "dp", axis=0, tiled=True),
        lax.all_gather(up_weight, "dp", axis=0, tiled=True),
        lax.all_gather(down_weight, "dp", axis=1, tiled=True),
        lax.all_gather(norm2_gain, "dp", axis=0, tiled=True),
        lax.all_gather(norm2_shift, "dp", axis=0, tiled=True),
    )


def gather_rows(rows):
    return lax.all_gather(rows, "tensor", axis=0, tiled=True)


def sum_rows(partial_value):
    return lax.psum_scatter(
        partial_value.astype(jnp.bfloat16), "tensor", scatter_dimension=0, tiled=True
    ).astype(jnp.float32)


def gather_grads(rows):
    return lax.all_gather(rows, "tensor", axis=0, tiled=True)


def sum_grads(partial_value):
    return lax.psum_scatter(
        partial_value.astype(jnp.bfloat16), "tensor", scatter_dimension=0, tiled=True
    ).astype(jnp.float32)


def local(
    tokens,
    qkv_weight,
    qkv_bias,
    out_weight,
    norm1_gain,
    norm1_shift,
    gate_weight,
    up_weight,
    down_weight,
    norm2_gain,
    norm2_shift,
    cotangent,
):
    scale = HEAD_DIM ** (-0.5)
    input_rows = tokens.astype(jnp.float32)
    wqkv, bqkv, wout, first_norm_scale, first_norm_bias = attn_params(
        qkv_weight, qkv_bias, out_weight, norm1_gain, norm1_shift
    )
    first_normed_rows, first_standardized, first_inverse_deviation = apply_layer_norm(
        input_rows, first_norm_scale, first_norm_bias
    )
    rows1 = gather_rows(first_normed_rows.astype(jnp.bfloat16))
    length = rows1.shape[0]
    width = wqkv.shape[2]
    local_heads = width // HEAD_DIM
    pre = (
        jnp.einsum("sd,jdc->jsc", rows1, wqkv, preferred_element_type=jnp.float32)
        + bqkv.astype(jnp.float32)[:, None, :]
    )
    cosine, sine = tables(length)
    query = rotate(pre[0].reshape(length, local_heads, HEAD_DIM), cosine, sine).astype(jnp.bfloat16)
    keys = rotate(pre[1].reshape(length, local_heads, HEAD_DIM), cosine, sine).astype(jnp.bfloat16)
    values = pre[2].reshape(length, local_heads, HEAD_DIM).astype(jnp.bfloat16)
    block = min(length, 512)
    count = length // block
    cols = jnp.arange(length, dtype=jnp.int32)

    def block_probs(qblock, start):
        scores = (
            jnp.einsum("qhd,khd->hqk", qblock, keys, preferred_element_type=jnp.float32) * scale
        )
        rows = start + jnp.arange(block, dtype=jnp.int32)
        keep = rows[:, None] >= cols[None, :]
        return jnp.where(keep[None], scores, -1e30)

    def forward_block(index):
        qblock = lax.dynamic_slice_in_dim(query, index * block, block, 0)
        scores = block_probs(qblock, index * block)
        most = jnp.max(scores, -1, keepdims=True)
        expo = jnp.exp(scores - most)
        total = jnp.sum(expo, -1, keepdims=True)
        probs = (expo / total).astype(jnp.bfloat16)
        out_block = jnp.einsum("hqk,khd->qhd", probs, values, preferred_element_type=jnp.float32)
        return (out_block.astype(jnp.bfloat16), most[..., 0] + jnp.log(total[..., 0]))

    indices = jnp.arange(count, dtype=jnp.int32)
    out_blocks, lse = lax.map(forward_block, indices)
    attended = out_blocks.reshape(length, width)
    branch = jnp.dot(attended, wout, preferred_element_type=jnp.float32)
    hidden_state = input_rows + sum_rows(branch)
    wgate, wup, wdown, second_norm_scale, second_norm_bias = mlp_params(
        gate_weight, up_weight, down_weight, norm2_gain, norm2_shift
    )
    second_normed_rows, second_standardized, second_inverse_deviation = apply_layer_norm(
        hidden_state, second_norm_scale, second_norm_bias
    )
    rows2 = gather_rows(second_normed_rows.astype(jnp.bfloat16))
    gate = jnp.dot(rows2, wgate, preferred_element_type=jnp.float32)
    up = jnp.dot(rows2, wup, preferred_element_type=jnp.float32)
    sigma = jax.nn.sigmoid(gate)
    silu = gate * sigma
    act = (silu * up).astype(jnp.bfloat16)
    mixed = sum_rows(jnp.dot(act, wdown, preferred_element_type=jnp.float32))
    layer_output = (hidden_state + mixed).astype(jnp.bfloat16)
    wgate, wup, wdown, second_norm_scale, second_norm_bias = mlp_params(
        gate_weight, up_weight, down_weight, norm2_gain, norm2_shift
    )
    incoming_gradient = cotangent.astype(jnp.float32)
    down_rows = gather_grads(cotangent)
    down_grad = jnp.einsum("sf,sd->fd", act, down_rows, preferred_element_type=jnp.float32)
    dact = jnp.einsum("sd,fd->sf", down_rows, wdown, preferred_element_type=jnp.float32)
    dgate = (dact * up * (sigma * (1.0 + gate * (1.0 - sigma)))).astype(jnp.bfloat16)
    dup = (dact * silu).astype(jnp.bfloat16)
    gate_grad = jnp.einsum("sd,sf->df", rows2, dgate, preferred_element_type=jnp.float32)
    up_grad = jnp.einsum("sd,sf->df", rows2, dup, preferred_element_type=jnp.float32)
    second_norm_gradient = jnp.einsum(
        "sf,df->sd", dgate, wgate, preferred_element_type=jnp.float32
    ) + jnp.einsum("sf,df->sd", dup, wup, preferred_element_type=jnp.float32)
    second_norm_gradient = sum_grads(second_norm_gradient)
    second_scale_partial = jnp.sum(second_norm_gradient * second_standardized, 0)
    shift2_part = jnp.sum(second_norm_gradient, 0)
    hidden_gradient = incoming_gradient + layer_norm_backward(
        second_norm_gradient, second_standardized, second_inverse_deviation, second_norm_scale
    )
    gatew_grad, upw_grad, downw_grad, gain2_total, shift2_total = (
        lax.psum_scatter(
            gate_grad.astype(jnp.bfloat16), "dp", scatter_dimension=0, tiled=True
        ).astype(jnp.float32),
        lax.psum_scatter(
            up_grad.astype(jnp.bfloat16), "dp", scatter_dimension=0, tiled=True
        ).astype(jnp.float32),
        lax.psum_scatter(
            down_grad.astype(jnp.bfloat16), "dp", scatter_dimension=1, tiled=True
        ).astype(jnp.float32),
        lax.psum_scatter(
            second_scale_partial.astype(jnp.bfloat16), "dp", scatter_dimension=0, tiled=True
        ).astype(jnp.float32),
        lax.psum_scatter(
            shift2_part.astype(jnp.bfloat16), "dp", scatter_dimension=0, tiled=True
        ).astype(jnp.float32),
    )
    wqkv, bqkv, wout, first_norm_scale, first_norm_bias = attn_params(
        qkv_weight, qkv_bias, out_weight, norm1_gain, norm1_shift
    )
    branch_rows = gather_grads(hidden_gradient.astype(jnp.bfloat16))
    out_grad = jnp.einsum("sc,sd->cd", attended, branch_rows, preferred_element_type=jnp.float32)
    dattended = jnp.einsum(
        "sd,cd->sc", branch_rows, wout, preferred_element_type=jnp.float32
    ).astype(jnp.bfloat16)
    dattended = dattended.reshape(length, local_heads, HEAD_DIM)

    def backward_block(carry, item):
        dkeys, dvalues = carry
        index, block_lse = item
        qblock = lax.dynamic_slice_in_dim(query, index * block, block, 0)
        dblock = lax.dynamic_slice_in_dim(dattended, index * block, block, 0)
        scores = block_probs(qblock, index * block)
        probs = jnp.exp(scores - block_lse[..., None])
        probs16 = probs.astype(jnp.bfloat16)
        dvalues = dvalues + jnp.einsum(
            "hqk,qhd->khd", probs16, dblock, preferred_element_type=jnp.float32
        )
        dprobs = jnp.einsum("qhd,khd->hqk", dblock, values, preferred_element_type=jnp.float32)
        inner = jnp.sum(dprobs * probs, -1, keepdims=True)
        dscores = (probs * (dprobs - inner)).astype(jnp.bfloat16)
        dquery = (
            jnp.einsum("hqk,khd->qhd", dscores, keys, preferred_element_type=jnp.float32) * scale
        )
        dkeys = (
            dkeys
            + jnp.einsum("hqk,qhd->khd", dscores, qblock, preferred_element_type=jnp.float32)
            * scale
        )
        return ((dkeys, dvalues), dquery)

    empty = jnp.zeros((length, local_heads, HEAD_DIM), jnp.float32)
    (dkeys, dvalues), dquery = lax.scan(backward_block, (empty, empty), (indices, lse))
    dquery = dquery.reshape(length, local_heads, HEAD_DIM)
    dpre = jnp.stack(
        [
            unrotate(dquery, cosine, sine).reshape(length, width),
            unrotate(dkeys, cosine, sine).reshape(length, width),
            dvalues.reshape(length, width),
        ],
        0,
    ).astype(jnp.bfloat16)
    qkv_grad = jnp.einsum("sd,jsc->jdc", rows1, dpre, preferred_element_type=jnp.float32)
    bias_grad = jnp.sum(dpre, axis=1, dtype=jnp.float32)
    first_norm_gradient = sum_grads(
        jnp.einsum("jsc,jdc->sd", dpre, wqkv, preferred_element_type=jnp.float32)
    )
    first_scale_partial = jnp.sum(first_norm_gradient * first_standardized, 0)
    shift1_part = jnp.sum(first_norm_gradient, 0)
    token_gradient = (
        hidden_gradient
        + layer_norm_backward(
            first_norm_gradient, first_standardized, first_inverse_deviation, first_norm_scale
        )
    ).astype(jnp.bfloat16)
    qkvw_grad, qkvb_grad, outw_grad, gain1_total, shift1_total = (
        lax.psum_scatter(
            qkv_grad.astype(jnp.bfloat16), "dp", scatter_dimension=1, tiled=True
        ).astype(jnp.float32),
        lax.psum_scatter(
            bias_grad.astype(jnp.bfloat16), "dp", scatter_dimension=1, tiled=True
        ).astype(jnp.float32),
        lax.psum_scatter(
            out_grad.astype(jnp.bfloat16), "dp", scatter_dimension=1, tiled=True
        ).astype(jnp.float32),
        lax.psum_scatter(
            first_scale_partial.astype(jnp.bfloat16), "dp", scatter_dimension=0, tiled=True
        ).astype(jnp.float32),
        lax.psum_scatter(
            shift1_part.astype(jnp.bfloat16), "dp", scatter_dimension=0, tiled=True
        ).astype(jnp.float32),
    )
    gain1_grad, shift1_grad, gain2_grad, shift2_grad = lax.psum(
        (gain1_total, shift1_total, gain2_total, shift2_total), "tensor"
    )
    return (
        layer_output,
        token_gradient,
        qkvw_grad,
        qkvb_grad,
        outw_grad,
        gain1_grad,
        shift1_grad,
        gatew_grad,
        upw_grad,
        downw_grad,
        gain2_grad,
        shift2_grad,
    )


class LineScatter:
    def __init__(self, part, slot, chunks, d, z, line, send_sems, recv_sems):
        self.part, self.slot, self.chunks, self.d, self.z, self.line = part, slot, chunks, d, z, line
        self.ss, self.rs = send_sems, recv_sems

    def copy(self, s, h, way, target, place):
        return send(
            self.part(s, h), self.slot(place, h), self.ss.at[s, h], self.rs.at[place, h], self.d, target
        )

    def right(self, s, h):
        return self.copy(s, h, 0, self.z + 1, s)

    def left(self, s, h):
        return self.copy(s, h, 1, self.z - 1, jnp.where(self.z - 1 == s, self.line, s))

    def head(self, s):
        z, line = self.z, self.line
        for h in range(self.chunks):
            pl.when((z == 0) & (s > 0))(lambda: self.right(s, h).start())
            pl.when((z == line - 1) & (s < z))(lambda: self.left(s, h).start())

    def add(self, s, h):
        part = self.part(s, h)
        part[...] = (part[...].astype(F32) + self.slot(s, h)[...].astype(F32)).astype(BF)

    def relay(self, t):
        z, line = self.z, self.line
        up = line - 1 - t + z
        down = t - (line - 1 - z)
        for h in range(self.chunks):
            @pl.when((z > 0) & (up > z) & (up < line))
            def _():
                self.copy(z, h, 0, z, up).wait_recv()
                self.add(up, h)
                self.right(up, h).start()

            @pl.when((z < line - 1) & (down >= 0) & (down < z))
            def _():
                self.copy(z, h, 0, z, down).wait_recv()
                self.add(down, h)
                self.left(down, h).start()

    def arrive(self, h):
        z, line = self.z, self.line
        pl.when(z > 0)(lambda: self.copy(z, h, 0, z, z).wait_recv())
        pl.when(z < line - 1)(lambda: self.copy(z, h, 0, z, line).wait_recv())

    def total(self, h, rows):
        z = self.z
        return (
            self.part(z, h)[rows].astype(F32)
            + self.slot(z, h)[rows].astype(F32)
            + self.slot(self.line, h)[rows].astype(F32)
        )

    def finish(self):
        z = self.z
        for s in range(self.line):
            for h in range(self.chunks):
                pl.when(z != s)(lambda: self.copy(s, h, 0, z, s).wait_send())


def far_first(z, i):
    orders = ((3, 2, 1, 0), (3, 0, 2, 1), (0, 3, 1, 2), (0, 1, 2, 3))
    codes = [sum(s * 4**j for j, s in enumerate(o)) for o in orders]
    code = jnp.where(
        z == 0, codes[0], jnp.where(z == 1, codes[1], jnp.where(z == 2, codes[2], codes[3]))
    )
    power = jnp.where(i == 0, 1, jnp.where(i == 1, 4, jnp.where(i == 2, 16, 64)))
    return lax.rem(lax.div(code, power), 4)


class PlaneSum:
    def __init__(self, half, recv, d, z, flips, send_sems, recv_sems):
        self.half, self.recv, self.d, self.z, self.flips = half, recv, d, z, flips
        self.ss, self.rs = send_sems, recv_sems

    def copy(self, r):
        to, slot = self.d + self.flips[r], (r // 2 - 1) % self.recv.shape[0]
        return send(self.half.at[lax.div(to, 2)], self.recv.at[slot], self.ss.at[slot], self.rs.at[slot], to, self.z)

    def start(self, *which):
        for r in which:
            self.copy(r).start()

    def wait(self, *which):
        for r in which:
            self.copy(r).wait()


def mlp_kernel(
    n2, cot, cotnear, wgate, wup, wdown,
    dn2, mixed, mland, gex, uex, dex, ghalf, uhalf, dhalf, grecv, unear,
    nbuf, cbuf, gw, uw, dw, act, act_t, dga, dup, part, slots, mixbuf, wide, tall, wide_in, tall_in,
    ss, rs, css, crs, lss, lrs, local, lsem, mixsem, outsem, exs, exr, gss, grs, uss, urs,
):
    line = 4
    rows = n2.shape[0] // line
    model = n2.shape[1]
    hidden = wgate.shape[1]
    d, z, flips = place()
    greet(d, z, flips, line, (1, 2, 4, 6))
    core = lax.rem(d, 2)
    chip = lax.div(d, 2)
    parts = spans(hidden, 512)

    def rows_in(i):
        at = pl.ds(pl.multiple_of(far_first(z, i) * rows, rows), rows)
        return pltpu.make_async_copy(n2.at[at], nbuf.at[at], lsem.at[i])

    def columns_in(c):
        cols = pl.ds(*parts[c])
        return [
            pltpu.make_async_copy(wgate.at[:, cols], gw.at[:, cols], lsem.at[line + c]),
            pltpu.make_async_copy(wup.at[:, cols], uw.at[:, cols], lsem.at[line + len(parts) + c]),
        ]

    down_in = pltpu.make_async_copy(wdown, dw, lsem.at[line + 2 * len(parts)])
    first = [rows_in(jnp.int32(0))] + columns_in(0)
    for copy in first:
        copy.start()
    half = rows // 2
    scatter = LineScatter(
        lambda s, h: part.at[s, pl.ds(h * half, half)],
        lambda i, h: slots.at[i, pl.ds(h * half, half)],
        2, d, z, line, ss, rs,
    )
    pl.when(z == 0)(lambda: slots.__setitem__((0,), jnp.zeros((rows, model), BF)))
    pl.when(z == line - 1)(lambda: slots.__setitem__((line,), jnp.zeros((rows, model), BF)))
    cots = LineGather(
        lambda s, h: cbuf.at[pl.ds(pl.multiple_of(s * rows + h * half, half), half)], 2, d, z, line, css, crs
    )

    def near(s, k):
        return pltpu.make_async_copy(
            cot if k == 0 else cotnear.at[s], cbuf.at[pl.ds(pl.multiple_of(s * rows, rows), rows)], local.at[5 + k]
        )

    for h in (1, 0):
        @pl.when((z > 0) & (z < line - 1))
        def _():
            if h == 1:
                cots.copy(z - 1, h, 0, cotnear.at[z - 1, pl.ds(h * half, half)]).start()
                cots.copy(z + 1, h, 1, cotnear.at[z + 1, pl.ds(h * half, half)]).start()
            else:
                pl.when(z == 2)(lambda: cots.copy(z - 2, h, 0, cotnear.at[z - 2, pl.ds(0, half)]).start())
                pl.when(z == 1)(lambda: cots.copy(z + 2, h, 1, cotnear.at[z + 2, pl.ds(0, half)]).start())
    def first_half(s, k):
        return pltpu.make_async_copy(
            cotnear.at[s, pl.ds(0, half)], cbuf.at[pl.ds(pl.multiple_of(s * rows, rows), half)], local.at[8 + k]
        )

    pl.when(z >= 2)(lambda: first_half(z - 2, 0).start())
    pl.when(z + 2 < line)(lambda: first_half(z + 2, 1).start())
    for copy in first:
        copy.wait()
    for c in range(1, len(parts)):
        for copy in columns_in(c):
            copy.start()
    down_in.start()
    for i in range(1, line):
        rows_in(jnp.int32(i)).start()
    near(z, 0).start()
    pl.when(z > 0)(lambda: near(z - 1, 1).start())
    pl.when(z < line - 1)(lambda: near(z + 1, 2).start())

    def mixed_out(i):
        s = far_first(z, i)
        at = pl.ds(pl.multiple_of(s * rows, rows), rows)
        return pltpu.make_async_copy(mixbuf.at[lax.rem(i, 2)], mixed.at[at], mixsem.at[lax.rem(i, 2)])

    def mixed_ahead(i):
        at = pl.ds(pl.multiple_of(far_first(z, i) * rows, rows), rows)
        to = jnp.where(z == 0, 1, line - 2)
        return send(mixed.at[at], mland.at[i], lss.at[i], lrs.at[i], d, to)

    at_end = (z == 0) | (z == line - 1)

    @pl.loop(0, line)
    def _(i):
        s = far_first(z, i)
        at = pl.ds(pl.multiple_of(s * rows, rows), rows)
        pl.when(i > 0)(lambda: rows_in(i).wait())
        for c, (lo, size) in enumerate(parts):
            cols = pl.ds(lo, size)
            if c > 0:
                @pl.when(i == 0)
                def _():
                    for copy in columns_in(c):
                        copy.wait()

            gate = nn(nbuf[at, :], gw[:, cols])
            up = nn(nbuf[at, :], uw[:, cols])
            sigma = lax.logistic(gate)
            silu = gate * sigma
            value = (silu * up).astype(BF)
            act[:, cols] = value
            act_t[cols, at] = value.T
            dga[at, cols] = (up * (sigma * (1.0 + gate * (1.0 - sigma)))).astype(BF)
            dup[at, cols] = silu.astype(BF)
        pl.when(i == 0)(lambda: down_in.wait())
        for lo, size in spans(model, 512):
            mixbuf[lax.rem(i, 2), :, pl.ds(lo, size)] = nn(act[...], dw[:, pl.ds(lo, size)]).astype(BF)
        mixed_out(i).start()
        mixed_out(i).wait()
        pl.when(at_end & (i < 2))(lambda: mixed_ahead(i).start())
        pl.when(i == 1)(lambda: cots.step(2, 1))

    def add_mixed(s, slot, send_slot, to, lands):
        at = pl.ds(pl.multiple_of(s * rows, rows), rows)
        ins = [
            pltpu.make_async_copy(mixed.at[at], mixbuf.at[0], mixsem.at[0]),
            pltpu.make_async_copy(mland.at[slot], mixbuf.at[1], mixsem.at[1]),
        ]
        for copy in ins:
            copy.start()
        for copy in ins:
            copy.wait()

        @pl.loop(0, rows // 32)
        def _(i):
            piece = pl.ds(pl.multiple_of(i * 32, 32), 32)
            mixbuf[0, piece, :] = (mixbuf[0, piece, :].astype(F32) + mixbuf[1, piece, :].astype(F32)).astype(BF)

        back = pltpu.make_async_copy(mixbuf.at[0], mixed.at[at], mixsem.at[0])
        back.start()
        back.wait()
        send(mixed.at[at], mland.at[lands], lss.at[send_slot], lrs.at[lands], d, to).start()

    def landing(slot, send_slot):
        return send(mland.at[slot], mland.at[slot], lss.at[send_slot], lrs.at[slot], d, z)

    other = line - 1 - z
    edge = jnp.where(z == 1, 0, line - 1)

    def mixed_on(i):
        @pl.when(~at_end)
        def _():
            landing(i, i).wait_recv()
            add_mixed(line - 1 - edge if i == 0 else other, i, 2 + i, other, 2 + i)

    def mixed_relay():
        @pl.when(~at_end)
        def _():
            landing(2, 2).wait_recv()
            add_mixed(edge, 2, 0, edge, 3)

    mixed_on(0)
    near(z, 0).wait()
    pl.when(z >= 2)(lambda: first_half(z - 2, 0).wait())
    pl.when(z + 2 < line)(lambda: first_half(z + 2, 1).wait())
    pl.when(z > 0)(lambda: near(z - 1, 1).wait())
    pl.when(z < line - 1)(lambda: near(z + 1, 2).wait())
    for h in range(2):
        cots.step(3, h)

    @pl.loop(0, line)
    def _(i):
        s = far_first(z, i)
        at = pl.ds(pl.multiple_of(s * rows, rows), rows)
        for lo, size in spans(hidden, 512):
            cols = pl.ds(lo, size)
            dact = nt(cbuf[at, :], dw[cols, :])
            dga[at, cols] = (dact * dga[at, cols].astype(F32)).astype(BF)
            dup[at, cols] = (dact * dup[at, cols].astype(F32)).astype(BF)
        for lo, size in spans(model, 512):
            cols = pl.ds(lo, size)
            part[s, :, cols] = (nt(dga[at, :], gw[cols, :]) + nt(dup[at, :], uw[cols, :])).astype(BF)
        scatter.head(s)

    blocks = model // rows // 2

    def exchanged(m):
        outs = (ghalf, uhalf, dhalf)
        exes = (gex, uex, dex)
        stage = tall if m == 2 else wide
        stage_in = tall_in if m == 2 else wide_in

        def block(t):
            cols = pl.ds(pl.multiple_of(t * rows, rows), rows)
            if m == 2:
                return lambda lo, size: nn(act_t[pl.ds(lo, size), :], cbuf[:, cols])
            right = dga if m == 0 else dup
            return lambda lo, size: tn(nbuf[:, cols], right[:, pl.ds(lo, size)])

        def piece(ref, lo, size):
            return ref.at[pl.ds(lo, size), :] if m == 2 else ref.at[:, pl.ds(lo, size)]

        def away(k):
            slot = lax.rem(k, 2)
            return send(stage.at[slot], exes[m].at[k], exs.at[m, k], exr.at[m, k], d + flips[1], z)

        @pl.loop(0, blocks)
        def _(k):
            slot = lax.rem(k, 2)
            pl.when(k >= 2)(lambda: away(k - 2).wait_send())
            make = block(2 * k + 1 - core)
            for lo, size in spans(hidden, 512):
                piece(stage.at[slot], lo, size)[...] = make(lo, size).astype(BF)
            away(k).start()

        away(blocks - 2).wait_send()
        away(blocks - 1).wait_send()

        def chip_at(j):
            return lax.rem(chip + 1 + j, blocks)

        def store(j):
            slot = lax.rem(j, 2)
            return pltpu.make_async_copy(stage.at[slot], outs[m].at[chip_at(j)], outsem.at[slot])

        def onward(j):
            k = chip_at(j)
            return send(ghalf.at[k], grecv.at[blocks - 2 - j], gss.at[j], grs.at[blocks - 2 - j], 2 * k + core, z)

        @pl.loop(0, blocks)
        def _(j):
            slot = lax.rem(j, 2)
            k = chip_at(j)

            @pl.when(j >= 2)
            def _():
                store(j - 2).wait()
                if m == 0:
                    onward(j - 2).start()

            away(k).wait_recv()
            fetch = pltpu.make_async_copy(exes[m].at[k], stage_in, local.at[4])
            fetch.start()
            fetch.wait()
            make = block(2 * k + core)
            for lo, size in spans(hidden, 512):
                piece(stage.at[slot], lo, size)[...] = (
                    make(lo, size) + piece(stage_in, lo, size)[...].astype(F32)
                ).astype(BF)
            store(j).start()

        for j in (blocks - 2, blocks - 1):
            store(j).wait()
            if m == 0 and j < blocks - 1:
                onward(j).start()
        return onward

    mixed_on(1)
    onward = exchanged(0)
    scatter.relay(1)
    mixed_relay()

    exchanged(1)
    ups = PlaneSum(uhalf, unear, d, z, flips, uss, urs)
    ups.start(2, 4)
    scatter.relay(2)
    exchanged(2)
    for h in range(2):
        scatter.arrive(h)

        @pl.loop(0, half // 32)
        def _(i):
            rows_at = pl.ds(pl.multiple_of(i * 32, 32), 32)
            dn2[pl.ds(pl.multiple_of(h * half + i * 32, 32), 32), :] = scatter.total(h, rows_at)

    scatter.finish()
    for i in range(2):
        pl.when(at_end)(lambda: mixed_ahead(i).wait_send())
    for i in (0, 2, 3):
        pl.when(~at_end)(lambda: landing(3, i).wait_send())
    landing(3, 3).wait_recv()
    for k, h in ((1, 1), (2, 0), (2, 1)):
        pl.when((z - k >= 0) & (z < line - 1))(lambda: cots.copy(z - k, h, 0).wait_send())
        pl.when((z + k < line) & (z > 0))(lambda: cots.copy(z + k, h, 1).wait_send())
    for j in range(blocks - 1):
        onward(j).wait()
    ups.wait(2, 4)


def mlp(n2, cot, cotnear, wgate, wup, wdown):
    length, model = n2.shape
    hidden = wgate.shape[1]
    line = 4
    rows = length // line
    blocks = model // rows // 2
    sds = jax.ShapeDtypeStruct
    wide = sds((blocks, rows, hidden), BF)
    tall = sds((blocks, hidden, rows), BF)
    return pl.pallas_call(
        mlp_kernel,
        out_shape=(
            sds((rows, model), F32), sds((length, model), BF), sds((4, rows, model), BF),
            wide, wide, tall, wide, wide, tall, sds((blocks - 1, rows, hidden), BF), sds((2, rows, hidden), BF),
        ),
        in_specs=[ANY] * 6,
        out_specs=(INV,) + (ANY,) * 10,
        scratch_shapes=[
            pltpu.VMEM((length, model), BF),
            pltpu.VMEM((length, model), BF),
            pltpu.VMEM((model, hidden), BF),
            pltpu.VMEM((model, hidden), BF),
            pltpu.VMEM((hidden, model), BF),
            pltpu.VMEM((rows, hidden), BF),
            pltpu.VMEM((hidden, length), BF),
            pltpu.VMEM((length, hidden), BF),
            pltpu.VMEM((length, hidden), BF),
            pltpu.VMEM((line, rows, model), BF),
            pltpu.VMEM((line + 1, rows, model), BF),
            pltpu.VMEM((2, rows, model), BF),
            pltpu.VMEM((2, rows, hidden), BF),
            pltpu.VMEM((2, hidden, rows), BF),
            pltpu.VMEM((rows, hidden), BF),
            pltpu.VMEM((hidden, rows), BF),
            pltpu.SemaphoreType.DMA((line, 2)),
            pltpu.SemaphoreType.DMA((line + 1, 2)),
            pltpu.SemaphoreType.DMA((2, line, 2)),
            pltpu.SemaphoreType.DMA((line, 2)),
            pltpu.SemaphoreType.DMA((4,)),
            pltpu.SemaphoreType.DMA((4,)),
            pltpu.SemaphoreType.DMA((10,)),
            pltpu.SemaphoreType.DMA((line + 1 + 2 * len(spans(hidden, 512)),)),
            pltpu.SemaphoreType.DMA((2,)),
            pltpu.SemaphoreType.DMA((2,)),
            pltpu.SemaphoreType.DMA((3, blocks)),
            pltpu.SemaphoreType.DMA((3, blocks)),
            pltpu.SemaphoreType.DMA((blocks,)),
            pltpu.SemaphoreType.DMA((blocks,)),
            pltpu.SemaphoreType.DMA((2,)),
            pltpu.SemaphoreType.DMA((2,)),
        ],
        compiler_params=pltpu.CompilerParams(
            collective_id=2, has_side_effects=True, vmem_limit_bytes=62 * 1024 * 1024
        ),
        cost_estimate=pl.CostEstimate(flops=10**11, bytes_accessed=10**8, transcendentals=0),
        name="mlp",
    )(n2, cot, cotnear, wgate, wup, wdown)


def norm_parts(x):
    centred = x - jnp.mean(x, -1, keepdims=True)
    inverse = lax.rsqrt(jnp.mean(centred * centred, -1, keepdims=True) + 1e-05)
    return centred * inverse, inverse


def norm_back(grad, standard, inverse, gain):
    scaled = grad * gain
    return inverse * (
        scaled
        - jnp.mean(scaled, -1, keepdims=True)
        - standard * jnp.mean(scaled * standard, -1, keepdims=True)
    )


def each_piece(rows, piece, body):
    @pl.loop(0, rows // piece)
    def _(i):
        body(pl.ds(pl.multiple_of(i * piece, piece), piece))


class PlaneChain:
    def __init__(self, half, recv, mid, d, z, flips, send_sems, recv_sems):
        self.half, self.recv, self.mid, self.d, self.z, self.flips = half, recv, mid, d, z, flips
        self.ss, self.rs = send_sems, recv_sems
        self.rows = half.shape[1] // 2

    def block(self, r):
        return lax.div(self.d + self.flips[r], 2)

    def copy(self, key):
        block, over, part = ((6, 2, 0), (6, 4, 1), (4, 4, 1), (2, 2, 0), (4, 4, 0), (2, 2, 1))[key]
        at = pl.ds(part * self.rows, self.rows)
        dst = self.mid.at[key] if key < 2 else self.recv.at[0 if over == 2 else 1, at]
        return send(
            self.half.at[self.block(block), at], dst, self.ss.at[key], self.rs.at[key], self.d + self.flips[over], self.z
        )

    def start(self):
        for key in range(4):
            self.copy(key).start()

    def relay(self):
        for key, block, part in ((0, 4, 0), (1, 2, 1)):
            self.copy(key).wait_recv()
            k = self.block(block)
            piece = min(self.rows, 128)

            @pl.loop(0, self.rows // piece)
            def _(i):
                at = pl.ds(pl.multiple_of(part * self.rows + i * piece, piece), piece)
                mid = self.mid[key, pl.ds(pl.multiple_of(i * piece, piece), piece), :]
                self.half[k, at, :] = (self.half[k, at, :].astype(F32) + mid.astype(F32)).astype(BF)

            self.copy(key + 4).start()

    def arrive(self):
        for key in range(2, 6):
            self.copy(key).wait_recv()

    def total(self, at):
        return (
            self.half[(self.block(0),) + at].astype(F32)
            + self.recv[(0,) + at].astype(F32)
            + self.recv[(1,) + at].astype(F32)
        )

    def finish(self):
        for key in range(6):
            self.copy(key).wait_send()


class BlockSum:
    def __init__(self, own, recv, bufs, stage, out, in_sems, out_sems):
        self.ins = [own] + recv
        self.bufs, self.stage, self.out, self.in_sems, self.out_sems = bufs, stage, out, in_sems, out_sems

    def copies(self):
        return [pltpu.make_async_copy(a, b, self.in_sems.at[i]) for i, (a, b) in enumerate(zip(self.ins, self.bufs))]

    def fetch(self):
        for copy in self.copies():
            copy.start()

    def store(self, i):
        rows = self.stage.shape[1]
        at = pl.ds(pl.multiple_of(i * rows, rows), rows)
        return pltpu.make_async_copy(self.stage.at[lax.rem(i, 2)], self.out.at[at], self.out_sems.at[lax.rem(i, 2)])

    def add(self):
        for copy in self.copies():
            copy.wait()
        rows = self.stage.shape[1]
        pieces = self.out.shape[0] // rows
        small = 32

        @pl.loop(0, pieces)
        def _(i):
            pl.when(i >= 2)(lambda: self.store(i - 2).wait())

            @pl.loop(0, rows // small)
            def _(j):
                at = pl.ds(pl.multiple_of(i * rows + j * small, small), small)
                total = self.bufs[0][at, :].astype(F32)
                for buf in self.bufs[1:]:
                    total = total + buf[at, :].astype(F32)
                self.stage[lax.rem(i, 2), pl.ds(pl.multiple_of(j * small, small), small), :] = total

            self.store(i).start()

        self.store(jnp.int32(pieces - 2)).wait()
        self.store(jnp.int32(pieces - 1)).wait()


def attention_back_kernel(
    hid, small, lse_t, cos, sin, dn2, cot, tok, wout, attall, qkv, mixed, mland, ghalf, grecv, uhalf, unear, dhalf, wqkv, n1,
    tgrad, ograd, gains, bout, lay, ggrad, ugrad, dgrad, qgrad, urecv, drecv, oex, qex,
    wo, da, dhid, attr, att_t, attc, qbuf, dsend, datt, part, slots, marr, ofull, osum, orecv, omid, ozr,
    dq, dpre, nbuf, qstage, qfetch, qsum, qrecv, qmid, wide_sum, tall_sum, qtotal, sums, zsums, dsums, bsums,
    mss, mrs, ass, ars, oss, ors, pss, prs, uss, urs, zss, zrs,
    ss, rs, xss, xrs, qss, qrs, dss, drs, yss, yrs, gss, grs, bss, brs, local, tsem, fsem, gsem,
):
    line = 4
    rows, model = hid.shape
    length = rows * line
    width = attc.shape[1]
    pairs = width // 128
    blocks = model // rows // 2
    half = rows // 2
    d, z, flips = place()
    greet(d, z, flips, line, range(1, 8))
    core = lax.rem(d, 2)
    ups = PlaneSum(uhalf, urecv, d, z, flips, uss, urs)
    downs = PlaneSum(dhalf, drecv, d, z, flips, dss, drs)
    loads = [
        pltpu.make_async_copy(wout, wo, local.at[4]),
        pltpu.make_async_copy(attall.at[pl.ds(pl.multiple_of(z * rows, rows), rows)], attr, local.at[5]),
        pltpu.make_async_copy(attall.at[:, pl.ds(pl.multiple_of(z * width, width), width)], attc, local.at[6]),
        pltpu.make_async_copy(qkv, qbuf, local.at[7]),
    ]
    rows_in = [pltpu.make_async_copy(dn2, dhid, local.at[11]), pltpu.make_async_copy(cot, da, local.at[12])]
    for copy in rows_in:
        copy.start()

    at_end = (z == 0) | (z == line - 1)
    inner = jnp.where(z == 0, 1, line - 2)

    def mixed_last(h):
        at = pl.ds(pl.multiple_of(inner * rows + h * half, half), half)
        return send(mixed.at[at], marr.at[pl.ds(h * half, half)], mss.at[h], mrs.at[h], d, inner)

    pl.when(at_end)(lambda: mixed_last(0).start())
    pl.when(at_end)(lambda: marr.__setitem__(Ellipsis, jnp.zeros((rows, model), BF)))
    for copy in loads:
        copy.start()
    ups.start(6)
    downs.start(2, 4, 6)

    def chain(part, slots, send_sems, recv_sems):
        pl.when(z == 0)(lambda: slots.__setitem__((0,), jnp.zeros((rows, model), BF)))
        pl.when(z == line - 1)(lambda: slots.__setitem__((line,), jnp.zeros((rows, model), BF)))
        return LineScatter(
            lambda s, h: part.at[s, pl.ds(h * half, half)],
            lambda i, h: slots.at[i, pl.ds(h * half, half)],
            2, d, z, line, send_sems, recv_sems,
        )

    for copy in rows_in:
        copy.wait()
    sums[...] = jnp.zeros_like(sums)

    def back(at):
        grad = dhid[at, :]
        standard, inverse = norm_parts(hid[at, :])
        sums[2:3, :] += jnp.sum(grad * standard, 0, keepdims=True)
        sums[3:4, :] += jnp.sum(grad, 0, keepdims=True)
        total = da[at, :].astype(F32) + norm_back(grad, standard, inverse, small[2:3, :])
        dhid[at, :] = total
        da[at, :] = total.astype(BF)

    each_piece(rows, 32, back)
    for copy in loads:
        copy.wait()

    def away(k, p):
        to = lax.rem(z + k, line)
        cols = pl.ds(p * 128, 128)
        return send(
            dsend.at[to, :, cols], datt.at[pl.ds(pl.multiple_of(z * rows, rows), rows), cols],
            ass.at[k, p], ars.at[z, p], d, to,
        )

    def taken(k, p):
        frm = lax.rem(z + k, line)
        cols = pl.ds(pl.multiple_of(p * 128, 128), 128)
        return send(
            dsend.at[frm, :, cols], datt.at[pl.ds(pl.multiple_of(frm * rows, rows), rows), cols],
            ass.at[k, p], ars.at[frm, p], d, frm,
        )

    @pl.loop(1, line + 1)
    def _(k):
        to = lax.rem(z + k, line)
        dsend[to] = nt(da[...], wo[pl.ds(pl.multiple_of(to * width, width), width), :]).astype(BF)

    for p in range(pairs):
        for k in range(1, line):
            away(k, p).start()
    pl.when(at_end)(lambda: mixed_last(1).start())
    weights_in = pltpu.make_async_copy(wqkv, wo.at[:, pl.ds(0, 3 * width)], local.at[4])
    weights_in.start()
    datt[pl.ds(pl.multiple_of(z * rows, rows), rows), :] = dsend[z]
    for lo, size in spans(model, 512):
        att_t[pl.ds(lo, size), :] = attr[:, pl.ds(lo, size)].T
    tok_in = pltpu.make_async_copy(tok, attr, local.at[6])
    tok_in.start()

    def oblock(t):
        return nn(att_t[...], da[:, pl.ds(pl.multiple_of(t * rows, rows), rows)])

    def ostage(k):
        return wo.at[:, pl.ds(pl.multiple_of(3 * width + lax.rem(k, 2) * rows, rows), rows)]

    def oacross(k):
        return send(ostage(k), oex.at[k], oss.at[k], ors.at[k], d + flips[1], z)

    @pl.loop(0, blocks)
    def _(k):
        pl.when(k >= 2)(lambda: oacross(k - 2).wait_send())
        ostage(k)[...] = oblock(2 * k + 1 - core).astype(BF)
        oacross(k).start()

    lanes = lax.broadcasted_iota(jnp.int32, (1, 128), 1)
    mine = (lanes < 64, lanes >= 64)
    which = lax.broadcasted_iota(jnp.int32, (16, 128), 0)
    lane16 = lax.broadcasted_iota(jnp.int32, (16, 128), 1)
    pick = jnp.where(which == lax.div(lane16, 64), 1.0, 0.0).astype(BF)
    scale = HEAD_DIM**-0.5

    def zaway(k):
        to = lax.rem(z + k, line)
        return send(
            ofull.at[pl.ds(pl.multiple_of(to * width, width), width)], ozr.at[k - 1], zss.at[k], zrs.at[k - 1], d, to
        )

    def plane_total():
        oplanes.arrive()

        def add(at):
            ofull[at, :] = oplanes.total((at, slice(None))).astype(BF)

        each_piece(model, 256, add)
        for k in range(1, line):
            zaway(k).start()

    def back_pair(p):
        cols = pl.ds(pl.multiple_of(p * 128, 128), 128)
        do = datt[:, cols]
        prod = do.astype(F32) * attc[:, cols].astype(F32)
        high = prod.astype(BF)
        inner = nt(pick, high) + nt(pick, (prod - high.astype(F32)).astype(BF))
        q = qbuf[0, p] * BF(scale)
        dq[...] = jnp.zeros_like(dq)
        for kj in range(line):
            at = pl.ds(kj * rows, rows)
            lo, count = kj * rows, length - kj * rows
            k, v = qbuf[1, p, at, :], qbuf[2, p, at, :]
            row = lax.broadcasted_iota(jnp.int32, (rows, count), 0)
            col = lax.broadcasted_iota(jnp.int32, (rows, count), 1)
            keep = col >= row
            dk = jnp.zeros((rows, 128), F32)
            dv = jnp.zeros((rows, 128), F32)
            for a in range(2):
                km, vm = jnp.where(mine[a], k, BF(0)), jnp.where(mine[a], v, BF(0))
                qm, dm = jnp.where(mine[a], q[lo:], BF(0)), jnp.where(mine[a], do[lo:], BF(0))
                s = jnp.where(keep, nt(km, q[lo:]), -1e30)
                probs = jnp.exp(s - lse_t[pl.ds(2 * p + a, 1), pl.ds(lo, count)])
                dv += nn(probs.astype(BF), dm)
                dprobs = nt(vm, do[lo:])
                ds = (probs * (dprobs - inner[a : a + 1, lo:])).astype(BF)
                dk += nn(ds, qm)
                dq[pl.ds(lo, count), :] += tn(ds, km)
            dk = turn(dk, cos[at, :], sin[at, :], -1.0)
            dpre[at, pl.ds(pl.multiple_of(width + p * 128, 128), 128)] = dk.astype(BF)
            dpre[at, pl.ds(pl.multiple_of(2 * width + p * 128, 128), 128)] = dv.astype(BF)
        dpre[:, cols] = turn(dq[...] * scale, cos[...], sin[...], -1.0).astype(BF)

    @pl.loop(0, pairs)
    def _(p):
        for k in range(1, line):
            taken(k, p).wait_recv()
        back_pair(p)


    oacross(blocks - 2).wait_send()
    oacross(blocks - 1).wait_send()
    weights_in.wait()
    chains = chain(part, slots, ss, rs)

    @pl.loop(0, line)
    def _(i):
        s = far_first(z, i)
        at = pl.ds(pl.multiple_of(s * rows, rows), rows)
        for lo, size in spans(model, 512):
            part[s, :, pl.ds(lo, size)] = nt(dpre[at, :], wo[pl.ds(lo, size), pl.ds(0, 3 * width)]).astype(BF)
        chains.head(s)

    hidden = uhalf.shape[2]
    chip = lax.div(d, 2)

    def wide(i):
        return [wo.at[pl.ds((i + k) * rows, rows), pl.ds(0, hidden)] for k in range(blocks)]

    gate_sum = BlockSum(ghalf.at[chip], [grecv.at[k] for k in range(blocks - 1)], wide(0), wide_sum, ggrad, fsem.at[0], gsem)
    up_sum = BlockSum(uhalf.at[chip], [unear.at[0], unear.at[1], urecv.at[0]], wide(blocks), wide_sum, ugrad, fsem.at[1], gsem)
    tall = [osum.at[k, pl.ds(0, hidden)] for k in range(blocks)]
    down_sum = BlockSum(dhalf.at[chip], [drecv.at[k] for k in range(blocks - 1)], tall, tall_sum, dgrad, fsem.at[2], gsem)
    gate_sum.fetch()
    mixed_in = [
        pltpu.make_async_copy(mixed.at[pl.ds(pl.multiple_of(z * rows, rows), rows)], wo.at[pl.ds(4 * rows, rows)], local.at[0]),
        pltpu.make_async_copy(mland.at[3], wo.at[pl.ds(5 * rows, rows)], local.at[1]),
    ]
    for copy in mixed_in:
        copy.start()

    oplanes = PlaneChain(osum, orecv, omid, d, z, flips, pss, prs)

    @pl.loop(0, blocks)
    def _(k):
        oacross(k).wait_recv()
        fetch = pltpu.make_async_copy(oex.at[k], ofull, local.at[8])
        fetch.start()
        fetch.wait()
        osum[k] = (oblock(2 * k + core) + ofull[...].astype(F32)).astype(BF)

    oplanes.start()
    def tile_in(i):
        t = 2 * lax.rem(i, blocks) + jnp.where(i < blocks, 1 - core, core)
        cols = pl.ds(pl.multiple_of(t * rows, rows), rows)
        return pltpu.make_async_copy(n1.at[:, cols], nbuf.at[lax.rem(i, 2)], tsem.at[lax.rem(i, 2)])

    def qblock(i):
        tile_in(i).wait()
        pl.when(i < 2 * blocks - 1)(lambda: tile_in(i + 1).start())
        return lambda lo, size: tn(nbuf[lax.rem(i, 2)], dpre[:, pl.ds(lo, size)])

    tile_in(jnp.int32(0)).start()

    def qacross(k):
        return send(qstage.at[lax.rem(k, 2)], qex.at[k], xss.at[k], xrs.at[k], d + flips[1], z)

    @pl.loop(0, blocks)
    def _(k):
        pl.when(k >= 2)(lambda: qacross(k - 2).wait_send())
        make = qblock(k)
        for lo, size in spans(3 * width, 512):
            qstage[lax.rem(k, 2), :, pl.ds(lo, size)] = make(lo, size).astype(BF)
        qacross(k).start()

    chains.relay(1)
    qplanes = PlaneChain(qsum, qrecv, qmid, d, z, flips, qss, qrs)

    @pl.loop(0, blocks)
    def _(k):
        qacross(k).wait_recv()
        fetch = pltpu.make_async_copy(qex.at[k], qfetch, local.at[8])
        fetch.start()
        fetch.wait()
        make = qblock(k + blocks)
        for lo, size in spans(3 * width, 512):
            qsum[k, :, pl.ds(lo, size)] = (make(lo, size) + qfetch[:, pl.ds(lo, size)].astype(F32)).astype(BF)

    qplanes.start()
    oplanes.relay()
    for h in range(2):
        pl.when(~at_end)(lambda: mixed_last(h).wait_recv())

    for copy in mixed_in:
        copy.wait()

    @pl.loop(0, rows // 32)
    def _(i):
        at = pl.ds(pl.multiple_of(i * 32, 32), 32)
        total = marr[at, :].astype(F32)
        for k in (4, 5):
            total = total + wo[pl.ds(pl.multiple_of(k * rows + i * 32, 32), 32), :].astype(F32)
        da[at, :] = (hid[at, :] + total).astype(BF)

    lay_out = pltpu.make_async_copy(da, lay, local.at[0])
    lay_out.start()
    bsums[0] = jnp.zeros(bsums.shape[1:], F32)

    def bias(at):
        bsums[0, 0:1, :] += jnp.sum(dpre[at, :].astype(F32), 0, keepdims=True)

    each_piece(length, 64, bias)

    def bcopy(r):
        return send(bsums.at[0], bsums.at[r], bss.at[r], brs.at[r], d + flips[r], z)

    for r in range(1, 8):
        bcopy(r).start()
    ups.wait(6)
    up_sum.fetch()
    gate_sum.add()
    chains.relay(2)
    qplanes.relay()
    up_sum.add()
    plane_total()
    total = jnp.zeros(bout.shape, F32)
    for r in range(8):
        if r:
            bcopy(r).wait()
        total = total + bsums[r]
    bout[...] = total
    tok_in.wait()
    for h in range(2):
        chains.arrive(h)
        @pl.loop(0, half // 32)
        def _(i):
            at = pl.ds(pl.multiple_of(h * half + i * 32, 32), 32)
            grad = chains.total(h, pl.ds(pl.multiple_of(i * 32, 32), 32))
            standard, inverse = norm_parts(attr[at, :].astype(F32))
            sums[0:1, :] += jnp.sum(grad * standard, 0, keepdims=True)
            sums[1:2, :] += jnp.sum(grad, 0, keepdims=True)
            tgrad[at, :] = (dhid[at, :] + norm_back(grad, standard, inverse, small[0:1, :])).astype(BF)

    depth = gains.shape[1]

    def columns(i):
        return sums.at[:, pl.ds(pl.multiple_of(i * depth, 256), depth)]

    def dcopy(r):
        return send(columns(d + flips[r]), dsums.at[r], gss.at[r], grs.at[r], d + flips[r], z)

    def zcopy(k):
        return send(zsums.at[0], zsums.at[k], yss.at[k], yrs.at[k], d, lax.rem(z + k, line))

    for r in range(1, 8):
        dcopy(r).start()
    qplanes.arrive()
    piece = qtotal.shape[1]

    @pl.loop(0, rows // piece)
    def _(i):
        at = pl.ds(pl.multiple_of(i * piece, piece), piece)
        for j in range(3):
            qtotal[j] = qplanes.total((at, pl.ds(j * width, width)))
        back = pltpu.make_async_copy(qtotal, qgrad.at[:, at], local.at[1])
        back.start()
        back.wait()

    oplanes.finish()
    downs.wait(2, 4, 6)
    down_sum.fetch()
    total = columns(d)[...]
    for r in range(1, 8):
        dcopy(r).wait()
        total = total + dsums[r]
    zsums[0] = total
    for k in range(1, line):
        zcopy(k).start()
    down_sum.add()
    for k in range(1, line):
        zcopy(k).wait()
        total = total + zsums[k]
    gains[...] = total
    total = ofull[pl.ds(pl.multiple_of(z * width, width), width), :].astype(F32)
    for k in range(1, line):
        zaway(k).wait()
        total = total + ozr[k - 1].astype(F32)
    ograd[...] = total
    for k in range(1, line):
        for p in range(pairs):
            away(k, p).wait_send()
    qplanes.finish()
    qacross(blocks - 2).wait_send()
    qacross(blocks - 1).wait_send()
    lay_out.wait()
    for h in range(2):
        pl.when(at_end)(lambda: mixed_last(h).wait_send())
    chains.finish()


def attention_backward(dn2, hid, cot, small, lse, tok, tabs, wout, attall, qkv, mixed, mland, ghalf, grecv, uhalf, unear, dhalf, wqkv, n1):
    rows, model = hid.shape
    line = 4
    length = rows * line
    width = model // line
    pairs = width // 128
    blocks = model // rows // 2
    hidden = uhalf.shape[2]
    sds = jax.ShapeDtypeStruct
    dma = pltpu.SemaphoreType.DMA
    vmem = pltpu.VMEM
    return pl.pallas_call(
        attention_back_kernel,
        out_shape=(
            sds((rows, model), BF), sds((width, rows), F32),
            sds((8, rows), F32), sds((8, 3 * width), F32), sds((rows, model), BF),
            sds((rows, hidden), F32), sds((rows, hidden), F32), sds((hidden, rows), F32), sds((3, rows, width), F32),
            sds((1, rows, hidden), BF), sds((blocks - 1, hidden, rows), BF),
            sds((blocks, model, rows), BF), sds((blocks, rows, 3 * width), BF),
        ),
        in_specs=[INV] * 5 + [ANY] * 15,
        out_specs=(INV,) * 4 + (ANY,) * 9,
        scratch_shapes=[
            vmem((model, model), BF), vmem((rows, model), BF), vmem((rows, model), F32), vmem((rows, model), BF),
            vmem((model, rows), BF), vmem((length, width), BF), vmem((3, pairs, length, 128), BF),
            vmem((line, rows, width), BF), vmem((length, width), BF),
            vmem((line, rows, model), BF), vmem((line + 1, rows, model), BF),
            vmem((rows, model), BF),
            vmem((model, rows), BF), vmem((blocks, model, rows), BF),
            vmem((2, model, rows), BF), vmem((2, model // 2, rows), BF),
            vmem((line - 1, width, rows), BF),
            vmem((length, 128), F32), vmem((length, 3 * width), BF), vmem((2, length, rows), BF),
            vmem((2, rows, 3 * width), BF), vmem((rows, 3 * width), BF), vmem((blocks, rows, 3 * width), BF),
            vmem((2, rows, 3 * width), BF), vmem((2, rows // 2, 3 * width), BF),
            vmem((2, 64, hidden), F32), vmem((2, hidden // 4, rows), F32), vmem((3, 64, width), F32),
            vmem((8, model), F32), vmem((line, 8, rows), F32), vmem((8, 8, rows), F32), vmem((8, 8, 3 * width), F32),
            dma((2,)), dma((2,)), dma((line, pairs)), dma((line, pairs)), dma((blocks,)), dma((blocks,)),
            dma((6,)), dma((6,)), dma((3,)), dma((3,)), dma((line,)), dma((line,)),
            dma((line, 2)), dma((line + 1, 2)), dma((blocks,)), dma((blocks,)), dma((6,)), dma((6,)),
            dma((3,)), dma((3,)), dma((line,)), dma((line,)), dma((8,)), dma((8,)), dma((8,)), dma((8,)), dma((13,)), dma((2,)),
            dma((3, blocks)), dma((2,)),
        ],
        compiler_params=pltpu.CompilerParams(
            collective_id=3, has_side_effects=True, vmem_limit_bytes=63 * 1024 * 1024
        ),
        cost_estimate=pl.CostEstimate(flops=10**11, bytes_accessed=10**8, transcendentals=0),
        name="attention_backward",
    )(hid, small, lse, *tabs, dn2, cot, tok, wout, attall, qkv, mixed, mland, ghalf, grecv, uhalf, unear, dhalf, wqkv, n1)


def turn_tables(length):
    half = ROT // 2
    freqs = np.float32(10000.0) ** (-np.arange(0, ROT, 2, dtype=np.float32) / np.float32(ROT))
    angles = np.arange(length, dtype=np.float32)[:, None] * freqs[None, :]
    cos = np.ones((length, HEAD_DIM), np.float32)
    sin = np.zeros((length, HEAD_DIM), np.float32)
    cos[:, :half] = cos[:, half:ROT] = np.cos(angles)
    sin[:, half:ROT] = np.sin(angles)
    sin[:, :half] = -np.sin(angles)
    return tuple(jnp.asarray(np.tile(t, (1, 2))) for t in (cos, sin))


def pack_smalls(d, model, width, qkv_bias, *vectors):
    col = lax.broadcasted_iota(jnp.int32, (1, model), 1)
    each = vectors[0].shape[0]
    gains = jnp.stack([jnp.tile(v, model // each) for v in vectors], 0)
    gains = jnp.where(col // each == d, gains, 0)
    part = qkv_bias.shape[1]
    bias = jnp.tile(qkv_bias, (1, width // part)).reshape(1, 3 * width)
    bias = jnp.pad(bias, ((0, 0), (0, model - 3 * width)))
    bias = jnp.where(col % width // part == d, bias, 0)
    return jnp.concatenate([gains, bias, jnp.zeros((11, model), BF)], 0).astype(BF)


def fast(
    tokens, qkv_weight, qkv_bias, out_weight, norm1_gain, norm1_shift, gate_weight, up_weight,
    down_weight, norm2_gain, norm2_shift, cotangent,
):
    d = lax.axis_index("dp")
    rows, model = tokens.shape
    length = 4 * rows
    tabs = turn_tables(length)
    depth, width = qkv_weight.shape[1:]
    smalls = pack_smalls(d, model, width, qkv_bias, norm1_gain, norm1_shift, norm2_gain, norm2_shift)
    cotnear, n1, qkv, lse, attall, wqkv, small, wout, n2, hidden, wgate, wup, wdown = attention_forward(
        tokens, cotangent, qkv_weight, out_weight, gate_weight, up_weight, down_weight, smalls, tabs
    )
    dn2, mixed, mland, _, _, _, ghalf, uhalf, dhalf, grecv, unear = mlp(n2, cotangent, cotnear, wgate, wup, wdown)
    (
        token_gradient, outw_grad, gains, bias, layer_output, gatew_grad, upw_grad, downw_grad, qkvw_grad, _, _, _, _
    ) = attention_backward(
        dn2, hidden, cotangent, small, lse, tokens, tabs, wout, attall, qkv, mixed, mland, ghalf, grecv, uhalf, unear,
        dhalf, wqkv, n1,
    )
    part = qkv_bias.shape[1]
    bias = bias[0].reshape(3, width)
    qkvb_grad = lax.dynamic_slice_in_dim(bias, d * part, part, 1)
    return (
        layer_output, token_gradient, qkvw_grad, qkvb_grad, outw_grad, gains[0], gains[1],
        gatew_grad, upw_grad, downw_grad, gains[2], gains[3],
    )


def solution(mesh):
    placed = (
        P(("dp", "tensor"), None),
        P(None, "dp", "tensor"),
        P(None, ("tensor", "dp")),
        P("tensor", "dp"),
        P("dp"),
        P("dp"),
        P("dp", "tensor"),
        P("dp", "tensor"),
        P("tensor", "dp"),
        P("dp"),
        P("dp"),
        P(("dp", "tensor"), None),
    )
    return jax.shard_map(
        fast if dict(mesh.shape) == {"dp": 8, "tensor": 4} else local,
        mesh=mesh,
        in_specs=placed,
        out_specs=(
            P(("dp", "tensor"), None),
            P(("dp", "tensor"), None),
            P(None, "dp", "tensor"),
            P(None, ("tensor", "dp")),
            P("tensor", "dp"),
            P("dp"),
            P("dp"),
            P("dp", "tensor"),
            P("dp", "tensor"),
            P("tensor", "dp"),
            P("dp"),
            P("dp"),
        ),
        check_vma=False,
    )
```

```python
import functools

import jax
import jax.numpy as jnp
import numpy as np
from jax import lax
from jax.experimental import pallas as pl
from jax.experimental.pallas import tpu as pltpu
from jax.sharding import PartitionSpec as P

MESH = pl.DeviceIdType.MESH
HEAD_DIM = 64
ROT = 16
BF = jnp.bfloat16
F32 = jnp.float32
VMEM_LIMIT = 56 * 1024 * 1024
ANY = pl.BlockSpec(memory_space=pl.ANY)
INV = pl.BlockSpec(memory_space=pltpu.VMEM)


def nt(a, b):
    return lax.dot_general(a, b, (((1,), (1,)), ((), ())), preferred_element_type=F32)


def tn(a, b):
    return lax.dot_general(a, b, (((0,), (0,)), ((), ())), preferred_element_type=F32)


def nn(a, b):
    return jnp.dot(a, b, preferred_element_type=F32)


def spans(total, step):
    return [(i, min(step, total - i)) for i in range(0, total, step)]


def place():
    d = lax.axis_index("dp")
    z = lax.axis_index("tensor")
    dy = 4 * (1 - 2 * lax.div(d, 4))
    dx = 2 * (1 - 2 * lax.rem(lax.div(d, 2), 2))
    dc = 1 - 2 * lax.rem(d, 2)
    return d, z, (0, dc, dx, dx + dc, dy, dy + dc, dy + dx, dy + dx + dc)


def send(src, dst, ssem, rsem, d, z):
    return pltpu.make_async_remote_copy(
        src_ref=src, dst_ref=dst, send_sem=ssem, recv_sem=rsem, device_id=(d, z), device_id_type=MESH
    )


def greet(d, z, flips, line, plane):
    barrier = pltpu.get_barrier_semaphore()
    for k in range(1, line):
        pl.semaphore_signal(
            barrier, inc=1, device_id=(d, lax.rem(z + k, line)), device_id_type=MESH
        )
    for r in plane:
        pl.semaphore_signal(barrier, inc=1, device_id=(d + flips[r], z), device_id_type=MESH)
    pl.semaphore_wait(barrier, line - 1 + len(plane))


class LineGather:
    def __init__(self, view, chunks, d, z, line, send_sems, recv_sems):
        self.view, self.chunks, self.d, self.z, self.line = view, chunks, d, z, line
        self.ss, self.rs = send_sems, recv_sems

    def copy(self, s, h, way, src=None):
        ref = self.view(s, h)
        return send(
            ref if src is None else src, ref, self.ss.at[way, s, h], self.rs.at[s, h],
            self.d, self.z + (1 if way == 0 else -1),
        )

    def start(self, h, src=None):
        pl.when(self.z < self.line - 1)(lambda: self.copy(self.z, h, 0, src).start())
        pl.when(self.z > 0)(lambda: self.copy(self.z, h, 1, src).start())

    def step(self, k, h, forward=True):
        z, line = self.z, self.line

        @pl.when(z - k >= 0)
        def _():
            self.copy(z - k, h, 0).wait_recv()
            if forward:
                pl.when(z < line - 1)(lambda: self.copy(z - k, h, 0).start())

        @pl.when(z + k < line)
        def _():
            self.copy(z + k, h, 1).wait_recv()
            if forward:
                pl.when(z > 0)(lambda: self.copy(z + k, h, 1).start())

    def finish(self, first=0, last=None):
        z, line = self.z, self.line
        for k in range(first, line if last is None else last):
            for h in range(self.chunks):
                pl.when((z - k >= 0) & (z < line - 1))(lambda: self.copy(z - k, h, 0).wait_send())
                pl.when((z + k < line) & (z > 0))(lambda: self.copy(z + k, h, 1).wait_send())


class PlaneGather:
    def __init__(self, src, view, d, z, flips, send_sems, recv_sems):
        self.src, self.view, self.d, self.z, self.flips = src, view, d, z, flips
        self.ss, self.rs = send_sems, recv_sems
        self.half = src.shape[0] // 2

    def copy(self, key):
        d, f = self.d, self.flips
        block, to, part = {
            1: (0, 1, None), 2: (0, 2, None), 4: (0, 4, None), 3: (2, 1, None), 5: (4, 1, None),
            6: (2, 4, 0), 7: (4, 2, 1), 8: (6, 1, 0), 9: (6, 1, 1),
        }[key]
        dst = self.view(d + f[block])
        src = self.src if block == 0 else dst
        if part is not None:
            at = pl.ds(part * self.half, self.half)
            src, dst = src.at[at], dst.at[at]
        return send(src, dst, self.ss.at[key], self.rs.at[key], d + f[to], self.z)

    def start(self):
        for key in (4, 2, 1):
            self.copy(key).start()

    def relay(self):
        for key, onward in ((2, (6, 3)), (4, (7, 5))):
            self.copy(key).wait_recv()
            for to in onward:
                self.copy(to).start()

    def pass_on(self):
        for key, onward in ((6, 8), (7, 9)):
            self.copy(key).wait_recv()
            self.copy(onward).start()

    def arrive(self):
        for key in (1, 3, 5, 8, 9):
            self.copy(key).wait_recv()

    def finish(self):
        for key in range(1, 10):
            self.copy(key).wait_send()


def arrival(z, i):
    orders = ((0, 1, 2, 3), (1, 0, 2, 3), (2, 3, 1, 0), (3, 2, 1, 0))
    codes = [sum(s * 4**j for j, s in enumerate(o)) for o in orders]
    code = jnp.where(
        z == 0, codes[0], jnp.where(z == 1, codes[1], jnp.where(z == 2, codes[2], codes[3]))
    )
    power = jnp.where(i == 0, 1, jnp.where(i == 1, 4, jnp.where(i == 2, 16, 64)))
    return lax.rem(lax.div(code, power), 4)


def turn(u, cos, sin, sign=1.0):
    low = lax.rem(lax.broadcasted_iota(jnp.int32, (1, 128), 1), HEAD_DIM) < ROT // 2
    moved = jnp.where(low, pltpu.roll(u, 128 - ROT // 2, 1), pltpu.roll(u, ROT // 2, 1)) * sin
    return u * cos + moved if sign > 0 else u * cos - moved


def attention_kernel(
    tok, cot, wq, ow, gw, uw, dw, smalls, cos, sin,
    cotnear, n1, qkv, lse_t, attall, wqkv, small_sum, wout, n2, hidden, wgate, wup, wdown,
    xbuf, n1buf, wbuf, qbuf, attv, wz, wo, acc, smbuf, lse,
    tss, trs, css, crs, ass, ars, mss, mrs, yss, yrs, pss, prs, local,
):
    rows, model = tok.shape
    width = wq.shape[2]
    pairs = width // 128
    line = 4
    d, z, flips = place()
    greet(d, z, flips, line, range(1, 8))

    tok_in = pltpu.make_async_copy(tok, xbuf.at[z], local.at[0])
    tok_in.start()
    depth = wq.shape[1]

    def wblock(i):
        return wbuf.at[pl.ds(pl.multiple_of(i * depth, 256), depth), :]

    w_in = [
        pltpu.make_async_copy(wq.at[j], wblock(d).at[:, pl.ds(j * width, width)], local.at[(2, 1, 13)[j]])
        for j in range(3)
    ]
    for copy in w_in:
        copy.start()
    tall = ow.shape[0]

    def oview(s, h):
        return wz.at[pl.ds(pl.multiple_of(s * tall, tall), tall)]

    def oblock(i):
        return wo.at[:, pl.ds(pl.multiple_of(i * depth, 256), depth)]

    o_in = pltpu.make_async_copy(ow, oview(z, 0), local.at[14])
    o_in.start()
    outs_z = LineGather(oview, 1, d, z, line, yss, yrs)
    small_copies = [
        send(smalls, smbuf.at[r], mss.at[r], mrs.at[r], d + flips[r], z) for r in range(1, 8)
    ]
    for copy in small_copies:
        copy.start()
    tall_block = dw.shape[1]

    def rows_of(ref, i):
        return ref.at[pl.ds(pl.multiple_of(i * depth, 256), depth)]

    def columns_of(ref, i):
        return ref.at[:, pl.ds(pl.multiple_of(i * tall_block, 256), tall_block)]

    planes = [
        PlaneGather(src, view, d, z, flips, pss.at[i], prs.at[i])
        for i, (src, view) in enumerate((
            (wblock(d), wblock),
            (wz, oblock),
            (gw, lambda i: rows_of(wgate, i)),
            (uw, lambda i: rows_of(wup, i)),
            (dw, lambda i: columns_of(wdown, i)),
        ))
    ]
    qkv_plane, out_plane, gate_plane, up_plane, down_plane = planes
    keep_own = [
        pltpu.make_async_copy(gw, rows_of(wgate, d), local.at[10]),
        pltpu.make_async_copy(uw, rows_of(wup, d), local.at[11]),
        pltpu.make_async_copy(dw, columns_of(wdown, d), local.at[12]),
    ]
    for copy in keep_own:
        copy.start()
    half = rows // 2

    def tview(s, h):
        return xbuf.at[s, pl.ds(h * half, half)]

    def cview(s, h):
        return cotnear.at[s, pl.ds(h * half, half)]

    def aview(s, h):
        return attv.at[:, pl.ds(pl.multiple_of(s * width + h * 128, 128), 128)]

    toks = LineGather(tview, 2, d, z, line, tss, trs)
    cots = LineGather(cview, 2, d, z, line, css, crs)
    atts = LineGather(aview, pairs, d, z, line, ass, ars)
    tok_in.wait()
    for h in range(2):
        toks.start(h)
    for copy in w_in:
        copy.wait()
    qkv_plane.start()
    for copy in small_copies:
        copy.wait()
    total = smalls[...].astype(F32)
    for r in range(1, 8):
        total = total + smbuf[r].astype(F32)
    small_sum[...] = total

    def normalise(s):
        piece = 32

        @pl.loop(0, rows // piece)
        def _(i):
            at = pl.ds(pl.multiple_of(i * piece, piece), piece)
            x = xbuf[s, at, :].astype(F32)
            centred = x - jnp.mean(x, -1, keepdims=True)
            spread = jnp.mean(centred * centred, -1, keepdims=True)
            n = centred * lax.rsqrt(spread + 1e-05) * small_sum[0:1, :] + small_sum[1:2, :]
            n1buf[pl.ds(pl.multiple_of(s * rows + i * piece, piece), piece), :] = n.astype(BF)

    def project(s):
        at = pl.ds(pl.multiple_of(s * rows, rows), rows)
        for j in range(3):
            cols = pl.ds(j * width, width)
            pre = nn(n1buf[at, :], wbuf[:, cols]) + small_sum[4:5, cols]
            for p in range(pairs):
                part = pre[:, p * 128 : (p + 1) * 128]
                if j < 2:
                    part = turn(part, cos[at, :], sin[at, :])
                qbuf[j, p, at, :] = part.astype(BF)

    normalise(z)
    for h in range(2):
        toks.step(1, h)
    qkv_plane.relay()
    gate_plane.start()
    normalise(arrival(z, 1))
    qkv_plane.pass_on()
    for h in range(2):
        toks.step(2, h)
    normalise(arrival(z, 2))
    gate_plane.relay()
    qkv_plane.arrive()

    @pl.loop(0, line)
    def _(i):
        s = arrival(z, i)

        @pl.when(i == line - 1)
        def _():
            gate_plane.pass_on()
            up_plane.start()
            o_in.wait()
            outs_z.start(0)
            for h in range(2):
                toks.step(3, h)
            normalise(s)

        project(s)

    o_own = pltpu.make_async_copy(wz, oblock(d), local.at[15])
    outs = [
        pltpu.make_async_copy(n1buf, n1, local.at[3]),
        pltpu.make_async_copy(wbuf, wqkv, local.at[4]),
        pltpu.make_async_copy(qbuf, qkv, local.at[5]),
    ]
    for copy in outs:
        copy.start()

    lanes = lax.broadcasted_iota(jnp.int32, (1, 128), 1)
    first = lanes < 64
    lse[...] = jnp.zeros_like(lse)
    length = rows * line

    def attend(p):
        for qi in range(line):
            count = (qi + 1) * rows
            at = pl.ds(qi * rows, rows)
            q = qbuf[0, p, at, :] * BF(HEAD_DIM**-0.5)
            k = qbuf[1, p, pl.ds(0, count), :]
            v = qbuf[2, p, pl.ds(0, count), :]
            row = lax.broadcasted_iota(jnp.int32, (rows, count), 0) + qi * rows
            col = lax.broadcasted_iota(jnp.int32, (rows, count), 1)
            keep = row >= col
            results = []
            stats = lse[at, :]
            for a in range(2):
                mine = first if a == 0 else ~first
                s = nt(jnp.where(mine, q, BF(0)), k)
                s = jnp.where(keep, s, -1e30)
                most = jnp.max(s, -1, keepdims=True)
                e = jnp.exp(s - most)
                total = jnp.sum(e, -1, keepdims=True)
                results.append(nn(e.astype(BF), v) / total)
                stats = jnp.where(lanes == 2 * p + a, most + jnp.log(total), stats)
            lse[at, :] = stats
            attv[at, pl.ds(pl.multiple_of(z * width + p * 128, 128), 128)] = jnp.where(
                first, results[0], results[1]
            ).astype(BF)

    @pl.loop(0, pairs)
    def _(p):
        attend(p)
        atts.start(p)
        for k in range(1, line):
            pl.when(p == k - 1)(lambda: outs_z.step(k, 0))

        @pl.when(p == line - 2)
        def _():
            up_plane.relay()
            out_plane.start()
            o_own.start()

    lse_t[...] = lse[...].T
    for p in range(pairs):
        atts.step(1, p)
    up_plane.pass_on()
    out_plane.relay()
    down_plane.start()
    for p in range(pairs):
        atts.step(2, p)
    out_plane.pass_on()
    o_own.wait()
    out_plane.arrive()
    keep_wo = pltpu.make_async_copy(wo, wout, local.at[6])
    keep_wo.start()

    def project_out(s, at, lo, size):
        heads = pl.ds(pl.multiple_of(s * width, width), width)
        return nn(attv[at, heads], wo[heads, pl.ds(lo, size)])

    for i in range(line - 1):
        s = arrival(z, i)

        @pl.loop(0, line)
        def _(r):
            at = pl.ds(pl.multiple_of(r * rows, rows), rows)
            for lo, size in spans(model, 512):
                base = xbuf[r, :, pl.ds(lo, size)].astype(F32) if i == 0 else acc[at, pl.ds(lo, size)]
                acc[at, pl.ds(lo, size)] = base + project_out(s, at, lo, size)

        if i == 1:
            down_plane.relay()
    for copy in outs:
        copy.wait()
    for p in range(pairs):
        atts.step(3, p)
    cots.start(0, cot.at[pl.ds(0, half)])
    keep_att = pltpu.make_async_copy(attv, attall, local.at[7])
    keep_att.start()
    last = arrival(z, line - 1)

    @pl.loop(0, line)
    def _(r):
        at = pl.ds(pl.multiple_of(r * rows, rows), rows)
        for lo, size in spans(model, 512):
            acc[at, pl.ds(lo, size)] += project_out(last, at, lo, size)

        @pl.loop(0, rows // 32)
        def _(i):
            piece = pl.ds(pl.multiple_of(r * rows + i * 32, 32), 32)
            x = acc[piece, :]
            centred = x - jnp.mean(x, -1, keepdims=True)
            spread = jnp.mean(centred * centred, -1, keepdims=True)
            n = centred * lax.rsqrt(spread + 1e-05) * small_sum[2:3, :] + small_sum[3:4, :]
            n1buf[piece, :] = n.astype(BF)

    keep = [
        pltpu.make_async_copy(n1buf, n2, local.at[8]),
        pltpu.make_async_copy(acc.at[pl.ds(pl.multiple_of(z * rows, rows), rows)], hidden, local.at[9]),
        keep_wo, keep_att,
    ]
    for copy in keep[:2]:
        copy.start()
    down_plane.pass_on()
    for gather in (toks, atts, outs_z):
        gather.finish()
    cots.step(1, 0, forward=False)
    pl.when(z < line - 1)(lambda: cots.copy(z, 0, 0).wait_send())
    pl.when(z > 0)(lambda: cots.copy(z, 0, 1).wait_send())
    for plane in (gate_plane, up_plane, down_plane):
        plane.arrive()
    for plane in planes:
        plane.finish()
    for copy in keep_own:
        copy.wait()
    for copy in keep:
        copy.wait()


def attention_forward(tok, cot, wq, ow, gw, uw, dw, smalls, tabs):
    rows, model = tok.shape
    line = 4
    length = rows * line
    _, depth, width = wq.shape
    pairs = width // 128
    dp = model // depth
    hidden = gw.shape[1]
    sds = jax.ShapeDtypeStruct
    return pl.pallas_call(
        attention_kernel,
        out_shape=(
            sds((line, rows, model), BF), sds((length, model), BF),
            sds((3, pairs, length, 128), BF), sds((128, length), F32), sds((length, model), BF),
            sds((model, 3 * width), BF), sds((16, model), F32),
            sds((model, model), BF), sds((length, model), BF), sds((rows, model), F32),
            sds((model, hidden), BF), sds((model, hidden), BF), sds((hidden, model), BF),
        ),
        in_specs=[ANY] * 7 + [INV] * 3,
        out_specs=(ANY, ANY, ANY, INV, ANY, ANY, INV) + (ANY,) * 6,
        scratch_shapes=[
            pltpu.VMEM((line, rows, model), BF),
            pltpu.VMEM((length, model), BF),
            pltpu.VMEM((model, 3 * width), BF),
            pltpu.VMEM((3, pairs, length, 128), BF),
            pltpu.VMEM((length, model), BF),
            pltpu.VMEM((model, depth), BF),
            pltpu.VMEM((model, model), BF),
            pltpu.VMEM((length, model), F32),
            pltpu.VMEM((dp, 16, model), BF),
            pltpu.VMEM((length, 128), F32),
            pltpu.SemaphoreType.DMA((2, line, 2)),
            pltpu.SemaphoreType.DMA((line, 2)),
            pltpu.SemaphoreType.DMA((2, line, 2)),
            pltpu.SemaphoreType.DMA((line, 2)),
            pltpu.SemaphoreType.DMA((2, line, pairs)),
            pltpu.SemaphoreType.DMA((line, pairs)),
            pltpu.SemaphoreType.DMA((8,)),
            pltpu.SemaphoreType.DMA((8,)),
            pltpu.SemaphoreType.DMA((2, line, 1)),
            pltpu.SemaphoreType.DMA((line, 1)),
            pltpu.SemaphoreType.DMA((5, 10)),
            pltpu.SemaphoreType.DMA((5, 10)),
            pltpu.SemaphoreType.DMA((16,)),
        ],
        compiler_params=pltpu.CompilerParams(
            collective_id=1, has_side_effects=True, vmem_limit_bytes=VMEM_LIMIT
        ),
        cost_estimate=pl.CostEstimate(flops=2 * 10**11, bytes_accessed=10**8, transcendentals=0),
        name="attention_forward",
    )(tok, cot, wq, ow, gw, uw, dw, smalls, *tabs)


def apply_layer_norm(value, norm_scale, norm_bias):
    centered_input = value - jnp.mean(value, -1, keepdims=True)
    spread = jnp.mean(centered_input * centered_input, -1, keepdims=True)
    inverse_deviation = lax.rsqrt(spread + 1e-05)
    standardized_input = centered_input * inverse_deviation
    return (
        standardized_input * norm_scale.astype(jnp.float32) + norm_bias.astype(jnp.float32),
        standardized_input,
        inverse_deviation,
    )


def layer_norm_backward(output_gradient, standardized_input, inverse_deviation, norm_scale):
    scaled_gradient = output_gradient * norm_scale.astype(jnp.float32)
    return inverse_deviation * (
        scaled_gradient
        - jnp.mean(scaled_gradient, -1, keepdims=True)
        - standardized_input * jnp.mean(scaled_gradient * standardized_input, -1, keepdims=True)
    )


def tables(length):
    positions = jnp.arange(length, dtype=jnp.float32)
    freqs = 10000.0 ** (-jnp.arange(0, ROT, 2, dtype=jnp.float32) / ROT)
    angles = positions[:, None] * freqs[None, :]
    angles = jnp.concatenate([angles, angles], -1)
    return (jnp.cos(angles), jnp.sin(angles))


def rotate(heads, cosine, sine):
    half = ROT // 2
    part = heads[..., :ROT]
    turned = jnp.concatenate([-part[..., half:], part[..., :half]], -1)
    moved = part * cosine[:, None, :] + turned * sine[:, None, :]
    return jnp.concatenate([moved, heads[..., ROT:]], -1)


def unrotate(output_gradient, cosine, sine):
    half = ROT // 2
    part = output_gradient[..., :ROT]
    scaled_gradient = part * sine[:, None, :]
    back = jnp.concatenate([scaled_gradient[..., half:], -scaled_gradient[..., :half]], -1)
    moved = part * cosine[:, None, :] + back
    return jnp.concatenate([moved, output_gradient[..., ROT:]], -1)


def attn_params(qkv_weight, qkv_bias, out_weight, norm1_gain, norm1_shift):
    return (
        lax.all_gather(qkv_weight, "dp", axis=1, tiled=True),
        lax.all_gather(qkv_bias, "dp", axis=1, tiled=True),
        lax.all_gather(out_weight, "dp", axis=1, tiled=True),
        lax.all_gather(norm1_gain, "dp", axis=0, tiled=True),
        lax.all_gather(norm1_shift, "dp", axis=0, tiled=True),
    )


def mlp_params(gate_weight, up_weight, down_weight, norm2_gain, norm2_shift):
    return (
        lax.all_gather(gate_weight, "dp", axis=0, tiled=True),
        lax.all_gather(up_weight, "dp", axis=0, tiled=True),
        lax.all_gather(down_weight, "dp", axis=1, tiled=True),
        lax.all_gather(norm2_gain, "dp", axis=0, tiled=True),
        lax.all_gather(norm2_shift, "dp", axis=0, tiled=True),
    )


def gather_rows(rows):
    return lax.all_gather(rows, "tensor", axis=0, tiled=True)


def sum_rows(partial_value):
    return lax.psum_scatter(
        partial_value.astype(jnp.bfloat16), "tensor", scatter_dimension=0, tiled=True
    ).astype(jnp.float32)


def gather_grads(rows):
    return lax.all_gather(rows, "tensor", axis=0, tiled=True)


def sum_grads(partial_value):
    return lax.psum_scatter(
        partial_value.astype(jnp.bfloat16), "tensor", scatter_dimension=0, tiled=True
    ).astype(jnp.float32)


def local(
    tokens,
    qkv_weight,
    qkv_bias,
    out_weight,
    norm1_gain,
    norm1_shift,
    gate_weight,
    up_weight,
    down_weight,
    norm2_gain,
    norm2_shift,
    cotangent,
):
    scale = HEAD_DIM ** (-0.5)
    input_rows = tokens.astype(jnp.float32)
    wqkv, bqkv, wout, first_norm_scale, first_norm_bias = attn_params(
        qkv_weight, qkv_bias, out_weight, norm1_gain, norm1_shift
    )
    first_normed_rows, first_standardized, first_inverse_deviation = apply_layer_norm(
        input_rows, first_norm_scale, first_norm_bias
    )
    rows1 = gather_rows(first_normed_rows.astype(jnp.bfloat16))
    length = rows1.shape[0]
    width = wqkv.shape[2]
    local_heads = width // HEAD_DIM
    pre = (
        jnp.einsum("sd,jdc->jsc", rows1, wqkv, preferred_element_type=jnp.float32)
        + bqkv.astype(jnp.float32)[:, None, :]
    )
    cosine, sine = tables(length)
    query = rotate(pre[0].reshape(length, local_heads, HEAD_DIM), cosine, sine).astype(jnp.bfloat16)
    keys = rotate(pre[1].reshape(length, local_heads, HEAD_DIM), cosine, sine).astype(jnp.bfloat16)
    values = pre[2].reshape(length, local_heads, HEAD_DIM).astype(jnp.bfloat16)
    block = min(length, 512)
    count = length // block
    cols = jnp.arange(length, dtype=jnp.int32)

    def block_probs(qblock, start):
        scores = (
            jnp.einsum("qhd,khd->hqk", qblock, keys, preferred_element_type=jnp.float32) * scale
        )
        rows = start + jnp.arange(block, dtype=jnp.int32)
        keep = rows[:, None] >= cols[None, :]
        return jnp.where(keep[None], scores, -1e30)

    def forward_block(index):
        qblock = lax.dynamic_slice_in_dim(query, index * block, block, 0)
        scores = block_probs(qblock, index * block)
        most = jnp.max(scores, -1, keepdims=True)
        expo = jnp.exp(scores - most)
        total = jnp.sum(expo, -1, keepdims=True)
        probs = (expo / total).astype(jnp.bfloat16)
        out_block = jnp.einsum("hqk,khd->qhd", probs, values, preferred_element_type=jnp.float32)
        return (out_block.astype(jnp.bfloat16), most[..., 0] + jnp.log(total[..., 0]))

    indices = jnp.arange(count, dtype=jnp.int32)
    out_blocks, lse = lax.map(forward_block, indices)
    attended = out_blocks.reshape(length, width)
    branch = jnp.dot(attended, wout, preferred_element_type=jnp.float32)
    hidden_state = input_rows + sum_rows(branch)
    wgate, wup, wdown, second_norm_scale, second_norm_bias = mlp_params(
        gate_weight, up_weight, down_weight, norm2_gain, norm2_shift
    )
    second_normed_rows, second_standardized, second_inverse_deviation = apply_layer_norm(
        hidden_state, second_norm_scale, second_norm_bias
    )
    rows2 = gather_rows(second_normed_rows.astype(jnp.bfloat16))
    gate = jnp.dot(rows2, wgate, preferred_element_type=jnp.float32)
    up = jnp.dot(rows2, wup, preferred_element_type=jnp.float32)
    sigma = jax.nn.sigmoid(gate)
    silu = gate * sigma
    act = (silu * up).astype(jnp.bfloat16)
    mixed = sum_rows(jnp.dot(act, wdown, preferred_element_type=jnp.float32))
    layer_output = (hidden_state + mixed).astype(jnp.bfloat16)
    wgate, wup, wdown, second_norm_scale, second_norm_bias = mlp_params(
        gate_weight, up_weight, down_weight, norm2_gain, norm2_shift
    )
    incoming_gradient = cotangent.astype(jnp.float32)
    down_rows = gather_grads(cotangent)
    down_grad = jnp.einsum("sf,sd->fd", act, down_rows, preferred_element_type=jnp.float32)
    dact = jnp.einsum("sd,fd->sf", down_rows, wdown, preferred_element_type=jnp.float32)
    dgate = (dact * up * (sigma * (1.0 + gate * (1.0 - sigma)))).astype(jnp.bfloat16)
    dup = (dact * silu).astype(jnp.bfloat16)
    gate_grad = jnp.einsum("sd,sf->df", rows2, dgate, preferred_element_type=jnp.float32)
    up_grad = jnp.einsum("sd,sf->df", rows2, dup, preferred_element_type=jnp.float32)
    second_norm_gradient = jnp.einsum(
        "sf,df->sd", dgate, wgate, preferred_element_type=jnp.float32
    ) + jnp.einsum("sf,df->sd", dup, wup, preferred_element_type=jnp.float32)
    second_norm_gradient = sum_grads(second_norm_gradient)
    second_scale_partial = jnp.sum(second_norm_gradient * second_standardized, 0)
    shift2_part = jnp.sum(second_norm_gradient, 0)
    hidden_gradient = incoming_gradient + layer_norm_backward(
        second_norm_gradient, second_standardized, second_inverse_deviation, second_norm_scale
    )
    gatew_grad, upw_grad, downw_grad, gain2_total, shift2_total = (
        lax.psum_scatter(
            gate_grad.astype(jnp.bfloat16), "dp", scatter_dimension=0, tiled=True
        ).astype(jnp.float32),
        lax.psum_scatter(
            up_grad.astype(jnp.bfloat16), "dp", scatter_dimension=0, tiled=True
        ).astype(jnp.float32),
        lax.psum_scatter(
            down_grad.astype(jnp.bfloat16), "dp", scatter_dimension=1, tiled=True
        ).astype(jnp.float32),
        lax.psum_scatter(
            second_scale_partial.astype(jnp.bfloat16), "dp", scatter_dimension=0, tiled=True
        ).astype(jnp.float32),
        lax.psum_scatter(
            shift2_part.astype(jnp.bfloat16), "dp", scatter_dimension=0, tiled=True
        ).astype(jnp.float32),
    )
    wqkv, bqkv, wout, first_norm_scale, first_norm_bias = attn_params(
        qkv_weight, qkv_bias, out_weight, norm1_gain, norm1_shift
    )
    branch_rows = gather_grads(hidden_gradient.astype(jnp.bfloat16))
    out_grad = jnp.einsum("sc,sd->cd", attended, branch_rows, preferred_element_type=jnp.float32)
    dattended = jnp.einsum(
        "sd,cd->sc", branch_rows, wout, preferred_element_type=jnp.float32
    ).astype(jnp.bfloat16)
    dattended = dattended.reshape(length, local_heads, HEAD_DIM)

    def backward_block(carry, item):
        dkeys, dvalues = carry
        index, block_lse = item
        qblock = lax.dynamic_slice_in_dim(query, index * block, block, 0)
        dblock = lax.dynamic_slice_in_dim(dattended, index * block, block, 0)
        scores = block_probs(qblock, index * block)
        probs = jnp.exp(scores - block_lse[..., None])
        probs16 = probs.astype(jnp.bfloat16)
        dvalues = dvalues + jnp.einsum(
            "hqk,qhd->khd", probs16, dblock, preferred_element_type=jnp.float32
        )
        dprobs = jnp.einsum("qhd,khd->hqk", dblock, values, preferred_element_type=jnp.float32)
        inner = jnp.sum(dprobs * probs, -1, keepdims=True)
        dscores = (probs * (dprobs - inner)).astype(jnp.bfloat16)
        dquery = (
            jnp.einsum("hqk,khd->qhd", dscores, keys, preferred_element_type=jnp.float32) * scale
        )
        dkeys = (
            dkeys
            + jnp.einsum("hqk,qhd->khd", dscores, qblock, preferred_element_type=jnp.float32)
            * scale
        )
        return ((dkeys, dvalues), dquery)

    empty = jnp.zeros((length, local_heads, HEAD_DIM), jnp.float32)
    (dkeys, dvalues), dquery = lax.scan(backward_block, (empty, empty), (indices, lse))
    dquery = dquery.reshape(length, local_heads, HEAD_DIM)
    dpre = jnp.stack(
        [
            unrotate(dquery, cosine, sine).reshape(length, width),
            unrotate(dkeys, cosine, sine).reshape(length, width),
            dvalues.reshape(length, width),
        ],
        0,
    ).astype(jnp.bfloat16)
    qkv_grad = jnp.einsum("sd,jsc->jdc", rows1, dpre, preferred_element_type=jnp.float32)
    bias_grad = jnp.sum(dpre, axis=1, dtype=jnp.float32)
    first_norm_gradient = sum_grads(
        jnp.einsum("jsc,jdc->sd", dpre, wqkv, preferred_element_type=jnp.float32)
    )
    first_scale_partial = jnp.sum(first_norm_gradient * first_standardized, 0)
    shift1_part = jnp.sum(first_norm_gradient, 0)
    token_gradient = (
        hidden_gradient
        + layer_norm_backward(
            first_norm_gradient, first_standardized, first_inverse_deviation, first_norm_scale
        )
    ).astype(jnp.bfloat16)
    qkvw_grad, qkvb_grad, outw_grad, gain1_total, shift1_total = (
        lax.psum_scatter(
            qkv_grad.astype(jnp.bfloat16), "dp", scatter_dimension=1, tiled=True
        ).astype(jnp.float32),
        lax.psum_scatter(
            bias_grad.astype(jnp.bfloat16), "dp", scatter_dimension=1, tiled=True
        ).astype(jnp.float32),
        lax.psum_scatter(
            out_grad.astype(jnp.bfloat16), "dp", scatter_dimension=1, tiled=True
        ).astype(jnp.float32),
        lax.psum_scatter(
            first_scale_partial.astype(jnp.bfloat16), "dp", scatter_dimension=0, tiled=True
        ).astype(jnp.float32),
        lax.psum_scatter(
            shift1_part.astype(jnp.bfloat16), "dp", scatter_dimension=0, tiled=True
        ).astype(jnp.float32),
    )
    gain1_grad, shift1_grad, gain2_grad, shift2_grad = lax.psum(
        (gain1_total, shift1_total, gain2_total, shift2_total), "tensor"
    )
    return (
        layer_output,
        token_gradient,
        qkvw_grad,
        qkvb_grad,
        outw_grad,
        gain1_grad,
        shift1_grad,
        gatew_grad,
        upw_grad,
        downw_grad,
        gain2_grad,
        shift2_grad,
    )


class LineScatter:
    def __init__(self, part, slot, chunks, d, z, line, send_sems, recv_sems):
        self.part, self.slot, self.chunks, self.d, self.z, self.line = part, slot, chunks, d, z, line
        self.ss, self.rs = send_sems, recv_sems

    def copy(self, s, h, way, target, place):
        return send(
            self.part(s, h), self.slot(place, h), self.ss.at[s, h], self.rs.at[place, h], self.d, target
        )

    def right(self, s, h):
        return self.copy(s, h, 0, self.z + 1, s)

    def left(self, s, h):
        return self.copy(s, h, 1, self.z - 1, jnp.where(self.z - 1 == s, self.line, s))

    def head(self, s):
        z, line = self.z, self.line
        for h in range(self.chunks):
            pl.when((z == 0) & (s > 0))(lambda: self.right(s, h).start())
            pl.when((z == line - 1) & (s < z))(lambda: self.left(s, h).start())

    def add(self, s, h):
        part = self.part(s, h)
        part[...] = (part[...].astype(F32) + self.slot(s, h)[...].astype(F32)).astype(BF)

    def relay(self, t):
        z, line = self.z, self.line
        up = line - 1 - t + z
        down = t - (line - 1 - z)
        for h in range(self.chunks):
            @pl.when((z > 0) & (up > z) & (up < line))
            def _():
                self.copy(z, h, 0, z, up).wait_recv()
                self.add(up, h)
                self.right(up, h).start()

            @pl.when((z < line - 1) & (down >= 0) & (down < z))
            def _():
                self.copy(z, h, 0, z, down).wait_recv()
                self.add(down, h)
                self.left(down, h).start()

    def arrive(self, h):
        z, line = self.z, self.line
        pl.when(z > 0)(lambda: self.copy(z, h, 0, z, z).wait_recv())
        pl.when(z < line - 1)(lambda: self.copy(z, h, 0, z, line).wait_recv())

    def total(self, h, rows):
        z = self.z
        return (
            self.part(z, h)[rows].astype(F32)
            + self.slot(z, h)[rows].astype(F32)
            + self.slot(self.line, h)[rows].astype(F32)
        )

    def finish(self):
        z = self.z
        for s in range(self.line):
            for h in range(self.chunks):
                pl.when(z != s)(lambda: self.copy(s, h, 0, z, s).wait_send())


def far_first(z, i):
    orders = ((3, 2, 1, 0), (3, 0, 2, 1), (0, 3, 1, 2), (0, 1, 2, 3))
    codes = [sum(s * 4**j for j, s in enumerate(o)) for o in orders]
    code = jnp.where(
        z == 0, codes[0], jnp.where(z == 1, codes[1], jnp.where(z == 2, codes[2], codes[3]))
    )
    power = jnp.where(i == 0, 1, jnp.where(i == 1, 4, jnp.where(i == 2, 16, 64)))
    return lax.rem(lax.div(code, power), 4)


class PlaneSum:
    def __init__(self, half, recv, d, z, flips, send_sems, recv_sems):
        self.half, self.recv, self.d, self.z, self.flips = half, recv, d, z, flips
        self.ss, self.rs = send_sems, recv_sems

    def copy(self, r):
        to, slot = self.d + self.flips[r], (r // 2 - 1) % self.recv.shape[0]
        return send(self.half.at[lax.div(to, 2)], self.recv.at[slot], self.ss.at[slot], self.rs.at[slot], to, self.z)

    def start(self, *which):
        for r in which:
            self.copy(r).start()

    def wait(self, *which):
        for r in which:
            self.copy(r).wait()


def mlp_kernel(
    n2, cot, cotnear, wgate, wup, wdown,
    dn2, mixed, mland, gex, uex, dex, ghalf, uhalf, dhalf, grecv, unear,
    nbuf, cbuf, gw, uw, dw, act, act_t, dga, dup, part, slots, mixbuf, wide, tall, wide_in, tall_in,
    ss, rs, css, crs, lss, lrs, local, lsem, mixsem, outsem, exs, exr, gss, grs, uss, urs,
):
    line = 4
    rows = n2.shape[0] // line
    model = n2.shape[1]
    hidden = wgate.shape[1]
    d, z, flips = place()
    greet(d, z, flips, line, (1, 2, 4, 6))
    core = lax.rem(d, 2)
    chip = lax.div(d, 2)
    parts = spans(hidden, 512)

    def rows_in(i):
        at = pl.ds(pl.multiple_of(far_first(z, i) * rows, rows), rows)
        return pltpu.make_async_copy(n2.at[at], nbuf.at[at], lsem.at[i])

    def columns_in(c):
        cols = pl.ds(*parts[c])
        return [
            pltpu.make_async_copy(wgate.at[:, cols], gw.at[:, cols], lsem.at[line + c]),
            pltpu.make_async_copy(wup.at[:, cols], uw.at[:, cols], lsem.at[line + len(parts) + c]),
        ]

    down_in = pltpu.make_async_copy(wdown, dw, lsem.at[line + 2 * len(parts)])
    first = [rows_in(jnp.int32(0))] + columns_in(0)
    for copy in first:
        copy.start()
    half = rows // 2
    scatter = LineScatter(
        lambda s, h: part.at[s, pl.ds(h * half, half)],
        lambda i, h: slots.at[i, pl.ds(h * half, half)],
        2, d, z, line, ss, rs,
    )
    pl.when(z == 0)(lambda: slots.__setitem__((0,), jnp.zeros((rows, model), BF)))
    pl.when(z == line - 1)(lambda: slots.__setitem__((line,), jnp.zeros((rows, model), BF)))
    cots = LineGather(
        lambda s, h: cbuf.at[pl.ds(pl.multiple_of(s * rows + h * half, half), half)], 2, d, z, line, css, crs
    )

    own_cot = pltpu.make_async_copy(cot, cbuf.at[pl.ds(pl.multiple_of(z * rows, rows), rows)], local.at[5])
    @pl.when((z > 0) & (z < line - 1))
    def _():
        cots.copy(z - 1, 0, 0, cotnear.at[z - 1, pl.ds(0, half)]).start()
        cots.copy(z + 1, 0, 1, cotnear.at[z + 1, pl.ds(0, half)]).start()

    cots.start(1, cot.at[pl.ds(half, half)])

    def first_half(s, k):
        return pltpu.make_async_copy(
            cotnear.at[s, pl.ds(0, half)], cbuf.at[pl.ds(pl.multiple_of(s * rows, rows), half)], local.at[8 + k]
        )

    for copy in first:
        copy.wait()
    for c in range(1, len(parts)):
        for copy in columns_in(c):
            copy.start()
    down_in.start()
    for i in range(1, line):
        rows_in(jnp.int32(i)).start()
    own_cot.start()
    pl.when(z > 0)(lambda: first_half(z - 1, 0).start())
    pl.when(z < line - 1)(lambda: first_half(z + 1, 1).start())

    def mixed_out(i):
        s = far_first(z, i)
        at = pl.ds(pl.multiple_of(s * rows, rows), rows)
        return pltpu.make_async_copy(mixbuf.at[lax.rem(i, 2)], mixed.at[at], mixsem.at[lax.rem(i, 2)])

    def mixed_ahead(i):
        at = pl.ds(pl.multiple_of(far_first(z, i) * rows, rows), rows)
        to = jnp.where(z == 0, 1, line - 2)
        return send(mixed.at[at], mland.at[i], lss.at[i], lrs.at[i], d, to)

    at_end = (z == 0) | (z == line - 1)

    @pl.loop(0, line)
    def _(i):
        s = far_first(z, i)
        at = pl.ds(pl.multiple_of(s * rows, rows), rows)
        pl.when(i > 0)(lambda: rows_in(i).wait())
        for c, (lo, size) in enumerate(parts):
            cols = pl.ds(lo, size)
            if c > 0:
                @pl.when(i == 0)
                def _():
                    for copy in columns_in(c):
                        copy.wait()

            gate = nn(nbuf[at, :], gw[:, cols])
            up = nn(nbuf[at, :], uw[:, cols])
            sigma = lax.logistic(gate)
            silu = gate * sigma
            value = (silu * up).astype(BF)
            act[:, cols] = value
            act_t[cols, at] = value.T
            dga[at, cols] = (up * (sigma * (1.0 + gate * (1.0 - sigma)))).astype(BF)
            dup[at, cols] = silu.astype(BF)
        pl.when(i == 0)(lambda: down_in.wait())
        for lo, size in spans(model, 512):
            mixbuf[lax.rem(i, 2), :, pl.ds(lo, size)] = nn(act[...], dw[:, pl.ds(lo, size)]).astype(BF)
        mixed_out(i).start()
        mixed_out(i).wait()
        pl.when(at_end & (i < 2))(lambda: mixed_ahead(i).start())
        pl.when(i == 0)(lambda: cots.step(2, 0))
        pl.when(i == 1)(lambda: cots.step(1, 1))
        pl.when(i == 2)(lambda: cots.step(2, 1))

    def add_mixed(s, slot, send_slot, to, lands):
        at = pl.ds(pl.multiple_of(s * rows, rows), rows)
        ins = [
            pltpu.make_async_copy(mixed.at[at], mixbuf.at[0], mixsem.at[0]),
            pltpu.make_async_copy(mland.at[slot], mixbuf.at[1], mixsem.at[1]),
        ]
        for copy in ins:
            copy.start()
        for copy in ins:
            copy.wait()

        @pl.loop(0, rows // 32)
        def _(i):
            piece = pl.ds(pl.multiple_of(i * 32, 32), 32)
            mixbuf[0, piece, :] = (mixbuf[0, piece, :].astype(F32) + mixbuf[1, piece, :].astype(F32)).astype(BF)

        back = pltpu.make_async_copy(mixbuf.at[0], mixed.at[at], mixsem.at[0])
        back.start()
        back.wait()
        send(mixed.at[at], mland.at[lands], lss.at[send_slot], lrs.at[lands], d, to).start()

    def landing(slot, send_slot):
        return send(mland.at[slot], mland.at[slot], lss.at[send_slot], lrs.at[slot], d, z)

    other = line - 1 - z
    edge = jnp.where(z == 1, 0, line - 1)

    def mixed_on(i):
        @pl.when(~at_end)
        def _():
            landing(i, i).wait_recv()
            add_mixed(line - 1 - edge if i == 0 else other, i, 2 + i, other, 2 + i)

    def mixed_relay():
        @pl.when(~at_end)
        def _():
            landing(2, 2).wait_recv()
            add_mixed(edge, 2, 0, edge, 3)

    mixed_on(0)
    own_cot.wait()

    @pl.loop(0, line)
    def _(i):
        @pl.when(i == 1)
        def _():
            pl.when(z > 0)(lambda: first_half(z - 1, 0).wait())
            pl.when(z < line - 1)(lambda: first_half(z + 1, 1).wait())
            for h in range(2):
                cots.step(3, h)

        s = far_first(z, lax.rem(i + line - 1, line))
        at = pl.ds(pl.multiple_of(s * rows, rows), rows)
        for lo, size in spans(hidden, 512):
            cols = pl.ds(lo, size)
            dact = nt(cbuf[at, :], dw[cols, :])
            dga[at, cols] = (dact * dga[at, cols].astype(F32)).astype(BF)
            dup[at, cols] = (dact * dup[at, cols].astype(F32)).astype(BF)
        for lo, size in spans(model, 512):
            cols = pl.ds(lo, size)
            part[s, :, cols] = (nt(dga[at, :], gw[cols, :]) + nt(dup[at, :], uw[cols, :])).astype(BF)
        scatter.head(s)

    blocks = model // rows // 2

    def exchanged(m):
        outs = (ghalf, uhalf, dhalf)
        exes = (gex, uex, dex)
        stage = tall if m == 2 else wide
        stage_in = tall_in if m == 2 else wide_in

        def block(t):
            cols = pl.ds(pl.multiple_of(t * rows, rows), rows)
            if m == 2:
                return lambda lo, size: nn(act_t[pl.ds(lo, size), :], cbuf[:, cols])
            right = dga if m == 0 else dup
            return lambda lo, size: tn(nbuf[:, cols], right[:, pl.ds(lo, size)])

        def piece(ref, lo, size):
            return ref.at[pl.ds(lo, size), :] if m == 2 else ref.at[:, pl.ds(lo, size)]

        def away(k):
            slot = lax.rem(k, 2)
            return send(stage.at[slot], exes[m].at[k], exs.at[m, k], exr.at[m, k], d + flips[1], z)

        @pl.loop(0, blocks)
        def _(k):
            slot = lax.rem(k, 2)
            pl.when(k >= 2)(lambda: away(k - 2).wait_send())
            make = block(2 * k + 1 - core)
            for lo, size in spans(hidden, 512):
                piece(stage.at[slot], lo, size)[...] = make(lo, size).astype(BF)
            away(k).start()

        away(blocks - 2).wait_send()
        away(blocks - 1).wait_send()

        def chip_at(j):
            return lax.rem(chip + 1 + j, blocks)

        def store(j):
            slot = lax.rem(j, 2)
            return pltpu.make_async_copy(stage.at[slot], outs[m].at[chip_at(j)], outsem.at[slot])

        def onward(j):
            k = chip_at(j)
            return send(ghalf.at[k], grecv.at[blocks - 2 - j], gss.at[j], grs.at[blocks - 2 - j], 2 * k + core, z)

        @pl.loop(0, blocks)
        def _(j):
            slot = lax.rem(j, 2)
            k = chip_at(j)

            @pl.when(j >= 2)
            def _():
                store(j - 2).wait()
                if m == 0:
                    onward(j - 2).start()

            away(k).wait_recv()
            fetch = pltpu.make_async_copy(exes[m].at[k], stage_in, local.at[4])
            fetch.start()
            fetch.wait()
            make = block(2 * k + core)
            for lo, size in spans(hidden, 512):
                piece(stage.at[slot], lo, size)[...] = (
                    make(lo, size) + piece(stage_in, lo, size)[...].astype(F32)
                ).astype(BF)
            store(j).start()

        for j in (blocks - 2, blocks - 1):
            store(j).wait()
            if m == 0 and j < blocks - 1:
                onward(j).start()
        return onward

    mixed_on(1)
    onward = exchanged(0)
    scatter.relay(1)
    mixed_relay()

    exchanged(1)
    ups = PlaneSum(uhalf, unear, d, z, flips, uss, urs)
    ups.start(2, 4)
    scatter.relay(2)
    exchanged(2)
    for h in range(2):
        scatter.arrive(h)

        @pl.loop(0, half // 32)
        def _(i):
            rows_at = pl.ds(pl.multiple_of(i * 32, 32), 32)
            dn2[pl.ds(pl.multiple_of(h * half + i * 32, 32), 32), :] = scatter.total(h, rows_at)

    scatter.finish()
    for i in range(2):
        pl.when(at_end)(lambda: mixed_ahead(i).wait_send())
    for i in (0, 2, 3):
        pl.when(~at_end)(lambda: landing(3, i).wait_send())
    landing(3, 3).wait_recv()
    for k, h in ((0, 1), (1, 0), (1, 1), (2, 0), (2, 1)):
        pl.when((z - k >= 0) & (z < line - 1))(lambda: cots.copy(z - k, h, 0).wait_send())
        pl.when((z + k < line) & (z > 0))(lambda: cots.copy(z + k, h, 1).wait_send())
    for j in range(blocks - 1):
        onward(j).wait()
    ups.wait(2, 4)


def mlp(n2, cot, cotnear, wgate, wup, wdown):
    length, model = n2.shape
    hidden = wgate.shape[1]
    line = 4
    rows = length // line
    blocks = model // rows // 2
    sds = jax.ShapeDtypeStruct
    wide = sds((blocks, rows, hidden), BF)
    tall = sds((blocks, hidden, rows), BF)
    return pl.pallas_call(
        mlp_kernel,
        out_shape=(
            sds((rows, model), F32), sds((length, model), BF), sds((4, rows, model), BF),
            wide, wide, tall, wide, wide, tall, sds((blocks - 1, rows, hidden), BF), sds((2, rows, hidden), BF),
        ),
        in_specs=[ANY] * 6,
        out_specs=(INV,) + (ANY,) * 10,
        scratch_shapes=[
            pltpu.VMEM((length, model), BF),
            pltpu.VMEM((length, model), BF),
            pltpu.VMEM((model, hidden), BF),
            pltpu.VMEM((model, hidden), BF),
            pltpu.VMEM((hidden, model), BF),
            pltpu.VMEM((rows, hidden), BF),
            pltpu.VMEM((hidden, length), BF),
            pltpu.VMEM((length, hidden), BF),
            pltpu.VMEM((length, hidden), BF),
            pltpu.VMEM((line, rows, model), BF),
            pltpu.VMEM((line + 1, rows, model), BF),
            pltpu.VMEM((2, rows, model), BF),
            pltpu.VMEM((2, rows, hidden), BF),
            pltpu.VMEM((2, hidden, rows), BF),
            pltpu.VMEM((rows, hidden), BF),
            pltpu.VMEM((hidden, rows), BF),
            pltpu.SemaphoreType.DMA((line, 2)),
            pltpu.SemaphoreType.DMA((line + 1, 2)),
            pltpu.SemaphoreType.DMA((2, line, 2)),
            pltpu.SemaphoreType.DMA((line, 2)),
            pltpu.SemaphoreType.DMA((4,)),
            pltpu.SemaphoreType.DMA((4,)),
            pltpu.SemaphoreType.DMA((10,)),
            pltpu.SemaphoreType.DMA((line + 1 + 2 * len(spans(hidden, 512)),)),
            pltpu.SemaphoreType.DMA((2,)),
            pltpu.SemaphoreType.DMA((2,)),
            pltpu.SemaphoreType.DMA((3, blocks)),
            pltpu.SemaphoreType.DMA((3, blocks)),
            pltpu.SemaphoreType.DMA((blocks,)),
            pltpu.SemaphoreType.DMA((blocks,)),
            pltpu.SemaphoreType.DMA((2,)),
            pltpu.SemaphoreType.DMA((2,)),
        ],
        compiler_params=pltpu.CompilerParams(
            collective_id=2, has_side_effects=True, vmem_limit_bytes=62 * 1024 * 1024
        ),
        cost_estimate=pl.CostEstimate(flops=10**11, bytes_accessed=10**8, transcendentals=0),
        name="mlp",
    )(n2, cot, cotnear, wgate, wup, wdown)


def norm_parts(x):
    centred = x - jnp.mean(x, -1, keepdims=True)
    inverse = lax.rsqrt(jnp.mean(centred * centred, -1, keepdims=True) + 1e-05)
    return centred * inverse, inverse


def norm_back(grad, standard, inverse, gain):
    scaled = grad * gain
    return inverse * (
        scaled
        - jnp.mean(scaled, -1, keepdims=True)
        - standard * jnp.mean(scaled * standard, -1, keepdims=True)
    )


def each_piece(rows, piece, body):
    @pl.loop(0, rows // piece)
    def _(i):
        body(pl.ds(pl.multiple_of(i * piece, piece), piece))


class PlaneChain:
    def __init__(self, half, recv, mid, d, z, flips, send_sems, recv_sems):
        self.half, self.recv, self.mid, self.d, self.z, self.flips = half, recv, mid, d, z, flips
        self.ss, self.rs = send_sems, recv_sems
        self.rows = half.shape[1] // 2

    def block(self, r):
        return lax.div(self.d + self.flips[r], 2)

    def copy(self, key):
        block, over, part = ((6, 2, 0), (6, 4, 1), (4, 4, 1), (2, 2, 0), (4, 4, 0), (2, 2, 1))[key]
        at = pl.ds(part * self.rows, self.rows)
        dst = self.mid.at[key] if key < 2 else self.recv.at[0 if over == 2 else 1, at]
        return send(
            self.half.at[self.block(block), at], dst, self.ss.at[key], self.rs.at[key], self.d + self.flips[over], self.z
        )

    def start(self):
        for key in range(4):
            self.copy(key).start()

    def relay(self):
        for key, block, part in ((0, 4, 0), (1, 2, 1)):
            self.copy(key).wait_recv()
            k = self.block(block)
            piece = min(self.rows, 128)

            @pl.loop(0, self.rows // piece)
            def _(i):
                at = pl.ds(pl.multiple_of(part * self.rows + i * piece, piece), piece)
                mid = self.mid[key, pl.ds(pl.multiple_of(i * piece, piece), piece), :]
                self.half[k, at, :] = (self.half[k, at, :].astype(F32) + mid.astype(F32)).astype(BF)

            self.copy(key + 4).start()

    def arrive(self):
        for key in range(2, 6):
            self.copy(key).wait_recv()

    def total(self, at):
        return (
            self.half[(self.block(0),) + at].astype(F32)
            + self.recv[(0,) + at].astype(F32)
            + self.recv[(1,) + at].astype(F32)
        )

    def finish(self):
        for key in range(6):
            self.copy(key).wait_send()


class BlockSum:
    def __init__(self, own, recv, bufs, stage, out, in_sems, out_sems):
        self.ins = [own] + recv
        self.bufs, self.stage, self.out, self.in_sems, self.out_sems = bufs, stage, out, in_sems, out_sems

    def copies(self):
        return [pltpu.make_async_copy(a, b, self.in_sems.at[i]) for i, (a, b) in enumerate(zip(self.ins, self.bufs))]

    def fetch(self):
        for copy in self.copies():
            copy.start()

    def store(self, i):
        rows = self.stage.shape[1]
        at = pl.ds(pl.multiple_of(i * rows, rows), rows)
        return pltpu.make_async_copy(self.stage.at[lax.rem(i, 2)], self.out.at[at], self.out_sems.at[lax.rem(i, 2)])

    def add(self):
        for copy in self.copies():
            copy.wait()
        rows = self.stage.shape[1]
        pieces = self.out.shape[0] // rows
        small = 32

        @pl.loop(0, pieces)
        def _(i):
            pl.when(i >= 2)(lambda: self.store(i - 2).wait())

            @pl.loop(0, rows // small)
            def _(j):
                at = pl.ds(pl.multiple_of(i * rows + j * small, small), small)
                total = self.bufs[0][at, :].astype(F32)
                for buf in self.bufs[1:]:
                    total = total + buf[at, :].astype(F32)
                self.stage[lax.rem(i, 2), pl.ds(pl.multiple_of(j * small, small), small), :] = total

            self.store(i).start()

        self.store(jnp.int32(pieces - 2)).wait()
        self.store(jnp.int32(pieces - 1)).wait()


def attention_back_kernel(
    hid, small, lse_t, cos, sin, dn2, cot, tok, wout, attall, qkv, mixed, mland, ghalf, grecv, uhalf, unear, dhalf, wqkv, n1,
    tgrad, ograd, gains, bout, lay, ggrad, ugrad, dgrad, qgrad, urecv, drecv, oex, qex,
    wo, da, dhid, attr, att_t, attc, qbuf, dsend, datt, part, slots, marr, ofull, osum, orecv, omid, ozr,
    dq, dpre, nbuf, qstage, qfetch, qsum, qrecv, qmid, wide_sum, tall_sum, qtotal, sums, zsums, dsums, bsums,
    mss, mrs, ass, ars, oss, ors, pss, prs, uss, urs, zss, zrs,
    ss, rs, xss, xrs, qss, qrs, dss, drs, yss, yrs, gss, grs, bss, brs, local, tsem, fsem, gsem,
):
    line = 4
    rows, model = hid.shape
    length = rows * line
    width = attc.shape[1]
    pairs = width // 128
    blocks = model // rows // 2
    half = rows // 2
    d, z, flips = place()
    greet(d, z, flips, line, range(1, 8))
    core = lax.rem(d, 2)
    ups = PlaneSum(uhalf, urecv, d, z, flips, uss, urs)
    downs = PlaneSum(dhalf, drecv, d, z, flips, dss, drs)
    loads = [
        pltpu.make_async_copy(wout, wo, local.at[4]),
        pltpu.make_async_copy(attall.at[pl.ds(pl.multiple_of(z * rows, rows), rows)], attr, local.at[5]),
        pltpu.make_async_copy(attall.at[:, pl.ds(pl.multiple_of(z * width, width), width)], attc, local.at[6]),
        pltpu.make_async_copy(qkv, qbuf, local.at[7]),
    ]
    rows_in = [pltpu.make_async_copy(dn2, dhid, local.at[11]), pltpu.make_async_copy(cot, da, local.at[12])]
    for copy in rows_in:
        copy.start()

    at_end = (z == 0) | (z == line - 1)
    inner = jnp.where(z == 0, 1, line - 2)

    def mixed_last(h):
        at = pl.ds(pl.multiple_of(inner * rows + h * half, half), half)
        return send(mixed.at[at], marr.at[pl.ds(h * half, half)], mss.at[h], mrs.at[h], d, inner)

    pl.when(at_end)(lambda: mixed_last(0).start())
    pl.when(at_end)(lambda: marr.__setitem__(Ellipsis, jnp.zeros((rows, model), BF)))
    for copy in loads:
        copy.start()
    ups.start(6)
    downs.start(2, 4, 6)

    def chain(part, slots, send_sems, recv_sems):
        pl.when(z == 0)(lambda: slots.__setitem__((0,), jnp.zeros((rows, model), BF)))
        pl.when(z == line - 1)(lambda: slots.__setitem__((line,), jnp.zeros((rows, model), BF)))
        return LineScatter(
            lambda s, h: part.at[s, pl.ds(h * half, half)],
            lambda i, h: slots.at[i, pl.ds(h * half, half)],
            2, d, z, line, send_sems, recv_sems,
        )

    for copy in rows_in:
        copy.wait()
    sums[...] = jnp.zeros_like(sums)

    def back(at):
        grad = dhid[at, :]
        standard, inverse = norm_parts(hid[at, :])
        sums[2:3, :] += jnp.sum(grad * standard, 0, keepdims=True)
        sums[3:4, :] += jnp.sum(grad, 0, keepdims=True)
        total = da[at, :].astype(F32) + norm_back(grad, standard, inverse, small[2:3, :])
        dhid[at, :] = total
        da[at, :] = total.astype(BF)

    each_piece(rows, 32, back)
    for copy in loads:
        copy.wait()

    def away(k, p):
        to = lax.rem(z + k, line)
        cols = pl.ds(p * 128, 128)
        return send(
            dsend.at[to, :, cols], datt.at[pl.ds(pl.multiple_of(z * rows, rows), rows), cols],
            ass.at[k, p], ars.at[z, p], d, to,
        )

    def taken(k, p):
        frm = lax.rem(z + k, line)
        cols = pl.ds(pl.multiple_of(p * 128, 128), 128)
        return send(
            dsend.at[frm, :, cols], datt.at[pl.ds(pl.multiple_of(frm * rows, rows), rows), cols],
            ass.at[k, p], ars.at[frm, p], d, frm,
        )

    @pl.loop(1, line + 1)
    def _(k):
        to = lax.rem(z + k, line)
        dsend[to] = nt(da[...], wo[pl.ds(pl.multiple_of(to * width, width), width), :]).astype(BF)

    for p in range(pairs):
        for k in range(1, line):
            away(k, p).start()
    pl.when(at_end)(lambda: mixed_last(1).start())
    weights_in = pltpu.make_async_copy(wqkv, wo.at[:, pl.ds(0, 3 * width)], local.at[4])
    weights_in.start()
    datt[pl.ds(pl.multiple_of(z * rows, rows), rows), :] = dsend[z]
    for lo, size in spans(model, 512):
        att_t[pl.ds(lo, size), :] = attr[:, pl.ds(lo, size)].T
    tok_in = pltpu.make_async_copy(tok, attr, local.at[6])
    tok_in.start()

    def oblock(t):
        return nn(att_t[...], da[:, pl.ds(pl.multiple_of(t * rows, rows), rows)])

    def ostage(k):
        return wo.at[:, pl.ds(pl.multiple_of(3 * width + lax.rem(k, 2) * rows, rows), rows)]

    def oacross(k):
        return send(ostage(k), oex.at[k], oss.at[k], ors.at[k], d + flips[1], z)

    @pl.loop(0, blocks)
    def _(k):
        pl.when(k >= 2)(lambda: oacross(k - 2).wait_send())
        ostage(k)[...] = oblock(2 * k + 1 - core).astype(BF)
        oacross(k).start()

    lanes = lax.broadcasted_iota(jnp.int32, (1, 128), 1)
    mine = (lanes < 64, lanes >= 64)
    which = lax.broadcasted_iota(jnp.int32, (16, 128), 0)
    lane16 = lax.broadcasted_iota(jnp.int32, (16, 128), 1)
    pick = jnp.where(which == lax.div(lane16, 64), 1.0, 0.0).astype(BF)
    scale = HEAD_DIM**-0.5

    def zaway(k):
        to = lax.rem(z + k, line)
        return send(
            ofull.at[pl.ds(pl.multiple_of(to * width, width), width)], ozr.at[k - 1], zss.at[k], zrs.at[k - 1], d, to
        )

    def plane_total():
        oplanes.arrive()

        def add(at):
            ofull[at, :] = oplanes.total((at, slice(None))).astype(BF)

        each_piece(model, 256, add)
        for k in range(1, line):
            zaway(k).start()

    def back_pair(p):
        cols = pl.ds(pl.multiple_of(p * 128, 128), 128)
        do = datt[:, cols]
        prod = do.astype(F32) * attc[:, cols].astype(F32)
        high = prod.astype(BF)
        inner = nt(pick, high) + nt(pick, (prod - high.astype(F32)).astype(BF))
        q = qbuf[0, p] * BF(scale)
        dq[...] = jnp.zeros_like(dq)
        for kj in range(line):
            at = pl.ds(kj * rows, rows)
            lo, count = kj * rows, length - kj * rows
            k, v = qbuf[1, p, at, :], qbuf[2, p, at, :]
            row = lax.broadcasted_iota(jnp.int32, (rows, count), 0)
            col = lax.broadcasted_iota(jnp.int32, (rows, count), 1)
            keep = col >= row
            dk = jnp.zeros((rows, 128), F32)
            dv = jnp.zeros((rows, 128), F32)
            for a in range(2):
                km, vm = jnp.where(mine[a], k, BF(0)), jnp.where(mine[a], v, BF(0))
                qm, dm = jnp.where(mine[a], q[lo:], BF(0)), jnp.where(mine[a], do[lo:], BF(0))
                s = jnp.where(keep, nt(km, q[lo:]), -1e30)
                probs = jnp.exp(s - lse_t[pl.ds(2 * p + a, 1), pl.ds(lo, count)])
                dv += nn(probs.astype(BF), dm)
                dprobs = nt(vm, do[lo:])
                ds = (probs * (dprobs - inner[a : a + 1, lo:])).astype(BF)
                dk += nn(ds, qm)
                dq[pl.ds(lo, count), :] += tn(ds, km)
            dk = turn(dk, cos[at, :], sin[at, :], -1.0)
            dpre[at, pl.ds(pl.multiple_of(width + p * 128, 128), 128)] = dk.astype(BF)
            dpre[at, pl.ds(pl.multiple_of(2 * width + p * 128, 128), 128)] = dv.astype(BF)
        dpre[:, cols] = turn(dq[...] * scale, cos[...], sin[...], -1.0).astype(BF)

    @pl.loop(0, pairs)
    def _(p):
        for k in range(1, line):
            taken(k, p).wait_recv()
        back_pair(p)


    oacross(blocks - 2).wait_send()
    oacross(blocks - 1).wait_send()
    weights_in.wait()
    chains = chain(part, slots, ss, rs)

    @pl.loop(0, line)
    def _(i):
        s = far_first(z, i)
        at = pl.ds(pl.multiple_of(s * rows, rows), rows)
        for lo, size in spans(model, 512):
            part[s, :, pl.ds(lo, size)] = nt(dpre[at, :], wo[pl.ds(lo, size), pl.ds(0, 3 * width)]).astype(BF)
        chains.head(s)

    hidden = uhalf.shape[2]
    chip = lax.div(d, 2)

    def wide(i):
        return [wo.at[pl.ds((i + k) * rows, rows), pl.ds(0, hidden)] for k in range(blocks)]

    gate_sum = BlockSum(ghalf.at[chip], [grecv.at[k] for k in range(blocks - 1)], wide(0), wide_sum, ggrad, fsem.at[0], gsem)
    up_sum = BlockSum(uhalf.at[chip], [unear.at[0], unear.at[1], urecv.at[0]], wide(blocks), wide_sum, ugrad, fsem.at[1], gsem)
    tall = [osum.at[k, pl.ds(0, hidden)] for k in range(blocks)]
    down_sum = BlockSum(dhalf.at[chip], [drecv.at[k] for k in range(blocks - 1)], tall, tall_sum, dgrad, fsem.at[2], gsem)
    gate_sum.fetch()
    mixed_in = [
        pltpu.make_async_copy(mixed.at[pl.ds(pl.multiple_of(z * rows, rows), rows)], wo.at[pl.ds(4 * rows, rows)], local.at[0]),
        pltpu.make_async_copy(mland.at[3], wo.at[pl.ds(5 * rows, rows)], local.at[1]),
    ]
    for copy in mixed_in:
        copy.start()

    oplanes = PlaneChain(osum, orecv, omid, d, z, flips, pss, prs)

    @pl.loop(0, blocks)
    def _(k):
        oacross(k).wait_recv()
        fetch = pltpu.make_async_copy(oex.at[k], ofull, local.at[8])
        fetch.start()
        fetch.wait()
        osum[k] = (oblock(2 * k + core) + ofull[...].astype(F32)).astype(BF)

    oplanes.start()
    def tile_in(i):
        t = 2 * lax.rem(i, blocks) + jnp.where(i < blocks, 1 - core, core)
        cols = pl.ds(pl.multiple_of(t * rows, rows), rows)
        return pltpu.make_async_copy(n1.at[:, cols], nbuf.at[lax.rem(i, 2)], tsem.at[lax.rem(i, 2)])

    def qblock(i):
        tile_in(i).wait()
        pl.when(i < 2 * blocks - 1)(lambda: tile_in(i + 1).start())
        return lambda lo, size: tn(nbuf[lax.rem(i, 2)], dpre[:, pl.ds(lo, size)])

    tile_in(jnp.int32(0)).start()

    def qacross(k):
        return send(qstage.at[lax.rem(k, 2)], qex.at[k], xss.at[k], xrs.at[k], d + flips[1], z)

    @pl.loop(0, blocks)
    def _(k):
        pl.when(k >= 2)(lambda: qacross(k - 2).wait_send())
        make = qblock(k)
        for lo, size in spans(3 * width, 512):
            qstage[lax.rem(k, 2), :, pl.ds(lo, size)] = make(lo, size).astype(BF)
        qacross(k).start()

    chains.relay(1)
    qplanes = PlaneChain(qsum, qrecv, qmid, d, z, flips, qss, qrs)

    @pl.loop(0, blocks)
    def _(k):
        qacross(k).wait_recv()
        fetch = pltpu.make_async_copy(qex.at[k], qfetch, local.at[8])
        fetch.start()
        fetch.wait()
        make = qblock(k + blocks)
        for lo, size in spans(3 * width, 512):
            qsum[k, :, pl.ds(lo, size)] = (make(lo, size) + qfetch[:, pl.ds(lo, size)].astype(F32)).astype(BF)

    qplanes.start()
    oplanes.relay()
    for h in range(2):
        pl.when(~at_end)(lambda: mixed_last(h).wait_recv())

    for copy in mixed_in:
        copy.wait()

    @pl.loop(0, rows // 32)
    def _(i):
        at = pl.ds(pl.multiple_of(i * 32, 32), 32)
        total = marr[at, :].astype(F32)
        for k in (4, 5):
            total = total + wo[pl.ds(pl.multiple_of(k * rows + i * 32, 32), 32), :].astype(F32)
        da[at, :] = (hid[at, :] + total).astype(BF)

    lay_out = pltpu.make_async_copy(da, lay, local.at[0])
    lay_out.start()
    bsums[0] = jnp.zeros(bsums.shape[1:], F32)

    def bias(at):
        bsums[0, 0:1, :] += jnp.sum(dpre[at, :].astype(F32), 0, keepdims=True)

    each_piece(length, 64, bias)

    def bcopy(r):
        return send(bsums.at[0], bsums.at[r], bss.at[r], brs.at[r], d + flips[r], z)

    for r in range(1, 8):
        bcopy(r).start()
    ups.wait(6)
    up_sum.fetch()
    gate_sum.add()
    chains.relay(2)
    qplanes.relay()
    up_sum.add()
    plane_total()
    total = jnp.zeros(bout.shape, F32)
    for r in range(8):
        if r:
            bcopy(r).wait()
        total = total + bsums[r]
    bout[...] = total
    tok_in.wait()
    for h in range(2):
        chains.arrive(h)
        @pl.loop(0, half // 32)
        def _(i):
            at = pl.ds(pl.multiple_of(h * half + i * 32, 32), 32)
            grad = chains.total(h, pl.ds(pl.multiple_of(i * 32, 32), 32))
            standard, inverse = norm_parts(attr[at, :].astype(F32))
            sums[0:1, :] += jnp.sum(grad * standard, 0, keepdims=True)
            sums[1:2, :] += jnp.sum(grad, 0, keepdims=True)
            tgrad[at, :] = (dhid[at, :] + norm_back(grad, standard, inverse, small[0:1, :])).astype(BF)

    depth = gains.shape[1]

    def columns(i):
        return sums.at[:, pl.ds(pl.multiple_of(i * depth, 256), depth)]

    def dcopy(r):
        return send(columns(d + flips[r]), dsums.at[r], gss.at[r], grs.at[r], d + flips[r], z)

    def zcopy(k):
        return send(zsums.at[0], zsums.at[k], yss.at[k], yrs.at[k], d, lax.rem(z + k, line))

    for r in range(1, 8):
        dcopy(r).start()
    qplanes.arrive()
    piece = qtotal.shape[1]

    @pl.loop(0, rows // piece)
    def _(i):
        at = pl.ds(pl.multiple_of(i * piece, piece), piece)
        for j in range(3):
            qtotal[j] = qplanes.total((at, pl.ds(j * width, width)))
        back = pltpu.make_async_copy(qtotal, qgrad.at[:, at], local.at[1])
        back.start()
        back.wait()

    oplanes.finish()
    downs.wait(2, 4, 6)
    down_sum.fetch()
    total = columns(d)[...]
    for r in range(1, 8):
        dcopy(r).wait()
        total = total + dsums[r]
    zsums[0] = total
    for k in range(1, line):
        zcopy(k).start()
    down_sum.add()
    for k in range(1, line):
        zcopy(k).wait()
        total = total + zsums[k]
    gains[...] = total
    total = ofull[pl.ds(pl.multiple_of(z * width, width), width), :].astype(F32)
    for k in range(1, line):
        zaway(k).wait()
        total = total + ozr[k - 1].astype(F32)
    ograd[...] = total
    for k in range(1, line):
        for p in range(pairs):
            away(k, p).wait_send()
    qplanes.finish()
    qacross(blocks - 2).wait_send()
    qacross(blocks - 1).wait_send()
    lay_out.wait()
    for h in range(2):
        pl.when(at_end)(lambda: mixed_last(h).wait_send())
    chains.finish()


def attention_backward(dn2, hid, cot, small, lse, tok, tabs, wout, attall, qkv, mixed, mland, ghalf, grecv, uhalf, unear, dhalf, wqkv, n1):
    rows, model = hid.shape
    line = 4
    length = rows * line
    width = model // line
    pairs = width // 128
    blocks = model // rows // 2
    hidden = uhalf.shape[2]
    sds = jax.ShapeDtypeStruct
    dma = pltpu.SemaphoreType.DMA
    vmem = pltpu.VMEM
    return pl.pallas_call(
        attention_back_kernel,
        out_shape=(
            sds((rows, model), BF), sds((width, rows), F32),
            sds((8, rows), F32), sds((8, 3 * width), F32), sds((rows, model), BF),
            sds((rows, hidden), F32), sds((rows, hidden), F32), sds((hidden, rows), F32), sds((3, rows, width), F32),
            sds((1, rows, hidden), BF), sds((blocks - 1, hidden, rows), BF),
            sds((blocks, model, rows), BF), sds((blocks, rows, 3 * width), BF),
        ),
        in_specs=[INV] * 5 + [ANY] * 15,
        out_specs=(INV,) * 4 + (ANY,) * 9,
        scratch_shapes=[
            vmem((model, model), BF), vmem((rows, model), BF), vmem((rows, model), F32), vmem((rows, model), BF),
            vmem((model, rows), BF), vmem((length, width), BF), vmem((3, pairs, length, 128), BF),
            vmem((line, rows, width), BF), vmem((length, width), BF),
            vmem((line, rows, model), BF), vmem((line + 1, rows, model), BF),
            vmem((rows, model), BF),
            vmem((model, rows), BF), vmem((blocks, model, rows), BF),
            vmem((2, model, rows), BF), vmem((2, model // 2, rows), BF),
            vmem((line - 1, width, rows), BF),
            vmem((length, 128), F32), vmem((length, 3 * width), BF), vmem((2, length, rows), BF),
            vmem((2, rows, 3 * width), BF), vmem((rows, 3 * width), BF), vmem((blocks, rows, 3 * width), BF),
            vmem((2, rows, 3 * width), BF), vmem((2, rows // 2, 3 * width), BF),
            vmem((2, 64, hidden), F32), vmem((2, hidden // 4, rows), F32), vmem((3, 64, width), F32),
            vmem((8, model), F32), vmem((line, 8, rows), F32), vmem((8, 8, rows), F32), vmem((8, 8, 3 * width), F32),
            dma((2,)), dma((2,)), dma((line, pairs)), dma((line, pairs)), dma((blocks,)), dma((blocks,)),
            dma((6,)), dma((6,)), dma((3,)), dma((3,)), dma((line,)), dma((line,)),
            dma((line, 2)), dma((line + 1, 2)), dma((blocks,)), dma((blocks,)), dma((6,)), dma((6,)),
            dma((3,)), dma((3,)), dma((line,)), dma((line,)), dma((8,)), dma((8,)), dma((8,)), dma((8,)), dma((13,)), dma((2,)),
            dma((3, blocks)), dma((2,)),
        ],
        compiler_params=pltpu.CompilerParams(
            collective_id=3, has_side_effects=True, vmem_limit_bytes=63 * 1024 * 1024
        ),
        cost_estimate=pl.CostEstimate(flops=10**11, bytes_accessed=10**8, transcendentals=0),
        name="attention_backward",
    )(hid, small, lse, *tabs, dn2, cot, tok, wout, attall, qkv, mixed, mland, ghalf, grecv, uhalf, unear, dhalf, wqkv, n1)


def turn_tables(length):
    half = ROT // 2
    freqs = np.float32(10000.0) ** (-np.arange(0, ROT, 2, dtype=np.float32) / np.float32(ROT))
    angles = np.arange(length, dtype=np.float32)[:, None] * freqs[None, :]
    cos = np.ones((length, HEAD_DIM), np.float32)
    sin = np.zeros((length, HEAD_DIM), np.float32)
    cos[:, :half] = cos[:, half:ROT] = np.cos(angles)
    sin[:, half:ROT] = np.sin(angles)
    sin[:, :half] = -np.sin(angles)
    return tuple(jnp.asarray(np.tile(t, (1, 2))) for t in (cos, sin))


def pack_smalls(d, model, width, qkv_bias, *vectors):
    col = lax.broadcasted_iota(jnp.int32, (1, model), 1)
    each = vectors[0].shape[0]
    gains = jnp.stack([jnp.tile(v, model // each) for v in vectors], 0)
    gains = jnp.where(col // each == d, gains, 0)
    part = qkv_bias.shape[1]
    bias = jnp.tile(qkv_bias, (1, width // part)).reshape(1, 3 * width)
    bias = jnp.pad(bias, ((0, 0), (0, model - 3 * width)))
    bias = jnp.where(col % width // part == d, bias, 0)
    return jnp.concatenate([gains, bias, jnp.zeros((11, model), BF)], 0).astype(BF)


def fast(
    tokens, qkv_weight, qkv_bias, out_weight, norm1_gain, norm1_shift, gate_weight, up_weight,
    down_weight, norm2_gain, norm2_shift, cotangent,
):
    d = lax.axis_index("dp")
    rows, model = tokens.shape
    length = 4 * rows
    tabs = turn_tables(length)
    depth, width = qkv_weight.shape[1:]
    smalls = pack_smalls(d, model, width, qkv_bias, norm1_gain, norm1_shift, norm2_gain, norm2_shift)
    cotnear, n1, qkv, lse, attall, wqkv, small, wout, n2, hidden, wgate, wup, wdown = attention_forward(
        tokens, cotangent, qkv_weight, out_weight, gate_weight, up_weight, down_weight, smalls, tabs
    )
    dn2, mixed, mland, _, _, _, ghalf, uhalf, dhalf, grecv, unear = mlp(n2, cotangent, cotnear, wgate, wup, wdown)
    (
        token_gradient, outw_grad, gains, bias, layer_output, gatew_grad, upw_grad, downw_grad, qkvw_grad, _, _, _, _
    ) = attention_backward(
        dn2, hidden, cotangent, small, lse, tokens, tabs, wout, attall, qkv, mixed, mland, ghalf, grecv, uhalf, unear,
        dhalf, wqkv, n1,
    )
    part = qkv_bias.shape[1]
    bias = bias[0].reshape(3, width)
    qkvb_grad = lax.dynamic_slice_in_dim(bias, d * part, part, 1)
    return (
        layer_output, token_gradient, qkvw_grad, qkvb_grad, outw_grad, gains[0], gains[1],
        gatew_grad, upw_grad, downw_grad, gains[2], gains[3],
    )


def solution(mesh):
    placed = (
        P(("dp", "tensor"), None),
        P(None, "dp", "tensor"),
        P(None, ("tensor", "dp")),
        P("tensor", "dp"),
        P("dp"),
        P("dp"),
        P("dp", "tensor"),
        P("dp", "tensor"),
        P("tensor", "dp"),
        P("dp"),
        P("dp"),
        P(("dp", "tensor"), None),
    )
    return jax.shard_map(
        fast if dict(mesh.shape) == {"dp": 8, "tensor": 4} else local,
        mesh=mesh,
        in_specs=placed,
        out_specs=(
            P(("dp", "tensor"), None),
            P(("dp", "tensor"), None),
            P(None, "dp", "tensor"),
            P(None, ("tensor", "dp")),
            P("tensor", "dp"),
            P("dp"),
            P("dp"),
            P("dp", "tensor"),
            P("dp", "tensor"),
            P("tensor", "dp"),
            P("dp"),
            P("dp"),
        ),
        check_vma=False,
    )
```

```python
import functools

import jax
import jax.numpy as jnp
import numpy as np
from jax import lax
from jax.experimental import pallas as pl
from jax.experimental.pallas import tpu as pltpu
from jax.sharding import PartitionSpec as P

MESH = pl.DeviceIdType.MESH
HEAD_DIM = 64
ROT = 16
BF = jnp.bfloat16
F32 = jnp.float32
VMEM_LIMIT = 56 * 1024 * 1024
ANY = pl.BlockSpec(memory_space=pl.ANY)
INV = pl.BlockSpec(memory_space=pltpu.VMEM)


def nt(a, b):
    return lax.dot_general(a, b, (((1,), (1,)), ((), ())), preferred_element_type=F32)


def tn(a, b):
    return lax.dot_general(a, b, (((0,), (0,)), ((), ())), preferred_element_type=F32)


def nn(a, b):
    return jnp.dot(a, b, preferred_element_type=F32)


def spans(total, step):
    return [(i, min(step, total - i)) for i in range(0, total, step)]


def place():
    d = lax.axis_index("dp")
    z = lax.axis_index("tensor")
    dy = 4 * (1 - 2 * lax.div(d, 4))
    dx = 2 * (1 - 2 * lax.rem(lax.div(d, 2), 2))
    dc = 1 - 2 * lax.rem(d, 2)
    return d, z, (0, dc, dx, dx + dc, dy, dy + dc, dy + dx, dy + dx + dc)


def send(src, dst, ssem, rsem, d, z):
    return pltpu.make_async_remote_copy(
        src_ref=src, dst_ref=dst, send_sem=ssem, recv_sem=rsem, device_id=(d, z), device_id_type=MESH
    )


def greet(d, z, flips, line, plane):
    barrier = pltpu.get_barrier_semaphore()
    for k in range(1, line):
        pl.semaphore_signal(
            barrier, inc=1, device_id=(d, lax.rem(z + k, line)), device_id_type=MESH
        )
    for r in plane:
        pl.semaphore_signal(barrier, inc=1, device_id=(d + flips[r], z), device_id_type=MESH)
    pl.semaphore_wait(barrier, line - 1 + len(plane))


class LineGather:
    def __init__(self, view, chunks, d, z, line, send_sems, recv_sems):
        self.view, self.chunks, self.d, self.z, self.line = view, chunks, d, z, line
        self.ss, self.rs = send_sems, recv_sems

    def copy(self, s, h, way, src=None):
        ref = self.view(s, h)
        return send(
            ref if src is None else src, ref, self.ss.at[way, s, h], self.rs.at[s, h],
            self.d, self.z + (1 if way == 0 else -1),
        )

    def start(self, h, src=None):
        pl.when(self.z < self.line - 1)(lambda: self.copy(self.z, h, 0, src).start())
        pl.when(self.z > 0)(lambda: self.copy(self.z, h, 1, src).start())

    def step(self, k, h, forward=True):
        z, line = self.z, self.line

        @pl.when(z - k >= 0)
        def _():
            self.copy(z - k, h, 0).wait_recv()
            if forward:
                pl.when(z < line - 1)(lambda: self.copy(z - k, h, 0).start())

        @pl.when(z + k < line)
        def _():
            self.copy(z + k, h, 1).wait_recv()
            if forward:
                pl.when(z > 0)(lambda: self.copy(z + k, h, 1).start())

    def finish(self, first=0, last=None):
        z, line = self.z, self.line
        for k in range(first, line if last is None else last):
            for h in range(self.chunks):
                pl.when((z - k >= 0) & (z < line - 1))(lambda: self.copy(z - k, h, 0).wait_send())
                pl.when((z + k < line) & (z > 0))(lambda: self.copy(z + k, h, 1).wait_send())


class PlaneGather:
    def __init__(self, src, view, d, z, flips, send_sems, recv_sems):
        self.src, self.view, self.d, self.z, self.flips = src, view, d, z, flips
        self.ss, self.rs = send_sems, recv_sems
        self.half = src.shape[0] // 2

    def copy(self, key):
        d, f = self.d, self.flips
        block, to, part = {
            1: (0, 1, None), 2: (0, 2, None), 4: (0, 4, None), 3: (2, 1, None), 5: (4, 1, None),
            6: (2, 4, 0), 7: (4, 2, 1), 8: (6, 1, 0), 9: (6, 1, 1),
        }[key]
        dst = self.view(d + f[block])
        src = self.src if block == 0 else dst
        if part is not None:
            at = pl.ds(part * self.half, self.half)
            src, dst = src.at[at], dst.at[at]
        return send(src, dst, self.ss.at[key], self.rs.at[key], d + f[to], self.z)

    def start(self):
        for key in (4, 2, 1):
            self.copy(key).start()

    def relay(self):
        for key, onward in ((2, (6, 3)), (4, (7, 5))):
            self.copy(key).wait_recv()
            for to in onward:
                self.copy(to).start()

    def pass_on(self):
        for key, onward in ((6, 8), (7, 9)):
            self.copy(key).wait_recv()
            self.copy(onward).start()

    def arrive(self):
        for key in (1, 3, 5, 8, 9):
            self.copy(key).wait_recv()

    def finish(self):
        for key in range(1, 10):
            self.copy(key).wait_send()


def arrival(z, i):
    orders = ((0, 1, 2, 3), (1, 0, 2, 3), (2, 3, 1, 0), (3, 2, 1, 0))
    codes = [sum(s * 4**j for j, s in enumerate(o)) for o in orders]
    code = jnp.where(
        z == 0, codes[0], jnp.where(z == 1, codes[1], jnp.where(z == 2, codes[2], codes[3]))
    )
    power = jnp.where(i == 0, 1, jnp.where(i == 1, 4, jnp.where(i == 2, 16, 64)))
    return lax.rem(lax.div(code, power), 4)


def turn(u, cos, sin, sign=1.0):
    low = lax.rem(lax.broadcasted_iota(jnp.int32, (1, 128), 1), HEAD_DIM) < ROT // 2
    moved = jnp.where(low, pltpu.roll(u, 128 - ROT // 2, 1), pltpu.roll(u, ROT // 2, 1)) * sin
    return u * cos + moved if sign > 0 else u * cos - moved


def attention_kernel(
    tok, cot, wq, ow, gw, uw, dw, smalls, cos, sin,
    cotnear, n1, qkv, lse_t, attall, wqkv, small_sum, wout, n2, hidden, wgate, wup, wdown,
    xbuf, n1buf, wbuf, qbuf, attv, wz, wo, acc, smbuf, lse,
    tss, trs, css, crs, ass, ars, mss, mrs, yss, yrs, pss, prs, local,
):
    rows, model = tok.shape
    width = wq.shape[2]
    pairs = width // 128
    line = 4
    d, z, flips = place()
    greet(d, z, flips, line, range(1, 8))

    tok_in = pltpu.make_async_copy(tok, xbuf.at[z], local.at[0])
    tok_in.start()
    depth = wq.shape[1]

    def wblock(i):
        return wbuf.at[pl.ds(pl.multiple_of(i * depth, 256), depth), :]

    w_in = [
        pltpu.make_async_copy(wq.at[j], wblock(d).at[:, pl.ds(j * width, width)], local.at[(2, 1, 13)[j]])
        for j in range(3)
    ]
    for copy in w_in:
        copy.start()
    tall = ow.shape[0]

    def oview(s, h):
        return wz.at[pl.ds(pl.multiple_of(s * tall, tall), tall)]

    def oblock(i):
        return wo.at[:, pl.ds(pl.multiple_of(i * depth, 256), depth)]

    o_in = pltpu.make_async_copy(ow, oview(z, 0), local.at[14])
    o_in.start()
    outs_z = LineGather(oview, 1, d, z, line, yss, yrs)
    small_copies = [
        send(smalls, smbuf.at[r], mss.at[r], mrs.at[r], d + flips[r], z) for r in range(1, 8)
    ]
    for copy in small_copies:
        copy.start()
    tall_block = dw.shape[1]

    def rows_of(ref, i):
        return ref.at[pl.ds(pl.multiple_of(i * depth, 256), depth)]

    def columns_of(ref, i):
        return ref.at[:, pl.ds(pl.multiple_of(i * tall_block, 256), tall_block)]

    planes = [
        PlaneGather(src, view, d, z, flips, pss.at[i], prs.at[i])
        for i, (src, view) in enumerate((
            (wblock(d), wblock),
            (wz, oblock),
            (gw, lambda i: rows_of(wgate, i)),
            (uw, lambda i: rows_of(wup, i)),
            (dw, lambda i: columns_of(wdown, i)),
        ))
    ]
    qkv_plane, out_plane, gate_plane, up_plane, down_plane = planes
    keep_own = [
        pltpu.make_async_copy(gw, rows_of(wgate, d), local.at[10]),
        pltpu.make_async_copy(uw, rows_of(wup, d), local.at[11]),
        pltpu.make_async_copy(dw, columns_of(wdown, d), local.at[12]),
    ]
    for copy in keep_own:
        copy.start()
    half = rows // 2

    def tview(s, h):
        return xbuf.at[s, pl.ds(h * half, half)]

    def cview(s, h):
        return cotnear.at[s, pl.ds(h * half, half)]

    def aview(s, h):
        return attv.at[:, pl.ds(pl.multiple_of(s * width + h * 128, 128), 128)]

    toks = LineGather(tview, 2, d, z, line, tss, trs)
    cots = LineGather(cview, 2, d, z, line, css, crs)
    atts = LineGather(aview, pairs, d, z, line, ass, ars)
    tok_in.wait()
    for h in range(2):
        toks.start(h)
    for copy in w_in:
        copy.wait()
    qkv_plane.start()
    for copy in small_copies:
        copy.wait()
    total = smalls[...].astype(F32)
    for r in range(1, 8):
        total = total + smbuf[r].astype(F32)
    small_sum[...] = total

    def normalise(s):
        piece = 32

        @pl.loop(0, rows // piece)
        def _(i):
            at = pl.ds(pl.multiple_of(i * piece, piece), piece)
            x = xbuf[s, at, :].astype(F32)
            centred = x - jnp.mean(x, -1, keepdims=True)
            spread = jnp.mean(centred * centred, -1, keepdims=True)
            n = centred * lax.rsqrt(spread + 1e-05) * small_sum[0:1, :] + small_sum[1:2, :]
            n1buf[pl.ds(pl.multiple_of(s * rows + i * piece, piece), piece), :] = n.astype(BF)

    def project(s):
        at = pl.ds(pl.multiple_of(s * rows, rows), rows)
        for j in range(3):
            cols = pl.ds(j * width, width)
            pre = nn(n1buf[at, :], wbuf[:, cols]) + small_sum[4:5, cols]
            for p in range(pairs):
                part = pre[:, p * 128 : (p + 1) * 128]
                if j < 2:
                    part = turn(part, cos[at, :], sin[at, :])
                qbuf[j, p, at, :] = part.astype(BF)

    normalise(z)
    for h in range(2):
        toks.step(1, h)
    qkv_plane.relay()
    gate_plane.start()
    normalise(arrival(z, 1))
    qkv_plane.pass_on()
    for h in range(2):
        toks.step(2, h)
    normalise(arrival(z, 2))
    gate_plane.relay()
    qkv_plane.arrive()

    @pl.loop(0, line)
    def _(i):
        s = arrival(z, i)

        @pl.when(i == line - 1)
        def _():
            gate_plane.pass_on()
            up_plane.start()
            o_in.wait()
            outs_z.start(0)
            for h in range(2):
                toks.step(3, h)
            normalise(s)

        project(s)

    o_own = pltpu.make_async_copy(wz, oblock(d), local.at[15])
    outs = [
        pltpu.make_async_copy(n1buf, n1, local.at[3]),
        pltpu.make_async_copy(wbuf, wqkv, local.at[4]),
        pltpu.make_async_copy(qbuf, qkv, local.at[5]),
    ]
    for copy in outs:
        copy.start()

    lanes = lax.broadcasted_iota(jnp.int32, (1, 128), 1)
    first = lanes < 64
    lse[...] = jnp.zeros_like(lse)
    length = rows * line

    def attend(p):
        for qi in range(line):
            count = (qi + 1) * rows
            at = pl.ds(qi * rows, rows)
            q = qbuf[0, p, at, :] * BF(HEAD_DIM**-0.5)
            k = qbuf[1, p, pl.ds(0, count), :]
            v = qbuf[2, p, pl.ds(0, count), :]
            row = lax.broadcasted_iota(jnp.int32, (rows, count), 0) + qi * rows
            col = lax.broadcasted_iota(jnp.int32, (rows, count), 1)
            keep = row >= col
            results = []
            stats = lse[at, :]
            for a in range(2):
                mine = first if a == 0 else ~first
                s = nt(jnp.where(mine, q, BF(0)), k)
                s = jnp.where(keep, s, -1e30)
                most = jnp.max(s, -1, keepdims=True)
                e = jnp.exp(s - most)
                total = jnp.sum(e, -1, keepdims=True)
                results.append(nn(e.astype(BF), v) / total)
                stats = jnp.where(lanes == 2 * p + a, most + jnp.log(total), stats)
            lse[at, :] = stats
            attv[at, pl.ds(pl.multiple_of(z * width + p * 128, 128), 128)] = jnp.where(
                first, results[0], results[1]
            ).astype(BF)

    @pl.loop(0, pairs)
    def _(p):
        attend(p)
        atts.start(p)
        for k in range(1, line):
            pl.when(p == k - 1)(lambda: outs_z.step(k, 0))

        @pl.when(p == line - 2)
        def _():
            up_plane.relay()
            out_plane.start()
            o_own.start()

    lse_t[...] = lse[...].T
    for p in range(pairs):
        atts.step(1, p)
    up_plane.pass_on()
    out_plane.relay()
    down_plane.start()
    for p in range(pairs):
        atts.step(2, p)
    out_plane.pass_on()
    o_own.wait()
    out_plane.arrive()
    keep_wo = pltpu.make_async_copy(wo, wout, local.at[6])
    keep_wo.start()

    def project_out(s, at, lo, size):
        heads = pl.ds(pl.multiple_of(s * width, width), width)
        return nn(attv[at, heads], wo[heads, pl.ds(lo, size)])

    for i in range(line - 1):
        s = arrival(z, i)

        @pl.loop(0, line)
        def _(r):
            at = pl.ds(pl.multiple_of(r * rows, rows), rows)
            for lo, size in spans(model, 512):
                base = xbuf[r, :, pl.ds(lo, size)].astype(F32) if i == 0 else acc[at, pl.ds(lo, size)]
                acc[at, pl.ds(lo, size)] = base + project_out(s, at, lo, size)

        if i == 1:
            down_plane.relay()
    for copy in outs:
        copy.wait()
    for p in range(pairs):
        atts.step(3, p)
    cots.start(0, cot.at[pl.ds(0, half)])
    keep_att = pltpu.make_async_copy(attv, attall, local.at[7])
    keep_att.start()
    last = arrival(z, line - 1)

    @pl.loop(0, line)
    def _(r):
        at = pl.ds(pl.multiple_of(r * rows, rows), rows)
        for lo, size in spans(model, 512):
            acc[at, pl.ds(lo, size)] += project_out(last, at, lo, size)

        @pl.loop(0, rows // 32)
        def _(i):
            piece = pl.ds(pl.multiple_of(r * rows + i * 32, 32), 32)
            x = acc[piece, :]
            centred = x - jnp.mean(x, -1, keepdims=True)
            spread = jnp.mean(centred * centred, -1, keepdims=True)
            n = centred * lax.rsqrt(spread + 1e-05) * small_sum[2:3, :] + small_sum[3:4, :]
            n1buf[piece, :] = n.astype(BF)

    keep = [
        pltpu.make_async_copy(n1buf, n2, local.at[8]),
        pltpu.make_async_copy(acc.at[pl.ds(pl.multiple_of(z * rows, rows), rows)], hidden, local.at[9]),
        keep_wo, keep_att,
    ]
    for copy in keep[:2]:
        copy.start()
    down_plane.pass_on()
    for gather in (toks, atts, outs_z):
        gather.finish()
    cots.step(1, 0, forward=False)
    pl.when(z < line - 1)(lambda: cots.copy(z, 0, 0).wait_send())
    pl.when(z > 0)(lambda: cots.copy(z, 0, 1).wait_send())
    for plane in (gate_plane, up_plane, down_plane):
        plane.arrive()
    for plane in planes:
        plane.finish()
    for copy in keep_own:
        copy.wait()
    for copy in keep:
        copy.wait()


def attention_forward(tok, cot, wq, ow, gw, uw, dw, smalls, tabs):
    rows, model = tok.shape
    line = 4
    length = rows * line
    _, depth, width = wq.shape
    pairs = width // 128
    dp = model // depth
    hidden = gw.shape[1]
    sds = jax.ShapeDtypeStruct
    return pl.pallas_call(
        attention_kernel,
        out_shape=(
            sds((line, rows, model), BF), sds((length, model), BF),
            sds((3, pairs, length, 128), BF), sds((128, length), F32), sds((length, model), BF),
            sds((model, 3 * width), BF), sds((16, model), F32),
            sds((model, model), BF), sds((length, model), BF), sds((rows, model), F32),
            sds((model, hidden), BF), sds((model, hidden), BF), sds((hidden, model), BF),
        ),
        in_specs=[ANY] * 7 + [INV] * 3,
        out_specs=(ANY, ANY, ANY, INV, ANY, ANY, INV) + (ANY,) * 6,
        scratch_shapes=[
            pltpu.VMEM((line, rows, model), BF),
            pltpu.VMEM((length, model), BF),
            pltpu.VMEM((model, 3 * width), BF),
            pltpu.VMEM((3, pairs, length, 128), BF),
            pltpu.VMEM((length, model), BF),
            pltpu.VMEM((model, depth), BF),
            pltpu.VMEM((model, model), BF),
            pltpu.VMEM((length, model), F32),
            pltpu.VMEM((dp, 16, model), BF),
            pltpu.VMEM((length, 128), F32),
            pltpu.SemaphoreType.DMA((2, line, 2)),
            pltpu.SemaphoreType.DMA((line, 2)),
            pltpu.SemaphoreType.DMA((2, line, 2)),
            pltpu.SemaphoreType.DMA((line, 2)),
            pltpu.SemaphoreType.DMA((2, line, pairs)),
            pltpu.SemaphoreType.DMA((line, pairs)),
            pltpu.SemaphoreType.DMA((8,)),
            pltpu.SemaphoreType.DMA((8,)),
            pltpu.SemaphoreType.DMA((2, line, 1)),
            pltpu.SemaphoreType.DMA((line, 1)),
            pltpu.SemaphoreType.DMA((5, 10)),
            pltpu.SemaphoreType.DMA((5, 10)),
            pltpu.SemaphoreType.DMA((16,)),
        ],
        compiler_params=pltpu.CompilerParams(
            collective_id=1, has_side_effects=True, vmem_limit_bytes=VMEM_LIMIT
        ),
        cost_estimate=pl.CostEstimate(flops=2 * 10**11, bytes_accessed=10**8, transcendentals=0),
        name="attention_forward",
    )(tok, cot, wq, ow, gw, uw, dw, smalls, *tabs)


def apply_layer_norm(value, norm_scale, norm_bias):
    centered_input = value - jnp.mean(value, -1, keepdims=True)
    spread = jnp.mean(centered_input * centered_input, -1, keepdims=True)
    inverse_deviation = lax.rsqrt(spread + 1e-05)
    standardized_input = centered_input * inverse_deviation
    return (
        standardized_input * norm_scale.astype(jnp.float32) + norm_bias.astype(jnp.float32),
        standardized_input,
        inverse_deviation,
    )


def layer_norm_backward(output_gradient, standardized_input, inverse_deviation, norm_scale):
    scaled_gradient = output_gradient * norm_scale.astype(jnp.float32)
    return inverse_deviation * (
        scaled_gradient
        - jnp.mean(scaled_gradient, -1, keepdims=True)
        - standardized_input * jnp.mean(scaled_gradient * standardized_input, -1, keepdims=True)
    )


def tables(length):
    positions = jnp.arange(length, dtype=jnp.float32)
    freqs = 10000.0 ** (-jnp.arange(0, ROT, 2, dtype=jnp.float32) / ROT)
    angles = positions[:, None] * freqs[None, :]
    angles = jnp.concatenate([angles, angles], -1)
    return (jnp.cos(angles), jnp.sin(angles))


def rotate(heads, cosine, sine):
    half = ROT // 2
    part = heads[..., :ROT]
    turned = jnp.concatenate([-part[..., half:], part[..., :half]], -1)
    moved = part * cosine[:, None, :] + turned * sine[:, None, :]
    return jnp.concatenate([moved, heads[..., ROT:]], -1)


def unrotate(output_gradient, cosine, sine):
    half = ROT // 2
    part = output_gradient[..., :ROT]
    scaled_gradient = part * sine[:, None, :]
    back = jnp.concatenate([scaled_gradient[..., half:], -scaled_gradient[..., :half]], -1)
    moved = part * cosine[:, None, :] + back
    return jnp.concatenate([moved, output_gradient[..., ROT:]], -1)


def attn_params(qkv_weight, qkv_bias, out_weight, norm1_gain, norm1_shift):
    return (
        lax.all_gather(qkv_weight, "dp", axis=1, tiled=True),
        lax.all_gather(qkv_bias, "dp", axis=1, tiled=True),
        lax.all_gather(out_weight, "dp", axis=1, tiled=True),
        lax.all_gather(norm1_gain, "dp", axis=0, tiled=True),
        lax.all_gather(norm1_shift, "dp", axis=0, tiled=True),
    )


def mlp_params(gate_weight, up_weight, down_weight, norm2_gain, norm2_shift):
    return (
        lax.all_gather(gate_weight, "dp", axis=0, tiled=True),
        lax.all_gather(up_weight, "dp", axis=0, tiled=True),
        lax.all_gather(down_weight, "dp", axis=1, tiled=True),
        lax.all_gather(norm2_gain, "dp", axis=0, tiled=True),
        lax.all_gather(norm2_shift, "dp", axis=0, tiled=True),
    )


def gather_rows(rows):
    return lax.all_gather(rows, "tensor", axis=0, tiled=True)


def sum_rows(partial_value):
    return lax.psum_scatter(
        partial_value.astype(jnp.bfloat16), "tensor", scatter_dimension=0, tiled=True
    ).astype(jnp.float32)


def gather_grads(rows):
    return lax.all_gather(rows, "tensor", axis=0, tiled=True)


def sum_grads(partial_value):
    return lax.psum_scatter(
        partial_value.astype(jnp.bfloat16), "tensor", scatter_dimension=0, tiled=True
    ).astype(jnp.float32)


def local(
    tokens,
    qkv_weight,
    qkv_bias,
    out_weight,
    norm1_gain,
    norm1_shift,
    gate_weight,
    up_weight,
    down_weight,
    norm2_gain,
    norm2_shift,
    cotangent,
):
    scale = HEAD_DIM ** (-0.5)
    input_rows = tokens.astype(jnp.float32)
    wqkv, bqkv, wout, first_norm_scale, first_norm_bias = attn_params(
        qkv_weight, qkv_bias, out_weight, norm1_gain, norm1_shift
    )
    first_normed_rows, first_standardized, first_inverse_deviation = apply_layer_norm(
        input_rows, first_norm_scale, first_norm_bias
    )
    rows1 = gather_rows(first_normed_rows.astype(jnp.bfloat16))
    length = rows1.shape[0]
    width = wqkv.shape[2]
    local_heads = width // HEAD_DIM
    pre = (
        jnp.einsum("sd,jdc->jsc", rows1, wqkv, preferred_element_type=jnp.float32)
        + bqkv.astype(jnp.float32)[:, None, :]
    )
    cosine, sine = tables(length)
    query = rotate(pre[0].reshape(length, local_heads, HEAD_DIM), cosine, sine).astype(jnp.bfloat16)
    keys = rotate(pre[1].reshape(length, local_heads, HEAD_DIM), cosine, sine).astype(jnp.bfloat16)
    values = pre[2].reshape(length, local_heads, HEAD_DIM).astype(jnp.bfloat16)
    block = min(length, 512)
    count = length // block
    cols = jnp.arange(length, dtype=jnp.int32)

    def block_probs(qblock, start):
        scores = (
            jnp.einsum("qhd,khd->hqk", qblock, keys, preferred_element_type=jnp.float32) * scale
        )
        rows = start + jnp.arange(block, dtype=jnp.int32)
        keep = rows[:, None] >= cols[None, :]
        return jnp.where(keep[None], scores, -1e30)

    def forward_block(index):
        qblock = lax.dynamic_slice_in_dim(query, index * block, block, 0)
        scores = block_probs(qblock, index * block)
        most = jnp.max(scores, -1, keepdims=True)
        expo = jnp.exp(scores - most)
        total = jnp.sum(expo, -1, keepdims=True)
        probs = (expo / total).astype(jnp.bfloat16)
        out_block = jnp.einsum("hqk,khd->qhd", probs, values, preferred_element_type=jnp.float32)
        return (out_block.astype(jnp.bfloat16), most[..., 0] + jnp.log(total[..., 0]))

    indices = jnp.arange(count, dtype=jnp.int32)
    out_blocks, lse = lax.map(forward_block, indices)
    attended = out_blocks.reshape(length, width)
    branch = jnp.dot(attended, wout, preferred_element_type=jnp.float32)
    hidden_state = input_rows + sum_rows(branch)
    wgate, wup, wdown, second_norm_scale, second_norm_bias = mlp_params(
        gate_weight, up_weight, down_weight, norm2_gain, norm2_shift
    )
    second_normed_rows, second_standardized, second_inverse_deviation = apply_layer_norm(
        hidden_state, second_norm_scale, second_norm_bias
    )
    rows2 = gather_rows(second_normed_rows.astype(jnp.bfloat16))
    gate = jnp.dot(rows2, wgate, preferred_element_type=jnp.float32)
    up = jnp.dot(rows2, wup, preferred_element_type=jnp.float32)
    sigma = jax.nn.sigmoid(gate)
    silu = gate * sigma
    act = (silu * up).astype(jnp.bfloat16)
    mixed = sum_rows(jnp.dot(act, wdown, preferred_element_type=jnp.float32))
    layer_output = (hidden_state + mixed).astype(jnp.bfloat16)
    wgate, wup, wdown, second_norm_scale, second_norm_bias = mlp_params(
        gate_weight, up_weight, down_weight, norm2_gain, norm2_shift
    )
    incoming_gradient = cotangent.astype(jnp.float32)
    down_rows = gather_grads(cotangent)
    down_grad = jnp.einsum("sf,sd->fd", act, down_rows, preferred_element_type=jnp.float32)
    dact = jnp.einsum("sd,fd->sf", down_rows, wdown, preferred_element_type=jnp.float32)
    dgate = (dact * up * (sigma * (1.0 + gate * (1.0 - sigma)))).astype(jnp.bfloat16)
    dup = (dact * silu).astype(jnp.bfloat16)
    gate_grad = jnp.einsum("sd,sf->df", rows2, dgate, preferred_element_type=jnp.float32)
    up_grad = jnp.einsum("sd,sf->df", rows2, dup, preferred_element_type=jnp.float32)
    second_norm_gradient = jnp.einsum(
        "sf,df->sd", dgate, wgate, preferred_element_type=jnp.float32
    ) + jnp.einsum("sf,df->sd", dup, wup, preferred_element_type=jnp.float32)
    second_norm_gradient = sum_grads(second_norm_gradient)
    second_scale_partial = jnp.sum(second_norm_gradient * second_standardized, 0)
    shift2_part = jnp.sum(second_norm_gradient, 0)
    hidden_gradient = incoming_gradient + layer_norm_backward(
        second_norm_gradient, second_standardized, second_inverse_deviation, second_norm_scale
    )
    gatew_grad, upw_grad, downw_grad, gain2_total, shift2_total = (
        lax.psum_scatter(
            gate_grad.astype(jnp.bfloat16), "dp", scatter_dimension=0, tiled=True
        ).astype(jnp.float32),
        lax.psum_scatter(
            up_grad.astype(jnp.bfloat16), "dp", scatter_dimension=0, tiled=True
        ).astype(jnp.float32),
        lax.psum_scatter(
            down_grad.astype(jnp.bfloat16), "dp", scatter_dimension=1, tiled=True
        ).astype(jnp.float32),
        lax.psum_scatter(
            second_scale_partial.astype(jnp.bfloat16), "dp", scatter_dimension=0, tiled=True
        ).astype(jnp.float32),
        lax.psum_scatter(
            shift2_part.astype(jnp.bfloat16), "dp", scatter_dimension=0, tiled=True
        ).astype(jnp.float32),
    )
    wqkv, bqkv, wout, first_norm_scale, first_norm_bias = attn_params(
        qkv_weight, qkv_bias, out_weight, norm1_gain, norm1_shift
    )
    branch_rows = gather_grads(hidden_gradient.astype(jnp.bfloat16))
    out_grad = jnp.einsum("sc,sd->cd", attended, branch_rows, preferred_element_type=jnp.float32)
    dattended = jnp.einsum(
        "sd,cd->sc", branch_rows, wout, preferred_element_type=jnp.float32
    ).astype(jnp.bfloat16)
    dattended = dattended.reshape(length, local_heads, HEAD_DIM)

    def backward_block(carry, item):
        dkeys, dvalues = carry
        index, block_lse = item
        qblock = lax.dynamic_slice_in_dim(query, index * block, block, 0)
        dblock = lax.dynamic_slice_in_dim(dattended, index * block, block, 0)
        scores = block_probs(qblock, index * block)
        probs = jnp.exp(scores - block_lse[..., None])
        probs16 = probs.astype(jnp.bfloat16)
        dvalues = dvalues + jnp.einsum(
            "hqk,qhd->khd", probs16, dblock, preferred_element_type=jnp.float32
        )
        dprobs = jnp.einsum("qhd,khd->hqk", dblock, values, preferred_element_type=jnp.float32)
        inner = jnp.sum(dprobs * probs, -1, keepdims=True)
        dscores = (probs * (dprobs - inner)).astype(jnp.bfloat16)
        dquery = (
            jnp.einsum("hqk,khd->qhd", dscores, keys, preferred_element_type=jnp.float32) * scale
        )
        dkeys = (
            dkeys
            + jnp.einsum("hqk,qhd->khd", dscores, qblock, preferred_element_type=jnp.float32)
            * scale
        )
        return ((dkeys, dvalues), dquery)

    empty = jnp.zeros((length, local_heads, HEAD_DIM), jnp.float32)
    (dkeys, dvalues), dquery = lax.scan(backward_block, (empty, empty), (indices, lse))
    dquery = dquery.reshape(length, local_heads, HEAD_DIM)
    dpre = jnp.stack(
        [
            unrotate(dquery, cosine, sine).reshape(length, width),
            unrotate(dkeys, cosine, sine).reshape(length, width),
            dvalues.reshape(length, width),
        ],
        0,
    ).astype(jnp.bfloat16)
    qkv_grad = jnp.einsum("sd,jsc->jdc", rows1, dpre, preferred_element_type=jnp.float32)
    bias_grad = jnp.sum(dpre, axis=1, dtype=jnp.float32)
    first_norm_gradient = sum_grads(
        jnp.einsum("jsc,jdc->sd", dpre, wqkv, preferred_element_type=jnp.float32)
    )
    first_scale_partial = jnp.sum(first_norm_gradient * first_standardized, 0)
    shift1_part = jnp.sum(first_norm_gradient, 0)
    token_gradient = (
        hidden_gradient
        + layer_norm_backward(
            first_norm_gradient, first_standardized, first_inverse_deviation, first_norm_scale
        )
    ).astype(jnp.bfloat16)
    qkvw_grad, qkvb_grad, outw_grad, gain1_total, shift1_total = (
        lax.psum_scatter(
            qkv_grad.astype(jnp.bfloat16), "dp", scatter_dimension=1, tiled=True
        ).astype(jnp.float32),
        lax.psum_scatter(
            bias_grad.astype(jnp.bfloat16), "dp", scatter_dimension=1, tiled=True
        ).astype(jnp.float32),
        lax.psum_scatter(
            out_grad.astype(jnp.bfloat16), "dp", scatter_dimension=1, tiled=True
        ).astype(jnp.float32),
        lax.psum_scatter(
            first_scale_partial.astype(jnp.bfloat16), "dp", scatter_dimension=0, tiled=True
        ).astype(jnp.float32),
        lax.psum_scatter(
            shift1_part.astype(jnp.bfloat16), "dp", scatter_dimension=0, tiled=True
        ).astype(jnp.float32),
    )
    gain1_grad, shift1_grad, gain2_grad, shift2_grad = lax.psum(
        (gain1_total, shift1_total, gain2_total, shift2_total), "tensor"
    )
    return (
        layer_output,
        token_gradient,
        qkvw_grad,
        qkvb_grad,
        outw_grad,
        gain1_grad,
        shift1_grad,
        gatew_grad,
        upw_grad,
        downw_grad,
        gain2_grad,
        shift2_grad,
    )


class LineScatter:
    def __init__(self, part, slot, chunks, d, z, line, send_sems, recv_sems):
        self.part, self.slot, self.chunks, self.d, self.z, self.line = part, slot, chunks, d, z, line
        self.ss, self.rs = send_sems, recv_sems

    def copy(self, s, h, way, target, place):
        return send(
            self.part(s, h), self.slot(place, h), self.ss.at[s, h], self.rs.at[place, h], self.d, target
        )

    def right(self, s, h):
        return self.copy(s, h, 0, self.z + 1, s)

    def left(self, s, h):
        return self.copy(s, h, 1, self.z - 1, jnp.where(self.z - 1 == s, self.line, s))

    def head(self, s):
        z, line = self.z, self.line
        for h in range(self.chunks):
            pl.when((z == 0) & (s > 0))(lambda: self.right(s, h).start())
            pl.when((z == line - 1) & (s < z))(lambda: self.left(s, h).start())

    def add(self, s, h):
        part = self.part(s, h)
        part[...] = (part[...].astype(F32) + self.slot(s, h)[...].astype(F32)).astype(BF)

    def relay(self, t):
        z, line = self.z, self.line
        up = line - 1 - t + z
        down = t - (line - 1 - z)
        for h in range(self.chunks):
            @pl.when((z > 0) & (up > z) & (up < line))
            def _():
                self.copy(z, h, 0, z, up).wait_recv()
                self.add(up, h)
                self.right(up, h).start()

            @pl.when((z < line - 1) & (down >= 0) & (down < z))
            def _():
                self.copy(z, h, 0, z, down).wait_recv()
                self.add(down, h)
                self.left(down, h).start()

    def arrive(self, h):
        z, line = self.z, self.line
        pl.when(z > 0)(lambda: self.copy(z, h, 0, z, z).wait_recv())
        pl.when(z < line - 1)(lambda: self.copy(z, h, 0, z, line).wait_recv())

    def total(self, h, rows):
        z = self.z
        return (
            self.part(z, h)[rows].astype(F32)
            + self.slot(z, h)[rows].astype(F32)
            + self.slot(self.line, h)[rows].astype(F32)
        )

    def finish(self):
        z = self.z
        for s in range(self.line):
            for h in range(self.chunks):
                pl.when(z != s)(lambda: self.copy(s, h, 0, z, s).wait_send())


def far_first(z, i):
    orders = ((3, 2, 1, 0), (3, 0, 2, 1), (0, 3, 1, 2), (0, 1, 2, 3))
    codes = [sum(s * 4**j for j, s in enumerate(o)) for o in orders]
    code = jnp.where(
        z == 0, codes[0], jnp.where(z == 1, codes[1], jnp.where(z == 2, codes[2], codes[3]))
    )
    power = jnp.where(i == 0, 1, jnp.where(i == 1, 4, jnp.where(i == 2, 16, 64)))
    return lax.rem(lax.div(code, power), 4)


class PlaneSum:
    def __init__(self, half, recv, d, z, flips, send_sems, recv_sems):
        self.half, self.recv, self.d, self.z, self.flips = half, recv, d, z, flips
        self.ss, self.rs = send_sems, recv_sems

    def copy(self, r):
        to, slot = self.d + self.flips[r], (r // 2 - 1) % self.recv.shape[0]
        return send(self.half.at[lax.div(to, 2)], self.recv.at[slot], self.ss.at[slot], self.rs.at[slot], to, self.z)

    def start(self, *which):
        for r in which:
            self.copy(r).start()

    def wait(self, *which):
        for r in which:
            self.copy(r).wait()


def mlp_kernel(
    n2, cot, cotnear, wgate, wup, wdown,
    dn2, mixed, mland, gex, uex, dex, ghalf, uhalf, dhalf, grecv, unear,
    nbuf, cbuf, gw, uw, dw, act, act_t, dga, dup, part, slots, mixbuf, wide, tall, wide_in, tall_in,
    ss, rs, css, crs, lss, lrs, local, lsem, mixsem, outsem, exs, exr, gss, grs, uss, urs,
):
    line = 4
    rows = n2.shape[0] // line
    model = n2.shape[1]
    hidden = wgate.shape[1]
    d, z, flips = place()
    greet(d, z, flips, line, (1, 2, 4, 6))
    core = lax.rem(d, 2)
    chip = lax.div(d, 2)
    parts = spans(hidden, 512)

    def rows_in(i):
        at = pl.ds(pl.multiple_of(far_first(z, i) * rows, rows), rows)
        return pltpu.make_async_copy(n2.at[at], nbuf.at[at], lsem.at[i])

    def columns_in(c):
        cols = pl.ds(*parts[c])
        return [
            pltpu.make_async_copy(wgate.at[:, cols], gw.at[:, cols], lsem.at[line + c]),
            pltpu.make_async_copy(wup.at[:, cols], uw.at[:, cols], lsem.at[line + len(parts) + c]),
        ]

    down_in = pltpu.make_async_copy(wdown, dw, lsem.at[line + 2 * len(parts)])
    first = [rows_in(jnp.int32(0))] + columns_in(0)
    for copy in first:
        copy.start()
    half = rows // 2
    scatter = LineScatter(
        lambda s, h: part.at[s, pl.ds(h * half, half)],
        lambda i, h: slots.at[i, pl.ds(h * half, half)],
        2, d, z, line, ss, rs,
    )
    pl.when(z == 0)(lambda: slots.__setitem__((0,), jnp.zeros((rows, model), BF)))
    pl.when(z == line - 1)(lambda: slots.__setitem__((line,), jnp.zeros((rows, model), BF)))
    cots = LineGather(
        lambda s, h: cbuf.at[pl.ds(pl.multiple_of(s * rows + h * half, half), half)], 2, d, z, line, css, crs
    )

    own_cot = pltpu.make_async_copy(cot, cbuf.at[pl.ds(pl.multiple_of(z * rows, rows), rows)], local.at[5])
    @pl.when((z > 0) & (z < line - 1))
    def _():
        cots.copy(z - 1, 0, 0, cotnear.at[z - 1, pl.ds(0, half)]).start()
        cots.copy(z + 1, 0, 1, cotnear.at[z + 1, pl.ds(0, half)]).start()

    cots.start(1, cot.at[pl.ds(half, half)])

    def first_half(s, k):
        return pltpu.make_async_copy(
            cotnear.at[s, pl.ds(0, half)], cbuf.at[pl.ds(pl.multiple_of(s * rows, rows), half)], local.at[8 + k]
        )

    for copy in first:
        copy.wait()
    for c in range(1, len(parts)):
        for copy in columns_in(c):
            copy.start()
    down_in.start()
    for i in range(1, line):
        rows_in(jnp.int32(i)).start()
    own_cot.start()
    pl.when(z > 0)(lambda: first_half(z - 1, 0).start())
    pl.when(z < line - 1)(lambda: first_half(z + 1, 1).start())

    def mixed_out(i):
        s = far_first(z, i)
        at = pl.ds(pl.multiple_of(s * rows, rows), rows)
        return pltpu.make_async_copy(mixbuf.at[lax.rem(i, 2)], mixed.at[at], mixsem.at[lax.rem(i, 2)])

    def mixed_ahead(i):
        at = pl.ds(pl.multiple_of(far_first(z, i) * rows, rows), rows)
        to = jnp.where(z == 0, 1, line - 2)
        return send(mixed.at[at], mland.at[i], lss.at[i], lrs.at[i], d, to)

    at_end = (z == 0) | (z == line - 1)

    @pl.loop(0, line)
    def _(i):
        s = far_first(z, i)
        at = pl.ds(pl.multiple_of(s * rows, rows), rows)
        pl.when(i > 0)(lambda: rows_in(i).wait())
        for c, (lo, size) in enumerate(parts):
            cols = pl.ds(lo, size)
            if c > 0:
                @pl.when(i == 0)
                def _():
                    for copy in columns_in(c):
                        copy.wait()

            gate = nn(nbuf[at, :], gw[:, cols])
            up = nn(nbuf[at, :], uw[:, cols])
            sigma = lax.logistic(gate)
            silu = gate * sigma
            value = (silu * up).astype(BF)
            act[:, cols] = value
            act_t[cols, at] = value.T
            dga[at, cols] = (up * (sigma * (1.0 + gate * (1.0 - sigma)))).astype(BF)
            dup[at, cols] = silu.astype(BF)
        pl.when(i == 0)(lambda: down_in.wait())
        for lo, size in spans(model, 512):
            mixbuf[lax.rem(i, 2), :, pl.ds(lo, size)] = nn(act[...], dw[:, pl.ds(lo, size)]).astype(BF)
        mixed_out(i).start()
        mixed_out(i).wait()
        pl.when(at_end & (i < 2))(lambda: mixed_ahead(i).start())
        pl.when(i == 0)(lambda: cots.step(2, 0))
        pl.when(i == 1)(lambda: cots.step(1, 1))
        pl.when(i == 2)(lambda: cots.step(2, 1))

    def add_mixed(s, slot, send_slot, to, lands):
        at = pl.ds(pl.multiple_of(s * rows, rows), rows)
        ins = [
            pltpu.make_async_copy(mixed.at[at], mixbuf.at[0], mixsem.at[0]),
            pltpu.make_async_copy(mland.at[slot], mixbuf.at[1], mixsem.at[1]),
        ]
        for copy in ins:
            copy.start()
        for copy in ins:
            copy.wait()

        @pl.loop(0, rows // 32)
        def _(i):
            piece = pl.ds(pl.multiple_of(i * 32, 32), 32)
            mixbuf[0, piece, :] = (mixbuf[0, piece, :].astype(F32) + mixbuf[1, piece, :].astype(F32)).astype(BF)

        back = pltpu.make_async_copy(mixbuf.at[0], mixed.at[at], mixsem.at[0])
        back.start()
        back.wait()
        send(mixed.at[at], mland.at[lands], lss.at[send_slot], lrs.at[lands], d, to).start()

    def landing(slot, send_slot):
        return send(mland.at[slot], mland.at[slot], lss.at[send_slot], lrs.at[slot], d, z)

    other = line - 1 - z
    edge = jnp.where(z == 1, 0, line - 1)

    def mixed_on(i):
        @pl.when(~at_end)
        def _():
            landing(i, i).wait_recv()
            add_mixed(line - 1 - edge if i == 0 else other, i, 2 + i, other, 2 + i)

    def mixed_relay():
        @pl.when(~at_end)
        def _():
            landing(2, 2).wait_recv()
            add_mixed(edge, 2, 0, edge, 3)

    mixed_on(0)
    own_cot.wait()

    @pl.loop(0, line)
    def _(i):
        @pl.when(i == 1)
        def _():
            pl.when(z > 0)(lambda: first_half(z - 1, 0).wait())
            pl.when(z < line - 1)(lambda: first_half(z + 1, 1).wait())
            for h in range(2):
                cots.step(3, h)

        pl.when(i == line - 1)(lambda: mixed_on(1))
        s = far_first(z, lax.rem(i + line - 1, line))
        at = pl.ds(pl.multiple_of(s * rows, rows), rows)
        for lo, size in spans(hidden, 512):
            cols = pl.ds(lo, size)
            dact = nt(cbuf[at, :], dw[cols, :])
            dga[at, cols] = (dact * dga[at, cols].astype(F32)).astype(BF)
            dup[at, cols] = (dact * dup[at, cols].astype(F32)).astype(BF)
        for lo, size in spans(model, 512):
            cols = pl.ds(lo, size)
            part[s, :, cols] = (nt(dga[at, :], gw[cols, :]) + nt(dup[at, :], uw[cols, :])).astype(BF)
        scatter.head(s)

    blocks = model // rows // 2

    def exchanged(m):
        outs = (ghalf, uhalf, dhalf)
        exes = (gex, uex, dex)
        stage = tall if m == 2 else wide
        stage_in = tall_in if m == 2 else wide_in

        def block(t):
            cols = pl.ds(pl.multiple_of(t * rows, rows), rows)
            if m == 2:
                return lambda lo, size: nn(act_t[pl.ds(lo, size), :], cbuf[:, cols])
            right = dga if m == 0 else dup
            return lambda lo, size: tn(nbuf[:, cols], right[:, pl.ds(lo, size)])

        def piece(ref, lo, size):
            return ref.at[pl.ds(lo, size), :] if m == 2 else ref.at[:, pl.ds(lo, size)]

        def away(k):
            slot = lax.rem(k, 2)
            return send(stage.at[slot], exes[m].at[k], exs.at[m, k], exr.at[m, k], d + flips[1], z)

        @pl.loop(0, blocks)
        def _(k):
            slot = lax.rem(k, 2)
            pl.when(k >= 2)(lambda: away(k - 2).wait_send())
            make = block(2 * k + 1 - core)
            for lo, size in spans(hidden, 512):
                piece(stage.at[slot], lo, size)[...] = make(lo, size).astype(BF)
            away(k).start()

        away(blocks - 2).wait_send()
        away(blocks - 1).wait_send()

        def chip_at(j):
            return lax.rem(chip + 1 + j, blocks)

        def store(j):
            slot = lax.rem(j, 2)
            return pltpu.make_async_copy(stage.at[slot], outs[m].at[chip_at(j)], outsem.at[slot])

        def onward(j):
            k = chip_at(j)
            return send(ghalf.at[k], grecv.at[blocks - 2 - j], gss.at[j], grs.at[blocks - 2 - j], 2 * k + core, z)

        @pl.loop(0, blocks)
        def _(j):
            slot = lax.rem(j, 2)
            k = chip_at(j)

            @pl.when(j >= 2)
            def _():
                store(j - 2).wait()
                if m == 0:
                    onward(j - 2).start()

            away(k).wait_recv()
            fetch = pltpu.make_async_copy(exes[m].at[k], stage_in, local.at[4])
            fetch.start()
            fetch.wait()
            make = block(2 * k + core)
            for lo, size in spans(hidden, 512):
                piece(stage.at[slot], lo, size)[...] = (
                    make(lo, size) + piece(stage_in, lo, size)[...].astype(F32)
                ).astype(BF)
            store(j).start()

        for j in (blocks - 2, blocks - 1):
            store(j).wait()
            if m == 0 and j < blocks - 1:
                onward(j).start()
        return onward

    onward = exchanged(0)
    scatter.relay(1)
    mixed_relay()

    exchanged(1)
    ups = PlaneSum(uhalf, unear, d, z, flips, uss, urs)
    ups.start(2, 4)
    scatter.relay(2)
    exchanged(2)
    for h in range(2):
        scatter.arrive(h)

        @pl.loop(0, half // 32)
        def _(i):
            rows_at = pl.ds(pl.multiple_of(i * 32, 32), 32)
            dn2[pl.ds(pl.multiple_of(h * half + i * 32, 32), 32), :] = scatter.total(h, rows_at)

    scatter.finish()
    for i in range(2):
        pl.when(at_end)(lambda: mixed_ahead(i).wait_send())
    for i in (0, 2, 3):
        pl.when(~at_end)(lambda: landing(3, i).wait_send())
    landing(3, 3).wait_recv()
    for k, h in ((0, 1), (1, 0), (1, 1), (2, 0), (2, 1)):
        pl.when((z - k >= 0) & (z < line - 1))(lambda: cots.copy(z - k, h, 0).wait_send())
        pl.when((z + k < line) & (z > 0))(lambda: cots.copy(z + k, h, 1).wait_send())
    for j in range(blocks - 1):
        onward(j).wait()
    ups.wait(2, 4)


def mlp(n2, cot, cotnear, wgate, wup, wdown):
    length, model = n2.shape
    hidden = wgate.shape[1]
    line = 4
    rows = length // line
    blocks = model // rows // 2
    sds = jax.ShapeDtypeStruct
    wide = sds((blocks, rows, hidden), BF)
    tall = sds((blocks, hidden, rows), BF)
    return pl.pallas_call(
        mlp_kernel,
        out_shape=(
            sds((rows, model), F32), sds((length, model), BF), sds((4, rows, model), BF),
            wide, wide, tall, wide, wide, tall, sds((blocks - 1, rows, hidden), BF), sds((2, rows, hidden), BF),
        ),
        in_specs=[ANY] * 6,
        out_specs=(INV,) + (ANY,) * 10,
        scratch_shapes=[
            pltpu.VMEM((length, model), BF),
            pltpu.VMEM((length, model), BF),
            pltpu.VMEM((model, hidden), BF),
            pltpu.VMEM((model, hidden), BF),
            pltpu.VMEM((hidden, model), BF),
            pltpu.VMEM((rows, hidden), BF),
            pltpu.VMEM((hidden, length), BF),
            pltpu.VMEM((length, hidden), BF),
            pltpu.VMEM((length, hidden), BF),
            pltpu.VMEM((line, rows, model), BF),
            pltpu.VMEM((line + 1, rows, model), BF),
            pltpu.VMEM((2, rows, model), BF),
            pltpu.VMEM((2, rows, hidden), BF),
            pltpu.VMEM((2, hidden, rows), BF),
            pltpu.VMEM((rows, hidden), BF),
            pltpu.VMEM((hidden, rows), BF),
            pltpu.SemaphoreType.DMA((line, 2)),
            pltpu.SemaphoreType.DMA((line + 1, 2)),
            pltpu.SemaphoreType.DMA((2, line, 2)),
            pltpu.SemaphoreType.DMA((line, 2)),
            pltpu.SemaphoreType.DMA((4,)),
            pltpu.SemaphoreType.DMA((4,)),
            pltpu.SemaphoreType.DMA((10,)),
            pltpu.SemaphoreType.DMA((line + 1 + 2 * len(spans(hidden, 512)),)),
            pltpu.SemaphoreType.DMA((2,)),
            pltpu.SemaphoreType.DMA((2,)),
            pltpu.SemaphoreType.DMA((3, blocks)),
            pltpu.SemaphoreType.DMA((3, blocks)),
            pltpu.SemaphoreType.DMA((blocks,)),
            pltpu.SemaphoreType.DMA((blocks,)),
            pltpu.SemaphoreType.DMA((2,)),
            pltpu.SemaphoreType.DMA((2,)),
        ],
        compiler_params=pltpu.CompilerParams(
            collective_id=2, has_side_effects=True, vmem_limit_bytes=62 * 1024 * 1024
        ),
        cost_estimate=pl.CostEstimate(flops=10**11, bytes_accessed=10**8, transcendentals=0),
        name="mlp",
    )(n2, cot, cotnear, wgate, wup, wdown)


def norm_parts(x):
    centred = x - jnp.mean(x, -1, keepdims=True)
    inverse = lax.rsqrt(jnp.mean(centred * centred, -1, keepdims=True) + 1e-05)
    return centred * inverse, inverse


def norm_back(grad, standard, inverse, gain):
    scaled = grad * gain
    return inverse * (
        scaled
        - jnp.mean(scaled, -1, keepdims=True)
        - standard * jnp.mean(scaled * standard, -1, keepdims=True)
    )


def each_piece(rows, piece, body):
    @pl.loop(0, rows // piece)
    def _(i):
        body(pl.ds(pl.multiple_of(i * piece, piece), piece))


class PlaneChain:
    def __init__(self, half, recv, mid, d, z, flips, send_sems, recv_sems):
        self.half, self.recv, self.mid, self.d, self.z, self.flips = half, recv, mid, d, z, flips
        self.ss, self.rs = send_sems, recv_sems
        self.rows = half.shape[1] // 2

    def block(self, r):
        return lax.div(self.d + self.flips[r], 2)

    def copy(self, key):
        block, over, part = ((6, 2, 0), (6, 4, 1), (4, 4, 1), (2, 2, 0), (4, 4, 0), (2, 2, 1))[key]
        at = pl.ds(part * self.rows, self.rows)
        dst = self.mid.at[key] if key < 2 else self.recv.at[0 if over == 2 else 1, at]
        return send(
            self.half.at[self.block(block), at], dst, self.ss.at[key], self.rs.at[key], self.d + self.flips[over], self.z
        )

    def start(self):
        for key in range(4):
            self.copy(key).start()

    def relay(self):
        for key, block, part in ((0, 4, 0), (1, 2, 1)):
            self.copy(key).wait_recv()
            k = self.block(block)
            piece = min(self.rows, 128)

            @pl.loop(0, self.rows // piece)
            def _(i):
                at = pl.ds(pl.multiple_of(part * self.rows + i * piece, piece), piece)
                mid = self.mid[key, pl.ds(pl.multiple_of(i * piece, piece), piece), :]
                self.half[k, at, :] = (self.half[k, at, :].astype(F32) + mid.astype(F32)).astype(BF)

            self.copy(key + 4).start()

    def arrive(self):
        for key in range(2, 6):
            self.copy(key).wait_recv()

    def total(self, at):
        return (
            self.half[(self.block(0),) + at].astype(F32)
            + self.recv[(0,) + at].astype(F32)
            + self.recv[(1,) + at].astype(F32)
        )

    def finish(self):
        for key in range(6):
            self.copy(key).wait_send()


class BlockSum:
    def __init__(self, own, recv, bufs, stage, out, in_sems, out_sems):
        self.ins = [own] + recv
        self.bufs, self.stage, self.out, self.in_sems, self.out_sems = bufs, stage, out, in_sems, out_sems

    def copies(self):
        return [pltpu.make_async_copy(a, b, self.in_sems.at[i]) for i, (a, b) in enumerate(zip(self.ins, self.bufs))]

    def fetch(self):
        for copy in self.copies():
            copy.start()

    def store(self, i):
        rows = self.stage.shape[1]
        at = pl.ds(pl.multiple_of(i * rows, rows), rows)
        return pltpu.make_async_copy(self.stage.at[lax.rem(i, 2)], self.out.at[at], self.out_sems.at[lax.rem(i, 2)])

    def add(self):
        for copy in self.copies():
            copy.wait()
        rows = self.stage.shape[1]
        pieces = self.out.shape[0] // rows
        small = 32

        @pl.loop(0, pieces)
        def _(i):
            pl.when(i >= 2)(lambda: self.store(i - 2).wait())

            @pl.loop(0, rows // small)
            def _(j):
                at = pl.ds(pl.multiple_of(i * rows + j * small, small), small)
                total = self.bufs[0][at, :].astype(F32)
                for buf in self.bufs[1:]:
                    total = total + buf[at, :].astype(F32)
                self.stage[lax.rem(i, 2), pl.ds(pl.multiple_of(j * small, small), small), :] = total

            self.store(i).start()

        self.store(jnp.int32(pieces - 2)).wait()
        self.store(jnp.int32(pieces - 1)).wait()


def attention_back_kernel(
    hid, small, lse_t, cos, sin, dn2, cot, tok, wout, attall, qkv, mixed, mland, ghalf, grecv, uhalf, unear, dhalf, wqkv, n1,
    tgrad, ograd, gains, bout, lay, ggrad, ugrad, dgrad, qgrad, urecv, drecv, oex, qex,
    wo, da, dhid, attr, att_t, attc, qbuf, dsend, datt, part, slots, marr, ofull, osum, orecv, omid, ozr,
    dq, dpre, nbuf, qstage, qfetch, qsum, qrecv, qmid, wide_sum, tall_sum, qtotal, sums, zsums, dsums, bsums,
    mss, mrs, ass, ars, oss, ors, pss, prs, uss, urs, zss, zrs,
    ss, rs, xss, xrs, qss, qrs, dss, drs, yss, yrs, gss, grs, bss, brs, local, tsem, fsem, gsem,
):
    line = 4
    rows, model = hid.shape
    length = rows * line
    width = attc.shape[1]
    pairs = width // 128
    blocks = model // rows // 2
    half = rows // 2
    d, z, flips = place()
    greet(d, z, flips, line, range(1, 8))
    core = lax.rem(d, 2)
    ups = PlaneSum(uhalf, urecv, d, z, flips, uss, urs)
    downs = PlaneSum(dhalf, drecv, d, z, flips, dss, drs)
    loads = [
        pltpu.make_async_copy(wout, wo, local.at[4]),
        pltpu.make_async_copy(attall.at[pl.ds(pl.multiple_of(z * rows, rows), rows)], attr, local.at[5]),
        pltpu.make_async_copy(attall.at[:, pl.ds(pl.multiple_of(z * width, width), width)], attc, local.at[6]),
        pltpu.make_async_copy(qkv, qbuf, local.at[7]),
    ]
    rows_in = [pltpu.make_async_copy(dn2, dhid, local.at[11]), pltpu.make_async_copy(cot, da, local.at[12])]
    for copy in rows_in:
        copy.start()

    at_end = (z == 0) | (z == line - 1)
    inner = jnp.where(z == 0, 1, line - 2)

    def mixed_last(h):
        at = pl.ds(pl.multiple_of(inner * rows + h * half, half), half)
        return send(mixed.at[at], marr.at[pl.ds(h * half, half)], mss.at[h], mrs.at[h], d, inner)

    pl.when(at_end)(lambda: mixed_last(0).start())
    pl.when(at_end)(lambda: marr.__setitem__(Ellipsis, jnp.zeros((rows, model), BF)))
    for copy in loads:
        copy.start()
    ups.start(6)
    downs.start(2, 4, 6)

    def chain(part, slots, send_sems, recv_sems):
        pl.when(z == 0)(lambda: slots.__setitem__((0,), jnp.zeros((rows, model), BF)))
        pl.when(z == line - 1)(lambda: slots.__setitem__((line,), jnp.zeros((rows, model), BF)))
        return LineScatter(
            lambda s, h: part.at[s, pl.ds(h * half, half)],
            lambda i, h: slots.at[i, pl.ds(h * half, half)],
            2, d, z, line, send_sems, recv_sems,
        )

    for copy in rows_in:
        copy.wait()
    sums[...] = jnp.zeros_like(sums)

    def back(at):
        grad = dhid[at, :]
        standard, inverse = norm_parts(hid[at, :])
        sums[2:3, :] += jnp.sum(grad * standard, 0, keepdims=True)
        sums[3:4, :] += jnp.sum(grad, 0, keepdims=True)
        total = da[at, :].astype(F32) + norm_back(grad, standard, inverse, small[2:3, :])
        dhid[at, :] = total
        da[at, :] = total.astype(BF)

    each_piece(rows, 32, back)
    for copy in loads:
        copy.wait()

    def away(k, p):
        to = lax.rem(z + k, line)
        cols = pl.ds(p * 128, 128)
        return send(
            dsend.at[to, :, cols], datt.at[pl.ds(pl.multiple_of(z * rows, rows), rows), cols],
            ass.at[k, p], ars.at[z, p], d, to,
        )

    def taken(k, p):
        frm = lax.rem(z + k, line)
        cols = pl.ds(pl.multiple_of(p * 128, 128), 128)
        return send(
            dsend.at[frm, :, cols], datt.at[pl.ds(pl.multiple_of(frm * rows, rows), rows), cols],
            ass.at[k, p], ars.at[frm, p], d, frm,
        )

    @pl.loop(1, line + 1)
    def _(k):
        to = lax.rem(z + k, line)
        dsend[to] = nt(da[...], wo[pl.ds(pl.multiple_of(to * width, width), width), :]).astype(BF)

    for p in range(pairs):
        for k in range(1, line):
            away(k, p).start()
    pl.when(at_end)(lambda: mixed_last(1).start())
    weights_in = pltpu.make_async_copy(wqkv, wo.at[:, pl.ds(0, 3 * width)], local.at[4])
    weights_in.start()
    datt[pl.ds(pl.multiple_of(z * rows, rows), rows), :] = dsend[z]
    for lo, size in spans(model, 512):
        att_t[pl.ds(lo, size), :] = attr[:, pl.ds(lo, size)].T
    tok_in = pltpu.make_async_copy(tok, attr, local.at[6])
    tok_in.start()

    def oblock(t):
        return nn(att_t[...], da[:, pl.ds(pl.multiple_of(t * rows, rows), rows)])

    def ostage(k):
        return wo.at[:, pl.ds(pl.multiple_of(3 * width + lax.rem(k, 2) * rows, rows), rows)]

    def oacross(k):
        return send(ostage(k), oex.at[k], oss.at[k], ors.at[k], d + flips[1], z)

    @pl.loop(0, blocks)
    def _(k):
        pl.when(k >= 2)(lambda: oacross(k - 2).wait_send())
        ostage(k)[...] = oblock(2 * k + 1 - core).astype(BF)
        oacross(k).start()

    lanes = lax.broadcasted_iota(jnp.int32, (1, 128), 1)
    mine = (lanes < 64, lanes >= 64)
    which = lax.broadcasted_iota(jnp.int32, (16, 128), 0)
    lane16 = lax.broadcasted_iota(jnp.int32, (16, 128), 1)
    pick = jnp.where(which == lax.div(lane16, 64), 1.0, 0.0).astype(BF)
    scale = HEAD_DIM**-0.5

    def zaway(k):
        to = lax.rem(z + k, line)
        return send(
            ofull.at[pl.ds(pl.multiple_of(to * width, width), width)], ozr.at[k - 1], zss.at[k], zrs.at[k - 1], d, to
        )

    def plane_total():
        oplanes.arrive()

        def add(at):
            ofull[at, :] = oplanes.total((at, slice(None))).astype(BF)

        each_piece(model, 256, add)
        for k in range(1, line):
            zaway(k).start()

    def back_pair(p):
        cols = pl.ds(pl.multiple_of(p * 128, 128), 128)
        do = datt[:, cols]
        prod = do.astype(F32) * attc[:, cols].astype(F32)
        high = prod.astype(BF)
        inner = nt(pick, high) + nt(pick, (prod - high.astype(F32)).astype(BF))
        q = qbuf[0, p] * BF(scale)
        dq[...] = jnp.zeros_like(dq)
        for kj in range(line):
            at = pl.ds(kj * rows, rows)
            lo, count = kj * rows, length - kj * rows
            k, v = qbuf[1, p, at, :], qbuf[2, p, at, :]
            row = lax.broadcasted_iota(jnp.int32, (rows, count), 0)
            col = lax.broadcasted_iota(jnp.int32, (rows, count), 1)
            keep = col >= row
            dk = jnp.zeros((rows, 128), F32)
            dv = jnp.zeros((rows, 128), F32)
            for a in range(2):
                km, vm = jnp.where(mine[a], k, BF(0)), jnp.where(mine[a], v, BF(0))
                qm, dm = jnp.where(mine[a], q[lo:], BF(0)), jnp.where(mine[a], do[lo:], BF(0))
                s = jnp.where(keep, nt(km, q[lo:]), -1e30)
                probs = jnp.exp(s - lse_t[pl.ds(2 * p + a, 1), pl.ds(lo, count)])
                dv += nn(probs.astype(BF), dm)
                dprobs = nt(vm, do[lo:])
                ds = (probs * (dprobs - inner[a : a + 1, lo:])).astype(BF)
                dk += nn(ds, qm)
                dq[pl.ds(lo, count), :] += tn(ds, km)
            dk = turn(dk, cos[at, :], sin[at, :], -1.0)
            dpre[at, pl.ds(pl.multiple_of(width + p * 128, 128), 128)] = dk.astype(BF)
            dpre[at, pl.ds(pl.multiple_of(2 * width + p * 128, 128), 128)] = dv.astype(BF)
        dpre[:, cols] = turn(dq[...] * scale, cos[...], sin[...], -1.0).astype(BF)

    @pl.loop(0, pairs)
    def _(p):
        for k in range(1, line):
            taken(k, p).wait_recv()
        back_pair(p)


    oacross(blocks - 2).wait_send()
    oacross(blocks - 1).wait_send()
    weights_in.wait()
    chains = chain(part, slots, ss, rs)

    @pl.loop(0, line)
    def _(i):
        s = far_first(z, i)
        at = pl.ds(pl.multiple_of(s * rows, rows), rows)
        for lo, size in spans(model, 512):
            part[s, :, pl.ds(lo, size)] = nt(dpre[at, :], wo[pl.ds(lo, size), pl.ds(0, 3 * width)]).astype(BF)
        chains.head(s)

    hidden = uhalf.shape[2]
    chip = lax.div(d, 2)

    def wide(i):
        return [wo.at[pl.ds((i + k) * rows, rows), pl.ds(0, hidden)] for k in range(blocks)]

    gate_sum = BlockSum(ghalf.at[chip], [grecv.at[k] for k in range(blocks - 1)], wide(0), wide_sum, ggrad, fsem.at[0], gsem)
    up_sum = BlockSum(uhalf.at[chip], [unear.at[0], unear.at[1], urecv.at[0]], wide(blocks), wide_sum, ugrad, fsem.at[1], gsem)
    tall = [osum.at[k, pl.ds(0, hidden)] for k in range(blocks)]
    down_sum = BlockSum(dhalf.at[chip], [drecv.at[k] for k in range(blocks - 1)], tall, tall_sum, dgrad, fsem.at[2], gsem)
    gate_sum.fetch()
    mixed_in = [
        pltpu.make_async_copy(mixed.at[pl.ds(pl.multiple_of(z * rows, rows), rows)], wo.at[pl.ds(4 * rows, rows)], local.at[0]),
        pltpu.make_async_copy(mland.at[3], wo.at[pl.ds(5 * rows, rows)], local.at[1]),
    ]
    for copy in mixed_in:
        copy.start()

    oplanes = PlaneChain(osum, orecv, omid, d, z, flips, pss, prs)

    @pl.loop(0, blocks)
    def _(k):
        oacross(k).wait_recv()
        fetch = pltpu.make_async_copy(oex.at[k], ofull, local.at[8])
        fetch.start()
        fetch.wait()
        osum[k] = (oblock(2 * k + core) + ofull[...].astype(F32)).astype(BF)

    oplanes.start()
    def tile_in(i):
        t = 2 * lax.rem(i, blocks) + jnp.where(i < blocks, 1 - core, core)
        cols = pl.ds(pl.multiple_of(t * rows, rows), rows)
        return pltpu.make_async_copy(n1.at[:, cols], nbuf.at[lax.rem(i, 2)], tsem.at[lax.rem(i, 2)])

    def qblock(i):
        tile_in(i).wait()
        pl.when(i < 2 * blocks - 1)(lambda: tile_in(i + 1).start())
        return lambda lo, size: tn(nbuf[lax.rem(i, 2)], dpre[:, pl.ds(lo, size)])

    tile_in(jnp.int32(0)).start()

    def qacross(k):
        return send(qstage.at[lax.rem(k, 2)], qex.at[k], xss.at[k], xrs.at[k], d + flips[1], z)

    @pl.loop(0, blocks)
    def _(k):
        pl.when(k >= 2)(lambda: qacross(k - 2).wait_send())
        make = qblock(k)
        for lo, size in spans(3 * width, 512):
            qstage[lax.rem(k, 2), :, pl.ds(lo, size)] = make(lo, size).astype(BF)
        qacross(k).start()

    chains.relay(1)
    qplanes = PlaneChain(qsum, qrecv, qmid, d, z, flips, qss, qrs)

    @pl.loop(0, blocks)
    def _(k):
        qacross(k).wait_recv()
        fetch = pltpu.make_async_copy(qex.at[k], qfetch, local.at[8])
        fetch.start()
        fetch.wait()
        make = qblock(k + blocks)
        for lo, size in spans(3 * width, 512):
            qsum[k, :, pl.ds(lo, size)] = (make(lo, size) + qfetch[:, pl.ds(lo, size)].astype(F32)).astype(BF)

    qplanes.start()
    oplanes.relay()
    for h in range(2):
        pl.when(~at_end)(lambda: mixed_last(h).wait_recv())

    for copy in mixed_in:
        copy.wait()

    @pl.loop(0, rows // 32)
    def _(i):
        at = pl.ds(pl.multiple_of(i * 32, 32), 32)
        total = marr[at, :].astype(F32)
        for k in (4, 5):
            total = total + wo[pl.ds(pl.multiple_of(k * rows + i * 32, 32), 32), :].astype(F32)
        da[at, :] = (hid[at, :] + total).astype(BF)

    lay_out = pltpu.make_async_copy(da, lay, local.at[0])
    lay_out.start()
    bsums[0] = jnp.zeros(bsums.shape[1:], F32)

    def bias(at):
        bsums[0, 0:1, :] += jnp.sum(dpre[at, :].astype(F32), 0, keepdims=True)

    each_piece(length, 64, bias)

    def bcopy(r):
        return send(bsums.at[0], bsums.at[r], bss.at[r], brs.at[r], d + flips[r], z)

    for r in range(1, 8):
        bcopy(r).start()
    ups.wait(6)
    up_sum.fetch()
    gate_sum.add()
    chains.relay(2)
    qplanes.relay()
    up_sum.add()
    plane_total()
    total = jnp.zeros(bout.shape, F32)
    for r in range(8):
        if r:
            bcopy(r).wait()
        total = total + bsums[r]
    bout[...] = total
    tok_in.wait()
    for h in range(2):
        chains.arrive(h)
        @pl.loop(0, half // 32)
        def _(i):
            at = pl.ds(pl.multiple_of(h * half + i * 32, 32), 32)
            grad = chains.total(h, pl.ds(pl.multiple_of(i * 32, 32), 32))
            standard, inverse = norm_parts(attr[at, :].astype(F32))
            sums[0:1, :] += jnp.sum(grad * standard, 0, keepdims=True)
            sums[1:2, :] += jnp.sum(grad, 0, keepdims=True)
            tgrad[at, :] = (dhid[at, :] + norm_back(grad, standard, inverse, small[0:1, :])).astype(BF)

    depth = gains.shape[1]

    def columns(i):
        return sums.at[:, pl.ds(pl.multiple_of(i * depth, 256), depth)]

    def dcopy(r):
        return send(columns(d + flips[r]), dsums.at[r], gss.at[r], grs.at[r], d + flips[r], z)

    def zcopy(k):
        return send(zsums.at[0], zsums.at[k], yss.at[k], yrs.at[k], d, lax.rem(z + k, line))

    for r in range(1, 8):
        dcopy(r).start()
    qplanes.arrive()
    piece = qtotal.shape[1]

    @pl.loop(0, rows // piece)
    def _(i):
        at = pl.ds(pl.multiple_of(i * piece, piece), piece)
        for j in range(3):
            qtotal[j] = qplanes.total((at, pl.ds(j * width, width)))
        back = pltpu.make_async_copy(qtotal, qgrad.at[:, at], local.at[1])
        back.start()
        back.wait()

    oplanes.finish()
    downs.wait(2, 4, 6)
    down_sum.fetch()
    total = columns(d)[...]
    for r in range(1, 8):
        dcopy(r).wait()
        total = total + dsums[r]
    zsums[0] = total
    for k in range(1, line):
        zcopy(k).start()
    down_sum.add()
    for k in range(1, line):
        zcopy(k).wait()
        total = total + zsums[k]
    gains[...] = total
    total = ofull[pl.ds(pl.multiple_of(z * width, width), width), :].astype(F32)
    for k in range(1, line):
        zaway(k).wait()
        total = total + ozr[k - 1].astype(F32)
    ograd[...] = total
    for k in range(1, line):
        for p in range(pairs):
            away(k, p).wait_send()
    qplanes.finish()
    qacross(blocks - 2).wait_send()
    qacross(blocks - 1).wait_send()
    lay_out.wait()
    for h in range(2):
        pl.when(at_end)(lambda: mixed_last(h).wait_send())
    chains.finish()


def attention_backward(dn2, hid, cot, small, lse, tok, tabs, wout, attall, qkv, mixed, mland, ghalf, grecv, uhalf, unear, dhalf, wqkv, n1):
    rows, model = hid.shape
    line = 4
    length = rows * line
    width = model // line
    pairs = width // 128
    blocks = model // rows // 2
    hidden = uhalf.shape[2]
    sds = jax.ShapeDtypeStruct
    dma = pltpu.SemaphoreType.DMA
    vmem = pltpu.VMEM
    return pl.pallas_call(
        attention_back_kernel,
        out_shape=(
            sds((rows, model), BF), sds((width, rows), F32),
            sds((8, rows), F32), sds((8, 3 * width), F32), sds((rows, model), BF),
            sds((rows, hidden), F32), sds((rows, hidden), F32), sds((hidden, rows), F32), sds((3, rows, width), F32),
            sds((1, rows, hidden), BF), sds((blocks - 1, hidden, rows), BF),
            sds((blocks, model, rows), BF), sds((blocks, rows, 3 * width), BF),
        ),
        in_specs=[INV] * 5 + [ANY] * 15,
        out_specs=(INV,) * 4 + (ANY,) * 9,
        scratch_shapes=[
            vmem((model, model), BF), vmem((rows, model), BF), vmem((rows, model), F32), vmem((rows, model), BF),
            vmem((model, rows), BF), vmem((length, width), BF), vmem((3, pairs, length, 128), BF),
            vmem((line, rows, width), BF), vmem((length, width), BF),
            vmem((line, rows, model), BF), vmem((line + 1, rows, model), BF),
            vmem((rows, model), BF),
            vmem((model, rows), BF), vmem((blocks, model, rows), BF),
            vmem((2, model, rows), BF), vmem((2, model // 2, rows), BF),
            vmem((line - 1, width, rows), BF),
            vmem((length, 128), F32), vmem((length, 3 * width), BF), vmem((2, length, rows), BF),
            vmem((2, rows, 3 * width), BF), vmem((rows, 3 * width), BF), vmem((blocks, rows, 3 * width), BF),
            vmem((2, rows, 3 * width), BF), vmem((2, rows // 2, 3 * width), BF),
            vmem((2, 64, hidden), F32), vmem((2, hidden // 4, rows), F32), vmem((3, 64, width), F32),
            vmem((8, model), F32), vmem((line, 8, rows), F32), vmem((8, 8, rows), F32), vmem((8, 8, 3 * width), F32),
            dma((2,)), dma((2,)), dma((line, pairs)), dma((line, pairs)), dma((blocks,)), dma((blocks,)),
            dma((6,)), dma((6,)), dma((3,)), dma((3,)), dma((line,)), dma((line,)),
            dma((line, 2)), dma((line + 1, 2)), dma((blocks,)), dma((blocks,)), dma((6,)), dma((6,)),
            dma((3,)), dma((3,)), dma((line,)), dma((line,)), dma((8,)), dma((8,)), dma((8,)), dma((8,)), dma((13,)), dma((2,)),
            dma((3, blocks)), dma((2,)),
        ],
        compiler_params=pltpu.CompilerParams(
            collective_id=3, has_side_effects=True, vmem_limit_bytes=63 * 1024 * 1024
        ),
        cost_estimate=pl.CostEstimate(flops=10**11, bytes_accessed=10**8, transcendentals=0),
        name="attention_backward",
    )(hid, small, lse, *tabs, dn2, cot, tok, wout, attall, qkv, mixed, mland, ghalf, grecv, uhalf, unear, dhalf, wqkv, n1)


def turn_tables(length):
    half = ROT // 2
    freqs = np.float32(10000.0) ** (-np.arange(0, ROT, 2, dtype=np.float32) / np.float32(ROT))
    angles = np.arange(length, dtype=np.float32)[:, None] * freqs[None, :]
    cos = np.ones((length, HEAD_DIM), np.float32)
    sin = np.zeros((length, HEAD_DIM), np.float32)
    cos[:, :half] = cos[:, half:ROT] = np.cos(angles)
    sin[:, half:ROT] = np.sin(angles)
    sin[:, :half] = -np.sin(angles)
    return tuple(jnp.asarray(np.tile(t, (1, 2))) for t in (cos, sin))


def pack_smalls(d, model, width, qkv_bias, *vectors):
    col = lax.broadcasted_iota(jnp.int32, (1, model), 1)
    each = vectors[0].shape[0]
    gains = jnp.stack([jnp.tile(v, model // each) for v in vectors], 0)
    gains = jnp.where(col // each == d, gains, 0)
    part = qkv_bias.shape[1]
    bias = jnp.tile(qkv_bias, (1, width // part)).reshape(1, 3 * width)
    bias = jnp.pad(bias, ((0, 0), (0, model - 3 * width)))
    bias = jnp.where(col % width // part == d, bias, 0)
    return jnp.concatenate([gains, bias, jnp.zeros((11, model), BF)], 0).astype(BF)


def fast(
    tokens, qkv_weight, qkv_bias, out_weight, norm1_gain, norm1_shift, gate_weight, up_weight,
    down_weight, norm2_gain, norm2_shift, cotangent,
):
    d = lax.axis_index("dp")
    rows, model = tokens.shape
    length = 4 * rows
    tabs = turn_tables(length)
    depth, width = qkv_weight.shape[1:]
    smalls = pack_smalls(d, model, width, qkv_bias, norm1_gain, norm1_shift, norm2_gain, norm2_shift)
    cotnear, n1, qkv, lse, attall, wqkv, small, wout, n2, hidden, wgate, wup, wdown = attention_forward(
        tokens, cotangent, qkv_weight, out_weight, gate_weight, up_weight, down_weight, smalls, tabs
    )
    dn2, mixed, mland, _, _, _, ghalf, uhalf, dhalf, grecv, unear = mlp(n2, cotangent, cotnear, wgate, wup, wdown)
    (
        token_gradient, outw_grad, gains, bias, layer_output, gatew_grad, upw_grad, downw_grad, qkvw_grad, _, _, _, _
    ) = attention_backward(
        dn2, hidden, cotangent, small, lse, tokens, tabs, wout, attall, qkv, mixed, mland, ghalf, grecv, uhalf, unear,
        dhalf, wqkv, n1,
    )
    part = qkv_bias.shape[1]
    bias = bias[0].reshape(3, width)
    qkvb_grad = lax.dynamic_slice_in_dim(bias, d * part, part, 1)
    return (
        layer_output, token_gradient, qkvw_grad, qkvb_grad, outw_grad, gains[0], gains[1],
        gatew_grad, upw_grad, downw_grad, gains[2], gains[3],
    )


def solution(mesh):
    placed = (
        P(("dp", "tensor"), None),
        P(None, "dp", "tensor"),
        P(None, ("tensor", "dp")),
        P("tensor", "dp"),
        P("dp"),
        P("dp"),
        P("dp", "tensor"),
        P("dp", "tensor"),
        P("tensor", "dp"),
        P("dp"),
        P("dp"),
        P(("dp", "tensor"), None),
    )
    return jax.shard_map(
        fast if dict(mesh.shape) == {"dp": 8, "tensor": 4} else local,
        mesh=mesh,
        in_specs=placed,
        out_specs=(
            P(("dp", "tensor"), None),
            P(("dp", "tensor"), None),
            P(None, "dp", "tensor"),
            P(None, ("tensor", "dp")),
            P("tensor", "dp"),
            P("dp"),
            P("dp"),
            P("dp", "tensor"),
            P("dp", "tensor"),
            P("tensor", "dp"),
            P("dp"),
            P("dp"),
        ),
        check_vma=False,
    )
```
